32 devices in a mesh: blk: 4 (over y, x), tile: 8 (over z, core).
Axes of the slice: x: 2, y: 2, z: 4, core: 2. Of those that a mesh axis runs over, the one named last changes fastest.
Arguments:
- qkv: bfloat16 [3, 1024, 1024], P(None, ('blk', 'tile')), may hold values from -33 to 33
- frame_clip: int32 [8], replicated, may hold values from 0 to 2, never falling along the last dimension, each value on 1 to 5 neighbouring positions
- w_out: bfloat16 [1024, 5120], P('tile'), may hold values from -0.5 to 0.5
Outputs:
- projected: bfloat16 [1024, 5120], P(('blk', 'tile'))
The draws below stay inside these ranges and needn't reach their ends.
All inputs are finite; a program needn't handle non-finite values.
Results may differ from the reference program's by a relative error of at most 0.023.
Values may be sent and summed in bfloat16 or wider, within the bound.
No kernel may reach another device: no remote copies, remote signals or barrier semaphores. Data moves between devices by JAX's collectives and lax.ppermute only.
A program may use at most 64 MiB of HBM per device.

```python
import math
import jax
import jax.numpy as jnp
import numpy as np
from jax import lax

HD = 128
D = 5120
FRB = 2
TPF = 16
CLIPS = 3
HEADS = 8
HH = 1024
TOK_DEV = 32
TOK_BLK = 256
TOKENS = 1024
FRAMES = 8
MOST = 5


def draw_qkv(key, part):
    base = jnp.clip(jax.random.normal(key, (3, TOKENS, HH), jnp.float32), -4.0, 4.0)
    return base.astype(jnp.bfloat16)


def level_of(key, extent, split, low, top_value):
    factor_of = 1.0
    for dim, blocks in split:
        draws = jax.random.uniform(jax.random.fold_in(jax.random.fold_in(key, 6), dim), (blocks,), jnp.float32, low / len(split), top_value / len(split))
        factor_of = factor_of * jnp.repeat(jnp.exp(draws), extent[dim] // blocks).reshape((-1,) + (1,) * (len(extent) - 1 - dim))
    return factor_of


def split_up(amount, total, most, lean):
    weights = [(1 << 20) // math.isqrt(grade ** lean) + 1 for grade in range(2, amount + 1)]
    surplus, given = total - most - (amount - 1), [1] * (amount - 1)
    while surplus > 0:
        candidates = [i for i in range(amount - 1) if given[i] < most]
        whole, left = sum([weights[i] for i in candidates]), surplus
        for i in candidates:
            addition = min(most - given[i], max(1, left * weights[i] // whole), surplus)
            given[i] = given[i] + addition
            surplus = surplus - addition
    return np.array([most] + given)


def ragged_sizes(key, amount, total, most, skew):
    if amount == 2:
        one = jax.random.randint(key, (), max(1, total - most), min(most, total - 1) + 1)
        return jnp.stack([one, total - one])
    lengths = jnp.asarray(split_up(amount, total, most, skew), jnp.int32)
    pairs = (amount - 1) // 2
    source_of, sink = lengths[1:1 + 2 * pairs:2], lengths[2:2 + 2 * pairs:2]
    room = jnp.minimum(source_of - 1, most - sink)
    moved = jax.random.randint(jax.random.fold_in(key, 1), (pairs,), 0, 1 << 20) % (room + 1)
    lengths = lengths.at[1:1 + 2 * pairs:2].set(source_of - moved).at[2:2 + 2 * pairs:2].set(sink + moved)
    return lengths[jax.random.permutation(jax.random.fold_in(key, 2), amount)]


def bell_draw(key, extent, deviation, limit, shards=(), kind=jnp.bfloat16):
    values = deviation * jax.random.normal(key, extent, jnp.float32)
    if shards:
        values = values * level_of(key, extent, shards, -0.22, 0.18)
    return jnp.clip(values, -limit, limit).astype(kind)


def setup_inputs(seed: int = 0) -> dict:
    splits = jax.random.split(jax.random.key(seed), 4)
    qkv = draw_qkv(jax.random.fold_in(splits[3], 71), 0)
    frame_clip = jnp.searchsorted(jnp.cumsum(ragged_sizes(splits[1], CLIPS, FRAMES, MOST, 0)), jnp.arange(FRAMES), side="right").astype(jnp.int32)
    w_out = bell_draw(splits[2], (HH, D), HD ** -0.5, 0.5, ((0, 8),))
    return dict(qkv=qkv, frame_clip=frame_clip, w_out=w_out)


def token_frames():
    rows = jnp.arange(TOKENS, dtype=jnp.int32)
    return rows // TOK_BLK * FRB + rows % TOK_DEV // TPF

def reference(qkv, frame_clip, w_out):
    clip_tok = frame_clip[token_frames()]
    scale = 1.0 / math.sqrt(HD)
    block_rows = math.gcd(TOKENS, 512)
    per_head = qkv.reshape(3, TOKENS, HEADS, HD).transpose(2, 0, 1, 3)

    def one_head(blocks):
        queries = blocks[0].reshape(TOKENS // block_rows, block_rows, HD)
        keys_h = blocks[1]
        values_h = blocks[2]
        query_clips = clip_tok.reshape(TOKENS // block_rows, block_rows)

        def one_block(pair):
            query_block, clip_block = pair
            scores = jnp.dot(query_block, keys_h.T, preferred_element_type=jnp.float32) * scale
            allowed = clip_block[:, None] == clip_tok[None, :]
            masked = jnp.where(allowed, scores, -1e+30)
            top = lax.optimization_barrier(jnp.max(masked, axis=1, keepdims=True))
            weights = jnp.where(allowed, jnp.exp(scores - top), 0.0)
            total = lax.optimization_barrier(jnp.sum(weights, axis=1, keepdims=True))
            summed = jnp.dot(weights.astype(jnp.bfloat16), values_h, preferred_element_type=jnp.float32)
            return (summed / total).astype(jnp.bfloat16)
        return lax.map(one_block, (queries, query_clips)).reshape(TOKENS, HD)
    attn = lax.map(one_head, per_head).transpose(1, 0, 2).reshape(TOKENS, HH)
    return jnp.dot(attn, w_out, preferred_element_type=jnp.float32).astype(jnp.bfloat16)
```

```python
import functools
import math

import jax
import jax.numpy as jnp
from jax import lax
from jax.experimental import pallas as pl
from jax.experimental.pallas import tpu as pltpu
from jax.sharding import Mesh
from jax.sharding import PartitionSpec as P

FRB = 2
TPF = 16
PLANE = ("blk", "core")
VMEM = pl.BlockSpec(memory_space=pltpu.VMEM)
SMEM = pl.BlockSpec(memory_space=pltpu.SMEM)
PARAMS = pltpu.CompilerParams(vmem_limit_bytes=48 * 1024 * 1024)


def pack_kernel(x_ref, out_ref):
    peers, _, width = out_ref.shape
    kinds, tok, _ = x_ref.shape
    for g in range(peers):
        for k in range(kinds):
            out_ref[g, k * tok:(k + 1) * tok, :] = x_ref[k, :, g * width:(g + 1) * width]


def pack(x, peers):
    kinds, tok, cols = x.shape
    return pl.pallas_call(
        pack_kernel,
        out_shape=jax.ShapeDtypeStruct((peers, kinds * tok, cols // peers), x.dtype),
        in_specs=[VMEM],
        out_specs=VMEM,
        compiler_params=PARAMS,
    )(x)


def clip_of(token, tok_dev, clip_ref):
    frame = token // (2 * tok_dev) * FRB + token % tok_dev // TPF
    clip = jnp.zeros_like(token)
    for f in range(clip_ref.shape[0]):
        clip = jnp.where(frame == f, clip_ref[f], clip)
    return clip


def attention_kernel(tok, head_dim, clip_ref, *refs):
    own_ref, *kv_refs, out_ref = refs
    peers, _, width = own_ref.shape
    count = peers * tok
    scale = 1.0 / math.sqrt(head_dim)
    row_clip = clip_of(lax.broadcasted_iota(jnp.int32, (count, 1), 0), tok, clip_ref)
    col_clip = clip_of(lax.broadcasted_iota(jnp.int32, (1, count), 1), tok, clip_ref)
    allowed = row_clip == col_clip
    sources = [(own_ref, tok)] + [(ref, 0) for ref in kv_refs]
    per_step = max(1, 1024 // count)
    for h in range(width // head_dim):
        cols = slice(h * head_dim, (h + 1) * head_dim)
        queries = own_ref[:, 0:tok, cols].reshape(count, head_dim)
        top = total = acc = None
        for first in range(0, len(sources), per_step):
            scores, values = [], []
            for ref, at in sources[first:first + per_step]:
                keys = ref[:, at:at + tok, cols].reshape(count, head_dim)
                values.append(ref[:, at + tok:at + 2 * tok, cols].reshape(count, head_dim))
                s = lax.dot_general(
                    queries, keys, (((1,), (1,)), ((), ())), preferred_element_type=jnp.float32
                )
                scores.append(jnp.where(allowed, s * scale, -1e30))
            new_top = functools.reduce(
                jnp.maximum, [jnp.max(s, axis=1, keepdims=True) for s in scores]
            )
            if top is not None:
                new_top = jnp.maximum(top, new_top)
                factor = jnp.exp(top - new_top)
                total, acc = total * factor, acc * factor
            top = new_top
            for s, v in zip(scores, values):
                p = jnp.where(allowed, jnp.exp(s - top), 0.0)
                part = jnp.sum(p, axis=1, keepdims=True)
                dot = jnp.dot(p.astype(jnp.bfloat16), v, preferred_element_type=jnp.float32)
                total = part if total is None else total + part
                acc = dot if acc is None else acc + dot
        out_ref[:, cols] = (acc / total).astype(out_ref.dtype)


def attention(own, others, frame_clip, tok, head_dim):
    peers, _, width = own.shape
    return pl.pallas_call(
        functools.partial(attention_kernel, tok, head_dim),
        out_shape=jax.ShapeDtypeStruct((peers * tok, width), own.dtype),
        in_specs=[SMEM] + [VMEM] * (1 + len(others)),
        out_specs=VMEM,
        compiler_params=PARAMS,
    )(frame_clip, own, *others)


def project_kernel(order_ref, attn_ref, *refs):
    *w_refs, out_ref, a_ref, w_all = refs
    peers, _, width = attn_ref.shape
    for g in range(peers):
        a_ref[:, g * width:(g + 1) * width] = attn_ref[g]
    rows = w_refs[0].shape[0]
    for i, ref in enumerate(w_refs):
        w_all[pl.ds(pl.multiple_of(order_ref[i] * rows, rows), rows), :] = ref[...]
    result = jnp.dot(a_ref[...], w_all[...], preferred_element_type=jnp.float32)
    out_ref[...] = result.astype(out_ref.dtype).reshape(out_ref.shape)


def project(attn_all, w_parts, order, tok):
    peers, count, width = attn_all.shape
    depth, cols = peers * width, w_parts[0].shape[1]
    return pl.pallas_call(
        project_kernel,
        out_shape=jax.ShapeDtypeStruct((peers, tok, cols), attn_all.dtype),
        in_specs=[SMEM] + [VMEM] * (1 + len(w_parts)),
        out_specs=VMEM,
        scratch_shapes=[
            pltpu.VMEM((count, depth), attn_all.dtype),
            pltpu.VMEM((depth, cols), attn_all.dtype),
        ],
        compiler_params=PARAMS,
    )(order, attn_all, *w_parts)


def unpack_kernel(x_ref, out_ref):
    peers, _, width = x_ref.shape
    for g in range(peers):
        out_ref[:, g * width:(g + 1) * width] = x_ref[g]


def unpack(x):
    peers, tok, width = x.shape
    return pl.pallas_call(
        unpack_kernel,
        out_shape=jax.ShapeDtypeStruct((tok, peers * width), x.dtype),
        in_specs=[VMEM],
        out_specs=VMEM,
        compiler_params=PARAMS,
    )(x)


def shift(x, axis, by):
    size = lax.axis_size(axis)
    return lax.ppermute(x, axis, [(i, (i + by) % size) for i in range(size)])


def on_device(qkv, frame_clip, w_out):
    rows, peers = lax.axis_size("row"), lax.axis_size("blk") * 2
    blk, row, core = lax.axis_index("blk"), lax.axis_index("row"), lax.axis_index("core")
    tok = qkv.shape[1]
    head_dim, model = w_out.shape
    cols = model // peers

    mine = lax.dynamic_slice(w_out, (0, (blk * 2 + core) * cols), (head_dim, cols))
    theirs = lax.dynamic_slice(w_out, (0, (blk * 2 + 1 - core) * cols), (head_dim, cols))
    got = shift(theirs, "core", 1)
    first = jnp.where(core == 0, mine, got)
    second = jnp.where(core == 0, got, mine)
    w_own = jnp.concatenate([first, second], axis=0)
    w_parts = [w_own] + [shift(w_own, "row", by) for by in range(1, rows)]
    order = jnp.stack([(row - by) % rows for by in range(rows)]).astype(jnp.int32)

    own = lax.all_to_all(pack(qkv, peers), PLANE, split_axis=0, concat_axis=0, tiled=True)
    kv = own[:, tok:]
    others = [shift(kv, "row", by) for by in range(1, rows)]
    attn = attention(own, others, frame_clip, tok, head_dim)
    attn_all = lax.all_gather(attn, PLANE, axis=0, tiled=False)
    part = project(attn_all, w_parts, order, tok)
    return unpack(lax.all_to_all(part, PLANE, split_axis=0, concat_axis=0, tiled=True))


def solution(mesh):
    blk, tile = mesh.shape["blk"], mesh.shape["tile"]
    fine = Mesh(mesh.devices.reshape(blk, tile // 2, 2), ("blk", "row", "core"))
    in_specs = (P(None, ("blk", "row", "core"), None), P(), P(("row", "core"), None))
    out_specs = P(("blk", "row", "core"), None)
    return jax.shard_map(
        on_device, mesh=fine, in_specs=in_specs, out_specs=out_specs, check_vma=False
    )
```

```python
import functools
import math

import jax
import jax.numpy as jnp
from jax import lax
from jax.experimental import pallas as pl
from jax.experimental.pallas import tpu as pltpu
from jax.sharding import Mesh
from jax.sharding import PartitionSpec as P

FRB = 2
TPF = 16
ALL = ("blk", "row", "core")
PLANE = ("blk", "core")
VMEM = pl.BlockSpec(memory_space=pltpu.VMEM)
SMEM = pl.BlockSpec(memory_space=pltpu.SMEM)
ANY = pl.BlockSpec(memory_space=pl.ANY)
PARAMS = pltpu.CompilerParams(vmem_limit_bytes=48 * 1024 * 1024)


def pack_kernel(rows, head_dim, x_ref, q_ref, kv_ref):
    peers, tok, width = q_ref.shape
    heads = width // head_dim
    for g in range(peers):
        for i in range(heads):
            head = (g // 2 * heads + i) * 2 + g % 2
            cols = slice(head * head_dim, (head + 1) * head_dim)
            at = slice(i * head_dim, (i + 1) * head_dim)
            q_ref[g, :, at] = x_ref[0, :, cols]
            for r in range(rows):
                to = (g // 2 * rows + r) * 2 + g % 2
                kv_ref[to, 0:tok, at] = x_ref[1, :, cols]
                kv_ref[to, tok:2 * tok, at] = x_ref[2, :, cols]


def pack(x, peers, rows, head_dim):
    _, tok, cols = x.shape
    width = cols // peers
    return pl.pallas_call(
        functools.partial(pack_kernel, rows, head_dim),
        out_shape=(
            jax.ShapeDtypeStruct((peers, tok, width), x.dtype),
            jax.ShapeDtypeStruct((peers * rows, 2 * tok, width), x.dtype),
        ),
        in_specs=[VMEM],
        out_specs=(VMEM, VMEM),
        compiler_params=PARAMS,
    )(x)


def clip_of(token, blk_tokens, tok_dev, clip_ref):
    frame = token // blk_tokens * FRB + token % tok_dev // TPF
    clip = jnp.zeros_like(token)
    for f in range(clip_ref.shape[0]):
        clip = jnp.where(frame == f, clip_ref[f], clip)
    return clip


def attention_kernel(tok, head_dim, clip_ref, q_ref, kv_ref, *refs):
    out_ref = refs[len(refs) // 2]
    peers, _, width = q_ref.shape
    count = peers * tok
    devices = kv_ref.shape[0]
    scale = 1.0 / math.sqrt(head_dim)
    row_clip = clip_of(
        lax.broadcasted_iota(jnp.int32, (count, 1), 0), 2 * tok, tok, clip_ref
    )
    step = min(devices, 32)
    for h in range(width // head_dim):
        cols = slice(h * head_dim, (h + 1) * head_dim)
        queries = q_ref[:, :, cols].reshape(count, head_dim)
        top = total = acc = None
        for at in range(0, devices, step):
            keys = kv_ref[at:at + step, 0:tok, cols].reshape(step * tok, head_dim)
            values = kv_ref[at:at + step, tok:2 * tok, cols].reshape(step * tok, head_dim)
            token = at * tok + lax.broadcasted_iota(jnp.int32, (1, step * tok), 1)
            col_clip = clip_of(token, devices // (peers // 2) * tok, tok, clip_ref)
            allowed = row_clip == col_clip
            s = lax.dot_general(
                queries, keys, (((1,), (1,)), ((), ())), preferred_element_type=jnp.float32
            )
            s = jnp.where(allowed, s * scale, -1e30)
            new_top = jnp.max(s, axis=1, keepdims=True)
            if top is not None:
                new_top = jnp.maximum(top, new_top)
                factor = jnp.exp(top - new_top)
                total, acc = total * factor, acc * factor
            top = new_top
            p = jnp.where(allowed, jnp.exp(s - top), 0.0)
            part = jnp.sum(p, axis=1, keepdims=True)
            dot = jnp.dot(p.astype(jnp.bfloat16), values, preferred_element_type=jnp.float32)
            total = part if total is None else total + part
            acc = dot if acc is None else acc + dot
        out_ref[:, cols] = (acc / total).astype(out_ref.dtype)


def attention(q, kv, frame_clip, head_dim, passed):
    peers, tok, width = q.shape
    like = jax.ShapeDtypeStruct((peers * tok, width), q.dtype)
    return pl.pallas_call(
        functools.partial(attention_kernel, tok, head_dim),
        out_shape=[like] + [jax.ShapeDtypeStruct(x.shape, x.dtype) for x in passed],
        in_specs=[SMEM, VMEM, VMEM] + [ANY] * len(passed),
        out_specs=[VMEM] + [ANY] * len(passed),
        input_output_aliases={3 + i: 1 + i for i in range(len(passed))},
        compiler_params=PARAMS,
    )(frame_clip, q, kv, *passed)


def project_kernel(row_ref, attn_ref, own_ref, *refs):
    *w_refs, out_ref, a_ref, w_all = refs
    blks, _, width = attn_ref.shape
    head_dim = own_ref.shape[0]
    rows = w_all.shape[0] // head_dim
    row = row_ref[0]
    for b in range(blks):
        a_ref[:, b * width:(b + 1) * width] = attn_ref[b]

    def put(ref, at):
        w_all[pl.ds(pl.multiple_of(at * head_dim, head_dim), head_dim), :] = ref[...]

    put(own_ref, row)
    for i in range(rows - 1):
        pl.when(row >= i + 1)(functools.partial(put, w_refs[2 * i], row - i - 1))
        pl.when(row + i + 1 < rows)(functools.partial(put, w_refs[2 * i + 1], row + i + 1))
    result = jnp.dot(a_ref[...], w_all[...], preferred_element_type=jnp.float32)
    out_ref[...] = result.astype(out_ref.dtype).reshape(out_ref.shape)


def project(attn_all, w_parts, row, tok):
    blks, count, width = attn_all.shape
    depth, cols = blks * width, w_parts[0].shape[1]
    return pl.pallas_call(
        project_kernel,
        out_shape=jax.ShapeDtypeStruct((count // tok, tok, cols), attn_all.dtype),
        in_specs=[SMEM] + [VMEM] * (1 + len(w_parts)),
        out_specs=VMEM,
        scratch_shapes=[
            pltpu.VMEM((count, depth), attn_all.dtype),
            pltpu.VMEM((depth, cols), attn_all.dtype),
        ],
        compiler_params=PARAMS,
    )(row, attn_all, *w_parts)


def unpack_kernel(x_ref, out_ref):
    peers, _, width = x_ref.shape
    for b in range(peers // 2):
        both = x_ref[2 * b].astype(jnp.float32) + x_ref[2 * b + 1].astype(jnp.float32)
        out_ref[:, b * width:(b + 1) * width] = both.astype(out_ref.dtype)


def unpack(x):
    peers, tok, width = x.shape
    return pl.pallas_call(
        unpack_kernel,
        out_shape=jax.ShapeDtypeStruct((tok, peers // 2 * width), x.dtype),
        in_specs=[VMEM],
        out_specs=VMEM,
        compiler_params=PARAMS,
    )(x)


def shift(x, axis, by):
    size = lax.axis_size(axis)
    return lax.ppermute(x, axis, [(i, i + by) for i in range(size) if 0 <= i + by < size])


def on_device(qkv, frame_clip, w_out):
    rows, blks = lax.axis_size("row"), lax.axis_size("blk")
    peers = 2 * blks
    head_dim, model = w_out.shape
    cols = model // blks

    own = lax.dynamic_slice(w_out, (0, lax.axis_index("blk") * cols), (head_dim, cols))
    below, above = shift(own, "row", 1), shift(own, "row", -1)

    q_out, kv_out = pack(qkv, peers, rows, head_dim)
    kv = lax.all_to_all(kv_out, ALL, split_axis=0, concat_axis=0, tiled=True)
    q = lax.all_to_all(q_out, PLANE, split_axis=0, concat_axis=0, tiled=True)
    attn, below, above = attention(q, kv, frame_clip, head_dim, (below, above))

    w_parts = [own, below, above]
    for by in range(1, rows - 1):
        w_parts += [shift(below, "row", by), shift(above, "row", -by)]
    attn_all = lax.all_gather(attn, "blk", axis=0, tiled=False)
    row = lax.axis_index("row").astype(jnp.int32).reshape(1)
    part = project(attn_all, w_parts, row, qkv.shape[1])
    return unpack(lax.all_to_all(part, PLANE, split_axis=0, concat_axis=0, tiled=True))


def solution(mesh):
    blk, tile = mesh.shape["blk"], mesh.shape["tile"]
    fine = Mesh(mesh.devices.reshape(blk, tile // 2, 2), ALL)
    in_specs = (P(None, ALL, None), P(), P(("row", "core"), None))
    return jax.shard_map(
        on_device, mesh=fine, in_specs=in_specs, out_specs=P(ALL, None), check_vma=False
    )
```

```python
import functools
import math

import jax
import jax.numpy as jnp
from jax import lax
from jax.experimental import pallas as pl
from jax.experimental.pallas import tpu as pltpu
from jax.sharding import PartitionSpec as P

FRB = 2
TPF = 16
VMEM = pl.BlockSpec(memory_space=pltpu.VMEM)
SMEM = pl.BlockSpec(memory_space=pltpu.SMEM)
PARAMS = pltpu.CompilerParams(vmem_limit_bytes=48 * 1024 * 1024)


def pack_kernel(x_ref, out_ref):
    tiles, _, width = out_ref.shape
    kinds, tok, _ = x_ref.shape
    for g in range(tiles):
        for k in range(kinds):
            out_ref[g, k * tok:(k + 1) * tok, :] = x_ref[k, :, g * width:(g + 1) * width]


def pack(x, tiles):
    kinds, tok, cols = x.shape
    return pl.pallas_call(
        pack_kernel,
        out_shape=jax.ShapeDtypeStruct((tiles, kinds * tok, cols // tiles), x.dtype),
        in_specs=[VMEM],
        out_specs=VMEM,
        compiler_params=PARAMS,
    )(x)


def pack_rows_kernel(blk_ref, x_ref, out_ref):
    tiles, _, width = out_ref.shape
    for g in range(tiles):
        out_ref[g] = x_ref[:, g * width:(g + 1) * width]


def pack_rows(x, blk, blks, tiles):
    depth, cols = x.shape
    shape = (tiles, depth // blks, cols // tiles)
    return pl.pallas_call(
        pack_rows_kernel,
        out_shape=jax.ShapeDtypeStruct(shape, x.dtype),
        grid_spec=pltpu.PrefetchScalarGridSpec(
            num_scalar_prefetch=1,
            grid=(1,),
            in_specs=[pl.BlockSpec((depth // blks, cols), lambda i, at: (at[0], 0))],
            out_specs=pl.BlockSpec(shape, lambda i, at: (0, 0, 0)),
        ),
        compiler_params=PARAMS,
    )(blk, x)


def attention_kernel(tok, blk_ref, clip_ref, own_ref, *refs):
    *kv_refs, out_ref = refs
    tiles, _, head_dim = own_ref.shape
    count = tiles * tok
    scale = 1.0 / math.sqrt(head_dim)
    blk = blk_ref[0]

    def clips(at, shape, axis):
        first, second = clip_ref[at * FRB], clip_ref[at * FRB + 1]
        token = lax.broadcasted_iota(jnp.int32, shape, axis)
        return jnp.where(token % tok // TPF == 0, first, second)

    row_clip = clips(blk, (count, 1), 0)
    queries = own_ref[:, 0:tok, :].reshape(count, head_dim)
    sources = [(own_ref, tok)] + [(ref, 0) for ref in kv_refs]
    per_step = max(1, 1024 // count)
    top = total = acc = None
    for start in range(0, len(sources), per_step):
        scores, masks, values = [], [], []
        for k in range(start, min(start + per_step, len(sources))):
            ref, at = sources[k]
            keys = ref[:, at:at + tok, :].reshape(count, head_dim)
            values.append(ref[:, at + tok:at + 2 * tok, :].reshape(count, head_dim))
            s = lax.dot_general(
                queries, keys, (((1,), (1,)), ((), ())), preferred_element_type=jnp.float32
            )
            masks.append(row_clip == clips(blk ^ k, (1, count), 1))
            scores.append(jnp.where(masks[-1], s * scale, -1e30))
        new_top = functools.reduce(
            jnp.maximum, [jnp.max(s, axis=1, keepdims=True) for s in scores]
        )
        if top is not None:
            new_top = jnp.maximum(top, new_top)
            factor = jnp.exp(top - new_top)
            total, acc = total * factor, acc * factor
        top = new_top
        for s, allowed, v in zip(scores, masks, values):
            p = jnp.where(allowed, jnp.exp(s - top), 0.0)
            part = jnp.sum(p, axis=1, keepdims=True)
            dot = jnp.dot(p.astype(jnp.bfloat16), v, preferred_element_type=jnp.float32)
            total = part if total is None else total + part
            acc = dot if acc is None else acc + dot
    out_ref[...] = (acc / total).astype(out_ref.dtype)


def attention(own, others, blk, frame_clip):
    tiles, depth, head_dim = own.shape
    tok = depth // 3
    return pl.pallas_call(
        functools.partial(attention_kernel, tok),
        out_shape=jax.ShapeDtypeStruct((tiles * tok, head_dim), own.dtype),
        in_specs=[SMEM, SMEM] + [VMEM] * (1 + len(others)),
        out_specs=VMEM,
        compiler_params=PARAMS,
    )(blk, frame_clip, own, *others)


def project_kernel(blk_ref, attn_ref, *refs):
    *w_refs, out_ref, a_ref, w_all = refs
    tiles, _, head_dim = attn_ref.shape
    rows = w_refs[0].shape[1]
    for g in range(tiles):
        a_ref[:, g * head_dim:(g + 1) * head_dim] = attn_ref[g]
        for k, ref in enumerate(w_refs):
            at = pl.multiple_of(g * head_dim + (blk_ref[0] ^ k) * rows, rows)
            w_all[pl.ds(at, rows), :] = ref[g]
    result = jnp.dot(a_ref[...], w_all[...], preferred_element_type=jnp.float32)
    out_ref[...] = result.astype(out_ref.dtype).reshape(out_ref.shape)


def project(attn_all, w_parts, blk):
    tiles, count, head_dim = attn_all.shape
    depth, cols = tiles * head_dim, w_parts[0].shape[2]
    return pl.pallas_call(
        project_kernel,
        out_shape=jax.ShapeDtypeStruct((tiles, count // tiles, cols), attn_all.dtype),
        in_specs=[SMEM] + [VMEM] * (1 + len(w_parts)),
        out_specs=VMEM,
        scratch_shapes=[
            pltpu.VMEM((count, depth), attn_all.dtype),
            pltpu.VMEM((depth, cols), attn_all.dtype),
        ],
        compiler_params=PARAMS,
    )(blk, attn_all, *w_parts)


def unpack_kernel(x_ref, out_ref):
    tiles, _, width = x_ref.shape
    for g in range(tiles):
        out_ref[:, g * width:(g + 1) * width] = x_ref[g]


def unpack(x):
    tiles, tok, width = x.shape
    return pl.pallas_call(
        unpack_kernel,
        out_shape=jax.ShapeDtypeStruct((tok, tiles * width), x.dtype),
        in_specs=[VMEM],
        out_specs=VMEM,
        compiler_params=PARAMS,
    )(x)


def exchange(x, axis):
    return lax.all_to_all(x, axis, split_axis=0, concat_axis=0, tiled=True)


def from_others(x):
    blks = lax.axis_size("blk")
    return [
        lax.ppermute(x, "blk", [(i, i ^ k) for i in range(blks)]) for k in range(1, blks)
    ]


def on_device(qkv, frame_clip, w_out):
    tiles, blks = lax.axis_size("tile"), lax.axis_size("blk")
    blk = lax.axis_index("blk").astype(jnp.int32).reshape(1)
    tok = qkv.shape[1]

    own = exchange(pack(qkv, tiles), "tile")
    others = from_others(own[:, tok:])

    w_own = exchange(pack_rows(w_out, blk, blks, tiles), "tile")
    w_parts = [w_own] + from_others(w_own)

    attn = attention(own, others, blk, frame_clip)
    attn_all = lax.all_gather(attn, "tile", axis=0, tiled=False)
    return unpack(exchange(project(attn_all, w_parts, blk), "tile"))


def solution(mesh):
    in_specs = (P(None, ("blk", "tile"), None), P(), P("tile", None))
    out_specs = P(("blk", "tile"), None)
    return jax.shard_map(
        on_device, mesh=mesh, in_specs=in_specs, out_specs=out_specs, check_vma=False
    )
```

```python
import functools
import math

import jax
import jax.numpy as jnp
from jax import lax
from jax.experimental import pallas as pl
from jax.experimental.pallas import tpu as pltpu
from jax.sharding import Mesh
from jax.sharding import PartitionSpec as P

FRB = 2
TPF = 16
ALL = ("blk", "row", "core")
PLANE = ("blk", "core")
VMEM = pl.BlockSpec(memory_space=pltpu.VMEM)
SMEM = pl.BlockSpec(memory_space=pltpu.SMEM)
ANY = pl.BlockSpec(memory_space=pl.ANY)
PARAMS = pltpu.CompilerParams(vmem_limit_bytes=48 * 1024 * 1024)


def pack_kernel(head_dim, x_ref, out_ref):
    peers, _, width = out_ref.shape
    kinds, tok, _ = x_ref.shape
    heads = width // head_dim
    for g in range(peers):
        for i in range(heads):
            head = (g // 2 * heads + i) * 2 + g % 2
            for k in range(kinds):
                out_ref[g, k * tok:(k + 1) * tok, i * head_dim:(i + 1) * head_dim] = x_ref[
                    k, :, head * head_dim:(head + 1) * head_dim
                ]


def pack(x, peers, head_dim):
    kinds, tok, cols = x.shape
    return pl.pallas_call(
        functools.partial(pack_kernel, head_dim),
        out_shape=jax.ShapeDtypeStruct((peers, kinds * tok, cols // peers), x.dtype),
        in_specs=[VMEM],
        out_specs=VMEM,
        compiler_params=PARAMS,
    )(x)


def columns_kernel(at_ref, x_ref, out_ref):
    out_ref[...] = x_ref[...]


def columns(x, at, parts):
    depth, cols = x.shape
    return pl.pallas_call(
        columns_kernel,
        out_shape=jax.ShapeDtypeStruct((depth, cols // parts), x.dtype),
        grid_spec=pltpu.PrefetchScalarGridSpec(
            num_scalar_prefetch=1,
            grid=(1,),
            in_specs=[pl.BlockSpec((depth, cols // parts), lambda i, at: (0, at[0]))],
            out_specs=pl.BlockSpec((depth, cols // parts), lambda i, at: (0, 0)),
        ),
        compiler_params=PARAMS,
    )(at, x)


def clip_of(token, blk_tokens, tok_dev, clip_ref):
    frame = token // blk_tokens * FRB + token % tok_dev // TPF
    clip = jnp.zeros_like(token)
    for f in range(clip_ref.shape[0]):
        clip = jnp.where(frame == f, clip_ref[f], clip)
    return clip


def attention_kernel(tok, head_dim, n_kv, clip_ref, own_ref, *refs):
    kv_refs, out_ref = refs[:n_kv], refs[len(refs) - 1 - (len(refs) - 1 - n_kv) // 2]
    peers, _, width = own_ref.shape
    count = peers * tok
    scale = 1.0 / math.sqrt(head_dim)
    row_clip = clip_of(
        lax.broadcasted_iota(jnp.int32, (count, 1), 0), 2 * tok, tok, clip_ref
    )
    col_clip = clip_of(
        lax.broadcasted_iota(jnp.int32, (1, count), 1), 2 * tok, tok, clip_ref
    )
    allowed = row_clip == col_clip
    sources = [(own_ref, tok)] + [(ref, 0) for ref in kv_refs]
    per_step = max(1, 1024 // count)
    for h in range(width // head_dim):
        cols = slice(h * head_dim, (h + 1) * head_dim)
        queries = own_ref[:, 0:tok, cols].reshape(count, head_dim)
        top = total = acc = None
        for first in range(0, len(sources), per_step):
            scores, values = [], []
            for ref, at in sources[first:first + per_step]:
                keys = ref[:, at:at + tok, cols].reshape(count, head_dim)
                values.append(ref[:, at + tok:at + 2 * tok, cols].reshape(count, head_dim))
                s = lax.dot_general(
                    queries, keys, (((1,), (1,)), ((), ())), preferred_element_type=jnp.float32
                )
                scores.append(jnp.where(allowed, s * scale, -1e30))
            new_top = functools.reduce(
                jnp.maximum, [jnp.max(s, axis=1, keepdims=True) for s in scores]
            )
            if top is not None:
                new_top = jnp.maximum(top, new_top)
                factor = jnp.exp(top - new_top)
                total, acc = total * factor, acc * factor
            top = new_top
            for s, v in zip(scores, values):
                p = jnp.where(allowed, jnp.exp(s - top), 0.0)
                part = jnp.sum(p, axis=1, keepdims=True)
                dot = jnp.dot(p.astype(jnp.bfloat16), v, preferred_element_type=jnp.float32)
                total = part if total is None else total + part
                acc = dot if acc is None else acc + dot
        out_ref[:, cols] = (acc / total).astype(out_ref.dtype)


def attention(own, others, frame_clip, tok, head_dim, passed):
    peers, _, width = own.shape
    like = jax.ShapeDtypeStruct((peers * tok, width), own.dtype)
    return pl.pallas_call(
        functools.partial(attention_kernel, tok, head_dim, len(others)),
        out_shape=[like] + [jax.ShapeDtypeStruct(x.shape, x.dtype) for x in passed],
        in_specs=[SMEM] + [VMEM] * (1 + len(others)) + [ANY] * len(passed),
        out_specs=[VMEM] + [ANY] * len(passed),
        input_output_aliases={2 + len(others) + i: 1 + i for i in range(len(passed))},
        compiler_params=PARAMS,
    )(frame_clip, own, *others, *passed)


def project_kernel(at_ref, core_ref, attn_ref, *refs):
    *w_refs, mine_ref, theirs_ref, a_ref, w_all = refs
    blks, _, width = attn_ref.shape
    head_dim, cols = w_refs[0].shape
    half = cols // 2
    for b in range(blks):
        a_ref[:, b * width:(b + 1) * width] = attn_ref[b]
    for i, ref in enumerate(w_refs):
        w_all[pl.ds(pl.multiple_of(at_ref[i] * head_dim, head_dim), head_dim), :] = ref[...]
    result = jnp.dot(a_ref[...], w_all[...], preferred_element_type=jnp.float32)
    result = result.astype(mine_ref.dtype)
    first = result[:, :half].reshape(mine_ref.shape)
    second = result[:, half:].reshape(mine_ref.shape)
    core = core_ref[0]

    @pl.when(core == 0)
    def _():
        mine_ref[...] = first
        theirs_ref[...] = second

    @pl.when(core != 0)
    def _():
        mine_ref[...] = second
        theirs_ref[...] = first


def project(attn_all, w_parts, at, core, tok):
    blks, count, width = attn_all.shape
    depth, cols = blks * width, w_parts[0].shape[1]
    like = jax.ShapeDtypeStruct((count // tok, tok, cols // 2), attn_all.dtype)
    return pl.pallas_call(
        project_kernel,
        out_shape=(like, like),
        in_specs=[SMEM, SMEM] + [VMEM] * (1 + len(w_parts)),
        out_specs=(VMEM, VMEM),
        scratch_shapes=[
            pltpu.VMEM((count, depth), attn_all.dtype),
            pltpu.VMEM((depth, cols), attn_all.dtype),
        ],
        compiler_params=PARAMS,
    )(at, core, attn_all, *w_parts)


def add_kernel(x_ref, y_ref, out_ref):
    both = x_ref[...].astype(jnp.float32) + y_ref[...].astype(jnp.float32)
    out_ref[...] = both.astype(out_ref.dtype)


def add(x, y):
    return pl.pallas_call(
        add_kernel,
        out_shape=jax.ShapeDtypeStruct(x.shape, x.dtype),
        in_specs=[VMEM, VMEM],
        out_specs=VMEM,
        compiler_params=PARAMS,
    )(x, y)


def unpack_kernel(x_ref, out_ref):
    peers, _, width = x_ref.shape
    for g in range(peers):
        out_ref[:, g * width:(g + 1) * width] = x_ref[g]


def unpack(x):
    peers, tok, width = x.shape
    return pl.pallas_call(
        unpack_kernel,
        out_shape=jax.ShapeDtypeStruct((tok, peers * width), x.dtype),
        in_specs=[VMEM],
        out_specs=VMEM,
        compiler_params=PARAMS,
    )(x)


def xor(x, axis, by):
    return lax.ppermute(x, axis, [(i, i ^ by) for i in range(lax.axis_size(axis))])


def inner(x):
    return lax.ppermute(x, "row", [(0, 0), (1, 2), (2, 1), (3, 3)])


def exchange(x, axis):
    return lax.all_to_all(x, axis, split_axis=0, concat_axis=0, tiled=True)


def on_device(qkv, frame_clip, w_out):
    rows, blks = lax.axis_size("row"), lax.axis_size("blk")
    row, core = lax.axis_index("row"), lax.axis_index("core")
    tok = qkv.shape[1]
    head_dim = w_out.shape[0]

    w_own = columns(w_out, lax.axis_index("blk").astype(jnp.int32).reshape(1), blks)
    chain = rows == 4
    if chain:
        w_next, w_mid = xor(w_own, "row", 1), inner(w_own)
    own = exchange(pack(qkv, 2 * blks, head_dim), PLANE)
    kv = own[:, tok:]
    if chain:
        w_far, w_end = inner(w_next), xor(w_mid, "row", 1)
    others = [xor(kv, "row", by) for by in range(1, rows)]
    passed = (w_far,) if chain else (w_own,)
    attn, passed = attention(own, others, frame_clip, tok, head_dim, passed)
    if chain:
        w_parts = [w_own, w_next, w_mid, w_end, passed, xor(passed, "row", 1)]
        middle = (row == 1) | (row == 2)
        pick = lambda a, b: jnp.where(middle, a, b)
        at = [
            row, row ^ 1, pick(3 - row, row), pick(row ^ 1, 3 - (row ^ 1)),
            pick((3 - row) ^ 1, row ^ 1), pick(row, (3 - (row ^ 1)) ^ 1),
        ]
    else:
        w_parts = [passed] + [xor(passed, "row", by) for by in range(1, rows)]
        at = [row ^ by for by in range(rows)]
    attn_all = lax.all_gather(attn, "blk", axis=0, tiled=False)
    mine, theirs = project(
        attn_all, w_parts, jnp.stack(at).astype(jnp.int32),
        core.astype(jnp.int32).reshape(1), tok,
    )
    return unpack(exchange(add(mine, xor(theirs, "core", 1)), PLANE))


def solution(mesh):
    blk, tile = mesh.shape["blk"], mesh.shape["tile"]
    fine = Mesh(mesh.devices.reshape(blk, tile // 2, 2), ALL)
    in_specs = (P(None, ALL, None), P(), P(("row", "core"), None))
    return jax.shard_map(
        on_device, mesh=fine, in_specs=in_specs, out_specs=P(ALL, None), check_vma=False
    )
```

```python
import functools
import math

import jax
import jax.numpy as jnp
from jax import lax
from jax.experimental import pallas as pl
from jax.experimental.pallas import tpu as pltpu
from jax.sharding import Mesh
from jax.sharding import PartitionSpec as P

FRB = 2
TPF = 16
ALL = ("blk", "row", "core")
PLANE = ("blk", "core")
VMEM = pl.BlockSpec(memory_space=pltpu.VMEM)
SMEM = pl.BlockSpec(memory_space=pltpu.SMEM)
ANY = pl.BlockSpec(memory_space=pl.ANY)
PARAMS = pltpu.CompilerParams(vmem_limit_bytes=48 * 1024 * 1024)


def pack_kernel(head_dim, x_ref, out_ref):
    peers, _, width = out_ref.shape
    kinds, tok, _ = x_ref.shape
    heads = width // head_dim
    for g in range(peers):
        for i in range(heads):
            head = (g // 2 * heads + i) * 2 + g % 2
            for k in range(kinds):
                out_ref[g, k * tok:(k + 1) * tok, i * head_dim:(i + 1) * head_dim] = x_ref[
                    k, :, head * head_dim:(head + 1) * head_dim
                ]


def pack(x, peers, head_dim):
    kinds, tok, cols = x.shape
    return pl.pallas_call(
        functools.partial(pack_kernel, head_dim),
        out_shape=jax.ShapeDtypeStruct((peers, kinds * tok, cols // peers), x.dtype),
        in_specs=[VMEM],
        out_specs=VMEM,
        compiler_params=PARAMS,
    )(x)


def columns_kernel(at_ref, x_ref, out_ref):
    out_ref[...] = x_ref[...]


def columns(x, at, parts):
    depth, cols = x.shape
    return pl.pallas_call(
        columns_kernel,
        out_shape=jax.ShapeDtypeStruct((depth, cols // parts), x.dtype),
        grid_spec=pltpu.PrefetchScalarGridSpec(
            num_scalar_prefetch=1,
            grid=(1,),
            in_specs=[pl.BlockSpec((depth, cols // parts), lambda i, at: (0, at[0]))],
            out_specs=pl.BlockSpec((depth, cols // parts), lambda i, at: (0, 0)),
        ),
        compiler_params=PARAMS,
    )(at, x)


def clip_of(token, blk_tokens, tok_dev, clip_ref):
    frame = token // blk_tokens * FRB + token % tok_dev // TPF
    clip = jnp.zeros_like(token)
    for f in range(clip_ref.shape[0]):
        clip = jnp.where(frame == f, clip_ref[f], clip)
    return clip


def cut_kernel(tok, x_ref, *refs):
    refs[len(refs) // 2][...] = x_ref[:, tok:, :]


def cut(x, tok, passed):
    peers, depth, width = x.shape
    like = jax.ShapeDtypeStruct((peers, depth - tok, width), x.dtype)
    kv, *same = pl.pallas_call(
        functools.partial(cut_kernel, tok),
        out_shape=[like] + [jax.ShapeDtypeStruct(y.shape, y.dtype) for y in passed],
        in_specs=[VMEM] + [ANY] * len(passed),
        out_specs=[VMEM] + [ANY] * len(passed),
        input_output_aliases={1 + i: 1 + i for i in range(len(passed))},
        compiler_params=PARAMS,
    )(x, *passed)
    return kv, same


def attention_kernel(tok, head_dim, clip_ref, own_ref, *refs):
    *kv_refs, out_ref = refs
    peers, _, width = own_ref.shape
    count = peers * tok
    scale = 1.0 / math.sqrt(head_dim)
    row_clip = clip_of(
        lax.broadcasted_iota(jnp.int32, (count, 1), 0), 2 * tok, tok, clip_ref
    )
    col_clip = clip_of(
        lax.broadcasted_iota(jnp.int32, (1, count), 1), 2 * tok, tok, clip_ref
    )
    allowed = row_clip == col_clip
    sources = [(own_ref, tok)] + [(ref, 0) for ref in kv_refs]
    per_step = max(1, 1024 // count)
    for h in range(width // head_dim):
        cols = slice(h * head_dim, (h + 1) * head_dim)
        queries = own_ref[:, 0:tok, cols].reshape(count, head_dim)
        top = total = acc = None
        for first in range(0, len(sources), per_step):
            scores, values = [], []
            for ref, at in sources[first:first + per_step]:
                keys = ref[:, at:at + tok, cols].reshape(count, head_dim)
                values.append(ref[:, at + tok:at + 2 * tok, cols].reshape(count, head_dim))
                s = lax.dot_general(
                    queries, keys, (((1,), (1,)), ((), ())), preferred_element_type=jnp.float32
                )
                scores.append(jnp.where(allowed, s * scale, -1e30))
            new_top = functools.reduce(
                jnp.maximum, [jnp.max(s, axis=1, keepdims=True) for s in scores]
            )
            if top is not None:
                new_top = jnp.maximum(top, new_top)
                factor = jnp.exp(top - new_top)
                total, acc = total * factor, acc * factor
            top = new_top
            for s, v in zip(scores, values):
                p = jnp.where(allowed, jnp.exp(s - top), 0.0)
                part = jnp.sum(p, axis=1, keepdims=True)
                dot = jnp.dot(p.astype(jnp.bfloat16), v, preferred_element_type=jnp.float32)
                total = part if total is None else total + part
                acc = dot if acc is None else acc + dot
        out_ref[:, cols] = (acc / total).astype(out_ref.dtype)


def attention(own, others, frame_clip, tok, head_dim):
    peers, _, width = own.shape
    return pl.pallas_call(
        functools.partial(attention_kernel, tok, head_dim),
        out_shape=jax.ShapeDtypeStruct((peers * tok, width), own.dtype),
        in_specs=[SMEM] + [VMEM] * (1 + len(others)),
        out_specs=VMEM,
        compiler_params=PARAMS,
    )(frame_clip, own, *others)


def project_kernel(at_ref, core_ref, attn_ref, *refs):
    *w_refs, mine_ref, theirs_ref, a_ref, w_all = refs
    blks, _, width = attn_ref.shape
    head_dim, cols = w_refs[0].shape
    half = cols // 2
    for b in range(blks):
        a_ref[:, b * width:(b + 1) * width] = attn_ref[b]
    for i, ref in enumerate(w_refs):
        w_all[pl.ds(pl.multiple_of(at_ref[i] * head_dim, head_dim), head_dim), :] = ref[...]
    result = jnp.dot(a_ref[...], w_all[...], preferred_element_type=jnp.float32)
    result = result.astype(mine_ref.dtype)
    first = result[:, :half].reshape(mine_ref.shape)
    second = result[:, half:].reshape(mine_ref.shape)
    core = core_ref[0]

    @pl.when(core == 0)
    def _():
        mine_ref[...] = first
        theirs_ref[...] = second

    @pl.when(core != 0)
    def _():
        mine_ref[...] = second
        theirs_ref[...] = first


def project(attn_all, w_parts, at, core, tok):
    blks, count, width = attn_all.shape
    depth, cols = blks * width, w_parts[0].shape[1]
    like = jax.ShapeDtypeStruct((count // tok, tok, cols // 2), attn_all.dtype)
    return pl.pallas_call(
        project_kernel,
        out_shape=(like, like),
        in_specs=[SMEM, SMEM] + [VMEM] * (1 + len(w_parts)),
        out_specs=(VMEM, VMEM),
        scratch_shapes=[
            pltpu.VMEM((count, depth), attn_all.dtype),
            pltpu.VMEM((depth, cols), attn_all.dtype),
        ],
        compiler_params=PARAMS,
    )(at, core, attn_all, *w_parts)


def add_kernel(x_ref, y_ref, out_ref):
    both = x_ref[...].astype(jnp.float32) + y_ref[...].astype(jnp.float32)
    out_ref[...] = both.astype(out_ref.dtype)


def add(x, y):
    return pl.pallas_call(
        add_kernel,
        out_shape=jax.ShapeDtypeStruct(x.shape, x.dtype),
        in_specs=[VMEM, VMEM],
        out_specs=VMEM,
        compiler_params=PARAMS,
    )(x, y)


def unpack_kernel(x_ref, out_ref):
    peers, _, width = x_ref.shape
    for g in range(peers):
        out_ref[:, g * width:(g + 1) * width] = x_ref[g]


def unpack(x):
    peers, tok, width = x.shape
    return pl.pallas_call(
        unpack_kernel,
        out_shape=jax.ShapeDtypeStruct((tok, peers * width), x.dtype),
        in_specs=[VMEM],
        out_specs=VMEM,
        compiler_params=PARAMS,
    )(x)


def xor(x, axis, by):
    return lax.ppermute(x, axis, [(i, i ^ by) for i in range(lax.axis_size(axis))])


def exchange(x, axis):
    return lax.all_to_all(x, axis, split_axis=0, concat_axis=0, tiled=True)


def on_device(qkv, frame_clip, w_out):
    rows, blks = lax.axis_size("row"), lax.axis_size("blk")
    row, core = lax.axis_index("row"), lax.axis_index("core")
    tok = qkv.shape[1]
    head_dim = w_out.shape[0]

    w_own = columns(w_out, lax.axis_index("blk").astype(jnp.int32).reshape(1), blks)
    half = rows == 4
    steps = [rows - 1] + list(range(1, 2 if half else rows - 1))
    w_others = [xor(w_own, "row", by) for by in steps]
    own = exchange(pack(qkv, 2 * blks, head_dim), PLANE)
    kv, w_others = cut(own, tok, w_others)
    others = [xor(kv, "row", by) for by in range(1, rows)]
    if half:
        steps.append(2)
        w_others.append(xor(w_others[0], "row", 1))
    w_parts = [w_own] + w_others
    at = [row] + [row ^ by for by in steps]
    attn = attention(own, others, frame_clip, tok, head_dim)
    attn_all = lax.all_gather(attn, "blk", axis=0, tiled=False)
    mine, theirs = project(
        attn_all, w_parts, jnp.stack(at).astype(jnp.int32),
        core.astype(jnp.int32).reshape(1), tok,
    )
    return unpack(exchange(add(mine, xor(theirs, "core", 1)), PLANE))


def solution(mesh):
    blk, tile = mesh.shape["blk"], mesh.shape["tile"]
    fine = Mesh(mesh.devices.reshape(blk, tile // 2, 2), ALL)
    in_specs = (P(None, ALL, None), P(), P(("row", "core"), None))
    return jax.shard_map(
        on_device, mesh=fine, in_specs=in_specs, out_specs=P(ALL, None), check_vma=False
    )
```

```python
import functools
import math

import jax
import jax.numpy as jnp
from jax import lax
from jax.experimental import pallas as pl
from jax.experimental.pallas import tpu as pltpu
from jax.sharding import Mesh
from jax.sharding import PartitionSpec as P

FRB = 2
TPF = 16
ALL = ("blk", "row", "core")
PLANE = ("blk", "core")
VMEM = pl.BlockSpec(memory_space=pltpu.VMEM)
SMEM = pl.BlockSpec(memory_space=pltpu.SMEM)
ANY = pl.BlockSpec(memory_space=pl.ANY)
PARAMS = pltpu.CompilerParams(vmem_limit_bytes=48 * 1024 * 1024)


def pack_kernel(head_dim, at_ref, x_ref, *out_refs):
    kinds, tok, _ = x_ref.shape
    heads = out_refs[0].shape[1] // head_dim
    for m, out_ref in enumerate(out_refs):
        place = at_ref[0] ^ m
        for i in range(heads):
            head = (place // 2 * heads + i) * 2 + place % 2
            cols = pl.ds(pl.multiple_of(head * head_dim, head_dim), head_dim)
            for k in range(kinds):
                out_ref[k * tok:(k + 1) * tok, i * head_dim:(i + 1) * head_dim] = x_ref[k, :, cols]


def pack(x, place, peers, head_dim):
    kinds, tok, cols = x.shape
    like = jax.ShapeDtypeStruct((kinds * tok, cols // peers), x.dtype)
    return pl.pallas_call(
        functools.partial(pack_kernel, head_dim),
        out_shape=[like] * peers,
        in_specs=[SMEM, VMEM],
        out_specs=[VMEM] * peers,
        compiler_params=PARAMS,
    )(place, x)


def columns_kernel(at_ref, x_ref, out_ref, sem):
    cols = out_ref.shape[1]
    start = pl.multiple_of(at_ref[0] * cols, cols)
    copy = pltpu.make_async_copy(x_ref.at[:, pl.ds(start, cols)], out_ref, sem)
    copy.start()
    copy.wait()


def columns(x, at, parts):
    depth, cols = x.shape
    return pl.pallas_call(
        columns_kernel,
        out_shape=jax.ShapeDtypeStruct((depth, cols // parts), x.dtype),
        in_specs=[SMEM, pl.BlockSpec(memory_space=pltpu.HBM)],
        out_specs=VMEM,
        scratch_shapes=[pltpu.SemaphoreType.DMA],
        compiler_params=PARAMS,
    )(at, x)


def sort_kernel(at_ref, *refs):
    *in_refs, q_ref, kv_ref = refs
    tok = q_ref.shape[1]
    for m, ref in enumerate(in_refs):
        place = at_ref[0] ^ m
        q_ref[place] = ref[0:tok, :]
        kv_ref[place] = ref[tok:, :]


def sort(parts, place):
    depth, width = parts[0].shape
    tok, peers = depth // 3, len(parts)
    return pl.pallas_call(
        sort_kernel,
        out_shape=(
            jax.ShapeDtypeStruct((peers, tok, width), parts[0].dtype),
            jax.ShapeDtypeStruct((peers, 2 * tok, width), parts[0].dtype),
        ),
        in_specs=[SMEM] + [VMEM] * peers,
        out_specs=(VMEM, VMEM),
        compiler_params=PARAMS,
    )(place, *parts)


def clip_of(token, blk_tokens, tok_dev, clip_ref):
    frame = token // blk_tokens * FRB + token % tok_dev // TPF
    clip = jnp.zeros_like(token)
    for f in range(clip_ref.shape[0]):
        clip = jnp.where(frame == f, clip_ref[f], clip)
    return clip


def attention_kernel(head_dim, n_kv, clip_ref, q_ref, *refs):
    kv_refs, out_ref = refs[:n_kv], refs[(len(refs) + n_kv) // 2]
    peers, tok, width = q_ref.shape
    count = peers * tok
    scale = 1.0 / math.sqrt(head_dim)
    row_clip = clip_of(
        lax.broadcasted_iota(jnp.int32, (count, 1), 0), 2 * tok, tok, clip_ref
    )
    col_clip = clip_of(
        lax.broadcasted_iota(jnp.int32, (1, count), 1), 2 * tok, tok, clip_ref
    )
    allowed = row_clip == col_clip
    per_step = max(1, 1024 // count)
    for h in range(width // head_dim):
        cols = slice(h * head_dim, (h + 1) * head_dim)
        queries = q_ref[:, :, cols].reshape(count, head_dim)
        top = total = acc = None
        for first in range(0, n_kv, per_step):
            scores, values = [], []
            for ref in kv_refs[first:first + per_step]:
                keys = ref[:, 0:tok, cols].reshape(count, head_dim)
                values.append(ref[:, tok:2 * tok, cols].reshape(count, head_dim))
                s = lax.dot_general(
                    queries, keys, (((1,), (1,)), ((), ())), preferred_element_type=jnp.float32
                )
                scores.append(jnp.where(allowed, s * scale, -1e30))
            new_top = functools.reduce(
                jnp.maximum, [jnp.max(s, axis=1, keepdims=True) for s in scores]
            )
            if top is not None:
                new_top = jnp.maximum(top, new_top)
                factor = jnp.exp(top - new_top)
                total, acc = total * factor, acc * factor
            top = new_top
            for s, v in zip(scores, values):
                p = jnp.where(allowed, jnp.exp(s - top), 0.0)
                part = jnp.sum(p, axis=1, keepdims=True)
                dot = jnp.dot(p.astype(jnp.bfloat16), v, preferred_element_type=jnp.float32)
                total = part if total is None else total + part
                acc = dot if acc is None else acc + dot
        out_ref[:, cols] = (acc / total).astype(out_ref.dtype)


def attention(q, kvs, frame_clip, head_dim, passed):
    peers, tok, width = q.shape
    like = jax.ShapeDtypeStruct((peers * tok, width), q.dtype)
    attn, *same = pl.pallas_call(
        functools.partial(attention_kernel, head_dim, len(kvs)),
        out_shape=[like] + [jax.ShapeDtypeStruct(x.shape, x.dtype) for x in passed],
        in_specs=[SMEM] + [VMEM] * (1 + len(kvs)) + [ANY] * len(passed),
        out_specs=[VMEM] + [ANY] * len(passed),
        input_output_aliases={2 + len(kvs) + i: 1 + i for i in range(len(passed))},
        compiler_params=PARAMS,
    )(frame_clip, q, *kvs, *passed)
    return attn, same


def project_kernel(n_attn, at_ref, place_ref, *refs):
    attn_refs, w_refs = refs[:n_attn], refs[n_attn:-3]
    mine_ref, theirs_ref, a_ref = refs[-3:]
    width = attn_refs[0].shape[1]
    head_dim, _ = w_refs[0].shape
    blks, tok, cols = mine_ref.shape
    blk, core = place_ref[0] // 2, place_ref[0] % 2
    for k, ref in enumerate(attn_refs):
        a_ref[:, pl.ds(pl.multiple_of((blk ^ k) * width, width), width)] = ref[...]
    result = None
    for i in range(0, len(w_refs), 2):
        left = [
            a_ref[:, pl.ds(pl.multiple_of(at_ref[j] * head_dim, head_dim), head_dim)]
            for j in (i, i + 1)
        ]
        right = [w_refs[j][...] for j in (i, i + 1)]
        part = jnp.dot(
            jnp.concatenate(left, axis=1), jnp.concatenate(right, axis=0),
            preferred_element_type=jnp.float32,
        )
        result = part if result is None else result + part
    result = result.astype(mine_ref.dtype).reshape(blks, 2, tok, cols)

    @pl.when(core == 0)
    def _():
        mine_ref[...] = result[:, 0]
        theirs_ref[...] = result[:, 1]

    @pl.when(core != 0)
    def _():
        mine_ref[...] = result[:, 1]
        theirs_ref[...] = result[:, 0]


def project(attns, w_parts, at, place, tok):
    count, width = attns[0].shape
    blks, cols = len(attns), w_parts[0].shape[1]
    like = jax.ShapeDtypeStruct((blks, tok, cols), attns[0].dtype)
    return pl.pallas_call(
        functools.partial(project_kernel, blks),
        out_shape=(like, like),
        in_specs=[SMEM, SMEM] + [VMEM] * (blks + len(w_parts)),
        out_specs=(VMEM, VMEM),
        scratch_shapes=[pltpu.VMEM((count, blks * width), attns[0].dtype)],
        compiler_params=PARAMS,
    )(at, place, *attns, *w_parts)


def add_kernel(place_ref, x_ref, y_ref, *out_refs):
    for k, out_ref in enumerate(out_refs):
        at = place_ref[0] // 2 ^ k
        both = x_ref[at].astype(jnp.float32) + y_ref[at].astype(jnp.float32)
        out_ref[...] = both.astype(out_ref.dtype)


def add(x, y, place):
    blks = x.shape[0]
    return pl.pallas_call(
        add_kernel,
        out_shape=[jax.ShapeDtypeStruct(x.shape[1:], x.dtype)] * blks,
        in_specs=[SMEM, VMEM, VMEM],
        out_specs=[VMEM] * blks,
        compiler_params=PARAMS,
    )(place, x, y)


def unpack_kernel(place_ref, *refs):
    *in_refs, out_ref = refs
    width = in_refs[0].shape[1]
    for k, ref in enumerate(in_refs):
        at = place_ref[0] // 2 ^ k
        out_ref[:, pl.ds(pl.multiple_of(at * width, width), width)] = ref[...]


def unpack(parts, place):
    tok, width = parts[0].shape
    return pl.pallas_call(
        unpack_kernel,
        out_shape=jax.ShapeDtypeStruct((tok, len(parts) * width), parts[0].dtype),
        in_specs=[SMEM] + [VMEM] * len(parts),
        out_specs=VMEM,
        compiler_params=PARAMS,
    )(place, *parts)


def xor(x, axis, by):
    size = math.prod(lax.axis_size(name) for name in axis)
    return lax.ppermute(x, axis, [(i, i ^ by) for i in range(size)])


def swap_all(parts, axis):
    return [parts[0]] + [xor(x, axis, m) for m, x in enumerate(parts) if m]


def on_device(qkv, frame_clip, w_out):
    rows, blks = lax.axis_size("row"), lax.axis_size("blk")
    row = lax.axis_index("row")
    tok = qkv.shape[1]
    head_dim = w_out.shape[0]
    blk = lax.axis_index("blk").astype(jnp.int32).reshape(1)
    place = blk * 2 + lax.axis_index("core").astype(jnp.int32)

    w_own = columns(w_out, blk, blks)
    half = rows == 4
    steps = [rows - 1] + list(range(1, 2 if half else rows - 1))
    w_others = [xor(w_own, ("row",), by) for by in steps]

    q, kv = sort(swap_all(pack(qkv, place, 2 * blks, head_dim), PLANE), place)
    kvs = [kv] + [xor(kv, ("row",), by) for by in range(1, rows)]
    attn, w_others = attention(q, kvs, frame_clip, head_dim, w_others)
    if half:
        steps.append(2)
        w_others.append(xor(w_others[0], ("row",), 1))
    attns = swap_all([attn] * blks, ("blk",))
    at = jnp.stack([row] + [row ^ by for by in steps]).astype(jnp.int32)
    mine, theirs = project(attns, [w_own] + w_others, at, place, tok)
    parts = add(mine, xor(theirs, ("core",), 1), place)
    return unpack(swap_all(parts, ("blk",)), place)


def solution(mesh):
    blk, tile = mesh.shape["blk"], mesh.shape["tile"]
    fine = Mesh(mesh.devices.reshape(blk, tile // 2, 2), ALL)
    in_specs = (P(None, ALL, None), P(), P(("row", "core"), None))
    return jax.shard_map(
        on_device, mesh=fine, in_specs=in_specs, out_specs=P(ALL, None), check_vma=False
    )
```

```python
import functools
import math

import jax
import jax.numpy as jnp
from jax import lax
from jax.experimental import pallas as pl
from jax.experimental.pallas import tpu as pltpu
from jax.sharding import Mesh
from jax.sharding import PartitionSpec as P

FRB = 2
TPF = 16
ALL = ("blk", "row", "core")
PLANE = ("blk", "core")
VMEM = pl.BlockSpec(memory_space=pltpu.VMEM)
SMEM = pl.BlockSpec(memory_space=pltpu.SMEM)
ANY = pl.BlockSpec(memory_space=pl.ANY)
PARAMS = pltpu.CompilerParams(vmem_limit_bytes=48 * 1024 * 1024)


def pack_kernel(head_dim, x_ref, out_ref):
    peers, _, width = out_ref.shape
    kinds, tok, _ = x_ref.shape
    heads = width // head_dim
    for g in range(peers):
        for i in range(heads):
            head = (g // 2 * heads + i) * 2 + g % 2
            for k in range(kinds):
                out_ref[g, k * tok:(k + 1) * tok, i * head_dim:(i + 1) * head_dim] = x_ref[
                    k, :, head * head_dim:(head + 1) * head_dim
                ]


def pack(x, peers, head_dim):
    kinds, tok, cols = x.shape
    return pl.pallas_call(
        functools.partial(pack_kernel, head_dim),
        out_shape=jax.ShapeDtypeStruct((peers, kinds * tok, cols // peers), x.dtype),
        in_specs=[VMEM],
        out_specs=VMEM,
        compiler_params=PARAMS,
    )(x)


def columns_kernel(at_ref, x_ref, out_ref, sem):
    cols = out_ref.shape[1]
    start = pl.multiple_of(at_ref[0] * cols, cols)
    copy = pltpu.make_async_copy(x_ref.at[:, pl.ds(start, cols)], out_ref, sem)
    copy.start()
    copy.wait()


def columns(x, at, parts):
    depth, cols = x.shape
    return pl.pallas_call(
        columns_kernel,
        out_shape=jax.ShapeDtypeStruct((depth, cols // parts), x.dtype),
        in_specs=[SMEM, pl.BlockSpec(memory_space=pltpu.HBM)],
        out_specs=VMEM,
        scratch_shapes=[pltpu.SemaphoreType.DMA],
        compiler_params=PARAMS,
    )(at, x)


def cut_kernel(x_ref, q_ref, kv_ref):
    tok = q_ref.shape[1]
    q_ref[...] = x_ref[:, :tok, :]
    kv_ref[...] = x_ref[:, tok:, :]


def cut(x):
    peers, depth, width = x.shape
    tok = depth // 3
    return pl.pallas_call(
        cut_kernel,
        out_shape=(
            jax.ShapeDtypeStruct((peers, tok, width), x.dtype),
            jax.ShapeDtypeStruct((peers, 2 * tok, width), x.dtype),
        ),
        in_specs=[VMEM],
        out_specs=(VMEM, VMEM),
        compiler_params=PARAMS,
    )(x)


def clip_of(token, blk_tokens, tok_dev, clip_ref):
    frame = token // blk_tokens * FRB + token % tok_dev // TPF
    clip = jnp.zeros_like(token)
    for f in range(clip_ref.shape[0]):
        clip = jnp.where(frame == f, clip_ref[f], clip)
    return clip


def attention_kernel(head_dim, n_kv, n_passed, last, clip_ref, q_ref, *refs):
    kv_refs, refs = refs[:n_kv], refs[n_kv:]
    state_refs, out_refs = refs[:3 if last else 0], refs[-n_passed - 1:] if last else refs
    peers, tok, width = q_ref.shape
    count = peers * tok
    scale = 1.0 / math.sqrt(head_dim)
    row_clip = clip_of(
        lax.broadcasted_iota(jnp.int32, (count, 1), 0), 2 * tok, tok, clip_ref
    )
    col_clip = clip_of(
        lax.broadcasted_iota(jnp.int32, (1, count), 1), 2 * tok, tok, clip_ref
    )
    allowed = row_clip == col_clip
    per_step = max(1, 1024 // count)
    for h in range(width // head_dim):
        cols = slice(h * head_dim, (h + 1) * head_dim)
        queries = q_ref[:, :, cols].reshape(count, head_dim)
        top = total = acc = None
        if last:
            top, total, acc = state_refs[0][h], state_refs[1][h], state_refs[2][:, cols]
        for first in range(0, n_kv, per_step):
            scores, values = [], []
            for ref in kv_refs[first:first + per_step]:
                keys = ref[:, 0:tok, cols].reshape(count, head_dim)
                values.append(ref[:, tok:2 * tok, cols].reshape(count, head_dim))
                s = lax.dot_general(
                    queries, keys, (((1,), (1,)), ((), ())), preferred_element_type=jnp.float32
                )
                scores.append(jnp.where(allowed, s * scale, -1e30))
            new_top = functools.reduce(
                jnp.maximum, [jnp.max(s, axis=1, keepdims=True) for s in scores]
            )
            if top is not None:
                new_top = jnp.maximum(top, new_top)
                factor = jnp.exp(top - new_top)
                total, acc = total * factor, acc * factor
            top = new_top
            for s, v in zip(scores, values):
                p = jnp.where(allowed, jnp.exp(s - top), 0.0)
                part = jnp.sum(p, axis=1, keepdims=True)
                dot = jnp.dot(p.astype(jnp.bfloat16), v, preferred_element_type=jnp.float32)
                total = part if total is None else total + part
                acc = dot if acc is None else acc + dot
        if last:
            out_refs[0][:, cols] = (acc / total).astype(out_refs[0].dtype)
        else:
            out_refs[0][h], out_refs[1][h], out_refs[2][:, cols] = top, total, acc


def attend(q, kvs, frame_clip, head_dim):
    peers, tok, width = q.shape
    count = peers * tok
    stat = jax.ShapeDtypeStruct((width // head_dim, count, 1), jnp.float32)
    return pl.pallas_call(
        functools.partial(attention_kernel, head_dim, len(kvs), 0, False),
        out_shape=(stat, stat, jax.ShapeDtypeStruct((count, width), jnp.float32)),
        in_specs=[SMEM] + [VMEM] * (1 + len(kvs)),
        out_specs=(VMEM, VMEM, VMEM),
        compiler_params=PARAMS,
    )(frame_clip, q, *kvs)


def finish(q, kvs, state, frame_clip, head_dim, passed):
    peers, tok, width = q.shape
    like = jax.ShapeDtypeStruct((peers * tok, width), q.dtype)
    attn, *same = pl.pallas_call(
        functools.partial(attention_kernel, head_dim, len(kvs), len(passed), True),
        out_shape=[like] + [jax.ShapeDtypeStruct(x.shape, x.dtype) for x in passed],
        in_specs=[SMEM] + [VMEM] * (4 + len(kvs)) + [ANY] * len(passed),
        out_specs=[VMEM] + [ANY] * len(passed),
        input_output_aliases={5 + len(kvs) + i: 1 + i for i in range(len(passed))},
        compiler_params=PARAMS,
    )(frame_clip, q, *kvs, *state, *passed)
    return attn, same


def project_kernel(n_attn, at_ref, place_ref, *refs):
    attn_refs, w_refs = refs[:n_attn], refs[n_attn:-3]
    mine_ref, theirs_ref, a_ref = refs[-3:]
    width = attn_refs[0].shape[1]
    head_dim, _ = w_refs[0].shape
    blks, tok, cols = mine_ref.shape
    blk, core = place_ref[0] // 2, place_ref[0] % 2
    for k, ref in enumerate(attn_refs):
        a_ref[:, pl.ds(pl.multiple_of((blk ^ k) * width, width), width)] = ref[...]
    result = None
    for i in range(0, len(w_refs), 2):
        left = [
            a_ref[:, pl.ds(pl.multiple_of(at_ref[j] * head_dim, head_dim), head_dim)]
            for j in (i, i + 1)
        ]
        right = [w_refs[j][...] for j in (i, i + 1)]
        part = jnp.dot(
            jnp.concatenate(left, axis=1), jnp.concatenate(right, axis=0),
            preferred_element_type=jnp.float32,
        )
        result = part if result is None else result + part
    result = result.astype(mine_ref.dtype).reshape(blks, 2, tok, cols)

    @pl.when(core == 0)
    def _():
        mine_ref[...] = result[:, 0]
        theirs_ref[...] = result[:, 1]

    @pl.when(core != 0)
    def _():
        mine_ref[...] = result[:, 1]
        theirs_ref[...] = result[:, 0]


def project(attns, w_parts, at, place, tok):
    count, width = attns[0].shape
    blks, cols = len(attns), w_parts[0].shape[1]
    like = jax.ShapeDtypeStruct((blks, tok, cols), attns[0].dtype)
    return pl.pallas_call(
        functools.partial(project_kernel, blks),
        out_shape=(like, like),
        in_specs=[SMEM, SMEM] + [VMEM] * (blks + len(w_parts)),
        out_specs=(VMEM, VMEM),
        scratch_shapes=[pltpu.VMEM((count, blks * width), attns[0].dtype)],
        compiler_params=PARAMS,
    )(at, place, *attns, *w_parts)


def add_kernel(place_ref, x_ref, y_ref, *out_refs):
    for k, out_ref in enumerate(out_refs):
        at = place_ref[0] // 2 ^ k
        both = x_ref[at].astype(jnp.float32) + y_ref[at].astype(jnp.float32)
        out_ref[...] = both.astype(out_ref.dtype)


def add(x, y, place):
    blks = x.shape[0]
    return pl.pallas_call(
        add_kernel,
        out_shape=[jax.ShapeDtypeStruct(x.shape[1:], x.dtype)] * blks,
        in_specs=[SMEM, VMEM, VMEM],
        out_specs=[VMEM] * blks,
        compiler_params=PARAMS,
    )(place, x, y)


def unpack_kernel(place_ref, *refs):
    *in_refs, out_ref = refs
    width = in_refs[0].shape[1]
    for k, ref in enumerate(in_refs):
        at = place_ref[0] // 2 ^ k
        out_ref[:, pl.ds(pl.multiple_of(at * width, width), width)] = ref[...]


def unpack(parts, place):
    tok, width = parts[0].shape
    return pl.pallas_call(
        unpack_kernel,
        out_shape=jax.ShapeDtypeStruct((tok, len(parts) * width), parts[0].dtype),
        in_specs=[SMEM] + [VMEM] * len(parts),
        out_specs=VMEM,
        compiler_params=PARAMS,
    )(place, *parts)


def xor(x, axis, by):
    size = math.prod(lax.axis_size(name) for name in axis)
    return lax.ppermute(x, axis, [(i, i ^ by) for i in range(size)])


def swap_all(parts, axis):
    return [parts[0]] + [xor(x, axis, m) for m, x in enumerate(parts) if m]


def along_rows(x):
    rows = lax.axis_size("row")
    if rows != 4:
        steps = list(range(1, rows))
        return [xor(x, ("row",), by) for by in steps], steps
    return [xor(x, ("row",), 3), xor(x, ("row",), 1)], [3, 1]


def on_device(qkv, frame_clip, w_out):
    rows, blks = lax.axis_size("row"), lax.axis_size("blk")
    row = lax.axis_index("row")
    tok = qkv.shape[1]
    head_dim = w_out.shape[0]
    blk = lax.axis_index("blk").astype(jnp.int32).reshape(1)
    place = blk * 2 + lax.axis_index("core").astype(jnp.int32)

    w_own = columns(w_out, blk, blks)
    w_others, steps = along_rows(w_own)

    packed = pack(qkv, 2 * blks, head_dim)
    q, kv = cut(lax.all_to_all(packed, PLANE, split_axis=0, concat_axis=0, tiled=True))
    others, _ = along_rows(kv)
    if rows == 4:
        others.append(xor(others[0], ("row",), 1))
    state = attend(q, [kv] + others[:-1], frame_clip, head_dim)
    attn, w_others = finish(q, others[-1:], state, frame_clip, head_dim, w_others)
    if rows == 4:
        steps.append(2)
        w_others.append(xor(w_others[0], ("row",), 1))
    attns = swap_all([attn] * blks, ("blk",))
    at = jnp.stack([row] + [row ^ by for by in steps]).astype(jnp.int32)
    mine, theirs = project(attns, [w_own] + w_others, at, place, tok)
    parts = add(mine, xor(theirs, ("core",), 1), place)
    return unpack(swap_all(parts, ("blk",)), place)


def solution(mesh):
    blk, tile = mesh.shape["blk"], mesh.shape["tile"]
    fine = Mesh(mesh.devices.reshape(blk, tile // 2, 2), ALL)
    in_specs = (P(None, ALL, None), P(), P(("row", "core"), None))
    return jax.shard_map(
        on_device, mesh=fine, in_specs=in_specs, out_specs=P(ALL, None), check_vma=False
    )
```

```python
import functools
import math

import jax
import jax.numpy as jnp
from jax import lax
from jax.experimental import pallas as pl
from jax.experimental.pallas import tpu as pltpu
from jax.sharding import Mesh
from jax.sharding import PartitionSpec as P

FRB = 2
TPF = 16
ALL = ("blk", "row", "core")
PLANE = ("blk", "core")
VMEM = pl.BlockSpec(memory_space=pltpu.VMEM)
SMEM = pl.BlockSpec(memory_space=pltpu.SMEM)
ANY = pl.BlockSpec(memory_space=pl.ANY)
PARAMS = pltpu.CompilerParams(vmem_limit_bytes=48 * 1024 * 1024)


def pack_kernel(head_dim, x_ref, out_ref):
    peers, _, width = out_ref.shape
    kinds, tok, _ = x_ref.shape
    heads = width // head_dim
    for g in range(peers):
        for i in range(heads):
            head = (g // 2 * heads + i) * 2 + g % 2
            for k in range(kinds):
                out_ref[g, k * tok:(k + 1) * tok, i * head_dim:(i + 1) * head_dim] = x_ref[
                    k, :, head * head_dim:(head + 1) * head_dim
                ]


def pack(x, peers, head_dim):
    kinds, tok, cols = x.shape
    return pl.pallas_call(
        functools.partial(pack_kernel, head_dim),
        out_shape=jax.ShapeDtypeStruct((peers, kinds * tok, cols // peers), x.dtype),
        in_specs=[VMEM],
        out_specs=VMEM,
        compiler_params=PARAMS,
    )(x)


def columns_kernel(at_ref, x_ref, out_ref, *refs):
    *part_refs, sem = refs
    cols = out_ref.shape[1]
    start = pl.multiple_of(at_ref[0] * cols, cols)
    copy = pltpu.make_async_copy(x_ref.at[:, pl.ds(start, cols)], out_ref, sem)
    copy.start()
    copy.wait()
    first = 0
    for ref in part_refs:
        ref[...] = out_ref[first:first + ref.shape[0], :]
        first += ref.shape[0]


def columns(x, at, parts, cuts):
    depth, cols = x.shape
    like = [jax.ShapeDtypeStruct((n, cols // parts), x.dtype) for n in (depth, *cuts)]
    return pl.pallas_call(
        columns_kernel,
        out_shape=like,
        in_specs=[SMEM, pl.BlockSpec(memory_space=pltpu.HBM)],
        out_specs=[VMEM] * len(like),
        scratch_shapes=[pltpu.SemaphoreType.DMA],
        compiler_params=PARAMS,
    )(at, x)


def cut_kernel(x_ref, *refs):
    q_ref, kv_ref = refs[len(refs) // 2 - 1:][:2]
    tok = q_ref.shape[1]
    q_ref[...] = x_ref[:, :tok, :]
    kv_ref[...] = x_ref[:, tok:, :]


def cut(x, passed):
    peers, depth, width = x.shape
    tok, n = depth // 3, len(passed)
    q, kv, *same = pl.pallas_call(
        cut_kernel,
        out_shape=[
            jax.ShapeDtypeStruct((peers, tok, width), x.dtype),
            jax.ShapeDtypeStruct((peers, 2 * tok, width), x.dtype),
        ] + [jax.ShapeDtypeStruct(y.shape, y.dtype) for y in passed],
        in_specs=[VMEM] + [ANY] * n,
        out_specs=[VMEM, VMEM] + [ANY] * n,
        input_output_aliases={1 + i: 2 + i for i in range(n)},
        compiler_params=PARAMS,
    )(x, *passed)
    return q, kv, same


def after_kernel(*refs):
    pass


def after(x, passed):
    return pl.pallas_call(
        after_kernel,
        out_shape=jax.ShapeDtypeStruct(passed.shape, passed.dtype),
        in_specs=[ANY, ANY],
        out_specs=ANY,
        input_output_aliases={1: 0},
        compiler_params=PARAMS,
    )(x, passed)


def clip_of(token, blk_tokens, tok_dev, clip_ref):
    frame = token // blk_tokens * FRB + token % tok_dev // TPF
    clip = jnp.zeros_like(token)
    for f in range(clip_ref.shape[0]):
        clip = jnp.where(frame == f, clip_ref[f], clip)
    return clip


def attention_kernel(head_dim, n_kv, n_passed, last, clip_ref, q_ref, *refs):
    kv_refs, refs = refs[:n_kv], refs[n_kv:]
    state_refs = refs[:3 if last else 0]
    out_refs = refs[len(state_refs) + n_passed:]
    peers, tok, width = q_ref.shape
    count = peers * tok
    scale = 1.0 / math.sqrt(head_dim)
    row_clip = clip_of(
        lax.broadcasted_iota(jnp.int32, (count, 1), 0), 2 * tok, tok, clip_ref
    )
    col_clip = clip_of(
        lax.broadcasted_iota(jnp.int32, (1, count), 1), 2 * tok, tok, clip_ref
    )
    allowed = row_clip == col_clip
    per_step = max(1, 1024 // count)
    for h in range(width // head_dim):
        cols = slice(h * head_dim, (h + 1) * head_dim)
        queries = q_ref[:, :, cols].reshape(count, head_dim)
        top = total = acc = None
        if last:
            top, total, acc = state_refs[0][h], state_refs[1][h], state_refs[2][:, cols]
        for first in range(0, n_kv, per_step):
            scores, values = [], []
            for ref in kv_refs[first:first + per_step]:
                keys = ref[:, 0:tok, cols].reshape(count, head_dim)
                values.append(ref[:, tok:2 * tok, cols].reshape(count, head_dim))
                s = lax.dot_general(
                    queries, keys, (((1,), (1,)), ((), ())), preferred_element_type=jnp.float32
                )
                scores.append(jnp.where(allowed, s * scale, -1e30))
            new_top = functools.reduce(
                jnp.maximum, [jnp.max(s, axis=1, keepdims=True) for s in scores]
            )
            if top is not None:
                new_top = jnp.maximum(top, new_top)
                factor = jnp.exp(top - new_top)
                total, acc = total * factor, acc * factor
            top = new_top
            for s, v in zip(scores, values):
                p = jnp.where(allowed, jnp.exp(s - top), 0.0)
                part = jnp.sum(p, axis=1, keepdims=True)
                dot = jnp.dot(p.astype(jnp.bfloat16), v, preferred_element_type=jnp.float32)
                total = part if total is None else total + part
                acc = dot if acc is None else acc + dot
        if last:
            out_refs[0][:, cols] = (acc / total).astype(out_refs[0].dtype)
        else:
            out_refs[0][h], out_refs[1][h], out_refs[2][:, cols] = top, total, acc


def attention(q, kvs, state, frame_clip, head_dim, passed):
    peers, tok, width = q.shape
    count = peers * tok
    stat = jax.ShapeDtypeStruct((width // head_dim, count, 1), jnp.float32)
    if state:
        out = [jax.ShapeDtypeStruct((count, width), q.dtype)]
    else:
        out = [stat, stat, jax.ShapeDtypeStruct((count, width), jnp.float32)]
    given, n = 2 + len(kvs) + len(state), len(passed)
    result = pl.pallas_call(
        functools.partial(attention_kernel, head_dim, len(kvs), n, bool(state)),
        out_shape=out + [jax.ShapeDtypeStruct(x.shape, x.dtype) for x in passed],
        in_specs=[SMEM] + [VMEM] * (given - 1) + [ANY] * n,
        out_specs=[VMEM] * len(out) + [ANY] * n,
        input_output_aliases={given + i: len(out) + i for i in range(n)},
        compiler_params=PARAMS,
    )(frame_clip, q, *kvs, *state, *passed)
    return result[:len(out)], result[len(out):]


def project_kernel(n_attn, sizes, at_ref, place_ref, *refs):
    attn_refs, pieces = refs[:n_attn], list(refs[n_attn:-3])
    mine_ref, theirs_ref, a_ref = refs[-3:]
    w_refs = [[pieces.pop(0) for _ in range(n)] for n in sizes]
    width = attn_refs[0].shape[1]
    head_dim = sum(ref.shape[0] for ref in w_refs[0])
    blks, tok, cols = mine_ref.shape
    blk, core = place_ref[0] // 2, place_ref[0] % 2
    for k, ref in enumerate(attn_refs):
        a_ref[:, pl.ds(pl.multiple_of((blk ^ k) * width, width), width)] = ref[...]
    result = None
    for i in range(0, len(w_refs), 2):
        left = [
            a_ref[:, pl.ds(pl.multiple_of(at_ref[j] * head_dim, head_dim), head_dim)]
            for j in (i, i + 1)
        ]
        right = [ref[...] for j in (i, i + 1) for ref in w_refs[j]]
        part = jnp.dot(
            jnp.concatenate(left, axis=1), jnp.concatenate(right, axis=0),
            preferred_element_type=jnp.float32,
        )
        result = part if result is None else result + part
    result = result.astype(mine_ref.dtype).reshape(blks, 2, tok, cols)

    @pl.when(core == 0)
    def _():
        mine_ref[...] = result[:, 0]
        theirs_ref[...] = result[:, 1]

    @pl.when(core != 0)
    def _():
        mine_ref[...] = result[:, 1]
        theirs_ref[...] = result[:, 0]


def project(attns, w_parts, at, place, tok):
    count, width = attns[0].shape
    blks, cols = len(attns), w_parts[0][0].shape[1]
    sizes = [len(pieces) for pieces in w_parts]
    like = jax.ShapeDtypeStruct((blks, tok, cols), attns[0].dtype)
    return pl.pallas_call(
        functools.partial(project_kernel, blks, sizes),
        out_shape=(like, like),
        in_specs=[SMEM, SMEM] + [VMEM] * (blks + sum(sizes)),
        out_specs=(VMEM, VMEM),
        scratch_shapes=[pltpu.VMEM((count, blks * width), attns[0].dtype)],
        compiler_params=PARAMS,
    )(at, place, *attns, *sum(w_parts, []))


def add_kernel(place_ref, x_ref, y_ref, *out_refs):
    for k, out_ref in enumerate(out_refs):
        at = place_ref[0] // 2 ^ k
        both = x_ref[at].astype(jnp.float32) + y_ref[at].astype(jnp.float32)
        out_ref[...] = both.astype(out_ref.dtype)


def add(x, y, place):
    blks = x.shape[0]
    return pl.pallas_call(
        add_kernel,
        out_shape=[jax.ShapeDtypeStruct(x.shape[1:], x.dtype)] * blks,
        in_specs=[SMEM, VMEM, VMEM],
        out_specs=[VMEM] * blks,
        compiler_params=PARAMS,
    )(place, x, y)


def unpack_kernel(place_ref, *refs):
    *in_refs, out_ref = refs
    width = in_refs[0].shape[1]
    for k, ref in enumerate(in_refs):
        at = place_ref[0] // 2 ^ k
        out_ref[:, pl.ds(pl.multiple_of(at * width, width), width)] = ref[...]


def unpack(parts, place):
    tok, width = parts[0].shape
    return pl.pallas_call(
        unpack_kernel,
        out_shape=jax.ShapeDtypeStruct((tok, len(parts) * width), parts[0].dtype),
        in_specs=[SMEM] + [VMEM] * len(parts),
        out_specs=VMEM,
        compiler_params=PARAMS,
    )(place, *parts)


def xor(x, axis, by):
    size = math.prod(lax.axis_size(name) for name in axis)
    return lax.ppermute(x, axis, [(i, i ^ by) for i in range(size)])


def swap_all(parts, axis):
    return [parts[0]] + [xor(x, axis, m) for m, x in enumerate(parts) if m]


def on_device(qkv, frame_clip, w_out):
    rows, blks = lax.axis_size("row"), lax.axis_size("blk")
    row = lax.axis_index("row")
    tok = qkv.shape[1]
    head_dim = w_out.shape[0]
    blk = lax.axis_index("blk").astype(jnp.int32).reshape(1)
    place = blk * 2 + lax.axis_index("core").astype(jnp.int32)
    along = lambda x, by: xor(x, ("row",), by)

    line = rows == 4
    last = head_dim // 4
    w_own, w_first, w_last = columns(w_out, blk, blks, (head_dim - last, last))
    packed = pack(qkv, 2 * blks, head_dim)
    own = lax.all_to_all(packed, PLANE, split_axis=0, concat_axis=0, tiled=True)
    if line:
        q, kv, (far_first, next_w) = cut(own, [along(w_first, 3), along(w_own, 1)])
        far, near = along(kv, 3), along(kv, 1)
        far_last = along(after(near, w_last), 3)
        end = along(far, 1)
        state, (far_first,) = attention(q, [kv, far, near], [], frame_clip, head_dim, [far_first])
        end_first = along(far_first, 1)
        (attn,), (far_last,) = attention(q, [end], state, frame_clip, head_dim, [far_last])
        end_last = along(far_last, 1)
        steps = [0, 1, 3, 2]
        w_parts = [[w_own], [next_w], [far_first, far_last], [end_first, end_last]]
    else:
        steps = list(range(rows))
        q, kv, _ = cut(own, [])
        kvs = [kv] + [along(kv, by) for by in steps[1:]]
        state, _ = attention(q, kvs[:-1], [], frame_clip, head_dim, [])
        (attn,), _ = attention(q, kvs[-1:], state, frame_clip, head_dim, [])
        w_parts = [[w_own]] + [[along(w_own, by)] for by in steps[1:]]
    attns = swap_all([attn] * blks, ("blk",))
    at = jnp.stack([row ^ by for by in steps]).astype(jnp.int32)
    mine, theirs = project(attns, w_parts, at, place, tok)
    parts = add(mine, xor(theirs, ("core",), 1), place)
    return unpack(swap_all(parts, ("blk",)), place)


def solution(mesh):
    blk, tile = mesh.shape["blk"], mesh.shape["tile"]
    fine = Mesh(mesh.devices.reshape(blk, tile // 2, 2), ALL)
    in_specs = (P(None, ALL, None), P(), P(("row", "core"), None))
    return jax.shard_map(
        on_device, mesh=fine, in_specs=in_specs, out_specs=P(ALL, None), check_vma=False
    )
```

```python
import functools
import math

import jax
import jax.numpy as jnp
from jax import lax
from jax.experimental import pallas as pl
from jax.experimental.pallas import tpu as pltpu
from jax.sharding import Mesh
from jax.sharding import PartitionSpec as P

FRB = 2
TPF = 16
VMEM = pl.BlockSpec(memory_space=pltpu.VMEM)
SMEM = pl.BlockSpec(memory_space=pltpu.SMEM)
ANY = pl.BlockSpec(memory_space=pl.ANY)
AHEAD = pl.CostEstimate(flops=20_000_000_000, bytes_accessed=1_000_000, transcendentals=0)
PARAMS = pltpu.CompilerParams(vmem_limit_bytes=48 * 1024 * 1024)


def pack_kernel(head_dim, x_ref, out_ref):
    peers, _, width = out_ref.shape
    kinds, tok, _ = x_ref.shape
    heads = width // head_dim
    for g in range(peers):
        for i in range(heads):
            head = (g // 2 * heads + i) * 2 + g % 2
            for k in range(kinds):
                out_ref[g, k * tok:(k + 1) * tok, i * head_dim:(i + 1) * head_dim] = x_ref[
                    k, :, head * head_dim:(head + 1) * head_dim
                ]


def pack(x, peers, head_dim):
    kinds, tok, cols = x.shape
    return pl.pallas_call(
        functools.partial(pack_kernel, head_dim),
        out_shape=jax.ShapeDtypeStruct((peers, kinds * tok, cols // peers), x.dtype),
        in_specs=[VMEM],
        out_specs=VMEM,
        compiler_params=PARAMS,
    )(x)


def columns_kernel(at_ref, x_ref, *refs):
    *out_refs, sems = refs
    copies = []
    for i, ref in enumerate(out_refs):
        depth, cols = ref.shape
        first = pl.multiple_of(at_ref[2 * i] * depth, depth)
        start = pl.multiple_of(at_ref[2 * i + 1] * cols, cols)
        copies.append(
            pltpu.make_async_copy(
                x_ref.at[pl.ds(first, depth), pl.ds(start, cols)], ref, sems.at[i]
            )
        )
    for copy in copies:
        copy.start()
    for copy in copies:
        copy.wait()


def columns(x, pieces, cols):
    at = jnp.stack([jnp.asarray(i, jnp.int32) for piece in pieces for i in piece[1:]])
    return pl.pallas_call(
        columns_kernel,
        out_shape=[jax.ShapeDtypeStruct((piece[0], cols), x.dtype) for piece in pieces],
        in_specs=[SMEM, pl.BlockSpec(memory_space=pltpu.HBM)],
        out_specs=[VMEM] * len(pieces),
        scratch_shapes=[pltpu.SemaphoreType.DMA((len(pieces),))],
        compiler_params=PARAMS,
    )(at, x)


def cut_kernel(x_ref, *refs):
    q_ref, kv_ref = refs[len(refs) // 2 - 1:][:2]
    tok = q_ref.shape[1]
    q_ref[...] = x_ref[:, :tok, :]
    kv_ref[...] = x_ref[:, tok:, :]


def cut(x, passed):
    peers, depth, width = x.shape
    tok, n = depth // 3, len(passed)
    q, kv, *same = pl.pallas_call(
        cut_kernel,
        out_shape=[
            jax.ShapeDtypeStruct((peers, tok, width), x.dtype),
            jax.ShapeDtypeStruct((peers, 2 * tok, width), x.dtype),
        ] + [jax.ShapeDtypeStruct(y.shape, y.dtype) for y in passed],
        in_specs=[VMEM] + [ANY] * n,
        out_specs=[VMEM, VMEM] + [ANY] * n,
        input_output_aliases={1 + i: 2 + i for i in range(n)},
        compiler_params=PARAMS,
    )(x, *passed)
    return q, kv, same


def after_kernel(*refs):
    pass


def after(x, passed):
    return pl.pallas_call(
        after_kernel,
        out_shape=jax.ShapeDtypeStruct(passed.shape, passed.dtype),
        in_specs=[ANY, ANY],
        out_specs=ANY,
        input_output_aliases={1: 0},
        compiler_params=PARAMS,
    )(x, passed)


def clip_of(token, base, span, tok_dev, clip_ref):
    frame = base + token // span * FRB + token % tok_dev // TPF
    clip = jnp.zeros_like(token)
    for f in range(clip_ref.shape[0]):
        clip = jnp.where(frame == f, clip_ref[f], clip)
    return clip


def attention_kernel(head_dim, span, base_ref, clip_ref, q_ref, *refs):
    *kv_refs, out_ref = refs
    peers, tok, width = q_ref.shape
    count = peers * tok
    scale = 1.0 / math.sqrt(head_dim)
    row = lax.broadcasted_iota(jnp.int32, (count, 1), 0)
    col = lax.broadcasted_iota(jnp.int32, (1, count), 1)
    row_clip = clip_of(row, base_ref[0], span, tok, clip_ref)
    per_step = max(1, 1024 // count)
    for h in range(width // head_dim):
        cols = slice(h * head_dim, (h + 1) * head_dim)
        queries = q_ref[:, :, cols].reshape(count, head_dim)
        top = total = acc = None
        for first in range(0, len(kv_refs), per_step):
            scores, masks, values = [], [], []
            for i, ref in enumerate(kv_refs[first:first + per_step], first):
                keys = ref[:, 0:tok, cols].reshape(count, head_dim)
                values.append(ref[:, tok:2 * tok, cols].reshape(count, head_dim))
                s = lax.dot_general(
                    queries, keys, (((1,), (1,)), ((), ())), preferred_element_type=jnp.float32
                )
                masks.append(row_clip == clip_of(col, base_ref[i], span, tok, clip_ref))
                scores.append(jnp.where(masks[-1], s * scale, -1e30))
            new_top = functools.reduce(
                jnp.maximum, [jnp.max(s, axis=1, keepdims=True) for s in scores]
            )
            if top is not None:
                new_top = jnp.maximum(top, new_top)
                factor = jnp.exp(top - new_top)
                total, acc = total * factor, acc * factor
            top = new_top
            for s, allowed, v in zip(scores, masks, values):
                p = jnp.where(allowed, jnp.exp(s - top), 0.0)
                part = jnp.sum(p, axis=1, keepdims=True)
                dot = jnp.dot(p.astype(jnp.bfloat16), v, preferred_element_type=jnp.float32)
                total = part if total is None else total + part
                acc = dot if acc is None else acc + dot
        out_ref[:, cols] = (acc / total).astype(out_ref.dtype)


def attention(q, kvs, bases, span, frame_clip, head_dim):
    peers, tok, width = q.shape
    return pl.pallas_call(
        functools.partial(attention_kernel, head_dim, span),
        out_shape=jax.ShapeDtypeStruct((peers * tok, width), q.dtype),
        in_specs=[SMEM, SMEM] + [VMEM] * (1 + len(kvs)),
        out_specs=VMEM,
        compiler_params=PARAMS,
        cost_estimate=AHEAD,
    )(jnp.stack([jnp.asarray(i, jnp.int32) for i in bases]), frame_clip, q, *kvs)


def project_kernel(n_attn, at_ref, place_ref, *refs):
    attn_refs, w_refs = refs[:n_attn], refs[n_attn:-4]
    mine_ref, theirs_ref, a_ref, w_all = refs[-4:]
    width = attn_refs[0].shape[1]
    blks, tok, cols = mine_ref.shape
    blk, core = place_ref[0] // 2, place_ref[0] % 2
    for k, ref in enumerate(attn_refs):
        a_ref[:, pl.ds(pl.multiple_of((blk ^ k) * width, width), width)] = ref[...]
    for i, ref in enumerate(w_refs):
        rows = ref.shape[0]
        w_all[pl.ds(pl.multiple_of(at_ref[i] * rows, rows), rows), :] = ref[...]
    result = jnp.dot(a_ref[...], w_all[...], preferred_element_type=jnp.float32)
    result = result.astype(mine_ref.dtype).reshape(blks, 2, tok, cols)

    @pl.when(core == 0)
    def _():
        mine_ref[...] = result[:, 0]
        theirs_ref[...] = result[:, 1]

    @pl.when(core != 0)
    def _():
        mine_ref[...] = result[:, 1]
        theirs_ref[...] = result[:, 0]


def project(attns, w_parts, at, place, tok):
    count, width = attns[0].shape
    blks, cols = len(attns), w_parts[0].shape[1]
    like = jax.ShapeDtypeStruct((blks, tok, cols), attns[0].dtype)
    return pl.pallas_call(
        functools.partial(project_kernel, blks),
        out_shape=(like, like),
        in_specs=[SMEM, SMEM] + [VMEM] * (blks + len(w_parts)),
        out_specs=(VMEM, VMEM),
        scratch_shapes=[
            pltpu.VMEM((count, blks * width), attns[0].dtype),
            pltpu.VMEM((blks * width, cols), attns[0].dtype),
        ],
        compiler_params=PARAMS,
    )(jnp.stack(at).astype(jnp.int32), place, *attns, *w_parts)


def add_kernel(place_ref, x_ref, y_ref, *out_refs):
    for k, out_ref in enumerate(out_refs):
        at = place_ref[0] // 2 ^ k
        both = x_ref[at].astype(jnp.float32) + y_ref[at].astype(jnp.float32)
        out_ref[...] = both.astype(out_ref.dtype)


def add(x, y, place):
    blks = x.shape[0]
    return pl.pallas_call(
        add_kernel,
        out_shape=[jax.ShapeDtypeStruct(x.shape[1:], x.dtype)] * blks,
        in_specs=[SMEM, VMEM, VMEM],
        out_specs=[VMEM] * blks,
        compiler_params=PARAMS,
    )(place, x, y)


def unpack_kernel(place_ref, *refs):
    *in_refs, out_ref = refs
    width = in_refs[0].shape[1]
    for k, ref in enumerate(in_refs):
        at = place_ref[0] // 2 ^ k
        out_ref[:, pl.ds(pl.multiple_of(at * width, width), width)] = ref[...]


def unpack(parts, place):
    tok, width = parts[0].shape
    return pl.pallas_call(
        unpack_kernel,
        out_shape=jax.ShapeDtypeStruct((tok, len(parts) * width), parts[0].dtype),
        in_specs=[SMEM] + [VMEM] * len(parts),
        out_specs=VMEM,
        compiler_params=PARAMS,
    )(place, *parts)


def xor(x, axis, by):
    size = math.prod(lax.axis_size(name) for name in axis)
    return lax.ppermute(x, axis, [(i, i ^ by) for i in range(size)])


def swap_all(parts, axis):
    return [parts[0]] + [xor(x, axis, m) for m, x in enumerate(parts) if m]


def squares(qkv, frame_clip, w_out):
    group, quarter = ("x", "zl", "core"), ("x", "zl")
    y, x, zh, zl, core = (lax.axis_index(n) for n in ("y", "x", "zh", "zl", "core"))
    tok, head_dim, cols = qkv.shape[1], w_out.shape[0], w_out.shape[1] // 4
    place = ((x * 2 + zl) * 2 + core).astype(jnp.int32).reshape(1)
    mine, theirs = x * 2 + zl, x * 2 + 1 - zl
    row, half = zh * 2 + zl, head_dim // 2

    w_own, w_far, w_corner, w_near = columns(
        w_out,
        [(head_dim, 0, mine), (half, y, mine), (half, y, theirs), (head_dim, 0, theirs)],
        cols,
    )
    far = xor(w_far, ("zh",), 1)
    near = xor(w_near, ("zl",), 1)
    packed = pack(qkv, 8, head_dim)
    own = lax.all_to_all(packed, group, split_axis=0, concat_axis=0, tiled=True)
    q, kv, (far, w_corner) = cut(own, [far, w_corner])
    kv_far, kv_near = xor(kv, ("zh",), 1), xor(kv, ("y",), 1)
    corner = xor(w_corner, ("zh", "zl"), 3)
    far_rest = xor(far, ("y",), 1)
    kv_end = xor(kv_far, ("y",), 1)

    base, other = y * 2 * FRB, (1 - y) * 2 * FRB
    attn = attention(
        q, [kv, kv_far, kv_near, kv_end], [base, base, other, other], 4 * tok, frame_clip, head_dim
    )
    corner = after(attn, corner)
    corner_rest = xor(corner, ("y",), 1)
    attns = swap_all([attn] * 4, quarter)
    w_parts = [w_own, near, far, far_rest, corner, corner_rest]
    at = [row, row ^ 1] + [2 * (row ^ by) + h for by in (2, 3) for h in (y, 1 - y)]
    ours, other_core = project(attns, w_parts, at, place, tok)
    parts = add(ours, xor(other_core, ("core",), 1), place)
    return unpack(swap_all(parts, quarter), place)


def layers(qkv, frame_clip, w_out):
    rows, blks = lax.axis_size("row"), lax.axis_size("blk")
    row, blk = lax.axis_index("row"), lax.axis_index("blk")
    tok, head_dim, cols = qkv.shape[1], w_out.shape[0], w_out.shape[1] // blks
    place = (blk * 2 + lax.axis_index("core")).astype(jnp.int32).reshape(1)
    others = range(1, rows)

    (w_own,) = columns(w_out, [(head_dim, 0, blk)], cols)
    w_parts = [w_own] + [xor(w_own, ("row",), by) for by in others]
    packed = pack(qkv, 2 * blks, head_dim)
    own = lax.all_to_all(packed, ("blk", "core"), split_axis=0, concat_axis=0, tiled=True)
    q, kv, _ = cut(own, [])
    kvs = [kv] + [xor(kv, ("row",), by) for by in others]
    attn = attention(q, kvs, [0] * rows, 2 * tok, frame_clip, head_dim)
    attns = swap_all([attn] * blks, ("blk",))
    ours, other_core = project(attns, w_parts, [row ^ by for by in range(rows)], place, tok)
    parts = add(ours, xor(other_core, ("core",), 1), place)
    return unpack(swap_all(parts, ("blk",)), place)


def solution(mesh):
    blk, tile = mesh.shape["blk"], mesh.shape["tile"]
    if (blk, tile) == (4, 8):
        plan, names, shape = squares, ("y", "x", "zh", "zl", "core"), (2, 2, 2, 2, 2)
    else:
        plan, names, shape = layers, ("blk", "row", "core"), (blk, tile // 2, 2)
    fine = Mesh(mesh.devices.reshape(shape), names)
    tiles = names[2:] if plan is squares else names[1:]
    in_specs = (P(None, names, None), P(), P(tiles, None))
    return jax.shard_map(
        plan, mesh=fine, in_specs=in_specs, out_specs=P(names, None), check_vma=False
    )
```

```python
import functools
import math

import jax
import jax.numpy as jnp
from jax import lax
from jax.experimental import pallas as pl
from jax.experimental.pallas import tpu as pltpu
from jax.sharding import Mesh
from jax.sharding import PartitionSpec as P

FRB = 2
TPF = 16
VMEM = pl.BlockSpec(memory_space=pltpu.VMEM)
SMEM = pl.BlockSpec(memory_space=pltpu.SMEM)
ANY = pl.BlockSpec(memory_space=pl.ANY)
AHEAD = pl.CostEstimate(flops=20_000_000_000, bytes_accessed=1_000_000, transcendentals=0)
PARAMS = pltpu.CompilerParams(vmem_limit_bytes=48 * 1024 * 1024)


def pack_kernel(head_dim, x_ref, out_ref):
    peers, _, width = out_ref.shape
    kinds, tok, _ = x_ref.shape
    heads = width // head_dim
    for g in range(peers):
        for i in range(heads):
            head = (g // 2 * heads + i) * 2 + g % 2
            for k in range(kinds):
                out_ref[g, k * tok:(k + 1) * tok, i * head_dim:(i + 1) * head_dim] = x_ref[
                    k, :, head * head_dim:(head + 1) * head_dim
                ]


def pack(x, peers, head_dim):
    kinds, tok, cols = x.shape
    return pl.pallas_call(
        functools.partial(pack_kernel, head_dim),
        out_shape=jax.ShapeDtypeStruct((peers, kinds * tok, cols // peers), x.dtype),
        in_specs=[VMEM],
        out_specs=VMEM,
        compiler_params=PARAMS,
    )(x)


def columns_kernel(at_ref, x_ref, *refs):
    *out_refs, sems = refs
    copies = []
    for i, ref in enumerate(out_refs):
        depth, cols = ref.shape
        first = pl.multiple_of(at_ref[2 * i] * depth, depth)
        start = pl.multiple_of(at_ref[2 * i + 1] * cols, cols)
        copies.append(
            pltpu.make_async_copy(
                x_ref.at[pl.ds(first, depth), pl.ds(start, cols)], ref, sems.at[i]
            )
        )
    for copy in copies:
        copy.start()
    for copy in copies:
        copy.wait()


def columns(x, pieces, cols):
    at = jnp.stack([jnp.asarray(i, jnp.int32) for piece in pieces for i in piece[1:]])
    return pl.pallas_call(
        columns_kernel,
        out_shape=[jax.ShapeDtypeStruct((piece[0], cols), x.dtype) for piece in pieces],
        in_specs=[SMEM, pl.BlockSpec(memory_space=pltpu.HBM)],
        out_specs=[VMEM] * len(pieces),
        scratch_shapes=[pltpu.SemaphoreType.DMA((len(pieces),))],
        compiler_params=PARAMS,
    )(at, x)


def cut_kernel(x_ref, *refs):
    q_ref, kv_ref = refs[len(refs) // 2 - 1:][:2]
    tok = q_ref.shape[1]
    q_ref[...] = x_ref[:, :tok, :]
    kv_ref[...] = x_ref[:, tok:, :]


def cut(x, passed):
    peers, depth, width = x.shape
    tok, n = depth // 3, len(passed)
    q, kv, *same = pl.pallas_call(
        cut_kernel,
        out_shape=[
            jax.ShapeDtypeStruct((peers, tok, width), x.dtype),
            jax.ShapeDtypeStruct((peers, 2 * tok, width), x.dtype),
        ] + [jax.ShapeDtypeStruct(y.shape, y.dtype) for y in passed],
        in_specs=[VMEM] + [ANY] * n,
        out_specs=[VMEM, VMEM] + [ANY] * n,
        input_output_aliases={1 + i: 2 + i for i in range(n)},
        compiler_params=PARAMS,
    )(x, *passed)
    return q, kv, same


def after_kernel(*refs):
    pass


def after(passed, *first, cost=None):
    return pl.pallas_call(
        after_kernel,
        out_shape=jax.ShapeDtypeStruct(passed.shape, passed.dtype),
        in_specs=[ANY] * (1 + len(first)),
        out_specs=ANY,
        input_output_aliases={0: 0},
        compiler_params=PARAMS,
        cost_estimate=cost,
    )(passed, *first)


def clip_of(token, base, span, tok_dev, clip_ref):
    frame = base + token // span * FRB + token % tok_dev // TPF
    clip = jnp.zeros_like(token)
    for f in range(clip_ref.shape[0]):
        clip = jnp.where(frame == f, clip_ref[f], clip)
    return clip


def attention_kernel(head_dim, span, base_ref, clip_ref, q_ref, *refs):
    *kv_refs, out_ref = refs
    peers, tok, width = q_ref.shape
    count = peers * tok
    scale = 1.0 / math.sqrt(head_dim)
    row = lax.broadcasted_iota(jnp.int32, (count, 1), 0)
    col = lax.broadcasted_iota(jnp.int32, (1, count), 1)
    row_clip = clip_of(row, base_ref[0], span, tok, clip_ref)
    per_step = max(1, 1024 // count)
    for h in range(width // head_dim):
        cols = slice(h * head_dim, (h + 1) * head_dim)
        queries = q_ref[:, :, cols].reshape(count, head_dim)
        top = total = acc = None
        for first in range(0, len(kv_refs), per_step):
            scores, masks, values = [], [], []
            for i, ref in enumerate(kv_refs[first:first + per_step], first):
                keys = ref[:, 0:tok, cols].reshape(count, head_dim)
                values.append(ref[:, tok:2 * tok, cols].reshape(count, head_dim))
                s = lax.dot_general(
                    queries, keys, (((1,), (1,)), ((), ())), preferred_element_type=jnp.float32
                )
                masks.append(row_clip == clip_of(col, base_ref[i], span, tok, clip_ref))
                scores.append(jnp.where(masks[-1], s * scale, -1e30))
            new_top = functools.reduce(
                jnp.maximum, [jnp.max(s, axis=1, keepdims=True) for s in scores]
            )
            if top is not None:
                new_top = jnp.maximum(top, new_top)
                factor = jnp.exp(top - new_top)
                total, acc = total * factor, acc * factor
            top = new_top
            for s, allowed, v in zip(scores, masks, values):
                p = jnp.where(allowed, jnp.exp(s - top), 0.0)
                part = jnp.sum(p, axis=1, keepdims=True)
                dot = jnp.dot(p.astype(jnp.bfloat16), v, preferred_element_type=jnp.float32)
                total = part if total is None else total + part
                acc = dot if acc is None else acc + dot
        out_ref[:, cols] = (acc / total).astype(out_ref.dtype)


def attention(q, kvs, bases, span, frame_clip, head_dim):
    peers, tok, width = q.shape
    return pl.pallas_call(
        functools.partial(attention_kernel, head_dim, span),
        out_shape=jax.ShapeDtypeStruct((peers * tok, width), q.dtype),
        in_specs=[SMEM, SMEM] + [VMEM] * (1 + len(kvs)),
        out_specs=VMEM,
        compiler_params=PARAMS,
    )(jnp.stack([jnp.asarray(i, jnp.int32) for i in bases]), frame_clip, q, *kvs)


def project_kernel(n_attn, at_ref, place_ref, *refs):
    attn_refs, w_refs = refs[:n_attn], refs[n_attn:-4]
    mine_ref, theirs_ref, a_ref, w_all = refs[-4:]
    width = attn_refs[0].shape[1]
    blks, tok, cols = mine_ref.shape
    blk, core = place_ref[0] // 2, place_ref[0] % 2
    for k, ref in enumerate(attn_refs):
        a_ref[:, pl.ds(pl.multiple_of((blk ^ k) * width, width), width)] = ref[...]
    for i, ref in enumerate(w_refs):
        rows = ref.shape[0]
        w_all[pl.ds(pl.multiple_of(at_ref[i] * rows, rows), rows), :] = ref[...]
    result = jnp.dot(a_ref[...], w_all[...], preferred_element_type=jnp.float32)
    result = result.astype(mine_ref.dtype).reshape(blks, 2, tok, cols)

    @pl.when(core == 0)
    def _():
        mine_ref[...] = result[:, 0]
        theirs_ref[...] = result[:, 1]

    @pl.when(core != 0)
    def _():
        mine_ref[...] = result[:, 1]
        theirs_ref[...] = result[:, 0]


def project(attns, w_parts, at, place, tok):
    count, width = attns[0].shape
    blks, cols = len(attns), w_parts[0].shape[1]
    like = jax.ShapeDtypeStruct((blks, tok, cols), attns[0].dtype)
    return pl.pallas_call(
        functools.partial(project_kernel, blks),
        out_shape=(like, like),
        in_specs=[SMEM, SMEM] + [VMEM] * (blks + len(w_parts)),
        out_specs=(VMEM, VMEM),
        scratch_shapes=[
            pltpu.VMEM((count, blks * width), attns[0].dtype),
            pltpu.VMEM((blks * width, cols), attns[0].dtype),
        ],
        compiler_params=PARAMS,
    )(jnp.stack(at).astype(jnp.int32), place, *attns, *w_parts)


def add_kernel(place_ref, x_ref, y_ref, *out_refs):
    for k, out_ref in enumerate(out_refs):
        at = place_ref[0] // 2 ^ k
        both = x_ref[at].astype(jnp.float32) + y_ref[at].astype(jnp.float32)
        out_ref[...] = both.astype(out_ref.dtype)


def add(x, y, place):
    blks = x.shape[0]
    return pl.pallas_call(
        add_kernel,
        out_shape=[jax.ShapeDtypeStruct(x.shape[1:], x.dtype)] * blks,
        in_specs=[SMEM, VMEM, VMEM],
        out_specs=[VMEM] * blks,
        compiler_params=PARAMS,
    )(place, x, y)


def unpack_kernel(place_ref, *refs):
    *in_refs, out_ref = refs
    width = in_refs[0].shape[1]
    for k, ref in enumerate(in_refs):
        at = place_ref[0] // 2 ^ k
        out_ref[:, pl.ds(pl.multiple_of(at * width, width), width)] = ref[...]


def unpack(parts, place):
    tok, width = parts[0].shape
    return pl.pallas_call(
        unpack_kernel,
        out_shape=jax.ShapeDtypeStruct((tok, len(parts) * width), parts[0].dtype),
        in_specs=[SMEM] + [VMEM] * len(parts),
        out_specs=VMEM,
        compiler_params=PARAMS,
    )(place, *parts)


def xor(x, axis, by):
    size = math.prod(lax.axis_size(name) for name in axis)
    return lax.ppermute(x, axis, [(i, i ^ by) for i in range(size)])


def swap_all(parts, axis):
    return [parts[0]] + [xor(x, axis, m) for m, x in enumerate(parts) if m]


def squares(qkv, frame_clip, w_out):
    group, quarter = ("x", "zl", "core"), ("x", "zl")
    y, x, zh, zl, core = (lax.axis_index(n) for n in ("y", "x", "zh", "zl", "core"))
    tok, head_dim, cols = qkv.shape[1], w_out.shape[0], w_out.shape[1] // 4
    place = ((x * 2 + zl) * 2 + core).astype(jnp.int32).reshape(1)
    mine, theirs = x * 2 + zl, x * 2 + 1 - zl
    row, half = zh * 2 + zl, head_dim // 2

    w_own, w_far, w_corner, w_near = columns(
        w_out,
        [(head_dim, 0, mine), (half, y, mine), (half, y, theirs), (head_dim, 0, theirs)],
        cols,
    )
    far = after(xor(w_far, ("zh",), 1), cost=AHEAD)
    near = xor(w_near, ("zl",), 1)
    packed = pack(qkv, 8, head_dim)
    own = lax.all_to_all(packed, group, split_axis=0, concat_axis=0, tiled=True)
    q, kv, (far, w_corner) = cut(own, [far, w_corner])
    kv_far, kv_near = xor(kv, ("zh",), 1), xor(kv, ("y",), 1)
    corner = xor(w_corner, ("zh", "zl"), 3)
    far_rest = xor(far, ("y",), 1)
    kv_end = xor(kv_far, ("y",), 1)

    base, other = y * 2 * FRB, (1 - y) * 2 * FRB
    attn = attention(
        q, [kv, kv_far, kv_near, kv_end], [base, base, other, other], 4 * tok, frame_clip, head_dim
    )
    corner = after(corner, attn)
    corner_rest = xor(corner, ("y",), 1)
    attns = swap_all([attn] * 4, quarter)
    w_parts = [w_own, near, far, far_rest, corner, corner_rest]
    at = [row, row ^ 1] + [2 * (row ^ by) + h for by in (2, 3) for h in (y, 1 - y)]
    ours, other_core = project(attns, w_parts, at, place, tok)
    parts = add(ours, xor(other_core, ("core",), 1), place)
    return unpack(swap_all(parts, quarter), place)


def layers(qkv, frame_clip, w_out):
    rows, blks = lax.axis_size("row"), lax.axis_size("blk")
    row, blk = lax.axis_index("row"), lax.axis_index("blk")
    tok, head_dim, cols = qkv.shape[1], w_out.shape[0], w_out.shape[1] // blks
    place = (blk * 2 + lax.axis_index("core")).astype(jnp.int32).reshape(1)
    others = range(1, rows)

    (w_own,) = columns(w_out, [(head_dim, 0, blk)], cols)
    w_parts = [w_own] + [xor(w_own, ("row",), by) for by in others]
    packed = pack(qkv, 2 * blks, head_dim)
    own = lax.all_to_all(packed, ("blk", "core"), split_axis=0, concat_axis=0, tiled=True)
    q, kv, _ = cut(own, [])
    kvs = [kv] + [xor(kv, ("row",), by) for by in others]
    attn = attention(q, kvs, [0] * rows, 2 * tok, frame_clip, head_dim)
    attns = swap_all([attn] * blks, ("blk",))
    ours, other_core = project(attns, w_parts, [row ^ by for by in range(rows)], place, tok)
    parts = add(ours, xor(other_core, ("core",), 1), place)
    return unpack(swap_all(parts, ("blk",)), place)


def solution(mesh):
    blk, tile = mesh.shape["blk"], mesh.shape["tile"]
    if (blk, tile) == (4, 8):
        plan, names, shape = squares, ("y", "x", "zh", "zl", "core"), (2, 2, 2, 2, 2)
    else:
        plan, names, shape = layers, ("blk", "row", "core"), (blk, tile // 2, 2)
    fine = Mesh(mesh.devices.reshape(shape), names)
    tiles = names[2:] if plan is squares else names[1:]
    in_specs = (P(None, names, None), P(), P(tiles, None))
    return jax.shard_map(
        plan, mesh=fine, in_specs=in_specs, out_specs=P(names, None), check_vma=False
    )
```

```python
import functools
import math

import jax
import jax.numpy as jnp
from jax import lax
from jax.experimental import pallas as pl
from jax.experimental.pallas import tpu as pltpu
from jax.sharding import Mesh
from jax.sharding import PartitionSpec as P

FRB = 2
TPF = 16
VMEM = pl.BlockSpec(memory_space=pltpu.VMEM)
SMEM = pl.BlockSpec(memory_space=pltpu.SMEM)
ANY = pl.BlockSpec(memory_space=pl.ANY)
AHEAD = pl.CostEstimate(flops=20_000_000_000, bytes_accessed=1_000_000, transcendentals=0)
PARAMS = pltpu.CompilerParams(vmem_limit_bytes=48 * 1024 * 1024)


def pack_kernel(head_dim, x_ref, out_ref):
    peers, _, width = out_ref.shape
    kinds, tok, _ = x_ref.shape
    heads = width // head_dim
    for g in range(peers):
        for i in range(heads):
            head = (g // 2 * heads + i) * 2 + g % 2
            for k in range(kinds):
                out_ref[g, k * tok:(k + 1) * tok, i * head_dim:(i + 1) * head_dim] = x_ref[
                    k, :, head * head_dim:(head + 1) * head_dim
                ]


def pack(x, peers, head_dim):
    kinds, tok, cols = x.shape
    return pl.pallas_call(
        functools.partial(pack_kernel, head_dim),
        out_shape=jax.ShapeDtypeStruct((peers, kinds * tok, cols // peers), x.dtype),
        in_specs=[VMEM],
        out_specs=VMEM,
        compiler_params=PARAMS,
    )(x)


def columns_kernel(at_ref, x_ref, *refs):
    *out_refs, sems = refs
    copies = []
    for i, ref in enumerate(out_refs):
        depth, cols = ref.shape
        first = pl.multiple_of(at_ref[2 * i] * depth, depth)
        start = pl.multiple_of(at_ref[2 * i + 1] * cols, cols)
        copies.append(
            pltpu.make_async_copy(
                x_ref.at[pl.ds(first, depth), pl.ds(start, cols)], ref, sems.at[i]
            )
        )
    for copy in copies:
        copy.start()
    for copy in copies:
        copy.wait()


def columns(x, pieces, cols):
    at = jnp.stack([jnp.asarray(i, jnp.int32) for piece in pieces for i in piece[1:]])
    return pl.pallas_call(
        columns_kernel,
        out_shape=[jax.ShapeDtypeStruct((piece[0], cols), x.dtype) for piece in pieces],
        in_specs=[SMEM, pl.BlockSpec(memory_space=pltpu.HBM)],
        out_specs=[VMEM] * len(pieces),
        scratch_shapes=[pltpu.SemaphoreType.DMA((len(pieces),))],
        compiler_params=PARAMS,
    )(at, pltpu.with_memory_space_constraint(x, pltpu.HBM))


def lane_kernel(head_dim, core_ref, x_ref, mine_ref, theirs_ref):
    kinds, tok, _ = x_ref.shape
    for out_ref, core in ((mine_ref, core_ref[0]), (theirs_ref, 1 - core_ref[0])):
        for g in range(out_ref.shape[0]):
            cols = pl.ds(pl.multiple_of((2 * g + core) * head_dim, head_dim), head_dim)
            for k in range(kinds):
                out_ref[g, k * tok:(k + 1) * tok, :] = x_ref[k, :, cols]


def lanes(x, core, head_dim):
    kinds, tok, cols = x.shape
    like = jax.ShapeDtypeStruct((cols // head_dim // 2, kinds * tok, head_dim), x.dtype)
    return pl.pallas_call(
        functools.partial(lane_kernel, head_dim),
        out_shape=(like, like),
        in_specs=[SMEM, VMEM],
        out_specs=(VMEM, VMEM),
        compiler_params=PARAMS,
    )(core, x)


def deal_kernel(place_ref, mine_ref, got_ref, *out_refs):
    quarter, core = place_ref[0] // 2, place_ref[0] % 2
    for k, out_ref in enumerate(out_refs):
        out_ref[core] = mine_ref[quarter ^ k]
        out_ref[1 - core] = got_ref[quarter ^ k]


def deal(mine, got, place):
    quarters, depth, width = mine.shape
    return pl.pallas_call(
        deal_kernel,
        out_shape=[jax.ShapeDtypeStruct((2, depth, width), mine.dtype)] * quarters,
        in_specs=[SMEM, VMEM, VMEM],
        out_specs=[VMEM] * quarters,
        compiler_params=PARAMS,
    )(place, mine, got)


def sort_kernel(n, place_ref, *refs):
    in_refs, (q_ref, k_ref, v_ref, kv_ref) = refs[:n], refs[-4:]
    tok = q_ref.shape[1]
    for i, ref in enumerate(in_refs):
        for core in range(2):
            at = (place_ref[0] // 2 ^ i) * 2 + core
            keys, values = ref[core, tok:2 * tok, :], ref[core, 2 * tok:, :]
            q_ref[at] = ref[core, 0:tok, :]
            k_ref[at] = keys
            v_ref[at] = values
            kv_ref[0, at] = keys
            kv_ref[1, at] = values


def sort(parts, place, passed):
    _, depth, width = parts[0].shape
    n = len(parts)
    one = (2 * n, depth // 3, width)
    like = [jax.ShapeDtypeStruct(shape, parts[0].dtype) for shape in (one, one, one, (2, *one))]
    same, *rest = pl.pallas_call(
        functools.partial(sort_kernel, n),
        out_shape=[jax.ShapeDtypeStruct(passed.shape, passed.dtype)] + like,
        in_specs=[SMEM] + [VMEM] * n + [ANY],
        out_specs=[ANY] + [VMEM] * 4,
        input_output_aliases={1 + n: 0},
        compiler_params=PARAMS,
    )(place, *parts, passed)
    return (*rest, same)


def cut_kernel(x_ref, q_ref, kv_ref):
    tok = q_ref.shape[1]
    q_ref[...] = x_ref[:, :tok, :]
    kv_ref[0] = x_ref[:, tok:2 * tok, :]
    kv_ref[1] = x_ref[:, 2 * tok:, :]


def cut(x):
    peers, depth, width = x.shape
    tok = depth // 3
    return pl.pallas_call(
        cut_kernel,
        out_shape=(
            jax.ShapeDtypeStruct((peers, tok, width), x.dtype),
            jax.ShapeDtypeStruct((2, peers, tok, width), x.dtype),
        ),
        in_specs=[VMEM],
        out_specs=(VMEM, VMEM),
        compiler_params=PARAMS,
    )(x)


def after_kernel(*refs):
    pass


def after(passed, *first, cost=None):
    return pl.pallas_call(
        after_kernel,
        out_shape=jax.ShapeDtypeStruct(passed.shape, passed.dtype),
        in_specs=[ANY] * (1 + len(first)),
        out_specs=ANY,
        input_output_aliases={0: 0},
        compiler_params=PARAMS,
        cost_estimate=cost,
    )(passed, *first)


def clip_of(token, base, span, tok_dev, clip_ref):
    frame = base + token // span * FRB + token % tok_dev // TPF
    clip = jnp.zeros_like(token)
    for f in range(clip_ref.shape[0]):
        clip = jnp.where(frame == f, clip_ref[f], clip)
    return clip


def attention_kernel(head_dim, span, joint, base_ref, clip_ref, q_ref, *refs):
    *refs, out_ref = refs
    k_refs, v_refs = [], []
    for both in joint:
        ref, *refs = refs
        k_refs.append(ref.at[0] if both else ref)
        if not both:
            value_ref, *refs = refs
        v_refs.append(ref.at[1] if both else value_ref)
    peers, tok, width = q_ref.shape
    count = peers * tok
    scale = math.log2(math.e) / math.sqrt(head_dim)
    row = lax.broadcasted_iota(jnp.int32, (count, 1), 0)
    col = lax.broadcasted_iota(jnp.int32, (1, count), 1)
    row_clip = clip_of(row, base_ref[0], span, tok, clip_ref)
    per_step = max(1, 1024 // count)
    for h in range(width // head_dim):
        cols = slice(h * head_dim, (h + 1) * head_dim)
        queries = q_ref[:, :, cols].reshape(count, head_dim)
        top = total = acc = None
        for first in range(0, len(k_refs), per_step):
            here = range(first, min(first + per_step, len(k_refs)))
            scores = []
            for i in here:
                keys = k_refs[i][:, :, cols].reshape(count, head_dim)
                s = lax.dot_general(
                    queries, keys, (((1,), (1,)), ((), ())), preferred_element_type=jnp.float32
                )
                allowed = row_clip == clip_of(col, base_ref[i], span, tok, clip_ref)
                scores.append(jnp.where(allowed, s * scale, -1e30))
            new_top = functools.reduce(
                jnp.maximum, [jnp.max(s, axis=1, keepdims=True) for s in scores]
            )
            if top is not None:
                new_top = jnp.maximum(top, new_top)
                factor = jnp.exp2(top - new_top)
                total, acc = total * factor, acc * factor
            top = new_top
            for i, s in zip(here, scores):
                p = jnp.exp2(s - top)
                part = jnp.sum(p, axis=1, keepdims=True)
                values = v_refs[i][:, :, cols].reshape(count, head_dim)
                dot = jnp.dot(
                    p.astype(jnp.bfloat16), values, preferred_element_type=jnp.float32
                )
                total = part if total is None else total + part
                acc = dot if acc is None else acc + dot
        out_ref[:, cols] = (acc / total).astype(out_ref.dtype)


def attention(q, kvs, bases, span, frame_clip, head_dim):
    peers, tok, width = q.shape
    joint = [not isinstance(kv, tuple) for kv in kvs]
    arrays = [x for kv, both in zip(kvs, joint) for x in ((kv,) if both else kv)]
    return pl.pallas_call(
        functools.partial(attention_kernel, head_dim, span, joint),
        out_shape=jax.ShapeDtypeStruct((peers * tok, width), q.dtype),
        in_specs=[SMEM, SMEM] + [VMEM] * (1 + len(arrays)),
        out_specs=VMEM,
        compiler_params=PARAMS,
    )(jnp.stack([jnp.asarray(i, jnp.int32) for i in bases]), frame_clip, q, *arrays)


def project_kernel(n_attn, at_ref, place_ref, *refs):
    attn_refs, w_refs = refs[:n_attn], refs[n_attn:-4]
    mine_ref, theirs_ref, a_ref, w_all = refs[-4:]
    width = attn_refs[0].shape[1]
    blks, tok, cols = mine_ref.shape
    blk, core = place_ref[0] // 2, place_ref[0] % 2
    for k, ref in enumerate(attn_refs):
        a_ref[:, pl.ds(pl.multiple_of((blk ^ k) * width, width), width)] = ref[...]
    for i, ref in enumerate(w_refs):
        rows = ref.shape[0]
        w_all[pl.ds(pl.multiple_of(at_ref[i] * rows, rows), rows), :] = ref[...]
    result = jnp.dot(a_ref[...], w_all[...], preferred_element_type=jnp.float32)
    result = result.astype(mine_ref.dtype).reshape(blks, 2, tok, cols)

    @pl.when(core == 0)
    def _():
        mine_ref[...] = result[:, 0]
        theirs_ref[...] = result[:, 1]

    @pl.when(core != 0)
    def _():
        mine_ref[...] = result[:, 1]
        theirs_ref[...] = result[:, 0]


def project(attns, w_parts, at, place, tok):
    count, width = attns[0].shape
    blks, cols = len(attns), w_parts[0].shape[1]
    like = jax.ShapeDtypeStruct((blks, tok, cols), attns[0].dtype)
    return pl.pallas_call(
        functools.partial(project_kernel, blks),
        out_shape=(like, like),
        in_specs=[SMEM, SMEM] + [VMEM] * (blks + len(w_parts)),
        out_specs=(VMEM, VMEM),
        scratch_shapes=[
            pltpu.VMEM((count, blks * width), attns[0].dtype),
            pltpu.VMEM((blks * width, cols), attns[0].dtype),
        ],
        compiler_params=PARAMS,
    )(jnp.stack(at).astype(jnp.int32), place, *attns, *w_parts)


def add_kernel(place_ref, x_ref, y_ref, *out_refs):
    for k, out_ref in enumerate(out_refs):
        at = place_ref[0] // 2 ^ k
        both = x_ref[at].astype(jnp.float32) + y_ref[at].astype(jnp.float32)
        out_ref[...] = both.astype(out_ref.dtype)


def add(x, y, place):
    blks = x.shape[0]
    return pl.pallas_call(
        add_kernel,
        out_shape=[jax.ShapeDtypeStruct(x.shape[1:], x.dtype)] * blks,
        in_specs=[SMEM, VMEM, VMEM],
        out_specs=[VMEM] * blks,
        compiler_params=PARAMS,
    )(place, x, y)


def unpack_kernel(place_ref, *refs):
    *in_refs, out_ref = refs
    width = in_refs[0].shape[1]
    for k, ref in enumerate(in_refs):
        at = place_ref[0] // 2 ^ k
        out_ref[:, pl.ds(pl.multiple_of(at * width, width), width)] = ref[...]


def unpack(parts, place):
    tok, width = parts[0].shape
    return pl.pallas_call(
        unpack_kernel,
        out_shape=jax.ShapeDtypeStruct((tok, len(parts) * width), parts[0].dtype),
        in_specs=[SMEM] + [VMEM] * len(parts),
        out_specs=VMEM,
        compiler_params=PARAMS,
    )(place, *parts)


def xor(x, axis, by):
    size = math.prod(lax.axis_size(name) for name in axis)
    return lax.ppermute(x, axis, [(i, i ^ by) for i in range(size)])


def swap_all(parts, axis):
    return [parts[0]] + [xor(x, axis, m) for m, x in enumerate(parts) if m]


def squares(qkv, frame_clip, w_out):
    quarter = ("x", "zl")
    y, x, zh, zl, core = (lax.axis_index(n) for n in ("y", "x", "zh", "zl", "core"))
    tok, head_dim, cols = qkv.shape[1], w_out.shape[0], w_out.shape[1] // 4
    place = ((x * 2 + zl) * 2 + core).astype(jnp.int32).reshape(1)
    mine, theirs = x * 2 + zl, x * 2 + 1 - zl
    row, half = zh * 2 + zl, head_dim // 2

    w_own, w_far, w_corner, w_near = columns(
        w_out,
        [(head_dim, 0, mine), (half, y, mine), (half, y, theirs), (head_dim, 0, theirs)],
        cols,
    )
    far = after(xor(w_far, ("zh",), 1), cost=AHEAD)
    near = xor(w_near, ("zl",), 1)
    kept, given = lanes(qkv, core.astype(jnp.int32).reshape(1), head_dim)
    parts = deal(kept, xor(given, ("core",), 1), place)
    q, k, v, kv, far = sort(swap_all(parts, quarter), place, far)
    w_corner = after(w_corner, k)
    k_far, v_far = xor(k, ("zh",), 1), xor(v, ("zh",), 1)
    corner = xor(w_corner, ("zh", "zl"), 3)
    kv_near = xor(kv, ("y",), 1)
    far_rest = xor(far, ("y",), 1)
    kvs = [kv, (k_far, v_far), kv_near, (xor(k_far, ("y",), 1), xor(v_far, ("y",), 1))]

    base, other = y * 2 * FRB, (1 - y) * 2 * FRB
    attn = attention(q, kvs, [base, base, other, other], 4 * tok, frame_clip, head_dim)
    corner = after(corner, attn)
    corner_rest = xor(corner, ("y",), 1)
    attns = swap_all([attn] * 4, quarter)
    w_parts = [w_own, near, far, far_rest, corner, corner_rest]
    at = [row, row ^ 1] + [2 * (row ^ by) + h for by in (2, 3) for h in (y, 1 - y)]
    ours, other_core = project(attns, w_parts, at, place, tok)
    parts = add(ours, xor(other_core, ("core",), 1), place)
    return unpack(swap_all(parts, quarter), place)


def layers(qkv, frame_clip, w_out):
    rows, blks = lax.axis_size("row"), lax.axis_size("blk")
    row, blk = lax.axis_index("row"), lax.axis_index("blk")
    tok, head_dim, cols = qkv.shape[1], w_out.shape[0], w_out.shape[1] // blks
    place = (blk * 2 + lax.axis_index("core")).astype(jnp.int32).reshape(1)
    others = range(1, rows)

    (w_own,) = columns(w_out, [(head_dim, 0, blk)], cols)
    w_parts = [w_own] + [xor(w_own, ("row",), by) for by in others]
    packed = pack(qkv, 2 * blks, head_dim)
    own = lax.all_to_all(packed, ("blk", "core"), split_axis=0, concat_axis=0, tiled=True)
    q, kv = cut(own)
    kvs = [kv] + [xor(kv, ("row",), by) for by in others]
    attn = attention(q, kvs, [0] * rows, 2 * tok, frame_clip, head_dim)
    attns = swap_all([attn] * blks, ("blk",))
    ours, other_core = project(attns, w_parts, [row ^ by for by in range(rows)], place, tok)
    parts = add(ours, xor(other_core, ("core",), 1), place)
    return unpack(swap_all(parts, ("blk",)), place)


def solution(mesh):
    blk, tile = mesh.shape["blk"], mesh.shape["tile"]
    if (blk, tile) == (4, 8):
        plan, names, shape = squares, ("y", "x", "zh", "zl", "core"), (2, 2, 2, 2, 2)
    else:
        plan, names, shape = layers, ("blk", "row", "core"), (blk, tile // 2, 2)
    fine = Mesh(mesh.devices.reshape(shape), names)
    tiles = names[2:] if plan is squares else names[1:]
    in_specs = (P(None, names, None), P(), P(tiles, None))
    return jax.shard_map(
        plan, mesh=fine, in_specs=in_specs, out_specs=P(names, None), check_vma=False
    )
```

```python
import functools
import math

import jax
import jax.numpy as jnp
from jax import lax
from jax.experimental import pallas as pl
from jax.experimental.pallas import tpu as pltpu
from jax.sharding import Mesh
from jax.sharding import PartitionSpec as P

FRB = 2
TPF = 16
LANES = 128
VMEM = pl.BlockSpec(memory_space=pltpu.VMEM)
SMEM = pl.BlockSpec(memory_space=pltpu.SMEM)
ANY = pl.BlockSpec(memory_space=pl.ANY)
PARAMS = pltpu.CompilerParams(vmem_limit_bytes=48 * 1024 * 1024)
AHEAD = pl.CostEstimate(flops=20_000_000_000, bytes_accessed=1_000_000, transcendentals=0)


def rows_at(index, size):
    return pl.ds(pl.multiple_of(index * size, size), size)


def index_array(*numbers):
    return jnp.stack([jnp.asarray(i, jnp.int32) for i in numbers])


def pack_kernel(head_dim, x_ref, out_ref):
    peers, _, width = out_ref.shape
    kinds, tok, _ = x_ref.shape
    heads = width // head_dim
    for g in range(peers):
        for i in range(heads):
            head = (g // 2 * heads + i) * 2 + g % 2
            for k in range(kinds):
                out_ref[g, k * tok:(k + 1) * tok, i * head_dim:(i + 1) * head_dim] = x_ref[
                    k, :, head * head_dim:(head + 1) * head_dim
                ]


def pack(x, peers, head_dim):
    kinds, tok, cols = x.shape
    return pl.pallas_call(
        functools.partial(pack_kernel, head_dim),
        out_shape=jax.ShapeDtypeStruct((peers, kinds * tok, cols // peers), x.dtype),
        in_specs=[VMEM],
        out_specs=VMEM,
        compiler_params=PARAMS,
    )(x)


def copy_all(copies):
    for copy in copies:
        copy.start()
    for copy in copies:
        copy.wait()


def columns_kernel(at_ref, x_ref, *refs):
    *out_refs, sems = refs
    copies = []
    for i, ref in enumerate(out_refs):
        depth, cols = ref.shape
        piece = x_ref.at[rows_at(at_ref[2 * i], depth), rows_at(at_ref[2 * i + 1], cols)]
        copies.append(pltpu.make_async_copy(piece, ref, sems.at[i]))
    copy_all(copies)


def columns(x, pieces, cols):
    return pl.pallas_call(
        columns_kernel,
        out_shape=[jax.ShapeDtypeStruct((piece[0], cols), x.dtype) for piece in pieces],
        in_specs=[SMEM, pl.BlockSpec(memory_space=pltpu.HBM)],
        out_specs=[VMEM] * len(pieces),
        scratch_shapes=[pltpu.SemaphoreType.DMA((len(pieces),))],
        compiler_params=PARAMS,
    )(
        index_array(*[i for piece in pieces for i in piece[1:]]),
        pltpu.with_memory_space_constraint(x, pltpu.HBM),
    )


def blocks_kernel(depth, at_ref, x_ref, out_ref, sems):
    blocks = out_ref.shape[0] // depth
    copies = []
    for j in range(blocks):
        piece = x_ref.at[rows_at(at_ref[0], depth), rows_at(at_ref[1] * blocks + j, LANES)]
        copies.append(pltpu.make_async_copy(piece, out_ref.at[j * depth:(j + 1) * depth], sems.at[j]))
    copy_all(copies)


def blocks(x, depth, row_at, col_at, cols):
    count = cols // LANES
    return pl.pallas_call(
        functools.partial(blocks_kernel, depth),
        out_shape=jax.ShapeDtypeStruct((count * depth, LANES), x.dtype),
        in_specs=[SMEM, pl.BlockSpec(memory_space=pltpu.HBM)],
        out_specs=VMEM,
        scratch_shapes=[pltpu.SemaphoreType.DMA((count,))],
        compiler_params=PARAMS,
    )(index_array(row_at, col_at), pltpu.with_memory_space_constraint(x, pltpu.HBM))


def lane_kernel(head_dim, core_ref, x_ref, mine_ref, theirs_ref):
    kinds, tok, _ = x_ref.shape
    for out_ref, core in ((mine_ref, core_ref[0]), (theirs_ref, 1 - core_ref[0])):
        for g in range(out_ref.shape[0]):
            cols = rows_at(2 * g + core, head_dim)
            for k in range(kinds):
                out_ref[g, k * tok:(k + 1) * tok, :] = x_ref[k, :, cols]


def lanes(x, core, head_dim):
    kinds, tok, cols = x.shape
    like = jax.ShapeDtypeStruct((cols // head_dim // 2, kinds * tok, head_dim), x.dtype)
    return pl.pallas_call(
        functools.partial(lane_kernel, head_dim),
        out_shape=(like, like),
        in_specs=[SMEM, VMEM],
        out_specs=(VMEM, VMEM),
        compiler_params=PARAMS,
    )(index_array(core), x)


def deal_kernel(place_ref, mine_ref, got_ref, *out_refs):
    quarter, core = place_ref[0] // 2, place_ref[0] % 2
    for k, out_ref in enumerate(out_refs):
        out_ref[core] = mine_ref[quarter ^ k]
        out_ref[1 - core] = got_ref[quarter ^ k]


def deal(mine, got, place):
    quarters, depth, width = mine.shape
    return pl.pallas_call(
        deal_kernel,
        out_shape=[jax.ShapeDtypeStruct((2, depth, width), mine.dtype)] * quarters,
        in_specs=[SMEM, VMEM, VMEM],
        out_specs=[VMEM] * quarters,
        compiler_params=PARAMS,
    )(place, mine, got)


def sort_kernel(n, place_ref, *refs):
    in_refs, (more_ref, q_ref, k_ref, v_ref, all_ref) = refs[:n], refs[n:]
    count = q_ref.shape[0]
    tok = count // (2 * n)
    for i, ref in enumerate(in_refs):
        for core in range(2):
            at = (place_ref[0] // 2 ^ i) * 2 + core
            keys, values = ref[core, tok:2 * tok, :], ref[core, 2 * tok:, :]
            q_ref[rows_at(at, tok), :] = ref[core, 0:tok, :]
            k_ref[rows_at(at, tok), :] = keys
            v_ref[rows_at(at, tok), :] = values
            all_ref[rows_at(at, tok), :] = keys
            all_ref[rows_at(at + 2 * n, tok), :] = values
    all_ref[2 * count:, :] = more_ref[...]


def sort(parts, place, more):
    _, depth, width = parts[0].shape
    n = len(parts)
    count = 2 * n * (depth // 3)
    sizes = (count, count, count, 2 * count + more.shape[0])
    return pl.pallas_call(
        functools.partial(sort_kernel, n),
        out_shape=[jax.ShapeDtypeStruct((size, width), more.dtype) for size in sizes],
        in_specs=[SMEM] + [VMEM] * (n + 1),
        out_specs=[VMEM] * 4,
        compiler_params=PARAMS,
    )(place, *parts, more)


def cut_kernel(x_ref, q_ref, kv_ref):
    peers, depth, _ = x_ref.shape
    tok = depth // 3
    for g in range(peers):
        q_ref[g * tok:(g + 1) * tok, :] = x_ref[g, :tok, :]
        for i in range(2):
            kv_ref[(i * peers + g) * tok:(i * peers + g + 1) * tok, :] = x_ref[
                g, (i + 1) * tok:(i + 2) * tok, :
            ]


def cut(x):
    peers, depth, width = x.shape
    count = peers * depth // 3
    return pl.pallas_call(
        cut_kernel,
        out_shape=[jax.ShapeDtypeStruct((size, width), x.dtype) for size in (count, 2 * count)],
        in_specs=[VMEM],
        out_specs=[VMEM, VMEM],
        compiler_params=PARAMS,
    )(x)


def after_kernel(*refs):
    pass


def after(passed, *first, cost=None):
    return pl.pallas_call(
        after_kernel,
        out_shape=jax.ShapeDtypeStruct(passed.shape, passed.dtype),
        in_specs=[ANY] * (1 + len(first)),
        out_specs=ANY,
        input_output_aliases={0: 0},
        compiler_params=PARAMS,
        cost_estimate=cost,
    )(passed, *first)


def clip_of(token, base, span, tok_dev, clip_ref):
    frame = base + token // span * FRB + token % tok_dev // TPF
    clip = jnp.zeros_like(token)
    for f in range(clip_ref.shape[0]):
        clip = jnp.where(frame == f, clip_ref[f], clip)
    return clip


def mask_kernel(span, tok, base_ref, clip_ref, *out_refs):
    count = out_refs[0].shape[0]
    row = lax.broadcasted_iota(jnp.int32, (count, 1), 0)
    col = lax.broadcasted_iota(jnp.int32, (1, count), 1)
    row_clip = clip_of(row, base_ref[0], span, tok, clip_ref)
    for i, out_ref in enumerate(out_refs):
        allowed = row_clip == clip_of(col, base_ref[i], span, tok, clip_ref)
        out_ref[...] = jnp.where(allowed, 0.0, -1e30)


def masks(bases, span, tok, count, frame_clip):
    return pl.pallas_call(
        functools.partial(mask_kernel, span, tok),
        out_shape=[jax.ShapeDtypeStruct((count, count), jnp.float32)] * len(bases),
        in_specs=[SMEM, SMEM],
        out_specs=[VMEM] * len(bases),
        compiler_params=PARAMS,
    )(index_array(*bases), frame_clip)


def attention_kernel(head_dim, n_mask, which, joint, q_ref, *refs):
    *refs, out_ref = refs
    mask_refs, refs = refs[:n_mask], refs[n_mask:]
    count, width = q_ref.shape
    k_refs, v_refs = [], []
    for both in joint:
        ref, *refs = refs
        if both:
            k_refs.append(ref.at[0:count])
            v_refs.append(ref.at[count:2 * count])
        else:
            value_ref, *refs = refs
            k_refs.append(ref)
            v_refs.append(value_ref)
    scale = math.log2(math.e) / math.sqrt(head_dim)
    per_step = max(1, 1024 // count)
    for h in range(width // head_dim):
        cols = slice(h * head_dim, (h + 1) * head_dim)
        queries = q_ref[:, cols]
        top = total = acc = None
        for first in range(0, len(k_refs), per_step):
            here = range(first, min(first + per_step, len(k_refs)))
            scores = []
            for i in here:
                s = lax.dot_general(
                    queries, k_refs[i][:, cols], (((1,), (1,)), ((), ())),
                    preferred_element_type=jnp.float32,
                )
                scores.append(s * scale + mask_refs[which[i]][...])
            new_top = functools.reduce(
                jnp.maximum, [jnp.max(s, axis=1, keepdims=True) for s in scores]
            )
            if top is not None:
                new_top = jnp.maximum(top, new_top)
                factor = jnp.exp2(top - new_top)
                total, acc = total * factor, acc * factor
            top = new_top
            for i, s in zip(here, scores):
                p = jnp.exp2(s - top)
                part = jnp.sum(p, axis=1, keepdims=True)
                dot = jnp.dot(
                    p.astype(jnp.bfloat16), v_refs[i][:, cols], preferred_element_type=jnp.float32
                )
                total = part if total is None else total + part
                acc = dot if acc is None else acc + dot
        out_ref[:, cols] = (acc / total).astype(out_ref.dtype)


def attention(q, kvs, mask_of, which, head_dim):
    joint = [not isinstance(kv, tuple) for kv in kvs]
    arrays = [x for kv, both in zip(kvs, joint) for x in ((kv,) if both else kv)]
    return pl.pallas_call(
        functools.partial(attention_kernel, head_dim, len(mask_of), which, joint),
        out_shape=jax.ShapeDtypeStruct(q.shape, q.dtype),
        in_specs=[VMEM] * (1 + len(mask_of) + len(arrays)),
        out_specs=VMEM,
        compiler_params=PARAMS,
    )(q, *mask_of, *arrays)


def project_kernel(n_attn, sizes, at_ref, place_ref, *refs):
    attn_refs, w_refs = refs[:n_attn], refs[n_attn:-4]
    mine_ref, theirs_ref, a_ref, w_all = refs[-4:]
    width = attn_refs[0].shape[1]
    blks, tok, cols = mine_ref.shape
    blk, core = place_ref[0] // 2, place_ref[0] % 2
    for k, ref in enumerate(attn_refs):
        a_ref[:, rows_at(blk ^ k, width)] = ref[...]
    for i, (ref, rows) in enumerate(zip(w_refs, sizes)):
        at = rows_at(at_ref[i], rows)
        if ref.shape[1] == cols:
            w_all[at, :] = ref[...]
        else:
            first = ref.shape[0] - cols // LANES * rows
            for j in range(cols // LANES):
                w_all[at, j * LANES:(j + 1) * LANES] = ref[first + j * rows:first + (j + 1) * rows]
    result = jnp.dot(a_ref[...], w_all[...], preferred_element_type=jnp.float32)
    result = result.astype(mine_ref.dtype).reshape(blks, 2, tok, cols)

    @pl.when(core == 0)
    def _():
        mine_ref[...] = result[:, 0]
        theirs_ref[...] = result[:, 1]

    @pl.when(core != 0)
    def _():
        mine_ref[...] = result[:, 1]
        theirs_ref[...] = result[:, 0]


def project(attns, w_parts, sizes, at, place, tok, cols):
    count, width = attns[0].shape
    blks = len(attns)
    like = jax.ShapeDtypeStruct((blks, tok, cols), attns[0].dtype)
    return pl.pallas_call(
        functools.partial(project_kernel, blks, sizes),
        out_shape=(like, like),
        in_specs=[SMEM, SMEM] + [VMEM] * (blks + len(w_parts)),
        out_specs=(VMEM, VMEM),
        scratch_shapes=[
            pltpu.VMEM((count, blks * width), attns[0].dtype),
            pltpu.VMEM((blks * width, cols), attns[0].dtype),
        ],
        compiler_params=PARAMS,
    )(index_array(*at), place, *attns, *w_parts)


def add_kernel(place_ref, x_ref, y_ref, *out_refs):
    for k, out_ref in enumerate(out_refs):
        at = place_ref[0] // 2 ^ k
        both = x_ref[at].astype(jnp.float32) + y_ref[at].astype(jnp.float32)
        out_ref[...] = both.astype(out_ref.dtype)


def add(x, y, place):
    blks = x.shape[0]
    return pl.pallas_call(
        add_kernel,
        out_shape=[jax.ShapeDtypeStruct(x.shape[1:], x.dtype)] * blks,
        in_specs=[SMEM, VMEM, VMEM],
        out_specs=[VMEM] * blks,
        compiler_params=PARAMS,
    )(place, x, y)


def unpack_kernel(place_ref, *refs):
    *in_refs, out_ref = refs
    width = in_refs[0].shape[1]
    for k, ref in enumerate(in_refs):
        out_ref[:, rows_at(place_ref[0] // 2 ^ k, width)] = ref[...]


def unpack(parts, place):
    tok, width = parts[0].shape
    return pl.pallas_call(
        unpack_kernel,
        out_shape=jax.ShapeDtypeStruct((tok, len(parts) * width), parts[0].dtype),
        in_specs=[SMEM] + [VMEM] * len(parts),
        out_specs=VMEM,
        compiler_params=PARAMS,
    )(place, *parts)


def xor(x, axis, by):
    size = math.prod(lax.axis_size(name) for name in axis)
    return lax.ppermute(x, axis, [(i, i ^ by) for i in range(size)])


def swap_all(parts, axis):
    last_first = [xor(parts[m], axis, m) for m in range(len(parts) - 1, 0, -1)]
    return [parts[0]] + last_first[::-1]


def squares(qkv, frame_clip, w_out):
    quarter = ("x", "zl")
    y, x, zh, zl, core = (lax.axis_index(n) for n in ("y", "x", "zh", "zl", "core"))
    tok, head_dim, cols = qkv.shape[1], w_out.shape[0], w_out.shape[1] // 4
    place = index_array((x * 2 + zl) * 2 + core)
    mine, theirs = x * 2 + zl, x * 2 + 1 - zl
    row, half = zh * 2 + zl, head_dim // 2

    far = after(xor(blocks(w_out, half, y, mine, cols), ("zh",), 1), cost=AHEAD)
    w_own, w_corner, w_near = columns(
        w_out, [(head_dim, 0, mine), (half, y, theirs), (head_dim, 0, theirs)], cols
    )
    kept, given = lanes(qkv, core, head_dim)
    parts = deal(kept, xor(given, ("core",), 1), place)
    q, k, v, k_v_far = sort(swap_all(parts, quarter), place, far)
    k_far, v_far = xor(k, ("zh",), 1), xor(v, ("zh",), 1)
    near = xor(k_v_far, ("y",), 1)
    corner = xor(after(w_corner, k), ("zh", "zl"), 3)
    w_next = xor(after(w_near, k), ("zl",), 1)
    kvs = [(k, v), (k_far, v_far), near, (xor(k_far, ("y",), 1), xor(v_far, ("y",), 1))]

    bases = [y * 2 * FRB, (1 - y) * 2 * FRB]
    mask_of = masks(bases, 4 * tok, tok, 8 * tok, frame_clip)
    attn = attention(q, kvs, mask_of, [0, 0, 1, 1], head_dim)
    corner = after(corner, attn)
    corner_rest = xor(corner, ("y",), 1)
    attns = swap_all([attn] * 4, quarter)
    w_parts = [w_own, w_next, far, near, corner, corner_rest]
    sizes = [head_dim, head_dim, half, half, half, half]
    at = [row, row ^ 1] + [2 * (row ^ by) + h for by in (2, 3) for h in (y, 1 - y)]
    ours, other_core = project(attns, w_parts, sizes, at, place, tok, cols)
    parts = add(ours, xor(other_core, ("core",), 1), place)
    return unpack(swap_all(parts, quarter), place)


def layers(qkv, frame_clip, w_out):
    rows, blks = lax.axis_size("row"), lax.axis_size("blk")
    row, blk = lax.axis_index("row"), lax.axis_index("blk")
    tok, head_dim, cols = qkv.shape[1], w_out.shape[0], w_out.shape[1] // blks
    place = index_array(blk * 2 + lax.axis_index("core"))
    others = range(1, rows)

    (w_own,) = columns(w_out, [(head_dim, 0, blk)], cols)
    w_parts = [w_own] + [xor(w_own, ("row",), by) for by in others]
    packed = pack(qkv, 2 * blks, head_dim)
    own = lax.all_to_all(packed, ("blk", "core"), split_axis=0, concat_axis=0, tiled=True)
    q, kv = cut(own)
    kvs = [kv] + [xor(kv, ("row",), by) for by in others]
    mask_of = masks([0], 2 * tok, tok, 2 * blks * tok, frame_clip)
    attn = attention(q, kvs, mask_of, [0] * rows, head_dim)
    attns = swap_all([attn] * blks, ("blk",))
    at = [row ^ by for by in range(rows)]
    ours, other_core = project(attns, w_parts, [head_dim] * rows, at, place, tok, cols)
    parts = add(ours, xor(other_core, ("core",), 1), place)
    return unpack(swap_all(parts, ("blk",)), place)


def solution(mesh):
    blk, tile = mesh.shape["blk"], mesh.shape["tile"]
    if (blk, tile) == (4, 8):
        plan, names, shape = squares, ("y", "x", "zh", "zl", "core"), (2, 2, 2, 2, 2)
    else:
        plan, names, shape = layers, ("blk", "row", "core"), (blk, tile // 2, 2)
    fine = Mesh(mesh.devices.reshape(shape), names)
    tiles = names[2:] if plan is squares else names[1:]
    in_specs = (P(None, names, None), P(), P(tiles, None))
    return jax.shard_map(
        plan, mesh=fine, in_specs=in_specs, out_specs=P(names, None), check_vma=False
    )
```

```python
import functools
import math

import jax
import jax.numpy as jnp
from jax import lax
from jax.experimental import pallas as pl
from jax.experimental.pallas import tpu as pltpu
from jax.sharding import Mesh
from jax.sharding import PartitionSpec as P

FRB = 2
TPF = 16
LANES = 128
VMEM = pl.BlockSpec(memory_space=pltpu.VMEM)
SMEM = pl.BlockSpec(memory_space=pltpu.SMEM)
ANY = pl.BlockSpec(memory_space=pl.ANY)
PARAMS = pltpu.CompilerParams(vmem_limit_bytes=48 * 1024 * 1024)
AHEAD = pl.CostEstimate(flops=20_000_000_000, bytes_accessed=1_000_000, transcendentals=0)
SOON = pl.CostEstimate(flops=6_000_000_000, bytes_accessed=1_000_000, transcendentals=0)


def rows_at(index, size):
    return pl.ds(pl.multiple_of(index * size, size), size)


def index_array(*numbers):
    return jnp.stack([jnp.asarray(i, jnp.int32) for i in numbers])


def pack_kernel(head_dim, x_ref, out_ref):
    peers, _, width = out_ref.shape
    kinds, tok, _ = x_ref.shape
    heads = width // head_dim
    for g in range(peers):
        for i in range(heads):
            head = (g // 2 * heads + i) * 2 + g % 2
            for k in range(kinds):
                out_ref[g, k * tok:(k + 1) * tok, i * head_dim:(i + 1) * head_dim] = x_ref[
                    k, :, head * head_dim:(head + 1) * head_dim
                ]


def pack(x, peers, head_dim):
    kinds, tok, cols = x.shape
    return pl.pallas_call(
        functools.partial(pack_kernel, head_dim),
        out_shape=jax.ShapeDtypeStruct((peers, kinds * tok, cols // peers), x.dtype),
        in_specs=[VMEM],
        out_specs=VMEM,
        compiler_params=PARAMS,
    )(x)


def columns_kernel(at_ref, x_ref, *refs):
    *out_refs, sems = refs
    copies = []
    for i, ref in enumerate(out_refs):
        depth, cols = ref.shape
        piece = x_ref.at[rows_at(at_ref[2 * i], depth), rows_at(at_ref[2 * i + 1], cols)]
        copies.append(pltpu.make_async_copy(piece, ref, sems.at[i]))
    for copy in copies:
        copy.start()
    for copy in copies:
        copy.wait()


def columns(x, pieces, cols):
    return pl.pallas_call(
        columns_kernel,
        out_shape=[jax.ShapeDtypeStruct((piece[0], cols), x.dtype) for piece in pieces],
        in_specs=[SMEM, pl.BlockSpec(memory_space=pltpu.HBM)],
        out_specs=[VMEM] * len(pieces),
        scratch_shapes=[pltpu.SemaphoreType.DMA((len(pieces),))],
        compiler_params=PARAMS,
    )(
        index_array(*[i for piece in pieces for i in piece[1:]]),
        pltpu.with_memory_space_constraint(x, pltpu.HBM),
    )


def pieces_kernel(at_ref, x_ref, far_ref, corner_ref, near_ref):
    half, cols = corner_ref.shape
    rows = rows_at(at_ref[0], half)
    count = cols // LANES
    for j in range(count):
        far_ref[j * half:(j + 1) * half, :] = x_ref[rows, rows_at(at_ref[1] * count + j, LANES)]
    corner_ref[...] = x_ref[rows, rows_at(at_ref[2], cols)]
    near_ref[...] = x_ref[:, rows_at(at_ref[2], cols)]


def pieces(x, half, first_at, second_at, cols):
    return pl.pallas_call(
        pieces_kernel,
        out_shape=(
            jax.ShapeDtypeStruct((cols // LANES * (x.shape[0] // 2), LANES), x.dtype),
            jax.ShapeDtypeStruct((x.shape[0] // 2, cols), x.dtype),
            jax.ShapeDtypeStruct((x.shape[0], cols), x.dtype),
        ),
        in_specs=[SMEM, VMEM],
        out_specs=(VMEM, VMEM, VMEM),
        compiler_params=PARAMS,
    )(index_array(half, first_at, second_at), x)


def lane_kernel(head_dim, core_ref, x_ref, mine_ref, theirs_ref):
    kinds, tok, _ = x_ref.shape
    for out_ref, core in ((mine_ref, core_ref[0]), (theirs_ref, 1 - core_ref[0])):
        for g in range(out_ref.shape[0]):
            cols = rows_at(2 * g + core, head_dim)
            for k in range(kinds):
                out_ref[g, k * tok:(k + 1) * tok, :] = x_ref[k, :, cols]


def lanes(x, core, head_dim):
    kinds, tok, cols = x.shape
    like = jax.ShapeDtypeStruct((cols // head_dim // 2, kinds * tok, head_dim), x.dtype)
    return pl.pallas_call(
        functools.partial(lane_kernel, head_dim),
        out_shape=(like, like),
        in_specs=[SMEM, VMEM],
        out_specs=(VMEM, VMEM),
        compiler_params=PARAMS,
    )(index_array(core), x)


def deal_kernel(place_ref, mine_ref, got_ref, *out_refs):
    quarter, core = place_ref[0] // 2, place_ref[0] % 2
    for k, out_ref in enumerate(out_refs):
        out_ref[core] = mine_ref[quarter ^ k]
        out_ref[1 - core] = got_ref[quarter ^ k]


def deal(mine, got, place):
    quarters, depth, width = mine.shape
    return pl.pallas_call(
        deal_kernel,
        out_shape=[jax.ShapeDtypeStruct((2, depth, width), mine.dtype)] * quarters,
        in_specs=[SMEM, VMEM, VMEM],
        out_specs=[VMEM] * quarters,
        compiler_params=PARAMS,
    )(place, mine, got)


def sort_kernel(place_ref, *refs):
    *in_refs, q_ref, k_ref, v_ref = refs
    tok = q_ref.shape[0] // (2 * len(in_refs))
    for i, ref in enumerate(in_refs):
        for core in range(2):
            at = rows_at((place_ref[0] // 2 ^ i) * 2 + core, tok)
            for j, out_ref in enumerate((q_ref, k_ref, v_ref)):
                out_ref[at, :] = ref[core, j * tok:(j + 1) * tok, :]


def sort(parts, place):
    both, depth, width = parts[0].shape
    count = both * len(parts) * (depth // 3)
    return pl.pallas_call(
        sort_kernel,
        out_shape=[jax.ShapeDtypeStruct((count, width), parts[0].dtype)] * 3,
        in_specs=[SMEM] + [VMEM] * len(parts),
        out_specs=[VMEM] * 3,
        compiler_params=PARAMS,
    )(place, *parts)


def join_kernel(*refs):
    *in_refs, out_ref = refs
    first = 0
    for ref in in_refs:
        out_ref[first:first + ref.shape[0], :] = ref[...]
        first += ref.shape[0]


def join(*arrays):
    depth = sum(x.shape[0] for x in arrays)
    return pl.pallas_call(
        join_kernel,
        out_shape=jax.ShapeDtypeStruct((depth, arrays[0].shape[1]), arrays[0].dtype),
        in_specs=[VMEM] * len(arrays),
        out_specs=VMEM,
        compiler_params=PARAMS,
    )(*arrays)


def cut_kernel(x_ref, q_ref, kv_ref):
    peers, depth, _ = x_ref.shape
    tok = depth // 3
    for g in range(peers):
        q_ref[g * tok:(g + 1) * tok, :] = x_ref[g, :tok, :]
        for i in range(2):
            kv_ref[(i * peers + g) * tok:(i * peers + g + 1) * tok, :] = x_ref[
                g, (i + 1) * tok:(i + 2) * tok, :
            ]


def cut(x):
    peers, depth, width = x.shape
    count = peers * depth // 3
    return pl.pallas_call(
        cut_kernel,
        out_shape=[jax.ShapeDtypeStruct((size, width), x.dtype) for size in (count, 2 * count)],
        in_specs=[VMEM],
        out_specs=[VMEM, VMEM],
        compiler_params=PARAMS,
    )(x)


def after_kernel(*refs):
    pass


def after(passed, *first, cost=None):
    return pl.pallas_call(
        after_kernel,
        out_shape=jax.ShapeDtypeStruct(passed.shape, passed.dtype),
        in_specs=[ANY] * (1 + len(first)),
        out_specs=ANY,
        input_output_aliases={0: 0},
        compiler_params=PARAMS,
        cost_estimate=cost,
    )(passed, *first)


def clip_of(token, base, span, tok_dev, clip_ref):
    frame = base + token // span * FRB + token % tok_dev // TPF
    clip = jnp.zeros_like(token)
    for f in range(clip_ref.shape[0]):
        clip = jnp.where(frame == f, clip_ref[f], clip)
    return clip


def mask_kernel(span, tok, base_ref, clip_ref, *out_refs):
    count = out_refs[0].shape[0]
    row = lax.broadcasted_iota(jnp.int32, (count, 1), 0)
    col = lax.broadcasted_iota(jnp.int32, (1, count), 1)
    row_clip = clip_of(row, base_ref[0], span, tok, clip_ref)
    for i, out_ref in enumerate(out_refs):
        allowed = row_clip == clip_of(col, base_ref[i], span, tok, clip_ref)
        out_ref[...] = jnp.where(allowed, 0.0, -1e30)


def masks(bases, span, tok, count, frame_clip):
    return pl.pallas_call(
        functools.partial(mask_kernel, span, tok),
        out_shape=[jax.ShapeDtypeStruct((count, count), jnp.float32)] * len(bases),
        in_specs=[SMEM, SMEM],
        out_specs=[VMEM] * len(bases),
        compiler_params=PARAMS,
    )(index_array(*bases), frame_clip)


def attention_kernel(head_dim, n_mask, which, joint, q_ref, *refs):
    *refs, out_ref = refs
    mask_refs, refs = refs[:n_mask], refs[n_mask:]
    count, width = q_ref.shape
    k_refs, v_refs = [], []
    for both in joint:
        ref, *refs = refs
        if both:
            k_refs.append(ref.at[0:count])
            v_refs.append(ref.at[count:2 * count])
        else:
            value_ref, *refs = refs
            k_refs.append(ref)
            v_refs.append(value_ref)
    scale = math.log2(math.e) / math.sqrt(head_dim)
    per_step = max(1, 1024 // count)
    for h in range(width // head_dim):
        cols = slice(h * head_dim, (h + 1) * head_dim)
        queries = q_ref[:, cols]
        top = total = acc = None
        for first in range(0, len(k_refs), per_step):
            here = range(first, min(first + per_step, len(k_refs)))
            scores = []
            for i in here:
                s = lax.dot_general(
                    queries, k_refs[i][:, cols], (((1,), (1,)), ((), ())),
                    preferred_element_type=jnp.float32,
                )
                scores.append(s * scale + mask_refs[which[i]][...])
            new_top = functools.reduce(
                jnp.maximum, [jnp.max(s, axis=1, keepdims=True) for s in scores]
            )
            if top is not None:
                new_top = jnp.maximum(top, new_top)
                factor = jnp.exp2(top - new_top)
                total, acc = total * factor, acc * factor
            top = new_top
            for i, s in zip(here, scores):
                p = jnp.exp2(s - top)
                part = jnp.sum(p, axis=1, keepdims=True)
                dot = jnp.dot(
                    p.astype(jnp.bfloat16), v_refs[i][:, cols], preferred_element_type=jnp.float32
                )
                total = part if total is None else total + part
                acc = dot if acc is None else acc + dot
        out_ref[:, cols] = (acc / total).astype(out_ref.dtype)


def attention(q, kvs, mask_of, which, head_dim):
    joint = [not isinstance(kv, tuple) for kv in kvs]
    arrays = [x for kv, both in zip(kvs, joint) for x in ((kv,) if both else kv)]
    return pl.pallas_call(
        functools.partial(attention_kernel, head_dim, len(mask_of), which, joint),
        out_shape=jax.ShapeDtypeStruct(q.shape, q.dtype),
        in_specs=[VMEM] * (1 + len(mask_of) + len(arrays)),
        out_specs=VMEM,
        compiler_params=PARAMS,
    )(q, *mask_of, *arrays)


def project_kernel(n_attn, sizes, at_ref, place_ref, *refs):
    attn_refs, w_refs = refs[:n_attn], refs[n_attn:-4]
    mine_ref, theirs_ref, a_ref, w_all = refs[-4:]
    width = attn_refs[0].shape[1]
    blks, tok, cols = mine_ref.shape
    blk, core = place_ref[0] // 2, place_ref[0] % 2
    for k, ref in enumerate(attn_refs):
        a_ref[:, rows_at(blk ^ k, width)] = ref[...]
    for i, (ref, rows) in enumerate(zip(w_refs, sizes)):
        at = rows_at(at_ref[i], rows)
        if ref.shape[1] >= cols:
            w_all[at, :] = ref[:, rows_at(blk, cols)] if ref.shape[1] > cols else ref[...]
        else:
            first = ref.shape[0] - cols // LANES * rows
            for j in range(cols // LANES):
                w_all[at, j * LANES:(j + 1) * LANES] = ref[first + j * rows:first + (j + 1) * rows]
    result = jnp.dot(a_ref[...], w_all[...], preferred_element_type=jnp.float32)
    result = result.astype(mine_ref.dtype).reshape(blks, 2, tok, cols)

    @pl.when(core == 0)
    def _():
        mine_ref[...] = result[:, 0]
        theirs_ref[...] = result[:, 1]

    @pl.when(core != 0)
    def _():
        mine_ref[...] = result[:, 1]
        theirs_ref[...] = result[:, 0]


def project(attns, w_parts, sizes, at, place, tok, cols):
    count, width = attns[0].shape
    blks = len(attns)
    like = jax.ShapeDtypeStruct((blks, tok, cols), attns[0].dtype)
    return pl.pallas_call(
        functools.partial(project_kernel, blks, sizes),
        out_shape=(like, like),
        in_specs=[SMEM, SMEM] + [VMEM] * (blks + len(w_parts)),
        out_specs=(VMEM, VMEM),
        scratch_shapes=[
            pltpu.VMEM((count, blks * width), attns[0].dtype),
            pltpu.VMEM((blks * width, cols), attns[0].dtype),
        ],
        compiler_params=PARAMS,
    )(index_array(*at), place, *attns, *w_parts)


def add_kernel(place_ref, x_ref, y_ref, *out_refs):
    for k, out_ref in enumerate(out_refs):
        at = place_ref[0] // 2 ^ k
        both = x_ref[at].astype(jnp.float32) + y_ref[at].astype(jnp.float32)
        out_ref[...] = both.astype(out_ref.dtype)


def add(x, y, place):
    blks = x.shape[0]
    return pl.pallas_call(
        add_kernel,
        out_shape=[jax.ShapeDtypeStruct(x.shape[1:], x.dtype)] * blks,
        in_specs=[SMEM, VMEM, VMEM],
        out_specs=[VMEM] * blks,
        compiler_params=PARAMS,
    )(place, x, y)


def unpack_kernel(place_ref, *refs):
    *in_refs, out_ref = refs
    width = in_refs[0].shape[1]
    for k, ref in enumerate(in_refs):
        out_ref[:, rows_at(place_ref[0] // 2 ^ k, width)] = ref[...]


def unpack(parts, place):
    tok, width = parts[0].shape
    return pl.pallas_call(
        unpack_kernel,
        out_shape=jax.ShapeDtypeStruct((tok, len(parts) * width), parts[0].dtype),
        in_specs=[SMEM] + [VMEM] * len(parts),
        out_specs=VMEM,
        compiler_params=PARAMS,
    )(place, *parts)


def xor(x, axis, by):
    size = math.prod(lax.axis_size(name) for name in axis)
    return lax.ppermute(x, axis, [(i, i ^ by) for i in range(size)])


def swap_all(parts, axis):
    last_first = [xor(parts[m], axis, m) for m in range(len(parts) - 1, 0, -1)]
    return [parts[0]] + last_first[::-1]


def squares(qkv, frame_clip, w_out):
    quarter = ("x", "zl")
    y, x, zh, zl, core = (lax.axis_index(n) for n in ("y", "x", "zh", "zl", "core"))
    tok, head_dim, cols = qkv.shape[1], w_out.shape[0], w_out.shape[1] // 4
    place = index_array((x * 2 + zl) * 2 + core)
    mine, theirs = x * 2 + zl, x * 2 + 1 - zl
    row, half = zh * 2 + zl, head_dim // 2

    w_far, w_corner, w_near = pieces(w_out, y, mine, theirs, cols)
    far = after(xor(w_far, ("zh",), 1), cost=AHEAD)
    kept, given = lanes(qkv, core, head_dim)
    shared = swap_all(deal(kept, xor(given, ("core",), 1), place), quarter)
    w_next = after(xor(after(w_near, shared[1]), ("zl",), 1), cost=AHEAD)
    q, k, v = sort(shared, place)
    k_far, v_far = xor(k, ("zh",), 1), xor(v, ("zh",), 1)
    near = xor(join(k, v, far), ("y",), 1)
    corner = xor(after(w_corner, k), ("zh", "zl"), 3)
    kvs = [(k, v), (k_far, v_far), near, (xor(k_far, ("y",), 1), xor(v_far, ("y",), 1))]

    bases = [y * 2 * FRB, (1 - y) * 2 * FRB]
    mask_of = masks(bases, 4 * tok, tok, 8 * tok, frame_clip)
    attn = attention(after(q, w_next), kvs, mask_of, [0, 0, 1, 1], head_dim)
    corner = after(corner, attn, cost=SOON)
    corner_rest = xor(corner, ("y",), 1)
    attns = swap_all([attn] * 4, quarter)
    w_next = after(w_next, attn, cost=AHEAD)
    w_parts = [w_out, w_next, far, near, corner, corner_rest]
    sizes = [head_dim, head_dim, half, half, half, half]
    at = [row, row ^ 1] + [2 * (row ^ by) + h for by in (2, 3) for h in (y, 1 - y)]
    ours, other_core = project(attns, w_parts, sizes, at, place, tok, cols)
    parts = add(ours, xor(other_core, ("core",), 1), place)
    return unpack(swap_all(parts, quarter), place)


def layers(qkv, frame_clip, w_out):
    rows, blks = lax.axis_size("row"), lax.axis_size("blk")
    row, blk = lax.axis_index("row"), lax.axis_index("blk")
    tok, head_dim, cols = qkv.shape[1], w_out.shape[0], w_out.shape[1] // blks
    place = index_array(blk * 2 + lax.axis_index("core"))
    others = range(1, rows)

    (w_own,) = columns(w_out, [(head_dim, 0, blk)], cols)
    w_parts = [w_out] + [xor(w_own, ("row",), by) for by in others]
    packed = pack(qkv, 2 * blks, head_dim)
    own = lax.all_to_all(packed, ("blk", "core"), split_axis=0, concat_axis=0, tiled=True)
    q, kv = cut(own)
    kvs = [kv] + [xor(kv, ("row",), by) for by in others]
    mask_of = masks([0], 2 * tok, tok, 2 * blks * tok, frame_clip)
    attn = attention(q, kvs, mask_of, [0] * rows, head_dim)
    attns = swap_all([attn] * blks, ("blk",))
    at = [row ^ by for by in range(rows)]
    ours, other_core = project(attns, w_parts, [head_dim] * rows, at, place, tok, cols)
    parts = add(ours, xor(other_core, ("core",), 1), place)
    return unpack(swap_all(parts, ("blk",)), place)


def solution(mesh):
    blk, tile = mesh.shape["blk"], mesh.shape["tile"]
    if (blk, tile) == (4, 8):
        plan, names, shape = squares, ("y", "x", "zh", "zl", "core"), (2, 2, 2, 2, 2)
    else:
        plan, names, shape = layers, ("blk", "row", "core"), (blk, tile // 2, 2)
    fine = Mesh(mesh.devices.reshape(shape), names)
    tiles = names[2:] if plan is squares else names[1:]
    in_specs = (P(None, names, None), P(), P(tiles, None))
    return jax.shard_map(
        plan, mesh=fine, in_specs=in_specs, out_specs=P(names, None), check_vma=False
    )
```

```python
import functools
import math

import jax
import jax.numpy as jnp
from jax import lax
from jax.experimental import pallas as pl
from jax.experimental.pallas import tpu as pltpu
from jax.sharding import Mesh
from jax.sharding import PartitionSpec as P

FRB = 2
TPF = 16
LANES = 128
VMEM = pl.BlockSpec(memory_space=pltpu.VMEM)
SMEM = pl.BlockSpec(memory_space=pltpu.SMEM)
ANY = pl.BlockSpec(memory_space=pl.ANY)
PARAMS = pltpu.CompilerParams(vmem_limit_bytes=48 * 1024 * 1024)
AHEAD = pl.CostEstimate(flops=20_000_000_000, bytes_accessed=1_000_000, transcendentals=0)
SOON = pl.CostEstimate(flops=6_000_000_000, bytes_accessed=1_000_000, transcendentals=0)


def rows_at(index, size):
    return pl.ds(pl.multiple_of(index * size, size), size)


def index_array(*numbers):
    return jnp.stack([jnp.asarray(i, jnp.int32) for i in numbers])


def pack_kernel(head_dim, x_ref, out_ref):
    peers, _, width = out_ref.shape
    kinds, tok, _ = x_ref.shape
    heads = width // head_dim
    for g in range(peers):
        for i in range(heads):
            head = (g // 2 * heads + i) * 2 + g % 2
            for k in range(kinds):
                out_ref[g, k * tok:(k + 1) * tok, i * head_dim:(i + 1) * head_dim] = x_ref[
                    k, :, head * head_dim:(head + 1) * head_dim
                ]


def pack(x, peers, head_dim):
    kinds, tok, cols = x.shape
    return pl.pallas_call(
        functools.partial(pack_kernel, head_dim),
        out_shape=jax.ShapeDtypeStruct((peers, kinds * tok, cols // peers), x.dtype),
        in_specs=[VMEM],
        out_specs=VMEM,
        compiler_params=PARAMS,
    )(x)


def columns_kernel(at_ref, x_ref, *refs):
    *out_refs, sems = refs
    copies = []
    for i, ref in enumerate(out_refs):
        depth, cols = ref.shape
        piece = x_ref.at[rows_at(at_ref[2 * i], depth), rows_at(at_ref[2 * i + 1], cols)]
        copies.append(pltpu.make_async_copy(piece, ref, sems.at[i]))
    for copy in copies:
        copy.start()
    for copy in copies:
        copy.wait()


def columns(x, pieces, cols):
    return pl.pallas_call(
        columns_kernel,
        out_shape=[jax.ShapeDtypeStruct((piece[0], cols), x.dtype) for piece in pieces],
        in_specs=[SMEM, pl.BlockSpec(memory_space=pltpu.HBM)],
        out_specs=[VMEM] * len(pieces),
        scratch_shapes=[pltpu.SemaphoreType.DMA((len(pieces),))],
        compiler_params=PARAMS,
    )(
        index_array(*[i for piece in pieces for i in piece[1:]]),
        pltpu.with_memory_space_constraint(x, pltpu.HBM),
    )


def pieces_kernel(at_ref, x_ref, far_ref, corner_ref, *near_refs):
    half, cols = corner_ref.shape
    rows = rows_at(at_ref[0], half)
    count = cols // LANES
    for j in range(count):
        far_ref[j * half:(j + 1) * half, :] = x_ref[rows, rows_at(at_ref[1] * count + j, LANES)]
    corner_ref[...] = x_ref[rows, rows_at(at_ref[2], cols)]
    for i, near_ref in enumerate(near_refs):
        near_ref[...] = x_ref[i * half:(i + 1) * half, rows_at(at_ref[2], cols)]


def pieces(x, half, first_at, second_at, cols):
    depth = x.shape[0] // 2
    like = jax.ShapeDtypeStruct((depth, cols), x.dtype)
    return pl.pallas_call(
        pieces_kernel,
        out_shape=[jax.ShapeDtypeStruct((cols // LANES * depth, LANES), x.dtype)] + [like] * 3,
        in_specs=[SMEM, VMEM],
        out_specs=[VMEM] * 4,
        compiler_params=PARAMS,
    )(index_array(half, first_at, second_at), x)


def lane_kernel(head_dim, core_ref, x_ref, mine_ref, theirs_ref):
    kinds, tok, _ = x_ref.shape
    for out_ref, core in ((mine_ref, core_ref[0]), (theirs_ref, 1 - core_ref[0])):
        for g in range(out_ref.shape[0]):
            cols = rows_at(2 * g + core, head_dim)
            for k in range(kinds):
                out_ref[g, k * tok:(k + 1) * tok, :] = x_ref[k, :, cols]


def lanes(x, core, head_dim):
    kinds, tok, cols = x.shape
    like = jax.ShapeDtypeStruct((cols // head_dim // 2, kinds * tok, head_dim), x.dtype)
    return pl.pallas_call(
        functools.partial(lane_kernel, head_dim),
        out_shape=(like, like),
        in_specs=[SMEM, VMEM],
        out_specs=(VMEM, VMEM),
        compiler_params=PARAMS,
    )(index_array(core), x)


def deal_kernel(place_ref, mine_ref, got_ref, *out_refs):
    quarter, core = place_ref[0] // 2, place_ref[0] % 2
    for k, out_ref in enumerate(out_refs):
        out_ref[core] = mine_ref[quarter ^ k]
        out_ref[1 - core] = got_ref[quarter ^ k]


def deal(mine, got, place):
    quarters, depth, width = mine.shape
    return pl.pallas_call(
        deal_kernel,
        out_shape=[jax.ShapeDtypeStruct((2, depth, width), mine.dtype)] * quarters,
        in_specs=[SMEM, VMEM, VMEM],
        out_specs=[VMEM] * quarters,
        compiler_params=PARAMS,
    )(place, mine, got)


def sort_kernel(place_ref, *refs):
    *in_refs, q_ref, k_ref, v_ref = refs
    tok = q_ref.shape[0] // (2 * len(in_refs))
    for i, ref in enumerate(in_refs):
        for core in range(2):
            at = rows_at((place_ref[0] // 2 ^ i) * 2 + core, tok)
            for j, out_ref in enumerate((q_ref, k_ref, v_ref)):
                out_ref[at, :] = ref[core, j * tok:(j + 1) * tok, :]


def sort(parts, place):
    both, depth, width = parts[0].shape
    count = both * len(parts) * (depth // 3)
    return pl.pallas_call(
        sort_kernel,
        out_shape=[jax.ShapeDtypeStruct((count, width), parts[0].dtype)] * 3,
        in_specs=[SMEM] + [VMEM] * len(parts),
        out_specs=[VMEM] * 3,
        compiler_params=PARAMS,
    )(place, *parts)


def join_kernel(*refs):
    *in_refs, out_ref = refs
    first = 0
    for ref in in_refs:
        out_ref[first:first + ref.shape[0], :] = ref[...]
        first += ref.shape[0]


def join(*arrays):
    depth = sum(x.shape[0] for x in arrays)
    return pl.pallas_call(
        join_kernel,
        out_shape=jax.ShapeDtypeStruct((depth, arrays[0].shape[1]), arrays[0].dtype),
        in_specs=[VMEM] * len(arrays),
        out_specs=VMEM,
        compiler_params=PARAMS,
    )(*arrays)


def cut_kernel(x_ref, q_ref, kv_ref):
    peers, depth, _ = x_ref.shape
    tok = depth // 3
    for g in range(peers):
        q_ref[g * tok:(g + 1) * tok, :] = x_ref[g, :tok, :]
        for i in range(2):
            kv_ref[(i * peers + g) * tok:(i * peers + g + 1) * tok, :] = x_ref[
                g, (i + 1) * tok:(i + 2) * tok, :
            ]


def cut(x):
    peers, depth, width = x.shape
    count = peers * depth // 3
    return pl.pallas_call(
        cut_kernel,
        out_shape=[jax.ShapeDtypeStruct((size, width), x.dtype) for size in (count, 2 * count)],
        in_specs=[VMEM],
        out_specs=[VMEM, VMEM],
        compiler_params=PARAMS,
    )(x)


def after_kernel(*refs):
    pass


def after(passed, *first, cost=None):
    return pl.pallas_call(
        after_kernel,
        out_shape=jax.ShapeDtypeStruct(passed.shape, passed.dtype),
        in_specs=[ANY] * (1 + len(first)),
        out_specs=ANY,
        input_output_aliases={0: 0},
        compiler_params=PARAMS,
        cost_estimate=cost,
    )(passed, *first)


def clip_of(token, base, span, tok_dev, clip_ref):
    frame = base + token // span * FRB + token % tok_dev // TPF
    clip = jnp.zeros_like(token)
    for f in range(clip_ref.shape[0]):
        clip = jnp.where(frame == f, clip_ref[f], clip)
    return clip


def mask_kernel(span, tok, base_ref, clip_ref, *out_refs):
    count = out_refs[0].shape[0]
    row = lax.broadcasted_iota(jnp.int32, (count, 1), 0)
    col = lax.broadcasted_iota(jnp.int32, (1, count), 1)
    row_clip = clip_of(row, base_ref[0], span, tok, clip_ref)
    for i, out_ref in enumerate(out_refs):
        allowed = row_clip == clip_of(col, base_ref[i], span, tok, clip_ref)
        out_ref[...] = jnp.where(allowed, 0.0, -1e30)


def masks(bases, span, tok, count, frame_clip):
    return pl.pallas_call(
        functools.partial(mask_kernel, span, tok),
        out_shape=[jax.ShapeDtypeStruct((count, count), jnp.float32)] * len(bases),
        in_specs=[SMEM, SMEM],
        out_specs=[VMEM] * len(bases),
        compiler_params=PARAMS,
    )(index_array(*bases), frame_clip)


def attention_kernel(head_dim, n_mask, which, joint, q_ref, *refs):
    *refs, out_ref = refs
    mask_refs, refs = refs[:n_mask], refs[n_mask:]
    count, width = q_ref.shape
    k_refs, v_refs = [], []
    for both in joint:
        ref, *refs = refs
        if both:
            k_refs.append(ref.at[0:count])
            v_refs.append(ref.at[count:2 * count])
        else:
            value_ref, *refs = refs
            k_refs.append(ref)
            v_refs.append(value_ref)
    scale = math.log2(math.e) / math.sqrt(head_dim)
    per_step = max(1, 1024 // count)
    for h in range(width // head_dim):
        cols = slice(h * head_dim, (h + 1) * head_dim)
        queries = q_ref[:, cols]
        top = total = acc = None
        for first in range(0, len(k_refs), per_step):
            here = range(first, min(first + per_step, len(k_refs)))
            scores = []
            for i in here:
                s = lax.dot_general(
                    queries, k_refs[i][:, cols], (((1,), (1,)), ((), ())),
                    preferred_element_type=jnp.float32,
                )
                scores.append(s * scale + mask_refs[which[i]][...])
            new_top = functools.reduce(
                jnp.maximum, [jnp.max(s, axis=1, keepdims=True) for s in scores]
            )
            if top is not None:
                new_top = jnp.maximum(top, new_top)
                factor = jnp.exp2(top - new_top)
                total, acc = total * factor, acc * factor
            top = new_top
            for i, s in zip(here, scores):
                p = jnp.exp2(s - top)
                part = jnp.sum(p, axis=1, keepdims=True)
                dot = jnp.dot(
                    p.astype(jnp.bfloat16), v_refs[i][:, cols], preferred_element_type=jnp.float32
                )
                total = part if total is None else total + part
                acc = dot if acc is None else acc + dot
        out_ref[:, cols] = (acc / total).astype(out_ref.dtype)


def attention(q, kvs, mask_of, which, head_dim):
    joint = [not isinstance(kv, tuple) for kv in kvs]
    arrays = [x for kv, both in zip(kvs, joint) for x in ((kv,) if both else kv)]
    return pl.pallas_call(
        functools.partial(attention_kernel, head_dim, len(mask_of), which, joint),
        out_shape=jax.ShapeDtypeStruct(q.shape, q.dtype),
        in_specs=[VMEM] * (1 + len(mask_of) + len(arrays)),
        out_specs=VMEM,
        compiler_params=PARAMS,
    )(q, *mask_of, *arrays)


def project_kernel(n_attn, sizes, at_ref, place_ref, *refs):
    attn_refs, w_refs = refs[:n_attn], refs[n_attn:-4]
    mine_ref, theirs_ref, a_ref, w_all = refs[-4:]
    width = attn_refs[0].shape[1]
    blks, tok, cols = mine_ref.shape
    blk, core = place_ref[0] // 2, place_ref[0] % 2
    for k, ref in enumerate(attn_refs):
        a_ref[:, rows_at(blk ^ k, width)] = ref[...]
    for i, (ref, rows) in enumerate(zip(w_refs, sizes)):
        at = rows_at(at_ref[i], rows)
        if ref.shape[1] >= cols:
            w_all[at, :] = ref[:, rows_at(blk, cols)] if ref.shape[1] > cols else ref[...]
        else:
            first = ref.shape[0] - cols // LANES * rows
            for j in range(cols // LANES):
                w_all[at, j * LANES:(j + 1) * LANES] = ref[first + j * rows:first + (j + 1) * rows]
    result = jnp.dot(a_ref[...], w_all[...], preferred_element_type=jnp.float32)
    result = result.astype(mine_ref.dtype).reshape(blks, 2, tok, cols)

    @pl.when(core == 0)
    def _():
        mine_ref[...] = result[:, 0]
        theirs_ref[...] = result[:, 1]

    @pl.when(core != 0)
    def _():
        mine_ref[...] = result[:, 1]
        theirs_ref[...] = result[:, 0]


def project(attns, w_parts, sizes, at, place, tok, cols):
    count, width = attns[0].shape
    blks = len(attns)
    like = jax.ShapeDtypeStruct((blks, tok, cols), attns[0].dtype)
    return pl.pallas_call(
        functools.partial(project_kernel, blks, sizes),
        out_shape=(like, like),
        in_specs=[SMEM, SMEM] + [VMEM] * (blks + len(w_parts)),
        out_specs=(VMEM, VMEM),
        scratch_shapes=[
            pltpu.VMEM((count, blks * width), attns[0].dtype),
            pltpu.VMEM((blks * width, cols), attns[0].dtype),
        ],
        compiler_params=PARAMS,
    )(index_array(*at), place, *attns, *w_parts)


def add_kernel(place_ref, x_ref, y_ref, *out_refs):
    for k, out_ref in enumerate(out_refs):
        at = place_ref[0] // 2 ^ k
        both = x_ref[at].astype(jnp.float32) + y_ref[at].astype(jnp.float32)
        out_ref[...] = both.astype(out_ref.dtype)


def add(x, y, place):
    blks = x.shape[0]
    return pl.pallas_call(
        add_kernel,
        out_shape=[jax.ShapeDtypeStruct(x.shape[1:], x.dtype)] * blks,
        in_specs=[SMEM, VMEM, VMEM],
        out_specs=[VMEM] * blks,
        compiler_params=PARAMS,
    )(place, x, y)


def unpack_kernel(place_ref, *refs):
    *in_refs, out_ref = refs
    width = in_refs[0].shape[1]
    for k, ref in enumerate(in_refs):
        out_ref[:, rows_at(place_ref[0] // 2 ^ k, width)] = ref[...]


def unpack(parts, place):
    tok, width = parts[0].shape
    return pl.pallas_call(
        unpack_kernel,
        out_shape=jax.ShapeDtypeStruct((tok, len(parts) * width), parts[0].dtype),
        in_specs=[SMEM] + [VMEM] * len(parts),
        out_specs=VMEM,
        compiler_params=PARAMS,
    )(place, *parts)


def xor(x, axis, by):
    size = math.prod(lax.axis_size(name) for name in axis)
    return lax.ppermute(x, axis, [(i, i ^ by) for i in range(size)])


def swap_all(parts, axis):
    last_first = [xor(parts[m], axis, m) for m in range(len(parts) - 1, 0, -1)]
    return [parts[0]] + last_first[::-1]


def squares(qkv, frame_clip, w_out):
    quarter = ("x", "zl")
    y, x, zh, zl, core = (lax.axis_index(n) for n in ("y", "x", "zh", "zl", "core"))
    tok, head_dim, cols = qkv.shape[1], w_out.shape[0], w_out.shape[1] // 4
    place = index_array((x * 2 + zl) * 2 + core)
    mine, theirs = x * 2 + zl, x * 2 + 1 - zl
    row, half = zh * 2 + zl, head_dim // 2

    w_far, w_corner, w_first, w_second = pieces(w_out, y, mine, theirs, cols)
    far = after(xor(w_far, ("zh",), 1), cost=AHEAD)
    kept, given = lanes(qkv, core, head_dim)
    shared = swap_all(deal(kept, xor(given, ("core",), 1), place), quarter)
    next_first = after(xor(after(w_first, shared[1]), ("zl",), 1), cost=AHEAD)
    q, k, v = sort(shared, place)
    k_far, v_far = xor(k, ("zh",), 1), xor(v, ("zh",), 1)
    near = xor(join(k, v, far), ("y",), 1)
    corner = xor(after(w_corner, k), ("zh", "zl"), 3)
    next_second = xor(after(w_second, k_far, v_far), ("zl",), 1)
    kvs = [(k, v), (k_far, v_far), near, (xor(k_far, ("y",), 1), xor(v_far, ("y",), 1))]

    bases = [y * 2 * FRB, (1 - y) * 2 * FRB]
    mask_of = masks(bases, 4 * tok, tok, 8 * tok, frame_clip)
    attn = attention(after(q, next_first), kvs, mask_of, [0, 0, 1, 1], head_dim)
    corner = after(corner, attn, cost=SOON)
    corner_rest = xor(corner, ("y",), 1)
    attns = swap_all([attn] * 4, quarter)
    next_second = after(next_second, attn, cost=AHEAD)
    w_parts = [w_out, next_first, next_second, far, near, corner, corner_rest]
    sizes = [head_dim] + [half] * 6
    at = [row] + [2 * (row ^ 1) + h for h in (0, 1)]
    at += [2 * (row ^ by) + h for by in (2, 3) for h in (y, 1 - y)]
    ours, other_core = project(attns, w_parts, sizes, at, place, tok, cols)
    parts = add(ours, xor(other_core, ("core",), 1), place)
    return unpack(swap_all(parts, quarter), place)


def layers(qkv, frame_clip, w_out):
    rows, blks = lax.axis_size("row"), lax.axis_size("blk")
    row, blk = lax.axis_index("row"), lax.axis_index("blk")
    tok, head_dim, cols = qkv.shape[1], w_out.shape[0], w_out.shape[1] // blks
    place = index_array(blk * 2 + lax.axis_index("core"))
    others = range(1, rows)

    (w_own,) = columns(w_out, [(head_dim, 0, blk)], cols)
    w_parts = [w_out] + [xor(w_own, ("row",), by) for by in others]
    packed = pack(qkv, 2 * blks, head_dim)
    own = lax.all_to_all(packed, ("blk", "core"), split_axis=0, concat_axis=0, tiled=True)
    q, kv = cut(own)
    kvs = [kv] + [xor(kv, ("row",), by) for by in others]
    mask_of = masks([0], 2 * tok, tok, 2 * blks * tok, frame_clip)
    attn = attention(q, kvs, mask_of, [0] * rows, head_dim)
    attns = swap_all([attn] * blks, ("blk",))
    at = [row ^ by for by in range(rows)]
    ours, other_core = project(attns, w_parts, [head_dim] * rows, at, place, tok, cols)
    parts = add(ours, xor(other_core, ("core",), 1), place)
    return unpack(swap_all(parts, ("blk",)), place)


def solution(mesh):
    blk, tile = mesh.shape["blk"], mesh.shape["tile"]
    if (blk, tile) == (4, 8):
        plan, names, shape = squares, ("y", "x", "zh", "zl", "core"), (2, 2, 2, 2, 2)
    else:
        plan, names, shape = layers, ("blk", "row", "core"), (blk, tile // 2, 2)
    fine = Mesh(mesh.devices.reshape(shape), names)
    tiles = names[2:] if plan is squares else names[1:]
    in_specs = (P(None, names, None), P(), P(tiles, None))
    return jax.shard_map(
        plan, mesh=fine, in_specs=in_specs, out_specs=P(names, None), check_vma=False
    )
```

```python
import functools
import math

import jax
import jax.numpy as jnp
from jax import lax
from jax.experimental import pallas as pl
from jax.experimental.pallas import tpu as pltpu
from jax.sharding import Mesh
from jax.sharding import PartitionSpec as P

FRB = 2
TPF = 16
LANES = 128
VMEM = pl.BlockSpec(memory_space=pltpu.VMEM)
SMEM = pl.BlockSpec(memory_space=pltpu.SMEM)
ANY = pl.BlockSpec(memory_space=pl.ANY)
PARAMS = pltpu.CompilerParams(vmem_limit_bytes=48 * 1024 * 1024)
AHEAD = pl.CostEstimate(flops=20_000_000_000, bytes_accessed=1_000_000, transcendentals=0)
SOON = pl.CostEstimate(flops=6_000_000_000, bytes_accessed=1_000_000, transcendentals=0)


def rows_at(index, size):
    return pl.ds(pl.multiple_of(index * size, size), size)


def index_array(*numbers):
    return jnp.stack([jnp.asarray(i, jnp.int32) for i in numbers])


def pack_kernel(head_dim, x_ref, out_ref):
    peers, _, width = out_ref.shape
    kinds, tok, _ = x_ref.shape
    heads = width // head_dim
    for g in range(peers):
        for i in range(heads):
            head = (g // 2 * heads + i) * 2 + g % 2
            for k in range(kinds):
                out_ref[g, k * tok:(k + 1) * tok, i * head_dim:(i + 1) * head_dim] = x_ref[
                    k, :, head * head_dim:(head + 1) * head_dim
                ]


def pack(x, peers, head_dim):
    kinds, tok, cols = x.shape
    return pl.pallas_call(
        functools.partial(pack_kernel, head_dim),
        out_shape=jax.ShapeDtypeStruct((peers, kinds * tok, cols // peers), x.dtype),
        in_specs=[VMEM],
        out_specs=VMEM,
        compiler_params=PARAMS,
    )(x)


def columns_kernel(at_ref, x_ref, *refs):
    *out_refs, sems = refs
    copies = []
    for i, ref in enumerate(out_refs):
        depth, cols = ref.shape
        piece = x_ref.at[rows_at(at_ref[2 * i], depth), rows_at(at_ref[2 * i + 1], cols)]
        copies.append(pltpu.make_async_copy(piece, ref, sems.at[i]))
    for copy in copies:
        copy.start()
    for copy in copies:
        copy.wait()


def columns(x, pieces, cols):
    return pl.pallas_call(
        columns_kernel,
        out_shape=[jax.ShapeDtypeStruct((piece[0], cols), x.dtype) for piece in pieces],
        in_specs=[SMEM, pl.BlockSpec(memory_space=pltpu.HBM)],
        out_specs=[VMEM] * len(pieces),
        scratch_shapes=[pltpu.SemaphoreType.DMA((len(pieces),))],
        compiler_params=PARAMS,
    )(
        index_array(*[i for piece in pieces for i in piece[1:]]),
        pltpu.with_memory_space_constraint(x, pltpu.HBM),
    )


def pieces_kernel(at_ref, x_ref, far_ref, corner_ref, near_ref):
    half, cols = corner_ref.shape
    rows = rows_at(at_ref[0], half)
    count = cols // LANES
    for j in range(count):
        far_ref[j * half:(j + 1) * half, :] = x_ref[rows, rows_at(at_ref[1] * count + j, LANES)]
    corner_ref[...] = x_ref[rows, rows_at(at_ref[2], cols)]
    near_ref[...] = x_ref[:, rows_at(at_ref[2], cols)]


def pieces(x, half, first_at, second_at, cols):
    return pl.pallas_call(
        pieces_kernel,
        out_shape=(
            jax.ShapeDtypeStruct((cols // LANES * (x.shape[0] // 2), LANES), x.dtype),
            jax.ShapeDtypeStruct((x.shape[0] // 2, cols), x.dtype),
            jax.ShapeDtypeStruct((x.shape[0], cols), x.dtype),
        ),
        in_specs=[SMEM, VMEM],
        out_specs=(VMEM, VMEM, VMEM),
        compiler_params=PARAMS,
    )(index_array(half, first_at, second_at), x)


def lane_kernel(head_dim, core_ref, x_ref, mine_ref, theirs_ref):
    kinds, tok, _ = x_ref.shape
    for out_ref, core in ((mine_ref, core_ref[0]), (theirs_ref, 1 - core_ref[0])):
        for g in range(out_ref.shape[0]):
            cols = rows_at(2 * g + core, head_dim)
            for k in range(kinds):
                out_ref[g, k * tok:(k + 1) * tok, :] = x_ref[k, :, cols]


def lanes(x, core, head_dim):
    kinds, tok, cols = x.shape
    like = jax.ShapeDtypeStruct((cols // head_dim // 2, kinds * tok, head_dim), x.dtype)
    return pl.pallas_call(
        functools.partial(lane_kernel, head_dim),
        out_shape=(like, like),
        in_specs=[SMEM, VMEM],
        out_specs=(VMEM, VMEM),
        compiler_params=PARAMS,
    )(index_array(core), x)


def deal_kernel(place_ref, mine_ref, got_ref, *out_refs):
    quarter, core = place_ref[0] // 2, place_ref[0] % 2
    for k, out_ref in enumerate(out_refs):
        out_ref[core] = mine_ref[quarter ^ k]
        out_ref[1 - core] = got_ref[quarter ^ k]


def deal(mine, got, place):
    quarters, depth, width = mine.shape
    return pl.pallas_call(
        deal_kernel,
        out_shape=[jax.ShapeDtypeStruct((2, depth, width), mine.dtype)] * quarters,
        in_specs=[SMEM, VMEM, VMEM],
        out_specs=[VMEM] * quarters,
        compiler_params=PARAMS,
    )(place, mine, got)


def sort_kernel(place_ref, *refs):
    *in_refs, q_ref, k_ref, v_ref = refs
    tok = q_ref.shape[0] // (2 * len(in_refs))
    for i, ref in enumerate(in_refs):
        for core in range(2):
            at = rows_at((place_ref[0] // 2 ^ i) * 2 + core, tok)
            for j, out_ref in enumerate((q_ref, k_ref, v_ref)):
                out_ref[at, :] = ref[core, j * tok:(j + 1) * tok, :]


def sort(parts, place):
    both, depth, width = parts[0].shape
    count = both * len(parts) * (depth // 3)
    return pl.pallas_call(
        sort_kernel,
        out_shape=[jax.ShapeDtypeStruct((count, width), parts[0].dtype)] * 3,
        in_specs=[SMEM] + [VMEM] * len(parts),
        out_specs=[VMEM] * 3,
        compiler_params=PARAMS,
    )(place, *parts)


def join_kernel(*refs):
    *in_refs, out_ref = refs
    first = 0
    for ref in in_refs:
        out_ref[first:first + ref.shape[0], :] = ref[...]
        first += ref.shape[0]


def join(*arrays):
    depth = sum(x.shape[0] for x in arrays)
    return pl.pallas_call(
        join_kernel,
        out_shape=jax.ShapeDtypeStruct((depth, arrays[0].shape[1]), arrays[0].dtype),
        in_specs=[VMEM] * len(arrays),
        out_specs=VMEM,
        compiler_params=PARAMS,
    )(*arrays)


def cut_kernel(x_ref, q_ref, kv_ref):
    peers, depth, _ = x_ref.shape
    tok = depth // 3
    for g in range(peers):
        q_ref[g * tok:(g + 1) * tok, :] = x_ref[g, :tok, :]
        for i in range(2):
            kv_ref[(i * peers + g) * tok:(i * peers + g + 1) * tok, :] = x_ref[
                g, (i + 1) * tok:(i + 2) * tok, :
            ]


def cut(x):
    peers, depth, width = x.shape
    count = peers * depth // 3
    return pl.pallas_call(
        cut_kernel,
        out_shape=[jax.ShapeDtypeStruct((size, width), x.dtype) for size in (count, 2 * count)],
        in_specs=[VMEM],
        out_specs=[VMEM, VMEM],
        compiler_params=PARAMS,
    )(x)


def after_kernel(*refs):
    pass


def after(passed, *first, cost=None):
    return pl.pallas_call(
        after_kernel,
        out_shape=jax.ShapeDtypeStruct(passed.shape, passed.dtype),
        in_specs=[ANY] * (1 + len(first)),
        out_specs=ANY,
        input_output_aliases={0: 0},
        compiler_params=PARAMS,
        cost_estimate=cost,
    )(passed, *first)


def clip_of(token, base, span, tok_dev, clip_ref):
    frame = base + token // span * FRB + token % tok_dev // TPF
    clip = jnp.zeros_like(token)
    for f in range(clip_ref.shape[0]):
        clip = jnp.where(frame == f, clip_ref[f], clip)
    return clip


def mask_kernel(span, tok, base_ref, clip_ref, *out_refs):
    count = out_refs[0].shape[0]
    row = lax.broadcasted_iota(jnp.int32, (count, 1), 0)
    col = lax.broadcasted_iota(jnp.int32, (1, count), 1)
    row_clip = clip_of(row, base_ref[0], span, tok, clip_ref)
    for i, out_ref in enumerate(out_refs):
        allowed = row_clip == clip_of(col, base_ref[i], span, tok, clip_ref)
        out_ref[...] = jnp.where(allowed, 0.0, -1e30)


def masks(bases, span, tok, count, frame_clip):
    return pl.pallas_call(
        functools.partial(mask_kernel, span, tok),
        out_shape=[jax.ShapeDtypeStruct((count, count), jnp.float32)] * len(bases),
        in_specs=[SMEM, SMEM],
        out_specs=[VMEM] * len(bases),
        compiler_params=PARAMS,
    )(index_array(*bases), frame_clip)


def attention_kernel(head_dim, n_mask, which, joint, q_ref, *refs):
    *refs, out_ref = refs
    mask_refs, refs = refs[:n_mask], refs[n_mask:]
    count, width = q_ref.shape
    k_refs, v_refs = [], []
    for both in joint:
        ref, *refs = refs
        if both:
            k_refs.append(ref.at[0:count])
            v_refs.append(ref.at[count:2 * count])
        else:
            value_ref, *refs = refs
            k_refs.append(ref)
            v_refs.append(value_ref)
    scale = math.log2(math.e) / math.sqrt(head_dim)
    per_step = max(1, 1024 // count)
    for h in range(width // head_dim):
        cols = slice(h * head_dim, (h + 1) * head_dim)
        queries = q_ref[:, cols]
        top = total = acc = None
        for first in range(0, len(k_refs), per_step):
            here = range(first, min(first + per_step, len(k_refs)))
            scores = []
            for i in here:
                s = lax.dot_general(
                    queries, k_refs[i][:, cols], (((1,), (1,)), ((), ())),
                    preferred_element_type=jnp.float32,
                )
                scores.append(s * scale + mask_refs[which[i]][...])
            new_top = functools.reduce(
                jnp.maximum, [jnp.max(s, axis=1, keepdims=True) for s in scores]
            )
            if top is not None:
                new_top = jnp.maximum(top, new_top)
                factor = jnp.exp2(top - new_top)
                total, acc = total * factor, acc * factor
            top = new_top
            for i, s in zip(here, scores):
                p = jnp.exp2(s - top)
                part = jnp.sum(p, axis=1, keepdims=True)
                dot = jnp.dot(
                    p.astype(jnp.bfloat16), v_refs[i][:, cols], preferred_element_type=jnp.float32
                )
                total = part if total is None else total + part
                acc = dot if acc is None else acc + dot
        out_ref[:, cols] = (acc / total).astype(out_ref.dtype)


def attention(q, kvs, mask_of, which, head_dim):
    joint = [not isinstance(kv, tuple) for kv in kvs]
    arrays = [x for kv, both in zip(kvs, joint) for x in ((kv,) if both else kv)]
    return pl.pallas_call(
        functools.partial(attention_kernel, head_dim, len(mask_of), which, joint),
        out_shape=jax.ShapeDtypeStruct(q.shape, q.dtype),
        in_specs=[VMEM] * (1 + len(mask_of) + len(arrays)),
        out_specs=VMEM,
        compiler_params=PARAMS,
    )(q, *mask_of, *arrays)


def project_kernel(n_attn, sizes, at_ref, place_ref, *refs):
    attn_refs, w_refs = refs[:n_attn], refs[n_attn:-4]
    mine_ref, theirs_ref, a_ref, w_all = refs[-4:]
    width = attn_refs[0].shape[1]
    blks, tok, cols = mine_ref.shape
    blk, core = place_ref[0] // 2, place_ref[0] % 2
    for k, ref in enumerate(attn_refs):
        a_ref[:, rows_at(blk ^ k, width)] = ref[...]
    for i, (ref, rows) in enumerate(zip(w_refs, sizes)):
        at = rows_at(at_ref[i], rows)
        if ref.shape[1] >= cols:
            w_all[at, :] = ref[:, rows_at(blk, cols)] if ref.shape[1] > cols else ref[...]
        else:
            first = ref.shape[0] - cols // LANES * rows
            for j in range(cols // LANES):
                w_all[at, j * LANES:(j + 1) * LANES] = ref[first + j * rows:first + (j + 1) * rows]
    result = jnp.dot(a_ref[...], w_all[...], preferred_element_type=jnp.float32)
    result = result.astype(mine_ref.dtype).reshape(blks, 2, tok, cols)

    @pl.when(core == 0)
    def _():
        mine_ref[...] = result[:, 0]
        theirs_ref[...] = result[:, 1]

    @pl.when(core != 0)
    def _():
        mine_ref[...] = result[:, 1]
        theirs_ref[...] = result[:, 0]


def project(attns, w_parts, sizes, at, place, tok, cols):
    count, width = attns[0].shape
    blks = len(attns)
    like = jax.ShapeDtypeStruct((blks, tok, cols), attns[0].dtype)
    return pl.pallas_call(
        functools.partial(project_kernel, blks, sizes),
        out_shape=(like, like),
        in_specs=[SMEM, SMEM] + [VMEM] * (blks + len(w_parts)),
        out_specs=(VMEM, VMEM),
        scratch_shapes=[
            pltpu.VMEM((count, blks * width), attns[0].dtype),
            pltpu.VMEM((blks * width, cols), attns[0].dtype),
        ],
        compiler_params=PARAMS,
    )(index_array(*at), place, *attns, *w_parts)


def add_kernel(place_ref, x_ref, y_ref, *out_refs):
    for k, out_ref in enumerate(out_refs):
        at = place_ref[0] // 2 ^ k
        both = x_ref[at].astype(jnp.float32) + y_ref[at].astype(jnp.float32)
        out_ref[...] = both.astype(out_ref.dtype)


def add(x, y, place):
    blks = x.shape[0]
    return pl.pallas_call(
        add_kernel,
        out_shape=[jax.ShapeDtypeStruct(x.shape[1:], x.dtype)] * blks,
        in_specs=[SMEM, VMEM, VMEM],
        out_specs=[VMEM] * blks,
        compiler_params=PARAMS,
    )(place, x, y)


def unpack_kernel(place_ref, *refs):
    *in_refs, out_ref = refs
    width = in_refs[0].shape[1]
    for k, ref in enumerate(in_refs):
        out_ref[:, rows_at(place_ref[0] // 2 ^ k, width)] = ref[...]


def unpack(parts, place):
    tok, width = parts[0].shape
    return pl.pallas_call(
        unpack_kernel,
        out_shape=jax.ShapeDtypeStruct((tok, len(parts) * width), parts[0].dtype),
        in_specs=[SMEM] + [VMEM] * len(parts),
        out_specs=VMEM,
        compiler_params=PARAMS,
    )(place, *parts)


def xor(x, axis, by):
    size = math.prod(lax.axis_size(name) for name in axis)
    return lax.ppermute(x, axis, [(i, i ^ by) for i in range(size)])


def swap_all(parts, axis):
    last_first = [xor(parts[m], axis, m) for m in range(len(parts) - 1, 0, -1)]
    return [parts[0]] + last_first[::-1]


def squares(qkv, frame_clip, w_out):
    quarter = ("x", "zl")
    y, x, zh, zl, core = (lax.axis_index(n) for n in ("y", "x", "zh", "zl", "core"))
    tok, head_dim, cols = qkv.shape[1], w_out.shape[0], w_out.shape[1] // 4
    place = index_array((x * 2 + zl) * 2 + core)
    mine, theirs = x * 2 + zl, x * 2 + 1 - zl
    row, half = zh * 2 + zl, head_dim // 2

    w_far, w_corner, w_near = pieces(w_out, y, mine, theirs, cols)
    far = after(xor(w_far, ("zh",), 1), cost=AHEAD)
    kept, given = lanes(qkv, core, head_dim)
    shared = swap_all(deal(kept, xor(given, ("core",), 1), place), quarter)
    q, k, v = sort(shared, place)
    k_far, v_far = xor(k, ("zh",), 1), xor(v, ("zh",), 1)
    near = xor(join(k, v, far), ("y",), 1)
    corner = xor(after(w_corner, k), ("zh", "zl"), 3)
    w_next = xor(after(w_near, k), ("zl",), 1)
    kvs = [(k, v), (k_far, v_far), near, (xor(k_far, ("y",), 1), xor(v_far, ("y",), 1))]

    bases = [y * 2 * FRB, (1 - y) * 2 * FRB]
    mask_of = masks(bases, 4 * tok, tok, 8 * tok, frame_clip)
    attn = attention(q, kvs, mask_of, [0, 0, 1, 1], head_dim)
    corner = after(corner, attn, cost=SOON)
    corner_rest = xor(corner, ("y",), 1)
    attns = swap_all([attn] * 4, quarter)
    w_next = after(w_next, attn, cost=AHEAD)
    w_parts = [w_out, w_next, far, near, corner, corner_rest]
    sizes = [head_dim, head_dim, half, half, half, half]
    at = [row, row ^ 1] + [2 * (row ^ by) + h for by in (2, 3) for h in (y, 1 - y)]
    ours, other_core = project(attns, w_parts, sizes, at, place, tok, cols)
    parts = add(ours, xor(other_core, ("core",), 1), place)
    return unpack(swap_all(parts, quarter), place)


def layers(qkv, frame_clip, w_out):
    rows, blks = lax.axis_size("row"), lax.axis_size("blk")
    row, blk = lax.axis_index("row"), lax.axis_index("blk")
    tok, head_dim, cols = qkv.shape[1], w_out.shape[0], w_out.shape[1] // blks
    place = index_array(blk * 2 + lax.axis_index("core"))
    others = range(1, rows)

    (w_own,) = columns(w_out, [(head_dim, 0, blk)], cols)
    w_parts = [w_out] + [xor(w_own, ("row",), by) for by in others]
    packed = pack(qkv, 2 * blks, head_dim)
    own = lax.all_to_all(packed, ("blk", "core"), split_axis=0, concat_axis=0, tiled=True)
    q, kv = cut(own)
    kvs = [kv] + [xor(kv, ("row",), by) for by in others]
    mask_of = masks([0], 2 * tok, tok, 2 * blks * tok, frame_clip)
    attn = attention(q, kvs, mask_of, [0] * rows, head_dim)
    attns = swap_all([attn] * blks, ("blk",))
    at = [row ^ by for by in range(rows)]
    ours, other_core = project(attns, w_parts, [head_dim] * rows, at, place, tok, cols)
    parts = add(ours, xor(other_core, ("core",), 1), place)
    return unpack(swap_all(parts, ("blk",)), place)


def solution(mesh):
    blk, tile = mesh.shape["blk"], mesh.shape["tile"]
    if (blk, tile) == (4, 8):
        plan, names, shape = squares, ("y", "x", "zh", "zl", "core"), (2, 2, 2, 2, 2)
    else:
        plan, names, shape = layers, ("blk", "row", "core"), (blk, tile // 2, 2)
    fine = Mesh(mesh.devices.reshape(shape), names)
    tiles = names[2:] if plan is squares else names[1:]
    in_specs = (P(None, names, None), P(), P(tiles, None))
    return jax.shard_map(
        plan, mesh=fine, in_specs=in_specs, out_specs=P(names, None), check_vma=False
    )
```

```python
import functools
import math

import jax
import jax.numpy as jnp
from jax import lax
from jax.experimental import pallas as pl
from jax.experimental.pallas import tpu as pltpu
from jax.sharding import Mesh
from jax.sharding import PartitionSpec as P

FRB = 2
TPF = 16
LANES = 128
VMEM = pl.BlockSpec(memory_space=pltpu.VMEM)
SMEM = pl.BlockSpec(memory_space=pltpu.SMEM)
ANY = pl.BlockSpec(memory_space=pl.ANY)
PARAMS = pltpu.CompilerParams(vmem_limit_bytes=48 * 1024 * 1024)
AHEAD = pl.CostEstimate(flops=20_000_000_000, bytes_accessed=1_000_000, transcendentals=0)
FIRST = pl.CostEstimate(flops=1_000_000_000, bytes_accessed=1_000_000, transcendentals=0)
SOON = pl.CostEstimate(flops=6_000_000_000, bytes_accessed=1_000_000, transcendentals=0)


def rows_at(index, size):
    return pl.ds(pl.multiple_of(index * size, size), size)


def index_array(*numbers):
    return jnp.stack([jnp.asarray(i, jnp.int32) for i in numbers])


def pack_kernel(head_dim, x_ref, out_ref):
    peers, _, width = out_ref.shape
    kinds, tok, _ = x_ref.shape
    heads = width // head_dim
    for g in range(peers):
        for i in range(heads):
            head = (g // 2 * heads + i) * 2 + g % 2
            for k in range(kinds):
                out_ref[g, k * tok:(k + 1) * tok, i * head_dim:(i + 1) * head_dim] = x_ref[
                    k, :, head * head_dim:(head + 1) * head_dim
                ]


def pack(x, peers, head_dim):
    kinds, tok, cols = x.shape
    return pl.pallas_call(
        functools.partial(pack_kernel, head_dim),
        out_shape=jax.ShapeDtypeStruct((peers, kinds * tok, cols // peers), x.dtype),
        in_specs=[VMEM],
        out_specs=VMEM,
        compiler_params=PARAMS,
    )(x)


def columns_kernel(at_ref, x_ref, *refs):
    *out_refs, sems = refs
    copies = []
    for i, ref in enumerate(out_refs):
        depth, cols = ref.shape
        piece = x_ref.at[rows_at(at_ref[2 * i], depth), rows_at(at_ref[2 * i + 1], cols)]
        copies.append(pltpu.make_async_copy(piece, ref, sems.at[i]))
    for copy in copies:
        copy.start()
    for copy in copies:
        copy.wait()


def columns(x, pieces, cols):
    return pl.pallas_call(
        columns_kernel,
        out_shape=[jax.ShapeDtypeStruct((piece[0], cols), x.dtype) for piece in pieces],
        in_specs=[SMEM, pl.BlockSpec(memory_space=pltpu.HBM)],
        out_specs=[VMEM] * len(pieces),
        scratch_shapes=[pltpu.SemaphoreType.DMA((len(pieces),))],
        compiler_params=PARAMS,
    )(
        index_array(*[i for piece in pieces for i in piece[1:]]),
        pltpu.with_memory_space_constraint(x, pltpu.HBM),
    )


def blocks_kernel(at_ref, x_ref, out_ref):
    half = x_ref.shape[0] // 2
    count = out_ref.shape[0] // half
    for j in range(count):
        out_ref[j * half:(j + 1) * half, :] = x_ref[
            rows_at(at_ref[0], half), rows_at(at_ref[1] * count + j, LANES)
        ]


def blocks(x, half, at, cols):
    like = jax.ShapeDtypeStruct((cols // LANES * (x.shape[0] // 2), LANES), x.dtype)
    return pl.pallas_call(
        blocks_kernel,
        out_shape=like,
        in_specs=[SMEM, VMEM],
        out_specs=VMEM,
        compiler_params=PARAMS,
    )(index_array(half, at), x)


def pieces_kernel(at_ref, x_ref, *refs):
    half_ref, all_ref = refs[-2:]
    half, cols = half_ref.shape
    half_ref[...] = x_ref[rows_at(at_ref[0], half), rows_at(at_ref[1], cols)]
    all_ref[...] = x_ref[:, rows_at(at_ref[1], cols)]


def pieces(x, half, at, cols, *first):
    depth = x.shape[0]
    return pl.pallas_call(
        pieces_kernel,
        out_shape=[jax.ShapeDtypeStruct((rows, cols), x.dtype) for rows in (depth // 2, depth)],
        in_specs=[SMEM, VMEM] + [ANY] * len(first),
        out_specs=[VMEM, VMEM],
        compiler_params=PARAMS,
    )(index_array(half, at), x, *first)


def lane_kernel(head_dim, core_ref, x_ref, mine_ref, theirs_ref):
    kinds, tok, _ = x_ref.shape
    for out_ref, core in ((mine_ref, core_ref[0]), (theirs_ref, 1 - core_ref[0])):
        for g in range(out_ref.shape[0]):
            cols = rows_at(2 * g + core, head_dim)
            for k in range(kinds):
                out_ref[g, k * tok:(k + 1) * tok, :] = x_ref[k, :, cols]


def lanes(x, core, head_dim):
    kinds, tok, cols = x.shape
    like = jax.ShapeDtypeStruct((cols // head_dim // 2, kinds * tok, head_dim), x.dtype)
    return pl.pallas_call(
        functools.partial(lane_kernel, head_dim),
        out_shape=(like, like),
        in_specs=[SMEM, VMEM],
        out_specs=(VMEM, VMEM),
        compiler_params=PARAMS,
    )(index_array(core), x)


def deal_kernel(place_ref, mine_ref, got_ref, *out_refs):
    quarter, core = place_ref[0] // 2, place_ref[0] % 2
    for k, out_ref in enumerate(out_refs):
        out_ref[core] = mine_ref[quarter ^ k]
        out_ref[1 - core] = got_ref[quarter ^ k]


def deal(mine, got, place):
    quarters, depth, width = mine.shape
    return pl.pallas_call(
        deal_kernel,
        out_shape=[jax.ShapeDtypeStruct((2, depth, width), mine.dtype)] * quarters,
        in_specs=[SMEM, VMEM, VMEM],
        out_specs=[VMEM] * quarters,
        compiler_params=PARAMS,
    )(place, mine, got)


def sort_kernel(place_ref, *refs):
    *in_refs, q_ref, k_ref, v_ref = refs
    tok = q_ref.shape[0] // (2 * len(in_refs))
    for i, ref in enumerate(in_refs):
        for core in range(2):
            at = rows_at((place_ref[0] // 2 ^ i) * 2 + core, tok)
            for j, out_ref in enumerate((q_ref, k_ref, v_ref)):
                out_ref[at, :] = ref[core, j * tok:(j + 1) * tok, :]


def sort(parts, place):
    both, depth, width = parts[0].shape
    count = both * len(parts) * (depth // 3)
    return pl.pallas_call(
        sort_kernel,
        out_shape=[jax.ShapeDtypeStruct((count, width), parts[0].dtype)] * 3,
        in_specs=[SMEM] + [VMEM] * len(parts),
        out_specs=[VMEM] * 3,
        compiler_params=PARAMS,
    )(place, *parts)


def join_kernel(*refs):
    *in_refs, out_ref = refs
    first = 0
    for ref in in_refs:
        out_ref[first:first + ref.shape[0], :] = ref[...]
        first += ref.shape[0]


def join(*arrays):
    depth = sum(x.shape[0] for x in arrays)
    return pl.pallas_call(
        join_kernel,
        out_shape=jax.ShapeDtypeStruct((depth, arrays[0].shape[1]), arrays[0].dtype),
        in_specs=[VMEM] * len(arrays),
        out_specs=VMEM,
        compiler_params=PARAMS,
    )(*arrays)


def cut_kernel(x_ref, q_ref, kv_ref):
    peers, depth, _ = x_ref.shape
    tok = depth // 3
    for g in range(peers):
        q_ref[g * tok:(g + 1) * tok, :] = x_ref[g, :tok, :]
        for i in range(2):
            kv_ref[(i * peers + g) * tok:(i * peers + g + 1) * tok, :] = x_ref[
                g, (i + 1) * tok:(i + 2) * tok, :
            ]


def cut(x):
    peers, depth, width = x.shape
    count = peers * depth // 3
    return pl.pallas_call(
        cut_kernel,
        out_shape=[jax.ShapeDtypeStruct((size, width), x.dtype) for size in (count, 2 * count)],
        in_specs=[VMEM],
        out_specs=[VMEM, VMEM],
        compiler_params=PARAMS,
    )(x)


def after_kernel(*refs):
    pass


def after(passed, *first, cost=None):
    return pl.pallas_call(
        after_kernel,
        out_shape=jax.ShapeDtypeStruct(passed.shape, passed.dtype),
        in_specs=[ANY] * (1 + len(first)),
        out_specs=ANY,
        input_output_aliases={0: 0},
        compiler_params=PARAMS,
        cost_estimate=cost,
    )(passed, *first)


def clip_of(token, base, span, tok_dev, clip_ref):
    frame = base + token // span * FRB + token % tok_dev // TPF
    clip = jnp.zeros_like(token)
    for f in range(clip_ref.shape[0]):
        clip = jnp.where(frame == f, clip_ref[f], clip)
    return clip


def mask_kernel(span, tok, base_ref, clip_ref, *out_refs):
    count = out_refs[0].shape[0]
    row = lax.broadcasted_iota(jnp.int32, (count, 1), 0)
    col = lax.broadcasted_iota(jnp.int32, (1, count), 1)
    row_clip = clip_of(row, base_ref[0], span, tok, clip_ref)
    for i, out_ref in enumerate(out_refs):
        allowed = row_clip == clip_of(col, base_ref[i], span, tok, clip_ref)
        out_ref[...] = jnp.where(allowed, 0.0, -1e30)


def masks(bases, span, tok, count, frame_clip):
    return pl.pallas_call(
        functools.partial(mask_kernel, span, tok),
        out_shape=[jax.ShapeDtypeStruct((count, count), jnp.float32)] * len(bases),
        in_specs=[SMEM, SMEM],
        out_specs=[VMEM] * len(bases),
        compiler_params=PARAMS,
    )(index_array(*bases), frame_clip)


def attention_kernel(head_dim, n_mask, which, joint, q_ref, *refs):
    *refs, out_ref = refs
    mask_refs, refs = refs[:n_mask], refs[n_mask:]
    count, width = q_ref.shape
    k_refs, v_refs = [], []
    for both in joint:
        ref, *refs = refs
        if both:
            k_refs.append(ref.at[0:count])
            v_refs.append(ref.at[count:2 * count])
        else:
            value_ref, *refs = refs
            k_refs.append(ref)
            v_refs.append(value_ref)
    scale = math.log2(math.e) / math.sqrt(head_dim)
    per_step = max(1, 1024 // count)
    for h in range(width // head_dim):
        cols = slice(h * head_dim, (h + 1) * head_dim)
        queries = q_ref[:, cols]
        top = total = acc = None
        for first in range(0, len(k_refs), per_step):
            here = range(first, min(first + per_step, len(k_refs)))
            scores = []
            for i in here:
                s = lax.dot_general(
                    queries, k_refs[i][:, cols], (((1,), (1,)), ((), ())),
                    preferred_element_type=jnp.float32,
                )
                scores.append(s * scale + mask_refs[which[i]][...])
            new_top = functools.reduce(
                jnp.maximum, [jnp.max(s, axis=1, keepdims=True) for s in scores]
            )
            if top is not None:
                new_top = jnp.maximum(top, new_top)
                factor = jnp.exp2(top - new_top)
                total, acc = total * factor, acc * factor
            top = new_top
            for i, s in zip(here, scores):
                p = jnp.exp2(s - top)
                part = jnp.sum(p, axis=1, keepdims=True)
                dot = jnp.dot(
                    p.astype(jnp.bfloat16), v_refs[i][:, cols], preferred_element_type=jnp.float32
                )
                total = part if total is None else total + part
                acc = dot if acc is None else acc + dot
        out_ref[:, cols] = (acc / total).astype(out_ref.dtype)


def attention(q, kvs, mask_of, which, head_dim):
    joint = [not isinstance(kv, tuple) for kv in kvs]
    arrays = [x for kv, both in zip(kvs, joint) for x in ((kv,) if both else kv)]
    return pl.pallas_call(
        functools.partial(attention_kernel, head_dim, len(mask_of), which, joint),
        out_shape=jax.ShapeDtypeStruct(q.shape, q.dtype),
        in_specs=[VMEM] * (1 + len(mask_of) + len(arrays)),
        out_specs=VMEM,
        compiler_params=PARAMS,
        cost_estimate=FIRST,
    )(q, *mask_of, *arrays)


def project_kernel(n_attn, sizes, at_ref, place_ref, *refs):
    attn_refs, w_refs = refs[:n_attn], refs[n_attn:-4]
    mine_ref, theirs_ref, a_ref, w_all = refs[-4:]
    width = attn_refs[0].shape[1]
    blks, tok, cols = mine_ref.shape
    blk, core = place_ref[0] // 2, place_ref[0] % 2
    for k, ref in enumerate(attn_refs):
        a_ref[:, rows_at(blk ^ k, width)] = ref[...]
    for i, (ref, rows) in enumerate(zip(w_refs, sizes)):
        at = rows_at(at_ref[i], rows)
        if ref.shape[1] >= cols:
            w_all[at, :] = ref[:, rows_at(blk, cols)] if ref.shape[1] > cols else ref[...]
        else:
            first = ref.shape[0] - cols // LANES * rows
            for j in range(cols // LANES):
                w_all[at, j * LANES:(j + 1) * LANES] = ref[first + j * rows:first + (j + 1) * rows]
    result = jnp.dot(a_ref[...], w_all[...], preferred_element_type=jnp.float32)
    result = result.astype(mine_ref.dtype).reshape(blks, 2, tok, cols)

    @pl.when(core == 0)
    def _():
        mine_ref[...] = result[:, 0]
        theirs_ref[...] = result[:, 1]

    @pl.when(core != 0)
    def _():
        mine_ref[...] = result[:, 1]
        theirs_ref[...] = result[:, 0]


def project(attns, w_parts, sizes, at, place, tok, cols):
    count, width = attns[0].shape
    blks = len(attns)
    like = jax.ShapeDtypeStruct((blks, tok, cols), attns[0].dtype)
    return pl.pallas_call(
        functools.partial(project_kernel, blks, sizes),
        out_shape=(like, like),
        in_specs=[SMEM, SMEM] + [VMEM] * (blks + len(w_parts)),
        out_specs=(VMEM, VMEM),
        scratch_shapes=[
            pltpu.VMEM((count, blks * width), attns[0].dtype),
            pltpu.VMEM((blks * width, cols), attns[0].dtype),
        ],
        compiler_params=PARAMS,
    )(index_array(*at), place, *attns, *w_parts)


def add_kernel(place_ref, x_ref, y_ref, *out_refs):
    for k, out_ref in enumerate(out_refs):
        at = place_ref[0] // 2 ^ k
        both = x_ref[at].astype(jnp.float32) + y_ref[at].astype(jnp.float32)
        out_ref[...] = both.astype(out_ref.dtype)


def add(x, y, place):
    blks = x.shape[0]
    return pl.pallas_call(
        add_kernel,
        out_shape=[jax.ShapeDtypeStruct(x.shape[1:], x.dtype)] * blks,
        in_specs=[SMEM, VMEM, VMEM],
        out_specs=[VMEM] * blks,
        compiler_params=PARAMS,
    )(place, x, y)


def unpack_kernel(place_ref, *refs):
    *in_refs, out_ref = refs
    width = in_refs[0].shape[1]
    for k, ref in enumerate(in_refs):
        out_ref[:, rows_at(place_ref[0] // 2 ^ k, width)] = ref[...]


def unpack(parts, place):
    tok, width = parts[0].shape
    return pl.pallas_call(
        unpack_kernel,
        out_shape=jax.ShapeDtypeStruct((tok, len(parts) * width), parts[0].dtype),
        in_specs=[SMEM] + [VMEM] * len(parts),
        out_specs=VMEM,
        compiler_params=PARAMS,
    )(place, *parts)


def xor(x, axis, by):
    size = math.prod(lax.axis_size(name) for name in axis)
    return lax.ppermute(x, axis, [(i, i ^ by) for i in range(size)])


def swap_all(parts, axis):
    last_first = [xor(parts[m], axis, m) for m in range(len(parts) - 1, 0, -1)]
    return [parts[0]] + last_first[::-1]


def squares(qkv, frame_clip, w_out):
    quarter = ("x", "zl")
    y, x, zh, zl, core = (lax.axis_index(n) for n in ("y", "x", "zh", "zl", "core"))
    tok, head_dim, cols = qkv.shape[1], w_out.shape[0], w_out.shape[1] // 4
    place = index_array((x * 2 + zl) * 2 + core)
    mine, theirs = x * 2 + zl, x * 2 + 1 - zl
    row, half = zh * 2 + zl, head_dim // 2

    far = after(xor(blocks(w_out, y, mine, cols), ("zh",), 1), cost=AHEAD)
    kept, given = lanes(qkv, core, head_dim)
    shared = swap_all(deal(kept, xor(given, ("core",), 1), place), quarter)
    q, k, v = sort(shared, place)
    k_far, v_far = xor(k, ("zh",), 1), xor(v, ("zh",), 1)
    near = xor(join(k, v, far), ("y",), 1)
    bases = [y * 2 * FRB, (1 - y) * 2 * FRB]
    mask_of = masks(bases, 4 * tok, tok, 8 * tok, after(frame_clip, k))
    w_corner, w_near = pieces(w_out, y, theirs, cols, mask_of[0])
    corner = xor(w_corner, ("zh", "zl"), 3)
    w_next = xor(w_near, ("zl",), 1)
    kvs = [(k, v), (k_far, v_far), near, (xor(k_far, ("y",), 1), xor(v_far, ("y",), 1))]
    attn = attention(q, kvs, mask_of, [0, 0, 1, 1], head_dim)
    corner = after(corner, attn, cost=SOON)
    corner_rest = xor(corner, ("y",), 1)
    attns = swap_all([attn] * 4, quarter)
    w_next = after(w_next, attn, cost=AHEAD)
    w_parts = [w_out, w_next, far, near, corner, corner_rest]
    sizes = [head_dim, head_dim, half, half, half, half]
    at = [row, row ^ 1] + [2 * (row ^ by) + h for by in (2, 3) for h in (y, 1 - y)]
    ours, other_core = project(attns, w_parts, sizes, at, place, tok, cols)
    parts = add(ours, xor(other_core, ("core",), 1), place)
    return unpack(swap_all(parts, quarter), place)


def layers(qkv, frame_clip, w_out):
    rows, blks = lax.axis_size("row"), lax.axis_size("blk")
    row, blk = lax.axis_index("row"), lax.axis_index("blk")
    tok, head_dim, cols = qkv.shape[1], w_out.shape[0], w_out.shape[1] // blks
    place = index_array(blk * 2 + lax.axis_index("core"))
    others = range(1, rows)

    (w_own,) = columns(w_out, [(head_dim, 0, blk)], cols)
    w_parts = [w_out] + [xor(w_own, ("row",), by) for by in others]
    packed = pack(qkv, 2 * blks, head_dim)
    own = lax.all_to_all(packed, ("blk", "core"), split_axis=0, concat_axis=0, tiled=True)
    q, kv = cut(own)
    kvs = [kv] + [xor(kv, ("row",), by) for by in others]
    mask_of = masks([0], 2 * tok, tok, 2 * blks * tok, frame_clip)
    attn = attention(q, kvs, mask_of, [0] * rows, head_dim)
    attns = swap_all([attn] * blks, ("blk",))
    at = [row ^ by for by in range(rows)]
    ours, other_core = project(attns, w_parts, [head_dim] * rows, at, place, tok, cols)
    parts = add(ours, xor(other_core, ("core",), 1), place)
    return unpack(swap_all(parts, ("blk",)), place)


def solution(mesh):
    blk, tile = mesh.shape["blk"], mesh.shape["tile"]
    if (blk, tile) == (4, 8):
        plan, names, shape = squares, ("y", "x", "zh", "zl", "core"), (2, 2, 2, 2, 2)
    else:
        plan, names, shape = layers, ("blk", "row", "core"), (blk, tile // 2, 2)
    fine = Mesh(mesh.devices.reshape(shape), names)
    tiles = names[2:] if plan is squares else names[1:]
    in_specs = (P(None, names, None), P(), P(tiles, None))
    return jax.shard_map(
        plan, mesh=fine, in_specs=in_specs, out_specs=P(names, None), check_vma=False
    )
```

```python
import functools
import math

import jax
import jax.numpy as jnp
from jax import lax
from jax.experimental import pallas as pl
from jax.experimental.pallas import tpu as pltpu
from jax.sharding import Mesh
from jax.sharding import PartitionSpec as P

FRB = 2
TPF = 16
LANES = 128
VMEM = pl.BlockSpec(memory_space=pltpu.VMEM)
SMEM = pl.BlockSpec(memory_space=pltpu.SMEM)
ANY = pl.BlockSpec(memory_space=pl.ANY)
PARAMS = pltpu.CompilerParams(vmem_limit_bytes=48 * 1024 * 1024)
AHEAD = pl.CostEstimate(flops=20_000_000_000, bytes_accessed=1_000_000, transcendentals=0)
SOON = pl.CostEstimate(flops=6_000_000_000, bytes_accessed=1_000_000, transcendentals=0)


def rows_at(index, size):
    return pl.ds(pl.multiple_of(index * size, size), size)


def index_array(*numbers):
    return jnp.stack([jnp.asarray(i, jnp.int32) for i in numbers])


def pack_kernel(head_dim, x_ref, out_ref):
    peers, _, width = out_ref.shape
    kinds, tok, _ = x_ref.shape
    heads = width // head_dim
    for g in range(peers):
        for i in range(heads):
            head = (g // 2 * heads + i) * 2 + g % 2
            for k in range(kinds):
                out_ref[g, k * tok:(k + 1) * tok, i * head_dim:(i + 1) * head_dim] = x_ref[
                    k, :, head * head_dim:(head + 1) * head_dim
                ]


def pack(x, peers, head_dim):
    kinds, tok, cols = x.shape
    return pl.pallas_call(
        functools.partial(pack_kernel, head_dim),
        out_shape=jax.ShapeDtypeStruct((peers, kinds * tok, cols // peers), x.dtype),
        in_specs=[VMEM],
        out_specs=VMEM,
        compiler_params=PARAMS,
    )(x)


def columns_kernel(at_ref, x_ref, *refs):
    *out_refs, sems = refs
    copies = []
    for i, ref in enumerate(out_refs):
        depth, cols = ref.shape
        piece = x_ref.at[rows_at(at_ref[2 * i], depth), rows_at(at_ref[2 * i + 1], cols)]
        copies.append(pltpu.make_async_copy(piece, ref, sems.at[i]))
    for copy in copies:
        copy.start()
    for copy in copies:
        copy.wait()


def columns(x, pieces, cols):
    return pl.pallas_call(
        columns_kernel,
        out_shape=[jax.ShapeDtypeStruct((piece[0], cols), x.dtype) for piece in pieces],
        in_specs=[SMEM, pl.BlockSpec(memory_space=pltpu.HBM)],
        out_specs=[VMEM] * len(pieces),
        scratch_shapes=[pltpu.SemaphoreType.DMA((len(pieces),))],
        compiler_params=PARAMS,
    )(
        index_array(*[i for piece in pieces for i in piece[1:]]),
        pltpu.with_memory_space_constraint(x, pltpu.HBM),
    )


def pieces_kernel(at_ref, x_ref, far_ref, corner_ref, near_ref):
    half, cols = corner_ref.shape
    rows = rows_at(at_ref[0], half)
    count = cols // LANES
    for j in range(count):
        far_ref[j * half:(j + 1) * half, :] = x_ref[rows, rows_at(at_ref[1] * count + j, LANES)]
    corner_ref[...] = x_ref[rows, rows_at(at_ref[2], cols)]
    near_ref[...] = x_ref[:, rows_at(at_ref[2], cols)]


def pieces(x, half, first_at, second_at, cols):
    return pl.pallas_call(
        pieces_kernel,
        out_shape=(
            jax.ShapeDtypeStruct((cols // LANES * (x.shape[0] // 2), LANES), x.dtype),
            jax.ShapeDtypeStruct((x.shape[0] // 2, cols), x.dtype),
            jax.ShapeDtypeStruct((x.shape[0], cols), x.dtype),
        ),
        in_specs=[SMEM, VMEM],
        out_specs=(VMEM, VMEM, VMEM),
        compiler_params=PARAMS,
    )(index_array(half, first_at, second_at), x)


def lane_kernel(head_dim, core_ref, x_ref, mine_ref, theirs_ref):
    kinds, tok, _ = x_ref.shape
    for out_ref, core in ((mine_ref, core_ref[0]), (theirs_ref, 1 - core_ref[0])):
        for g in range(out_ref.shape[0]):
            cols = rows_at(2 * g + core, head_dim)
            for k in range(kinds):
                out_ref[g, k * tok:(k + 1) * tok, :] = x_ref[k, :, cols]


def lanes(x, core, head_dim):
    kinds, tok, cols = x.shape
    like = jax.ShapeDtypeStruct((cols // head_dim // 2, kinds * tok, head_dim), x.dtype)
    return pl.pallas_call(
        functools.partial(lane_kernel, head_dim),
        out_shape=(like, like),
        in_specs=[SMEM, VMEM],
        out_specs=(VMEM, VMEM),
        compiler_params=PARAMS,
    )(index_array(core), x)


def deal_kernel(place_ref, mine_ref, got_ref, *out_refs):
    quarter, core = place_ref[0] // 2, place_ref[0] % 2
    for k, out_ref in enumerate(out_refs):
        out_ref[core] = mine_ref[quarter ^ k]
        out_ref[1 - core] = got_ref[quarter ^ k]


def deal(mine, got, place):
    quarters, depth, width = mine.shape
    return pl.pallas_call(
        deal_kernel,
        out_shape=[jax.ShapeDtypeStruct((2, depth, width), mine.dtype)] * quarters,
        in_specs=[SMEM, VMEM, VMEM],
        out_specs=[VMEM] * quarters,
        compiler_params=PARAMS,
    )(place, mine, got)


def sort_kernel(place_ref, *refs):
    *in_refs, q_ref, k_ref, v_ref = refs
    tok = q_ref.shape[0] // (2 * len(in_refs))
    for i, ref in enumerate(in_refs):
        for core in range(2):
            at = rows_at((place_ref[0] // 2 ^ i) * 2 + core, tok)
            for j, out_ref in enumerate((q_ref, k_ref, v_ref)):
                out_ref[at, :] = ref[core, j * tok:(j + 1) * tok, :]


def sort(parts, place):
    both, depth, width = parts[0].shape
    count = both * len(parts) * (depth // 3)
    return pl.pallas_call(
        sort_kernel,
        out_shape=[jax.ShapeDtypeStruct((count, width), parts[0].dtype)] * 3,
        in_specs=[SMEM] + [VMEM] * len(parts),
        out_specs=[VMEM] * 3,
        compiler_params=PARAMS,
    )(place, *parts)


def join_kernel(*refs):
    *in_refs, out_ref = refs
    first = 0
    for ref in in_refs:
        out_ref[first:first + ref.shape[0], :] = ref[...]
        first += ref.shape[0]


def join(*arrays):
    depth = sum(x.shape[0] for x in arrays)
    return pl.pallas_call(
        join_kernel,
        out_shape=jax.ShapeDtypeStruct((depth, arrays[0].shape[1]), arrays[0].dtype),
        in_specs=[VMEM] * len(arrays),
        out_specs=VMEM,
        compiler_params=PARAMS,
    )(*arrays)


def cut_kernel(x_ref, q_ref, kv_ref):
    peers, depth, _ = x_ref.shape
    tok = depth // 3
    for g in range(peers):
        q_ref[g * tok:(g + 1) * tok, :] = x_ref[g, :tok, :]
        for i in range(2):
            kv_ref[(i * peers + g) * tok:(i * peers + g + 1) * tok, :] = x_ref[
                g, (i + 1) * tok:(i + 2) * tok, :
            ]


def cut(x):
    peers, depth, width = x.shape
    count = peers * depth // 3
    return pl.pallas_call(
        cut_kernel,
        out_shape=[jax.ShapeDtypeStruct((size, width), x.dtype) for size in (count, 2 * count)],
        in_specs=[VMEM],
        out_specs=[VMEM, VMEM],
        compiler_params=PARAMS,
    )(x)


def after_kernel(*refs):
    pass


def after(passed, *first, cost=None):
    return pl.pallas_call(
        after_kernel,
        out_shape=jax.ShapeDtypeStruct(passed.shape, passed.dtype),
        in_specs=[ANY] * (1 + len(first)),
        out_specs=ANY,
        input_output_aliases={0: 0},
        compiler_params=PARAMS,
        cost_estimate=cost,
    )(passed, *first)


def clip_of(token, base, span, tok_dev, clip_ref):
    frame = base + token // span * FRB + token % tok_dev // TPF
    clip = jnp.zeros_like(token)
    for f in range(clip_ref.shape[0]):
        clip = jnp.where(frame == f, clip_ref[f], clip)
    return clip


def mask_kernel(span, tok, base_ref, clip_ref, *out_refs):
    count = out_refs[0].shape[0]
    row = lax.broadcasted_iota(jnp.int32, (count, 1), 0)
    col = lax.broadcasted_iota(jnp.int32, (1, count), 1)
    row_clip = clip_of(row, base_ref[0], span, tok, clip_ref)
    for i, out_ref in enumerate(out_refs):
        allowed = row_clip == clip_of(col, base_ref[i], span, tok, clip_ref)
        out_ref[...] = jnp.where(allowed, 0.0, -1e30)


def masks(bases, span, tok, count, frame_clip):
    return pl.pallas_call(
        functools.partial(mask_kernel, span, tok),
        out_shape=[jax.ShapeDtypeStruct((count, count), jnp.float32)] * len(bases),
        in_specs=[SMEM, SMEM],
        out_specs=[VMEM] * len(bases),
        compiler_params=PARAMS,
    )(index_array(*bases), frame_clip)


def attention_kernel(head_dim, n_mask, which, joint, q_ref, *refs):
    *refs, out_ref = refs
    mask_refs, refs = refs[:n_mask], refs[n_mask:]
    count, width = q_ref.shape
    k_refs, v_refs = [], []
    for both in joint:
        ref, *refs = refs
        if both:
            k_refs.append(ref.at[0:count])
            v_refs.append(ref.at[count:2 * count])
        else:
            value_ref, *refs = refs
            k_refs.append(ref)
            v_refs.append(value_ref)
    scale = math.log2(math.e) / math.sqrt(head_dim)
    per_step = max(1, 1024 // count)
    for h in range(width // head_dim):
        cols = slice(h * head_dim, (h + 1) * head_dim)
        queries = q_ref[:, cols]
        top = total = acc = None
        for first in range(0, len(k_refs), per_step):
            here = range(first, min(first + per_step, len(k_refs)))
            scores = []
            for i in here:
                s = lax.dot_general(
                    queries, k_refs[i][:, cols], (((1,), (1,)), ((), ())),
                    preferred_element_type=jnp.float32,
                )
                scores.append(s * scale + mask_refs[which[i]][...])
            new_top = functools.reduce(
                jnp.maximum, [jnp.max(s, axis=1, keepdims=True) for s in scores]
            )
            if top is not None:
                new_top = jnp.maximum(top, new_top)
                factor = jnp.exp2(top - new_top)
                total, acc = total * factor, acc * factor
            top = new_top
            for i, s in zip(here, scores):
                p = jnp.exp2(s - top)
                part = jnp.sum(p, axis=1, keepdims=True)
                dot = jnp.dot(
                    p.astype(jnp.bfloat16), v_refs[i][:, cols], preferred_element_type=jnp.float32
                )
                total = part if total is None else total + part
                acc = dot if acc is None else acc + dot
        out_ref[:, cols] = (acc / total).astype(out_ref.dtype)


def attention(q, kvs, mask_of, which, head_dim):
    joint = [not isinstance(kv, tuple) for kv in kvs]
    arrays = [x for kv, both in zip(kvs, joint) for x in ((kv,) if both else kv)]
    return pl.pallas_call(
        functools.partial(attention_kernel, head_dim, len(mask_of), which, joint),
        out_shape=jax.ShapeDtypeStruct(q.shape, q.dtype),
        in_specs=[VMEM] * (1 + len(mask_of) + len(arrays)),
        out_specs=VMEM,
        compiler_params=PARAMS,
    )(q, *mask_of, *arrays)


def project_kernel(n_attn, sizes, at_ref, place_ref, *refs):
    attn_refs, w_refs = refs[:n_attn], refs[n_attn:-4]
    mine_ref, theirs_ref, a_ref, w_all = refs[-4:]
    width = attn_refs[0].shape[1]
    blks, tok, cols = mine_ref.shape
    blk, core = place_ref[0] // 2, place_ref[0] % 2
    for k, ref in enumerate(attn_refs):
        a_ref[:, rows_at(blk ^ k, width)] = ref[...]
    for i, (ref, rows) in enumerate(zip(w_refs, sizes)):
        at = rows_at(at_ref[i], rows)
        if ref.shape[1] >= cols:
            w_all[at, :] = ref[:, rows_at(blk, cols)] if ref.shape[1] > cols else ref[...]
        else:
            first = ref.shape[0] - cols // LANES * rows
            for j in range(cols // LANES):
                w_all[at, j * LANES:(j + 1) * LANES] = ref[first + j * rows:first + (j + 1) * rows]
    result = jnp.dot(a_ref[...], w_all[...], preferred_element_type=jnp.float32)
    result = result.astype(mine_ref.dtype).reshape(blks, 2, tok, cols)

    @pl.when(core == 0)
    def _():
        mine_ref[...] = result[:, 0]
        theirs_ref[...] = result[:, 1]

    @pl.when(core != 0)
    def _():
        mine_ref[...] = result[:, 1]
        theirs_ref[...] = result[:, 0]


def project(attns, w_parts, sizes, at, place, tok, cols):
    count, width = attns[0].shape
    blks = len(attns)
    like = jax.ShapeDtypeStruct((blks, tok, cols), attns[0].dtype)
    return pl.pallas_call(
        functools.partial(project_kernel, blks, sizes),
        out_shape=(like, like),
        in_specs=[SMEM, SMEM] + [VMEM] * (blks + len(w_parts)),
        out_specs=(VMEM, VMEM),
        scratch_shapes=[
            pltpu.VMEM((count, blks * width), attns[0].dtype),
            pltpu.VMEM((blks * width, cols), attns[0].dtype),
        ],
        compiler_params=PARAMS,
    )(index_array(*at), place, *attns, *w_parts)


def add_kernel(place_ref, x_ref, y_ref, *out_refs):
    for k, out_ref in enumerate(out_refs):
        at = place_ref[0] // 2 ^ k
        both = x_ref[at].astype(jnp.float32) + y_ref[at].astype(jnp.float32)
        out_ref[...] = both.astype(out_ref.dtype)


def add(x, y, place):
    blks = x.shape[0]
    return pl.pallas_call(
        add_kernel,
        out_shape=[jax.ShapeDtypeStruct(x.shape[1:], x.dtype)] * blks,
        in_specs=[SMEM, VMEM, VMEM],
        out_specs=[VMEM] * blks,
        compiler_params=PARAMS,
    )(place, x, y)


def unpack_kernel(place_ref, *refs):
    *in_refs, out_ref = refs
    width = in_refs[0].shape[1]
    for k, ref in enumerate(in_refs):
        out_ref[:, rows_at(place_ref[0] // 2 ^ k, width)] = ref[...]


def unpack(parts, place):
    tok, width = parts[0].shape
    return pl.pallas_call(
        unpack_kernel,
        out_shape=jax.ShapeDtypeStruct((tok, len(parts) * width), parts[0].dtype),
        in_specs=[SMEM] + [VMEM] * len(parts),
        out_specs=VMEM,
        compiler_params=PARAMS,
    )(place, *parts)


def xor(x, axis, by):
    size = math.prod(lax.axis_size(name) for name in axis)
    return lax.ppermute(x, axis, [(i, i ^ by) for i in range(size)])


def swap_all(parts, axis):
    last_first = [xor(parts[m], axis, m) for m in range(len(parts) - 1, 0, -1)]
    return [parts[0]] + last_first[::-1]


def squares(qkv, frame_clip, w_out):
    quarter = ("x", "zl")
    y, x, zh, zl, core = (lax.axis_index(n) for n in ("y", "x", "zh", "zl", "core"))
    tok, head_dim, cols = qkv.shape[1], w_out.shape[0], w_out.shape[1] // 4
    place = index_array((x * 2 + zl) * 2 + core)
    mine, theirs = x * 2 + zl, x * 2 + 1 - zl
    row, half = zh * 2 + zl, head_dim // 2

    w_far, w_corner, w_near = pieces(w_out, y, mine, theirs, cols)
    far = after(xor(w_far, ("zh",), 1), cost=AHEAD)
    kept, given = lanes(qkv, core, head_dim)
    shared = swap_all(deal(kept, xor(given, ("core",), 1), place), quarter)
    q, k, v = sort(shared, place)
    k_far, v_far = xor(k, ("zh",), 1), xor(v, ("zh",), 1)
    near = xor(join(k, v, far), ("y",), 1)
    corner = xor(after(w_corner, k), ("zh", "zl"), 3)
    w_next = xor(after(w_near, k), ("zl",), 1)
    kvs = [(k, v), (k_far, v_far), near, (xor(k_far, ("y",), 1), xor(v_far, ("y",), 1))]

    bases = [y * 2 * FRB, (1 - y) * 2 * FRB]
    mask_of = masks(bases, 4 * tok, tok, 8 * tok, frame_clip)
    attn = attention(q, kvs, mask_of, [0, 0, 1, 1], head_dim)
    corner = after(corner, attn)
    corner_rest = xor(corner, ("y",), 1)
    attns = swap_all([attn] * 4, quarter)
    w_parts = [w_out, w_next, far, near, corner, corner_rest]
    sizes = [head_dim, head_dim, half, half, half, half]
    at = [row, row ^ 1] + [2 * (row ^ by) + h for by in (2, 3) for h in (y, 1 - y)]
    ours, other_core = project(attns, w_parts, sizes, at, place, tok, cols)
    parts = add(ours, xor(other_core, ("core",), 1), place)
    return unpack(swap_all(parts, quarter), place)


def layers(qkv, frame_clip, w_out):
    rows, blks = lax.axis_size("row"), lax.axis_size("blk")
    row, blk = lax.axis_index("row"), lax.axis_index("blk")
    tok, head_dim, cols = qkv.shape[1], w_out.shape[0], w_out.shape[1] // blks
    place = index_array(blk * 2 + lax.axis_index("core"))
    others = range(1, rows)

    (w_own,) = columns(w_out, [(head_dim, 0, blk)], cols)
    w_parts = [w_out] + [xor(w_own, ("row",), by) for by in others]
    packed = pack(qkv, 2 * blks, head_dim)
    own = lax.all_to_all(packed, ("blk", "core"), split_axis=0, concat_axis=0, tiled=True)
    q, kv = cut(own)
    kvs = [kv] + [xor(kv, ("row",), by) for by in others]
    mask_of = masks([0], 2 * tok, tok, 2 * blks * tok, frame_clip)
    attn = attention(q, kvs, mask_of, [0] * rows, head_dim)
    attns = swap_all([attn] * blks, ("blk",))
    at = [row ^ by for by in range(rows)]
    ours, other_core = project(attns, w_parts, [head_dim] * rows, at, place, tok, cols)
    parts = add(ours, xor(other_core, ("core",), 1), place)
    return unpack(swap_all(parts, ("blk",)), place)


def solution(mesh):
    blk, tile = mesh.shape["blk"], mesh.shape["tile"]
    if (blk, tile) == (4, 8):
        plan, names, shape = squares, ("y", "x", "zh", "zl", "core"), (2, 2, 2, 2, 2)
    else:
        plan, names, shape = layers, ("blk", "row", "core"), (blk, tile // 2, 2)
    fine = Mesh(mesh.devices.reshape(shape), names)
    tiles = names[2:] if plan is squares else names[1:]
    in_specs = (P(None, names, None), P(), P(tiles, None))
    return jax.shard_map(
        plan, mesh=fine, in_specs=in_specs, out_specs=P(names, None), check_vma=False
    )
```

```python
import functools
import math

import jax
import jax.numpy as jnp
from jax import lax
from jax.experimental import pallas as pl
from jax.experimental.pallas import tpu as pltpu
from jax.sharding import Mesh
from jax.sharding import PartitionSpec as P

FRB = 2
TPF = 16
LANES = 128
VMEM = pl.BlockSpec(memory_space=pltpu.VMEM)
SMEM = pl.BlockSpec(memory_space=pltpu.SMEM)
ANY = pl.BlockSpec(memory_space=pl.ANY)
PARAMS = pltpu.CompilerParams(vmem_limit_bytes=48 * 1024 * 1024)
AHEAD = pl.CostEstimate(flops=20_000_000_000, bytes_accessed=1_000_000, transcendentals=0)
SOON = pl.CostEstimate(flops=6_000_000_000, bytes_accessed=1_000_000, transcendentals=0)


def rows_at(index, size):
    return pl.ds(pl.multiple_of(index * size, size), size)


def index_array(*numbers):
    return jnp.stack([jnp.asarray(i, jnp.int32) for i in numbers])


def pack_kernel(head_dim, x_ref, out_ref):
    peers, _, width = out_ref.shape
    kinds, tok, _ = x_ref.shape
    heads = width // head_dim
    for g in range(peers):
        for i in range(heads):
            head = (g // 2 * heads + i) * 2 + g % 2
            for k in range(kinds):
                out_ref[g, k * tok:(k + 1) * tok, i * head_dim:(i + 1) * head_dim] = x_ref[
                    k, :, head * head_dim:(head + 1) * head_dim
                ]


def pack(x, peers, head_dim):
    kinds, tok, cols = x.shape
    return pl.pallas_call(
        functools.partial(pack_kernel, head_dim),
        out_shape=jax.ShapeDtypeStruct((peers, kinds * tok, cols // peers), x.dtype),
        in_specs=[VMEM],
        out_specs=VMEM,
        compiler_params=PARAMS,
    )(x)


def columns_kernel(at_ref, x_ref, *refs):
    *out_refs, sems = refs
    copies = []
    for i, ref in enumerate(out_refs):
        depth, cols = ref.shape
        piece = x_ref.at[rows_at(at_ref[2 * i], depth), rows_at(at_ref[2 * i + 1], cols)]
        copies.append(pltpu.make_async_copy(piece, ref, sems.at[i]))
    for copy in copies:
        copy.start()
    for copy in copies:
        copy.wait()


def columns(x, pieces, cols):
    return pl.pallas_call(
        columns_kernel,
        out_shape=[jax.ShapeDtypeStruct((piece[0], cols), x.dtype) for piece in pieces],
        in_specs=[SMEM, pl.BlockSpec(memory_space=pltpu.HBM)],
        out_specs=[VMEM] * len(pieces),
        scratch_shapes=[pltpu.SemaphoreType.DMA((len(pieces),))],
        compiler_params=PARAMS,
    )(
        index_array(*[i for piece in pieces for i in piece[1:]]),
        pltpu.with_memory_space_constraint(x, pltpu.HBM),
    )


def pieces_kernel(at_ref, x_ref, far_ref, first_ref, second_ref, near_ref):
    half, cols = x_ref.shape[0] // 2, near_ref.shape[1]
    rows = rows_at(at_ref[0], half)
    count = cols // LANES
    for j in range(count):
        far_ref[j * half:(j + 1) * half, :] = x_ref[rows, rows_at(at_ref[1] * count + j, LANES)]
    for i, ref in enumerate((first_ref, second_ref)):
        ref[...] = x_ref[rows_at(at_ref[0] * 2 + i, half // 2), rows_at(at_ref[2], cols)]
    near_ref[...] = x_ref[:, rows_at(at_ref[2], cols)]


def pieces(x, half, first_at, second_at, cols):
    depth = x.shape[0]
    shapes = [(cols // LANES * (depth // 2), LANES)]
    shapes += [(rows, cols) for rows in (depth // 4, depth // 4, depth)]
    return pl.pallas_call(
        pieces_kernel,
        out_shape=[jax.ShapeDtypeStruct(shape, x.dtype) for shape in shapes],
        in_specs=[SMEM, VMEM],
        out_specs=[VMEM] * 4,
        compiler_params=PARAMS,
    )(index_array(half, first_at, second_at), x)


def lane_kernel(head_dim, core_ref, x_ref, mine_ref, theirs_ref):
    kinds, tok, _ = x_ref.shape
    for out_ref, core in ((mine_ref, core_ref[0]), (theirs_ref, 1 - core_ref[0])):
        for g in range(out_ref.shape[0]):
            cols = rows_at(2 * g + core, head_dim)
            for k in range(kinds):
                out_ref[g, k * tok:(k + 1) * tok, :] = x_ref[k, :, cols]


def lanes(x, core, head_dim):
    kinds, tok, cols = x.shape
    like = jax.ShapeDtypeStruct((cols // head_dim // 2, kinds * tok, head_dim), x.dtype)
    return pl.pallas_call(
        functools.partial(lane_kernel, head_dim),
        out_shape=(like, like),
        in_specs=[SMEM, VMEM],
        out_specs=(VMEM, VMEM),
        compiler_params=PARAMS,
    )(index_array(core), x)


def deal_kernel(place_ref, mine_ref, got_ref, *out_refs):
    quarter, core = place_ref[0] // 2, place_ref[0] % 2
    for k, out_ref in enumerate(out_refs):
        out_ref[core] = mine_ref[quarter ^ k]
        out_ref[1 - core] = got_ref[quarter ^ k]


def deal(mine, got, place):
    quarters, depth, width = mine.shape
    return pl.pallas_call(
        deal_kernel,
        out_shape=[jax.ShapeDtypeStruct((2, depth, width), mine.dtype)] * quarters,
        in_specs=[SMEM, VMEM, VMEM],
        out_specs=[VMEM] * quarters,
        compiler_params=PARAMS,
    )(place, mine, got)


def sort_kernel(place_ref, *refs):
    *in_refs, q_ref, k_ref, v_ref = refs
    tok = q_ref.shape[0] // (2 * len(in_refs))
    for i, ref in enumerate(in_refs):
        for core in range(2):
            at = rows_at((place_ref[0] // 2 ^ i) * 2 + core, tok)
            for j, out_ref in enumerate((q_ref, k_ref, v_ref)):
                out_ref[at, :] = ref[core, j * tok:(j + 1) * tok, :]


def sort(parts, place):
    both, depth, width = parts[0].shape
    count = both * len(parts) * (depth // 3)
    return pl.pallas_call(
        sort_kernel,
        out_shape=[jax.ShapeDtypeStruct((count, width), parts[0].dtype)] * 3,
        in_specs=[SMEM] + [VMEM] * len(parts),
        out_specs=[VMEM] * 3,
        compiler_params=PARAMS,
    )(place, *parts)


def join_kernel(*refs):
    *in_refs, out_ref = refs
    first = 0
    for ref in in_refs:
        out_ref[first:first + ref.shape[0], :] = ref[...]
        first += ref.shape[0]


def join(*arrays):
    depth = sum(x.shape[0] for x in arrays)
    return pl.pallas_call(
        join_kernel,
        out_shape=jax.ShapeDtypeStruct((depth, arrays[0].shape[1]), arrays[0].dtype),
        in_specs=[VMEM] * len(arrays),
        out_specs=VMEM,
        compiler_params=PARAMS,
    )(*arrays)


def cut_kernel(x_ref, q_ref, kv_ref):
    peers, depth, _ = x_ref.shape
    tok = depth // 3
    for g in range(peers):
        q_ref[g * tok:(g + 1) * tok, :] = x_ref[g, :tok, :]
        for i in range(2):
            kv_ref[(i * peers + g) * tok:(i * peers + g + 1) * tok, :] = x_ref[
                g, (i + 1) * tok:(i + 2) * tok, :
            ]


def cut(x):
    peers, depth, width = x.shape
    count = peers * depth // 3
    return pl.pallas_call(
        cut_kernel,
        out_shape=[jax.ShapeDtypeStruct((size, width), x.dtype) for size in (count, 2 * count)],
        in_specs=[VMEM],
        out_specs=[VMEM, VMEM],
        compiler_params=PARAMS,
    )(x)


def after_kernel(*refs):
    pass


def after(passed, *first, cost=None):
    return pl.pallas_call(
        after_kernel,
        out_shape=jax.ShapeDtypeStruct(passed.shape, passed.dtype),
        in_specs=[ANY] * (1 + len(first)),
        out_specs=ANY,
        input_output_aliases={0: 0},
        compiler_params=PARAMS,
        cost_estimate=cost,
    )(passed, *first)


def clip_of(token, base, span, tok_dev, clip_ref):
    frame = base + token // span * FRB + token % tok_dev // TPF
    clip = jnp.zeros_like(token)
    for f in range(clip_ref.shape[0]):
        clip = jnp.where(frame == f, clip_ref[f], clip)
    return clip


def mask_kernel(span, tok, base_ref, clip_ref, *out_refs):
    count = out_refs[0].shape[0]
    row = lax.broadcasted_iota(jnp.int32, (count, 1), 0)
    col = lax.broadcasted_iota(jnp.int32, (1, count), 1)
    row_clip = clip_of(row, base_ref[0], span, tok, clip_ref)
    for i, out_ref in enumerate(out_refs):
        allowed = row_clip == clip_of(col, base_ref[i], span, tok, clip_ref)
        out_ref[...] = jnp.where(allowed, 0.0, -1e30)


def masks(bases, span, tok, count, frame_clip):
    return pl.pallas_call(
        functools.partial(mask_kernel, span, tok),
        out_shape=[jax.ShapeDtypeStruct((count, count), jnp.float32)] * len(bases),
        in_specs=[SMEM, SMEM],
        out_specs=[VMEM] * len(bases),
        compiler_params=PARAMS,
    )(index_array(*bases), frame_clip)


def attention_kernel(head_dim, n_mask, which, joint, q_ref, *refs):
    *refs, out_ref = refs
    mask_refs, refs = refs[:n_mask], refs[n_mask:]
    count, width = q_ref.shape
    k_refs, v_refs = [], []
    for both in joint:
        ref, *refs = refs
        if both:
            k_refs.append(ref.at[0:count])
            v_refs.append(ref.at[count:2 * count])
        else:
            value_ref, *refs = refs
            k_refs.append(ref)
            v_refs.append(value_ref)
    scale = math.log2(math.e) / math.sqrt(head_dim)
    per_step = max(1, 1024 // count)
    for h in range(width // head_dim):
        cols = slice(h * head_dim, (h + 1) * head_dim)
        queries = q_ref[:, cols]
        top = total = acc = None
        for first in range(0, len(k_refs), per_step):
            here = range(first, min(first + per_step, len(k_refs)))
            scores = []
            for i in here:
                s = lax.dot_general(
                    queries, k_refs[i][:, cols], (((1,), (1,)), ((), ())),
                    preferred_element_type=jnp.float32,
                )
                scores.append(s * scale + mask_refs[which[i]][...])
            new_top = functools.reduce(
                jnp.maximum, [jnp.max(s, axis=1, keepdims=True) for s in scores]
            )
            if top is not None:
                new_top = jnp.maximum(top, new_top)
                factor = jnp.exp2(top - new_top)
                total, acc = total * factor, acc * factor
            top = new_top
            for i, s in zip(here, scores):
                p = jnp.exp2(s - top)
                part = jnp.sum(p, axis=1, keepdims=True)
                dot = jnp.dot(
                    p.astype(jnp.bfloat16), v_refs[i][:, cols], preferred_element_type=jnp.float32
                )
                total = part if total is None else total + part
                acc = dot if acc is None else acc + dot
        out_ref[:, cols] = (acc / total).astype(out_ref.dtype)


def attention(q, kvs, mask_of, which, head_dim):
    joint = [not isinstance(kv, tuple) for kv in kvs]
    arrays = [x for kv, both in zip(kvs, joint) for x in ((kv,) if both else kv)]
    return pl.pallas_call(
        functools.partial(attention_kernel, head_dim, len(mask_of), which, joint),
        out_shape=jax.ShapeDtypeStruct(q.shape, q.dtype),
        in_specs=[VMEM] * (1 + len(mask_of) + len(arrays)),
        out_specs=VMEM,
        compiler_params=PARAMS,
    )(q, *mask_of, *arrays)


def project_kernel(n_attn, sizes, at_ref, place_ref, *refs):
    attn_refs, w_refs = refs[:n_attn], refs[n_attn:-4]
    mine_ref, theirs_ref, a_ref, w_all = refs[-4:]
    width = attn_refs[0].shape[1]
    blks, tok, cols = mine_ref.shape
    blk, core = place_ref[0] // 2, place_ref[0] % 2
    for k, ref in enumerate(attn_refs):
        a_ref[:, rows_at(blk ^ k, width)] = ref[...]
    for i, (ref, rows) in enumerate(zip(w_refs, sizes)):
        at = rows_at(at_ref[i], rows)
        if ref.shape[1] >= cols:
            w_all[at, :] = ref[:, rows_at(blk, cols)] if ref.shape[1] > cols else ref[...]
        else:
            first = ref.shape[0] - cols // LANES * rows
            for j in range(cols // LANES):
                w_all[at, j * LANES:(j + 1) * LANES] = ref[first + j * rows:first + (j + 1) * rows]
    result = jnp.dot(a_ref[...], w_all[...], preferred_element_type=jnp.float32)
    result = result.astype(mine_ref.dtype).reshape(blks, 2, tok, cols)

    @pl.when(core == 0)
    def _():
        mine_ref[...] = result[:, 0]
        theirs_ref[...] = result[:, 1]

    @pl.when(core != 0)
    def _():
        mine_ref[...] = result[:, 1]
        theirs_ref[...] = result[:, 0]


def project(attns, w_parts, sizes, at, place, tok, cols):
    count, width = attns[0].shape
    blks = len(attns)
    like = jax.ShapeDtypeStruct((blks, tok, cols), attns[0].dtype)
    return pl.pallas_call(
        functools.partial(project_kernel, blks, sizes),
        out_shape=(like, like),
        in_specs=[SMEM, SMEM] + [VMEM] * (blks + len(w_parts)),
        out_specs=(VMEM, VMEM),
        scratch_shapes=[
            pltpu.VMEM((count, blks * width), attns[0].dtype),
            pltpu.VMEM((blks * width, cols), attns[0].dtype),
        ],
        compiler_params=PARAMS,
    )(index_array(*at), place, *attns, *w_parts)


def add_kernel(place_ref, x_ref, y_ref, *out_refs):
    for k, out_ref in enumerate(out_refs):
        at = place_ref[0] // 2 ^ k
        both = x_ref[at].astype(jnp.float32) + y_ref[at].astype(jnp.float32)
        out_ref[...] = both.astype(out_ref.dtype)


def add(x, y, place):
    blks = x.shape[0]
    return pl.pallas_call(
        add_kernel,
        out_shape=[jax.ShapeDtypeStruct(x.shape[1:], x.dtype)] * blks,
        in_specs=[SMEM, VMEM, VMEM],
        out_specs=[VMEM] * blks,
        compiler_params=PARAMS,
    )(place, x, y)


def unpack_kernel(place_ref, *refs):
    *in_refs, out_ref = refs
    width = in_refs[0].shape[1]
    for k, ref in enumerate(in_refs):
        out_ref[:, rows_at(place_ref[0] // 2 ^ k, width)] = ref[...]


def unpack(parts, place):
    tok, width = parts[0].shape
    return pl.pallas_call(
        unpack_kernel,
        out_shape=jax.ShapeDtypeStruct((tok, len(parts) * width), parts[0].dtype),
        in_specs=[SMEM] + [VMEM] * len(parts),
        out_specs=VMEM,
        compiler_params=PARAMS,
    )(place, *parts)


def xor(x, axis, by):
    size = math.prod(lax.axis_size(name) for name in axis)
    return lax.ppermute(x, axis, [(i, i ^ by) for i in range(size)])


def swap_all(parts, axis):
    return [parts[0]] + [xor(parts[m], axis, m) for m in range(1, len(parts))]


def squares(qkv, frame_clip, w_out):
    quarter = ("x", "zl")
    y, x, zh, zl, core = (lax.axis_index(n) for n in ("y", "x", "zh", "zl", "core"))
    tok, head_dim, cols = qkv.shape[1], w_out.shape[0], w_out.shape[1] // 4
    place = index_array((x * 2 + zl) * 2 + core)
    mine, theirs = x * 2 + zl, x * 2 + 1 - zl
    row, half = zh * 2 + zl, head_dim // 2

    w_far, w_first, w_second, w_near = pieces(w_out, y, mine, theirs, cols)
    far = after(xor(w_far, ("zh",), 1), cost=AHEAD)
    kept, given = lanes(qkv, core, head_dim)
    shared = swap_all(deal(kept, xor(given, ("core",), 1), place), quarter)
    corner_first = after(xor(after(w_first, shared[1]), ("zh", "zl"), 3), cost=AHEAD)
    q, k, v = sort(shared, place)
    k_far, v_far = xor(k, ("zh",), 1), xor(v, ("zh",), 1)
    near = xor(join(k, v, after(far, corner_first)), ("y",), 1)
    corner_second = xor(after(w_second, k), ("zh", "zl"), 3)
    w_next = xor(after(w_near, k), ("zl",), 1)
    kvs = [(k, v), (k_far, v_far), near, (xor(k_far, ("y",), 1), xor(v_far, ("y",), 1))]

    bases = [y * 2 * FRB, (1 - y) * 2 * FRB]
    mask_of = masks(bases, 4 * tok, tok, 8 * tok, frame_clip)
    attn = attention(q, kvs, mask_of, [0, 0, 1, 1], head_dim)
    corner = join(corner_first, after(corner_second, attn))
    corner_rest = xor(corner, ("y",), 1)
    attns = swap_all([attn] * 4, quarter)
    w_parts = [w_out, w_next, far, near, corner, corner_rest]
    sizes = [head_dim, head_dim, half, half, half, half]
    at = [row, row ^ 1] + [2 * (row ^ by) + h for by in (2, 3) for h in (y, 1 - y)]
    ours, other_core = project(attns, w_parts, sizes, at, place, tok, cols)
    parts = add(ours, xor(other_core, ("core",), 1), place)
    return unpack(swap_all(parts, quarter), place)


def layers(qkv, frame_clip, w_out):
    rows, blks = lax.axis_size("row"), lax.axis_size("blk")
    row, blk = lax.axis_index("row"), lax.axis_index("blk")
    tok, head_dim, cols = qkv.shape[1], w_out.shape[0], w_out.shape[1] // blks
    place = index_array(blk * 2 + lax.axis_index("core"))
    others = range(1, rows)

    (w_own,) = columns(w_out, [(head_dim, 0, blk)], cols)
    w_parts = [w_out] + [xor(w_own, ("row",), by) for by in others]
    packed = pack(qkv, 2 * blks, head_dim)
    own = lax.all_to_all(packed, ("blk", "core"), split_axis=0, concat_axis=0, tiled=True)
    q, kv = cut(own)
    kvs = [kv] + [xor(kv, ("row",), by) for by in others]
    mask_of = masks([0], 2 * tok, tok, 2 * blks * tok, frame_clip)
    attn = attention(q, kvs, mask_of, [0] * rows, head_dim)
    attns = swap_all([attn] * blks, ("blk",))
    at = [row ^ by for by in range(rows)]
    ours, other_core = project(attns, w_parts, [head_dim] * rows, at, place, tok, cols)
    parts = add(ours, xor(other_core, ("core",), 1), place)
    return unpack(swap_all(parts, ("blk",)), place)


def solution(mesh):
    blk, tile = mesh.shape["blk"], mesh.shape["tile"]
    if (blk, tile) == (4, 8):
        plan, names, shape = squares, ("y", "x", "zh", "zl", "core"), (2, 2, 2, 2, 2)
    else:
        plan, names, shape = layers, ("blk", "row", "core"), (blk, tile // 2, 2)
    fine = Mesh(mesh.devices.reshape(shape), names)
    tiles = names[2:] if plan is squares else names[1:]
    in_specs = (P(None, names, None), P(), P(tiles, None))
    return jax.shard_map(
        plan, mesh=fine, in_specs=in_specs, out_specs=P(names, None), check_vma=False
    )
```

```python
import functools
import math

import jax
import jax.numpy as jnp
from jax import lax
from jax.experimental import pallas as pl
from jax.experimental.pallas import tpu as pltpu
from jax.sharding import Mesh
from jax.sharding import PartitionSpec as P

FRB = 2
TPF = 16
LANES = 128
VMEM = pl.BlockSpec(memory_space=pltpu.VMEM)
SMEM = pl.BlockSpec(memory_space=pltpu.SMEM)
ANY = pl.BlockSpec(memory_space=pl.ANY)
PARAMS = pltpu.CompilerParams(vmem_limit_bytes=48 * 1024 * 1024)
AHEAD = pl.CostEstimate(flops=20_000_000_000, bytes_accessed=1_000_000, transcendentals=0)
SOON = pl.CostEstimate(flops=6_000_000_000, bytes_accessed=1_000_000, transcendentals=0)


def rows_at(index, size):
    return pl.ds(pl.multiple_of(index * size, size), size)


def index_array(*numbers):
    return jnp.stack([jnp.asarray(i, jnp.int32) for i in numbers])


def pack_kernel(head_dim, x_ref, out_ref):
    peers, _, width = out_ref.shape
    kinds, tok, _ = x_ref.shape
    heads = width // head_dim
    for g in range(peers):
        for i in range(heads):
            head = (g // 2 * heads + i) * 2 + g % 2
            for k in range(kinds):
                out_ref[g, k * tok:(k + 1) * tok, i * head_dim:(i + 1) * head_dim] = x_ref[
                    k, :, head * head_dim:(head + 1) * head_dim
                ]


def pack(x, peers, head_dim):
    kinds, tok, cols = x.shape
    return pl.pallas_call(
        functools.partial(pack_kernel, head_dim),
        out_shape=jax.ShapeDtypeStruct((peers, kinds * tok, cols // peers), x.dtype),
        in_specs=[VMEM],
        out_specs=VMEM,
        compiler_params=PARAMS,
    )(x)


def columns_kernel(at_ref, x_ref, *refs):
    *out_refs, sems = refs
    copies = []
    for i, ref in enumerate(out_refs):
        depth, cols = ref.shape
        piece = x_ref.at[rows_at(at_ref[2 * i], depth), rows_at(at_ref[2 * i + 1], cols)]
        copies.append(pltpu.make_async_copy(piece, ref, sems.at[i]))
    for copy in copies:
        copy.start()
    for copy in copies:
        copy.wait()


def columns(x, pieces, cols):
    return pl.pallas_call(
        columns_kernel,
        out_shape=[jax.ShapeDtypeStruct((piece[0], cols), x.dtype) for piece in pieces],
        in_specs=[SMEM, pl.BlockSpec(memory_space=pltpu.HBM)],
        out_specs=[VMEM] * len(pieces),
        scratch_shapes=[pltpu.SemaphoreType.DMA((len(pieces),))],
        compiler_params=PARAMS,
    )(
        index_array(*[i for piece in pieces for i in piece[1:]]),
        pltpu.with_memory_space_constraint(x, pltpu.HBM),
    )


def blocks_kernel(row_axis, col_axes, x_ref, out_ref, held, sem):
    depth, cols = held.shape
    col = 0
    for axis in col_axes:
        col = col * lax.axis_size(axis) + lax.axis_index(axis)
    piece = x_ref.at[rows_at(lax.axis_index(row_axis), depth), rows_at(col, cols)]
    copy = pltpu.make_async_copy(piece, held, sem)
    copy.start()
    copy.wait()
    for j in range(cols // LANES):
        out_ref[j * depth:(j + 1) * depth, :] = held[:, j * LANES:(j + 1) * LANES]


def blocks(x, depth, cols, row_axis, col_axes):
    return pl.pallas_call(
        functools.partial(blocks_kernel, row_axis, col_axes),
        out_shape=jax.ShapeDtypeStruct((cols // LANES * depth, LANES), x.dtype),
        in_specs=[pl.BlockSpec(memory_space=pltpu.HBM)],
        out_specs=VMEM,
        scratch_shapes=[pltpu.VMEM((depth, cols), x.dtype), pltpu.SemaphoreType.DMA],
        compiler_params=PARAMS,
    )(pltpu.with_memory_space_constraint(x, pltpu.HBM))


def pieces_kernel(at_ref, x_ref, corner_ref, near_ref):
    half, cols = corner_ref.shape
    corner_ref[...] = x_ref[rows_at(at_ref[0], half), rows_at(at_ref[1], cols)]
    near_ref[...] = x_ref[:, rows_at(at_ref[1], cols)]


def pieces(x, half, at, cols):
    depth = x.shape[0]
    return pl.pallas_call(
        pieces_kernel,
        out_shape=[jax.ShapeDtypeStruct((rows, cols), x.dtype) for rows in (depth // 2, depth)],
        in_specs=[SMEM, VMEM],
        out_specs=[VMEM, VMEM],
        compiler_params=PARAMS,
    )(index_array(half, at), x)


def lane_kernel(head_dim, core_ref, x_ref, mine_ref, theirs_ref):
    kinds, tok, _ = x_ref.shape
    for out_ref, core in ((mine_ref, core_ref[0]), (theirs_ref, 1 - core_ref[0])):
        for g in range(out_ref.shape[0]):
            cols = rows_at(2 * g + core, head_dim)
            for k in range(kinds):
                out_ref[g, k * tok:(k + 1) * tok, :] = x_ref[k, :, cols]


def lanes(x, core, head_dim):
    kinds, tok, cols = x.shape
    like = jax.ShapeDtypeStruct((cols // head_dim // 2, kinds * tok, head_dim), x.dtype)
    return pl.pallas_call(
        functools.partial(lane_kernel, head_dim),
        out_shape=(like, like),
        in_specs=[SMEM, VMEM],
        out_specs=(VMEM, VMEM),
        compiler_params=PARAMS,
    )(index_array(core), x)


def deal_kernel(place_ref, mine_ref, got_ref, *out_refs):
    quarter, core = place_ref[0] // 2, place_ref[0] % 2
    for k, out_ref in enumerate(out_refs):
        out_ref[core] = mine_ref[quarter ^ k]
        out_ref[1 - core] = got_ref[quarter ^ k]


def deal(mine, got, place):
    quarters, depth, width = mine.shape
    return pl.pallas_call(
        deal_kernel,
        out_shape=[jax.ShapeDtypeStruct((2, depth, width), mine.dtype)] * quarters,
        in_specs=[SMEM, VMEM, VMEM],
        out_specs=[VMEM] * quarters,
        compiler_params=PARAMS,
    )(place, mine, got)


def sort_kernel(place_ref, *refs):
    *in_refs, q_ref, k_ref, v_ref = refs
    tok = q_ref.shape[0] // (2 * len(in_refs))
    for i, ref in enumerate(in_refs):
        for core in range(2):
            at = rows_at((place_ref[0] // 2 ^ i) * 2 + core, tok)
            for j, out_ref in enumerate((q_ref, k_ref, v_ref)):
                out_ref[at, :] = ref[core, j * tok:(j + 1) * tok, :]


def sort(parts, place):
    both, depth, width = parts[0].shape
    count = both * len(parts) * (depth // 3)
    return pl.pallas_call(
        sort_kernel,
        out_shape=[jax.ShapeDtypeStruct((count, width), parts[0].dtype)] * 3,
        in_specs=[SMEM] + [VMEM] * len(parts),
        out_specs=[VMEM] * 3,
        compiler_params=PARAMS,
    )(place, *parts)


def join_kernel(*refs):
    *in_refs, out_ref = refs
    first = 0
    for ref in in_refs:
        out_ref[first:first + ref.shape[0], :] = ref[...]
        first += ref.shape[0]


def join(*arrays):
    depth = sum(x.shape[0] for x in arrays)
    return pl.pallas_call(
        join_kernel,
        out_shape=jax.ShapeDtypeStruct((depth, arrays[0].shape[1]), arrays[0].dtype),
        in_specs=[VMEM] * len(arrays),
        out_specs=VMEM,
        compiler_params=PARAMS,
    )(*arrays)


def cut_kernel(x_ref, q_ref, kv_ref):
    peers, depth, _ = x_ref.shape
    tok = depth // 3
    for g in range(peers):
        q_ref[g * tok:(g + 1) * tok, :] = x_ref[g, :tok, :]
        for i in range(2):
            kv_ref[(i * peers + g) * tok:(i * peers + g + 1) * tok, :] = x_ref[
                g, (i + 1) * tok:(i + 2) * tok, :
            ]


def cut(x):
    peers, depth, width = x.shape
    count = peers * depth // 3
    return pl.pallas_call(
        cut_kernel,
        out_shape=[jax.ShapeDtypeStruct((size, width), x.dtype) for size in (count, 2 * count)],
        in_specs=[VMEM],
        out_specs=[VMEM, VMEM],
        compiler_params=PARAMS,
    )(x)


def after_kernel(*refs):
    pass


def after(passed, *first, cost=None):
    return pl.pallas_call(
        after_kernel,
        out_shape=jax.ShapeDtypeStruct(passed.shape, passed.dtype),
        in_specs=[ANY] * (1 + len(first)),
        out_specs=ANY,
        input_output_aliases={0: 0},
        compiler_params=PARAMS,
        cost_estimate=cost,
    )(passed, *first)


def clip_of(token, base, span, tok_dev, clip_ref):
    frame = base + token // span * FRB + token % tok_dev // TPF
    clip = jnp.zeros_like(token)
    for f in range(clip_ref.shape[0]):
        clip = jnp.where(frame == f, clip_ref[f], clip)
    return clip


def mask_kernel(span, tok, base_ref, clip_ref, *out_refs):
    count = out_refs[0].shape[0]
    row = lax.broadcasted_iota(jnp.int32, (count, 1), 0)
    col = lax.broadcasted_iota(jnp.int32, (1, count), 1)
    row_clip = clip_of(row, base_ref[0], span, tok, clip_ref)
    for i, out_ref in enumerate(out_refs):
        allowed = row_clip == clip_of(col, base_ref[i], span, tok, clip_ref)
        out_ref[...] = jnp.where(allowed, 0.0, -1e30)


def masks(bases, span, tok, count, frame_clip):
    return pl.pallas_call(
        functools.partial(mask_kernel, span, tok),
        out_shape=[jax.ShapeDtypeStruct((count, count), jnp.float32)] * len(bases),
        in_specs=[SMEM, SMEM],
        out_specs=[VMEM] * len(bases),
        compiler_params=PARAMS,
    )(index_array(*bases), frame_clip)


def attention_kernel(head_dim, n_mask, which, joint, q_ref, *refs):
    *refs, out_ref = refs
    mask_refs, refs = refs[:n_mask], refs[n_mask:]
    count, width = q_ref.shape
    k_refs, v_refs = [], []
    for both in joint:
        ref, *refs = refs
        if both:
            k_refs.append(ref.at[0:count])
            v_refs.append(ref.at[count:2 * count])
        else:
            value_ref, *refs = refs
            k_refs.append(ref)
            v_refs.append(value_ref)
    scale = math.log2(math.e) / math.sqrt(head_dim)
    per_step = max(1, 1024 // count)
    for h in range(width // head_dim):
        cols = slice(h * head_dim, (h + 1) * head_dim)
        queries = q_ref[:, cols]
        top = total = acc = None
        for first in range(0, len(k_refs), per_step):
            here = range(first, min(first + per_step, len(k_refs)))
            scores = []
            for i in here:
                s = lax.dot_general(
                    queries, k_refs[i][:, cols], (((1,), (1,)), ((), ())),
                    preferred_element_type=jnp.float32,
                )
                scores.append(s * scale + mask_refs[which[i]][...])
            new_top = functools.reduce(
                jnp.maximum, [jnp.max(s, axis=1, keepdims=True) for s in scores]
            )
            if top is not None:
                new_top = jnp.maximum(top, new_top)
                factor = jnp.exp2(top - new_top)
                total, acc = total * factor, acc * factor
            top = new_top
            for i, s in zip(here, scores):
                p = jnp.exp2(s - top)
                part = jnp.sum(p, axis=1, keepdims=True)
                dot = jnp.dot(
                    p.astype(jnp.bfloat16), v_refs[i][:, cols], preferred_element_type=jnp.float32
                )
                total = part if total is None else total + part
                acc = dot if acc is None else acc + dot
        out_ref[:, cols] = (acc / total).astype(out_ref.dtype)


def attention(q, kvs, mask_of, which, head_dim):
    joint = [not isinstance(kv, tuple) for kv in kvs]
    arrays = [x for kv, both in zip(kvs, joint) for x in ((kv,) if both else kv)]
    return pl.pallas_call(
        functools.partial(attention_kernel, head_dim, len(mask_of), which, joint),
        out_shape=jax.ShapeDtypeStruct(q.shape, q.dtype),
        in_specs=[VMEM] * (1 + len(mask_of) + len(arrays)),
        out_specs=VMEM,
        compiler_params=PARAMS,
    )(q, *mask_of, *arrays)


def project_kernel(n_attn, sizes, at_ref, place_ref, *refs):
    attn_refs, w_refs = refs[:n_attn], refs[n_attn:-3]
    out_ref, a_ref, w_all = refs[-3:]
    width = attn_refs[0].shape[1]
    blks, tok, cols = out_ref.shape
    blk, other = place_ref[0] // 2, 1 - place_ref[0] % 2
    for k, ref in enumerate(attn_refs):
        at = rows_at(blk ^ k, width)
        for b in range(blks):
            a_ref[b * tok:(b + 1) * tok, at] = ref[rows_at(2 * b + other, tok), :]
            a_ref[(blks + b) * tok:(blks + b + 1) * tok, at] = ref[rows_at(2 * b + 1 - other, tok), :]
    for i, (ref, rows) in enumerate(zip(w_refs, sizes)):
        at = rows_at(at_ref[i], rows)
        if ref.shape[1] >= cols:
            w_all[at, :] = ref[:, rows_at(blk, cols)] if ref.shape[1] > cols else ref[...]
        else:
            first = ref.shape[0] - cols // LANES * rows
            for j in range(cols // LANES):
                w_all[at, j * LANES:(j + 1) * LANES] = ref[first + j * rows:first + (j + 1) * rows]
    dot = jnp.dot(a_ref[:blks * tok, :], w_all[...], preferred_element_type=jnp.float32)
    out_ref[...] = dot.astype(out_ref.dtype).reshape(out_ref.shape)


def rest_kernel(a_ref, w_ref, out_ref):
    blks, tok, _ = out_ref.shape
    dot = jnp.dot(a_ref[blks * tok:, :], w_ref[...], preferred_element_type=jnp.float32)
    out_ref[...] = dot.astype(out_ref.dtype).reshape(out_ref.shape)


def project(attns, w_parts, sizes, at, place, tok, cols):
    count, width = attns[0].shape
    blks, dtype = len(attns), attns[0].dtype
    like = jax.ShapeDtypeStruct((blks, tok, cols), dtype)
    theirs, a_all, w_all = pl.pallas_call(
        functools.partial(project_kernel, blks, sizes),
        out_shape=(
            like,
            jax.ShapeDtypeStruct((count, blks * width), dtype),
            jax.ShapeDtypeStruct((blks * width, cols), dtype),
        ),
        in_specs=[SMEM, SMEM] + [VMEM] * (blks + len(w_parts)),
        out_specs=(VMEM, VMEM, VMEM),
        compiler_params=PARAMS,
    )(index_array(*at), place, *attns, *w_parts)
    got = xor(theirs, ("core",), 1)
    ours = pl.pallas_call(
        rest_kernel,
        out_shape=like,
        in_specs=[VMEM, VMEM],
        out_specs=VMEM,
        compiler_params=PARAMS,
    )(a_all, w_all)
    return add(ours, got, place)


def add_kernel(place_ref, x_ref, y_ref, *out_refs):
    for k, out_ref in enumerate(out_refs):
        at = place_ref[0] // 2 ^ k
        both = x_ref[at].astype(jnp.float32) + y_ref[at].astype(jnp.float32)
        out_ref[...] = both.astype(out_ref.dtype)


def add(x, y, place):
    blks = x.shape[0]
    return pl.pallas_call(
        add_kernel,
        out_shape=[jax.ShapeDtypeStruct(x.shape[1:], x.dtype)] * blks,
        in_specs=[SMEM, VMEM, VMEM],
        out_specs=[VMEM] * blks,
        compiler_params=PARAMS,
    )(place, x, y)


def unpack_kernel(place_ref, *refs):
    *in_refs, out_ref = refs
    width = in_refs[0].shape[1]
    for k, ref in enumerate(in_refs):
        out_ref[:, rows_at(place_ref[0] // 2 ^ k, width)] = ref[...]


def unpack(parts, place):
    tok, width = parts[0].shape
    return pl.pallas_call(
        unpack_kernel,
        out_shape=jax.ShapeDtypeStruct((tok, len(parts) * width), parts[0].dtype),
        in_specs=[SMEM] + [VMEM] * len(parts),
        out_specs=VMEM,
        compiler_params=PARAMS,
    )(place, *parts)


def xor(x, axis, by):
    size = math.prod(lax.axis_size(name) for name in axis)
    return lax.ppermute(x, axis, [(i, i ^ by) for i in range(size)])


def swap_all(parts, axis):
    return [parts[0]] + [xor(parts[m], axis, m) for m in range(1, len(parts))]


def squares(qkv, frame_clip, w_out):
    quarter = ("x", "zl")
    y, x, zh, zl, core = (lax.axis_index(n) for n in ("y", "x", "zh", "zl", "core"))
    tok, head_dim, cols = qkv.shape[1], w_out.shape[0], w_out.shape[1] // 4
    place = index_array((x * 2 + zl) * 2 + core)
    theirs = x * 2 + 1 - zl
    row, half = zh * 2 + zl, head_dim // 2

    w_far = blocks(w_out, half, cols, "y", quarter)
    far = after(xor(w_far, ("zh",), 1), cost=AHEAD)
    w_corner, w_near = pieces(w_out, y, theirs, cols)
    kept, given = lanes(qkv, core, head_dim)
    shared = swap_all(deal(kept, xor(given, ("core",), 1), place), quarter)
    q, k, v = sort(shared, place)
    k_far, v_far = xor(k, ("zh",), 1), xor(v, ("zh",), 1)
    near = xor(join(k, v, far), ("y",), 1)
    corner = xor(after(w_corner, k), ("zh", "zl"), 3)
    w_next = xor(after(w_near, k), ("zl",), 1)
    kvs = [(k, v), (k_far, v_far), near, (xor(k_far, ("y",), 1), xor(v_far, ("y",), 1))]

    bases = [y * 2 * FRB, (1 - y) * 2 * FRB]
    mask_of = masks(bases, 4 * tok, tok, 8 * tok, frame_clip)
    attn = attention(q, kvs, mask_of, [0, 0, 1, 1], head_dim)
    corner = after(corner, attn)
    corner_rest = xor(corner, ("y",), 1)
    attns = swap_all([attn] * 4, quarter)
    w_parts = [w_out, w_next, far, near, corner, corner_rest]
    sizes = [head_dim, head_dim, half, half, half, half]
    at = [row, row ^ 1] + [2 * (row ^ by) + h for by in (2, 3) for h in (y, 1 - y)]
    parts = project(attns, w_parts, sizes, at, place, tok, cols)
    return unpack(swap_all(parts, quarter), place)


def layers(qkv, frame_clip, w_out):
    rows, blks = lax.axis_size("row"), lax.axis_size("blk")
    row, blk = lax.axis_index("row"), lax.axis_index("blk")
    tok, head_dim, cols = qkv.shape[1], w_out.shape[0], w_out.shape[1] // blks
    place = index_array(blk * 2 + lax.axis_index("core"))
    others = range(1, rows)

    (w_own,) = columns(w_out, [(head_dim, 0, blk)], cols)
    w_parts = [w_out] + [xor(w_own, ("row",), by) for by in others]
    packed = pack(qkv, 2 * blks, head_dim)
    own = lax.all_to_all(packed, ("blk", "core"), split_axis=0, concat_axis=0, tiled=True)
    q, kv = cut(own)
    kvs = [kv] + [xor(kv, ("row",), by) for by in others]
    mask_of = masks([0], 2 * tok, tok, 2 * blks * tok, frame_clip)
    attn = attention(q, kvs, mask_of, [0] * rows, head_dim)
    attns = swap_all([attn] * blks, ("blk",))
    at = [row ^ by for by in range(rows)]
    parts = project(attns, w_parts, [head_dim] * rows, at, place, tok, cols)
    return unpack(swap_all(parts, ("blk",)), place)


def solution(mesh):
    blk, tile = mesh.shape["blk"], mesh.shape["tile"]
    if (blk, tile) == (4, 8):
        plan, names, shape = squares, ("y", "x", "zh", "zl", "core"), (2, 2, 2, 2, 2)
    else:
        plan, names, shape = layers, ("blk", "row", "core"), (blk, tile // 2, 2)
    fine = Mesh(mesh.devices.reshape(shape), names)
    tiles = names[2:] if plan is squares else names[1:]
    in_specs = (P(None, names, None), P(), P(tiles, None))
    return jax.shard_map(
        plan, mesh=fine, in_specs=in_specs, out_specs=P(names, None), check_vma=False
    )
```

```python
import functools
import math

import jax
import jax.numpy as jnp
from jax import lax
from jax.experimental import pallas as pl
from jax.experimental.pallas import tpu as pltpu
from jax.sharding import Mesh
from jax.sharding import PartitionSpec as P

FRB = 2
TPF = 16
LANES = 128
VMEM = pl.BlockSpec(memory_space=pltpu.VMEM)
SMEM = pl.BlockSpec(memory_space=pltpu.SMEM)
ANY = pl.BlockSpec(memory_space=pl.ANY)
PARAMS = pltpu.CompilerParams(vmem_limit_bytes=48 * 1024 * 1024)
AHEAD = pl.CostEstimate(flops=20_000_000_000, bytes_accessed=1_000_000, transcendentals=0)
SOON = pl.CostEstimate(flops=6_000_000_000, bytes_accessed=1_000_000, transcendentals=0)


def rows_at(index, size):
    return pl.ds(pl.multiple_of(index * size, size), size)


def index_array(*numbers):
    return jnp.stack([jnp.asarray(i, jnp.int32) for i in numbers])


def pack_kernel(head_dim, x_ref, out_ref):
    peers, _, width = out_ref.shape
    kinds, tok, _ = x_ref.shape
    heads = width // head_dim
    for g in range(peers):
        for i in range(heads):
            head = (g // 2 * heads + i) * 2 + g % 2
            for k in range(kinds):
                out_ref[g, k * tok:(k + 1) * tok, i * head_dim:(i + 1) * head_dim] = x_ref[
                    k, :, head * head_dim:(head + 1) * head_dim
                ]


def pack(x, peers, head_dim):
    kinds, tok, cols = x.shape
    return pl.pallas_call(
        functools.partial(pack_kernel, head_dim),
        out_shape=jax.ShapeDtypeStruct((peers, kinds * tok, cols // peers), x.dtype),
        in_specs=[VMEM],
        out_specs=VMEM,
        compiler_params=PARAMS,
    )(x)


def columns_kernel(at_ref, x_ref, *refs):
    *out_refs, sems = refs
    copies = []
    for i, ref in enumerate(out_refs):
        depth, cols = ref.shape
        piece = x_ref.at[rows_at(at_ref[2 * i], depth), rows_at(at_ref[2 * i + 1], cols)]
        copies.append(pltpu.make_async_copy(piece, ref, sems.at[i]))
    for copy in copies:
        copy.start()
    for copy in copies:
        copy.wait()


def columns(x, pieces, cols):
    return pl.pallas_call(
        columns_kernel,
        out_shape=[jax.ShapeDtypeStruct((piece[0], cols), x.dtype) for piece in pieces],
        in_specs=[SMEM, pl.BlockSpec(memory_space=pltpu.HBM)],
        out_specs=[VMEM] * len(pieces),
        scratch_shapes=[pltpu.SemaphoreType.DMA((len(pieces),))],
        compiler_params=PARAMS,
    )(
        index_array(*[i for piece in pieces for i in piece[1:]]),
        pltpu.with_memory_space_constraint(x, pltpu.HBM),
    )


def blocks_kernel(row_axis, col_axes, x_ref, out_ref, held, sem):
    depth, cols = held.shape
    col = 0
    for axis in col_axes:
        col = col * lax.axis_size(axis) + lax.axis_index(axis)
    piece = x_ref.at[rows_at(lax.axis_index(row_axis), depth), rows_at(col, cols)]
    copy = pltpu.make_async_copy(piece, held, sem)
    copy.start()
    copy.wait()
    for j in range(cols // LANES):
        out_ref[j * depth:(j + 1) * depth, :] = held[:, j * LANES:(j + 1) * LANES]


def blocks(x, depth, cols, row_axis, col_axes):
    return pl.pallas_call(
        functools.partial(blocks_kernel, row_axis, col_axes),
        out_shape=jax.ShapeDtypeStruct((cols // LANES * depth, LANES), x.dtype),
        in_specs=[pl.BlockSpec(memory_space=pltpu.HBM)],
        out_specs=VMEM,
        scratch_shapes=[pltpu.VMEM((depth, cols), x.dtype), pltpu.SemaphoreType.DMA],
        compiler_params=PARAMS,
    )(pltpu.with_memory_space_constraint(x, pltpu.HBM))


def pieces_kernel(at_ref, x_ref, corner_ref, near_ref):
    half, cols = corner_ref.shape
    corner_ref[...] = x_ref[rows_at(at_ref[0], half), rows_at(at_ref[1], cols)]
    near_ref[...] = x_ref[:, rows_at(at_ref[1], cols)]


def pieces(x, half, at, cols):
    depth = x.shape[0]
    return pl.pallas_call(
        pieces_kernel,
        out_shape=[jax.ShapeDtypeStruct((rows, cols), x.dtype) for rows in (depth // 2, depth)],
        in_specs=[SMEM, VMEM],
        out_specs=[VMEM, VMEM],
        compiler_params=PARAMS,
    )(index_array(half, at), x)


def lane_kernel(head_dim, core_ref, x_ref, mine_ref, theirs_ref):
    kinds, tok, _ = x_ref.shape
    for out_ref, core in ((mine_ref, core_ref[0]), (theirs_ref, 1 - core_ref[0])):
        for g in range(out_ref.shape[0]):
            cols = rows_at(2 * g + core, head_dim)
            for k in range(kinds):
                out_ref[g, k * tok:(k + 1) * tok, :] = x_ref[k, :, cols]


def lanes(x, core, head_dim):
    kinds, tok, cols = x.shape
    like = jax.ShapeDtypeStruct((cols // head_dim // 2, kinds * tok, head_dim), x.dtype)
    return pl.pallas_call(
        functools.partial(lane_kernel, head_dim),
        out_shape=(like, like),
        in_specs=[SMEM, VMEM],
        out_specs=(VMEM, VMEM),
        compiler_params=PARAMS,
    )(index_array(core), x)


def deal_kernel(place_ref, mine_ref, got_ref, *out_refs):
    quarter, core = place_ref[0] // 2, place_ref[0] % 2
    for k, out_ref in enumerate(out_refs):
        out_ref[core] = mine_ref[quarter ^ k]
        out_ref[1 - core] = got_ref[quarter ^ k]


def deal(mine, got, place):
    quarters, depth, width = mine.shape
    return pl.pallas_call(
        deal_kernel,
        out_shape=[jax.ShapeDtypeStruct((2, depth, width), mine.dtype)] * quarters,
        in_specs=[SMEM, VMEM, VMEM],
        out_specs=[VMEM] * quarters,
        compiler_params=PARAMS,
    )(place, mine, got)


def sort_kernel(place_ref, *refs):
    *in_refs, q_ref, k_ref, v_ref = refs
    tok = q_ref.shape[0] // (2 * len(in_refs))
    for i, ref in enumerate(in_refs):
        for core in range(2):
            at = rows_at((place_ref[0] // 2 ^ i) * 2 + core, tok)
            for j, out_ref in enumerate((q_ref, k_ref, v_ref)):
                out_ref[at, :] = ref[core, j * tok:(j + 1) * tok, :]


def sort(parts, place):
    both, depth, width = parts[0].shape
    count = both * len(parts) * (depth // 3)
    return pl.pallas_call(
        sort_kernel,
        out_shape=[jax.ShapeDtypeStruct((count, width), parts[0].dtype)] * 3,
        in_specs=[SMEM] + [VMEM] * len(parts),
        out_specs=[VMEM] * 3,
        compiler_params=PARAMS,
    )(place, *parts)


def join_kernel(*refs):
    *in_refs, out_ref = refs
    first = 0
    for ref in in_refs:
        out_ref[first:first + ref.shape[0], :] = ref[...]
        first += ref.shape[0]


def join(*arrays):
    depth = sum(x.shape[0] for x in arrays)
    return pl.pallas_call(
        join_kernel,
        out_shape=jax.ShapeDtypeStruct((depth, arrays[0].shape[1]), arrays[0].dtype),
        in_specs=[VMEM] * len(arrays),
        out_specs=VMEM,
        compiler_params=PARAMS,
    )(*arrays)


def cut_kernel(x_ref, q_ref, kv_ref):
    peers, depth, _ = x_ref.shape
    tok = depth // 3
    for g in range(peers):
        q_ref[g * tok:(g + 1) * tok, :] = x_ref[g, :tok, :]
        for i in range(2):
            kv_ref[(i * peers + g) * tok:(i * peers + g + 1) * tok, :] = x_ref[
                g, (i + 1) * tok:(i + 2) * tok, :
            ]


def cut(x):
    peers, depth, width = x.shape
    count = peers * depth // 3
    return pl.pallas_call(
        cut_kernel,
        out_shape=[jax.ShapeDtypeStruct((size, width), x.dtype) for size in (count, 2 * count)],
        in_specs=[VMEM],
        out_specs=[VMEM, VMEM],
        compiler_params=PARAMS,
    )(x)


def after_kernel(*refs):
    pass


def after(passed, *first, cost=None):
    return pl.pallas_call(
        after_kernel,
        out_shape=jax.ShapeDtypeStruct(passed.shape, passed.dtype),
        in_specs=[ANY] * (1 + len(first)),
        out_specs=ANY,
        input_output_aliases={0: 0},
        compiler_params=PARAMS,
        cost_estimate=cost,
    )(passed, *first)


def clip_of(token, base, span, tok_dev, clip_ref):
    frame = base + token // span * FRB + token % tok_dev // TPF
    clip = jnp.zeros_like(token)
    for f in range(clip_ref.shape[0]):
        clip = jnp.where(frame == f, clip_ref[f], clip)
    return clip


def mask_kernel(span, tok, base_ref, clip_ref, *out_refs):
    count = out_refs[0].shape[0]
    row = lax.broadcasted_iota(jnp.int32, (count, 1), 0)
    col = lax.broadcasted_iota(jnp.int32, (1, count), 1)
    row_clip = clip_of(row, base_ref[0], span, tok, clip_ref)
    for i, out_ref in enumerate(out_refs):
        allowed = row_clip == clip_of(col, base_ref[i], span, tok, clip_ref)
        out_ref[...] = jnp.where(allowed, 0.0, -1e30)


def masks(bases, span, tok, count, frame_clip):
    return pl.pallas_call(
        functools.partial(mask_kernel, span, tok),
        out_shape=[jax.ShapeDtypeStruct((count, count), jnp.float32)] * len(bases),
        in_specs=[SMEM, SMEM],
        out_specs=[VMEM] * len(bases),
        compiler_params=PARAMS,
    )(index_array(*bases), frame_clip)


def attention_kernel(head_dim, n_mask, which, joint, q_ref, *refs):
    *refs, out_ref = refs
    mask_refs, refs = refs[:n_mask], refs[n_mask:]
    count, width = q_ref.shape
    k_refs, v_refs = [], []
    for both in joint:
        ref, *refs = refs
        if both:
            k_refs.append(ref.at[0:count])
            v_refs.append(ref.at[count:2 * count])
        else:
            value_ref, *refs = refs
            k_refs.append(ref)
            v_refs.append(value_ref)
    scale = math.log2(math.e) / math.sqrt(head_dim)
    per_step = max(1, 1024 // count)
    for h in range(width // head_dim):
        cols = slice(h * head_dim, (h + 1) * head_dim)
        queries = q_ref[:, cols]
        top = total = acc = None
        for first in range(0, len(k_refs), per_step):
            here = range(first, min(first + per_step, len(k_refs)))
            scores = []
            for i in here:
                s = lax.dot_general(
                    queries, k_refs[i][:, cols], (((1,), (1,)), ((), ())),
                    preferred_element_type=jnp.float32,
                )
                scores.append(s * scale + mask_refs[which[i]][...])
            new_top = functools.reduce(
                jnp.maximum, [jnp.max(s, axis=1, keepdims=True) for s in scores]
            )
            if top is not None:
                new_top = jnp.maximum(top, new_top)
                factor = jnp.exp2(top - new_top)
                total, acc = total * factor, acc * factor
            top = new_top
            for i, s in zip(here, scores):
                p = jnp.exp2(s - top)
                part = jnp.sum(p, axis=1, keepdims=True)
                dot = jnp.dot(
                    p.astype(jnp.bfloat16), v_refs[i][:, cols], preferred_element_type=jnp.float32
                )
                total = part if total is None else total + part
                acc = dot if acc is None else acc + dot
        out_ref[:, cols] = (acc / total).astype(out_ref.dtype)


def attention(q, kvs, mask_of, which, head_dim):
    joint = [not isinstance(kv, tuple) for kv in kvs]
    arrays = [x for kv, both in zip(kvs, joint) for x in ((kv,) if both else kv)]
    return pl.pallas_call(
        functools.partial(attention_kernel, head_dim, len(mask_of), which, joint),
        out_shape=jax.ShapeDtypeStruct(q.shape, q.dtype),
        in_specs=[VMEM] * (1 + len(mask_of) + len(arrays)),
        out_specs=VMEM,
        compiler_params=PARAMS,
    )(q, *mask_of, *arrays)


def stack_kernel(n_blocks, info_ref, x_ref, *refs):
    *refs, out_ref = refs
    part_refs, block_refs = refs[:len(refs) - n_blocks], refs[len(refs) - n_blocks:]
    head_dim, cols = x_ref.shape[0], out_ref.shape[1]
    out_ref[0:head_dim, :] = x_ref[:, rows_at(info_ref[0] // 2, cols)]
    for i, ref in enumerate(part_refs):
        out_ref[(i + 1) * head_dim:(i + 2) * head_dim, :] = ref[...]
    first = (len(part_refs) + 1) * head_dim
    for i, ref in enumerate(block_refs):
        rows = head_dim // n_blocks
        at = pl.ds(pl.multiple_of(first + (info_ref[2] ^ i) * rows, rows), rows)
        head = ref.shape[0] - cols // LANES * rows
        for j in range(cols // LANES):
            out_ref[at, j * LANES:(j + 1) * LANES] = ref[head + j * rows:head + (j + 1) * rows]


def stack(info, w_out, parts, blocks, cols):
    depth = w_out.shape[0] * (1 + len(parts) + len(blocks) // 2)
    return pl.pallas_call(
        functools.partial(stack_kernel, len(blocks)),
        out_shape=jax.ShapeDtypeStruct((depth, cols), w_out.dtype),
        in_specs=[SMEM] + [VMEM] * (1 + len(parts) + len(blocks)),
        out_specs=VMEM,
        compiler_params=PARAMS,
    )(info, w_out, *parts, *blocks)


def halves(a_ref, rows, w_ref, late_ref):
    if late_ref is None:
        return jnp.dot(a_ref[rows, :], w_ref[...], preferred_element_type=jnp.float32)
    half = (w_ref.shape[0] + late_ref.shape[0]) // 2
    low = jnp.concatenate([w_ref[half:, :], late_ref[...]], axis=0)
    first = jnp.dot(a_ref[rows, :half], w_ref[:half, :], preferred_element_type=jnp.float32)
    return first + jnp.dot(a_ref[rows, half:], low, preferred_element_type=jnp.float32)


def project_kernel(n_attn, head_dim, info_ref, *refs):
    attn_refs, w_ref, refs = refs[:n_attn], refs[n_attn], refs[n_attn + 1:]
    late_refs, (out_ref, a_ref), late_ref = refs[:-2], refs[-2:], None
    if len(refs) > 2:
        late_refs, (out_ref, a_ref, late_ref) = refs[:2], refs[2:]
    blks, tok, _ = out_ref.shape
    blk, other = info_ref[0] // 2, 1 - info_ref[0] % 2
    heads = attn_refs[0].shape[1] // head_dim
    for k, ref in enumerate(attn_refs):
        for i in range(heads):
            at = rows_at(((blk ^ k) * heads + i) ^ info_ref[1], head_dim)
            cols = slice(i * head_dim, (i + 1) * head_dim)
            for b in range(blks):
                a_ref[b * tok:(b + 1) * tok, at] = ref[rows_at(2 * b + other, tok), cols]
                a_ref[(blks + b) * tok:(blks + b + 1) * tok, at] = ref[
                    rows_at(2 * b + 1 - other, tok), cols
                ]
    for i, ref in enumerate(late_refs):
        late_ref[rows_at(info_ref[2] ^ i, ref.shape[0]), :] = ref[...]
    dot = halves(a_ref, slice(0, blks * tok), w_ref, late_ref)
    out_ref[...] = dot.astype(out_ref.dtype).reshape(out_ref.shape)


def rest_kernel(a_ref, w_ref, *refs):
    *late_refs, out_ref = refs
    blks, tok, _ = out_ref.shape
    late_ref = late_refs[0] if late_refs else None
    dot = halves(a_ref, slice(blks * tok, None), w_ref, late_ref)
    out_ref[...] = dot.astype(out_ref.dtype).reshape(out_ref.shape)


def project(attns, w_all, late, info, head_dim, tok):
    count, width = attns[0].shape
    blks, dtype, cols = len(attns), attns[0].dtype, w_all.shape[1]
    like = jax.ShapeDtypeStruct((blks, tok, cols), dtype)
    below = [jax.ShapeDtypeStruct((head_dim, cols), dtype)] if late else []
    theirs, a_all, *late_all = pl.pallas_call(
        functools.partial(project_kernel, blks, head_dim),
        out_shape=[like, jax.ShapeDtypeStruct((count, blks * width), dtype)] + below,
        in_specs=[SMEM] + [VMEM] * (blks + 1 + len(late)),
        out_specs=[VMEM] * (2 + len(below)),
        compiler_params=PARAMS,
    )(info, *attns, w_all, *late)
    got = xor(theirs, ("core",), 1)
    ours = pl.pallas_call(
        rest_kernel,
        out_shape=like,
        in_specs=[VMEM] * (2 + len(below)),
        out_specs=VMEM,
        compiler_params=PARAMS,
    )(a_all, w_all, *late_all)
    far = [k for k in range(blks) if k != 1]
    parts = dict(zip(far, add(ours, got, info, far)))
    parts[1], = add(ours, got, info, [1], parts[far[-1]])
    return [parts[k] for k in range(blks)]


def add_kernel(which, info_ref, x_ref, y_ref, *refs):
    for k, out_ref in zip(which, refs[len(refs) - len(which):]):
        at = info_ref[0] // 2 ^ k
        both = x_ref[at].astype(jnp.float32) + y_ref[at].astype(jnp.float32)
        out_ref[...] = both.astype(out_ref.dtype)


def add(x, y, info, which, *first):
    return pl.pallas_call(
        functools.partial(add_kernel, which),
        out_shape=[jax.ShapeDtypeStruct(x.shape[1:], x.dtype)] * len(which),
        in_specs=[SMEM, VMEM, VMEM] + [ANY] * len(first),
        out_specs=[VMEM] * len(which),
        compiler_params=PARAMS,
    )(info, x, y, *first)


def unpack_kernel(which, n_in, info_ref, *refs):
    in_refs, (out_ref, sems) = refs[:len(which)], refs[n_in:]
    copies = []
    for i, (k, ref) in enumerate(zip(which, in_refs)):
        cols = rows_at(info_ref[0] // 2 ^ k, ref.shape[1])
        copies.append(pltpu.make_async_copy(ref, out_ref.at[:, cols], sems.at[i]))
    for copy in copies:
        copy.start()
    for copy in copies:
        copy.wait()


def unpack(parts, info):
    tok, width = parts[0].shape
    hbm = pl.BlockSpec(memory_space=pltpu.HBM)
    result = []
    for which in (range(0, 2), range(2, len(parts))):
        n = len(which)
        result = [pl.pallas_call(
            functools.partial(unpack_kernel, which, n + len(result)),
            out_shape=jax.ShapeDtypeStruct((tok, len(parts) * width), parts[0].dtype),
            in_specs=[SMEM] + [VMEM] * n + [hbm] * len(result),
            out_specs=hbm,
            input_output_aliases={1 + n: 0} if result else {},
            scratch_shapes=[pltpu.SemaphoreType.DMA((n,))],
            compiler_params=PARAMS,
        )(info, *[parts[k] for k in which], *result)]
    return result[0]


def xor(x, axis, by):
    size = math.prod(lax.axis_size(name) for name in axis)
    return lax.ppermute(x, axis, [(i, i ^ by) for i in range(size)])


def swap_all(parts, axis):
    return [parts[0]] + [xor(parts[m], axis, m) for m in range(1, len(parts))]


def squares(qkv, frame_clip, w_out):
    quarter = ("x", "zl")
    y, x, zh, zl, core = (lax.axis_index(n) for n in ("y", "x", "zh", "zl", "core"))
    tok, head_dim, cols = qkv.shape[1], w_out.shape[0], w_out.shape[1] // 4
    place = index_array((x * 2 + zl) * 2 + core)
    theirs = x * 2 + 1 - zl
    info = index_array((x * 2 + zl) * 2 + core, zh * 2 + zl, y)
    half = head_dim // 2

    w_far = blocks(w_out, half, cols, "y", quarter)
    far = after(xor(w_far, ("zh",), 1), cost=AHEAD)
    w_corner, w_near = pieces(w_out, y, theirs, cols)
    kept, given = lanes(qkv, core, head_dim)
    shared = swap_all(deal(kept, xor(given, ("core",), 1), place), quarter)
    q, k, v = sort(shared, place)
    k_far, v_far = xor(k, ("zh",), 1), xor(v, ("zh",), 1)
    near = xor(join(k, v, far), ("y",), 1)
    corner = xor(after(w_corner, k), ("zh", "zl"), 3)
    w_next = xor(after(w_near, k), ("zl",), 1)
    kvs = [(k, v), (k_far, v_far), near, (xor(k_far, ("y",), 1), xor(v_far, ("y",), 1))]

    bases = [y * 2 * FRB, (1 - y) * 2 * FRB]
    mask_of = masks(bases, 4 * tok, tok, 8 * tok, frame_clip)
    attn = attention(q, kvs, mask_of, [0, 0, 1, 1], head_dim)
    corner = after(corner, attn)
    corner_rest = xor(corner, ("y",), 1)
    attns = swap_all([attn] * 4, quarter)
    w_all = stack(info, w_out, [w_next], [far, near], cols)
    parts = project(attns, w_all, [corner, corner_rest], info, head_dim, tok)
    return unpack(swap_all(parts, quarter), info)


def layers(qkv, frame_clip, w_out):
    rows, blks = lax.axis_size("row"), lax.axis_size("blk")
    row, blk = lax.axis_index("row"), lax.axis_index("blk")
    tok, head_dim, cols = qkv.shape[1], w_out.shape[0], w_out.shape[1] // blks
    info = index_array(blk * 2 + lax.axis_index("core"), row)
    others = range(1, rows)

    (w_own,) = columns(w_out, [(head_dim, 0, blk)], cols)
    w_parts = [xor(w_own, ("row",), by) for by in others]
    packed = pack(qkv, 2 * blks, head_dim)
    own = lax.all_to_all(packed, ("blk", "core"), split_axis=0, concat_axis=0, tiled=True)
    q, kv = cut(own)
    kvs = [kv] + [xor(kv, ("row",), by) for by in others]
    mask_of = masks([0], 2 * tok, tok, 2 * blks * tok, frame_clip)
    attn = attention(q, kvs, mask_of, [0] * rows, head_dim)
    attns = swap_all([attn] * blks, ("blk",))
    w_all = stack(info, w_out, w_parts, [], cols)
    parts = project(attns, w_all, [], info, head_dim, tok)
    return unpack(swap_all(parts, ("blk",)), info)


def solution(mesh):
    blk, tile = mesh.shape["blk"], mesh.shape["tile"]
    if (blk, tile) == (4, 8):
        plan, names, shape = squares, ("y", "x", "zh", "zl", "core"), (2, 2, 2, 2, 2)
    else:
        plan, names, shape = layers, ("blk", "row", "core"), (blk, tile // 2, 2)
    fine = Mesh(mesh.devices.reshape(shape), names)
    tiles = names[2:] if plan is squares else names[1:]
    in_specs = (P(None, names, None), P(), P(tiles, None))
    return jax.shard_map(
        plan, mesh=fine, in_specs=in_specs, out_specs=P(names, None), check_vma=False
    )
```

```python
import functools
import math

import jax
import jax.numpy as jnp
from jax import lax
from jax.experimental import pallas as pl
from jax.experimental.pallas import tpu as pltpu
from jax.sharding import Mesh
from jax.sharding import PartitionSpec as P

FRB = 2
TPF = 16
LANES = 128
VMEM = pl.BlockSpec(memory_space=pltpu.VMEM)
SMEM = pl.BlockSpec(memory_space=pltpu.SMEM)
ANY = pl.BlockSpec(memory_space=pl.ANY)
PARAMS = pltpu.CompilerParams(vmem_limit_bytes=48 * 1024 * 1024)
AHEAD = pl.CostEstimate(flops=20_000_000_000, bytes_accessed=1_000_000, transcendentals=0)
SOON = pl.CostEstimate(flops=6_000_000_000, bytes_accessed=1_000_000, transcendentals=0)


def rows_at(index, size):
    return pl.ds(pl.multiple_of(index * size, size), size)


def index_array(*numbers):
    return jnp.stack([jnp.asarray(i, jnp.int32) for i in numbers])


def pack_kernel(head_dim, x_ref, out_ref):
    peers, _, width = out_ref.shape
    kinds, tok, _ = x_ref.shape
    heads = width // head_dim
    for g in range(peers):
        for i in range(heads):
            head = (g // 2 * heads + i) * 2 + g % 2
            for k in range(kinds):
                out_ref[g, k * tok:(k + 1) * tok, i * head_dim:(i + 1) * head_dim] = x_ref[
                    k, :, head * head_dim:(head + 1) * head_dim
                ]


def pack(x, peers, head_dim):
    kinds, tok, cols = x.shape
    return pl.pallas_call(
        functools.partial(pack_kernel, head_dim),
        out_shape=jax.ShapeDtypeStruct((peers, kinds * tok, cols // peers), x.dtype),
        in_specs=[VMEM],
        out_specs=VMEM,
        compiler_params=PARAMS,
    )(x)


def columns_kernel(at_ref, x_ref, *refs):
    *out_refs, sems = refs
    copies = []
    for i, ref in enumerate(out_refs):
        depth, cols = ref.shape
        piece = x_ref.at[rows_at(at_ref[2 * i], depth), rows_at(at_ref[2 * i + 1], cols)]
        copies.append(pltpu.make_async_copy(piece, ref, sems.at[i]))
    for copy in copies:
        copy.start()
    for copy in copies:
        copy.wait()


def columns(x, pieces, cols):
    return pl.pallas_call(
        columns_kernel,
        out_shape=[jax.ShapeDtypeStruct((piece[0], cols), x.dtype) for piece in pieces],
        in_specs=[SMEM, pl.BlockSpec(memory_space=pltpu.HBM)],
        out_specs=[VMEM] * len(pieces),
        scratch_shapes=[pltpu.SemaphoreType.DMA((len(pieces),))],
        compiler_params=PARAMS,
    )(
        index_array(*[i for piece in pieces for i in piece[1:]]),
        pltpu.with_memory_space_constraint(x, pltpu.HBM),
    )


def blocks_kernel(row_axis, col_axes, x_ref, out_ref, held, sem):
    depth, cols = held.shape
    col = 0
    for axis in col_axes:
        col = col * lax.axis_size(axis) + lax.axis_index(axis)
    piece = x_ref.at[rows_at(lax.axis_index(row_axis), depth), rows_at(col, cols)]
    copy = pltpu.make_async_copy(piece, held, sem)
    copy.start()
    copy.wait()
    for j in range(cols // LANES):
        out_ref[j * depth:(j + 1) * depth, :] = held[:, j * LANES:(j + 1) * LANES]


def blocks(x, depth, cols, row_axis, col_axes):
    return pl.pallas_call(
        functools.partial(blocks_kernel, row_axis, col_axes),
        out_shape=jax.ShapeDtypeStruct((cols // LANES * depth, LANES), x.dtype),
        in_specs=[pl.BlockSpec(memory_space=pltpu.HBM)],
        out_specs=VMEM,
        scratch_shapes=[pltpu.VMEM((depth, cols), x.dtype), pltpu.SemaphoreType.DMA],
        compiler_params=PARAMS,
    )(pltpu.with_memory_space_constraint(x, pltpu.HBM))


def pieces_kernel(at_ref, x_ref, corner_ref, near_ref):
    half, cols = corner_ref.shape
    corner_ref[...] = x_ref[rows_at(at_ref[0], half), rows_at(at_ref[1], cols)]
    near_ref[...] = x_ref[:, rows_at(at_ref[1], cols)]


def pieces(x, half, at, cols):
    depth = x.shape[0]
    return pl.pallas_call(
        pieces_kernel,
        out_shape=[jax.ShapeDtypeStruct((rows, cols), x.dtype) for rows in (depth // 2, depth)],
        in_specs=[SMEM, VMEM],
        out_specs=[VMEM, VMEM],
        compiler_params=PARAMS,
    )(index_array(half, at), x)


def lane_kernel(head_dim, core_ref, x_ref, mine_ref, theirs_ref):
    kinds, tok, _ = x_ref.shape
    for out_ref, core in ((mine_ref, core_ref[0]), (theirs_ref, 1 - core_ref[0])):
        for g in range(out_ref.shape[0]):
            cols = rows_at(2 * g + core, head_dim)
            for k in range(kinds):
                out_ref[g, k * tok:(k + 1) * tok, :] = x_ref[k, :, cols]


def lanes(x, core, head_dim):
    kinds, tok, cols = x.shape
    like = jax.ShapeDtypeStruct((cols // head_dim // 2, kinds * tok, head_dim), x.dtype)
    return pl.pallas_call(
        functools.partial(lane_kernel, head_dim),
        out_shape=(like, like),
        in_specs=[SMEM, VMEM],
        out_specs=(VMEM, VMEM),
        compiler_params=PARAMS,
    )(index_array(core), x)


def deal_kernel(place_ref, mine_ref, got_ref, *out_refs):
    quarter, core = place_ref[0] // 2, place_ref[0] % 2
    for k, out_ref in enumerate(out_refs):
        out_ref[core] = mine_ref[quarter ^ k]
        out_ref[1 - core] = got_ref[quarter ^ k]


def deal(mine, got, place):
    quarters, depth, width = mine.shape
    return pl.pallas_call(
        deal_kernel,
        out_shape=[jax.ShapeDtypeStruct((2, depth, width), mine.dtype)] * quarters,
        in_specs=[SMEM, VMEM, VMEM],
        out_specs=[VMEM] * quarters,
        compiler_params=PARAMS,
    )(place, mine, got)


def sort_kernel(place_ref, *refs):
    *in_refs, q_ref, k_ref, v_ref = refs
    tok = q_ref.shape[0] // (2 * len(in_refs))
    for i, ref in enumerate(in_refs[::-1]):
        for core in range(2):
            at = rows_at((place_ref[0] // 2 ^ i) * 2 + core, tok)
            for j, out_ref in enumerate((q_ref, k_ref, v_ref)):
                out_ref[at, :] = ref[core, j * tok:(j + 1) * tok, :]


def sort(parts, place):
    both, depth, width = parts[0].shape
    count = both * len(parts) * (depth // 3)
    return pl.pallas_call(
        sort_kernel,
        out_shape=[jax.ShapeDtypeStruct((count, width), parts[0].dtype)] * 3,
        in_specs=[SMEM] + [VMEM] * len(parts),
        out_specs=[VMEM] * 3,
        compiler_params=PARAMS,
    )(place, *parts[::-1])


def join_kernel(*refs):
    *in_refs, out_ref = refs
    first = 0
    for ref in in_refs:
        out_ref[first:first + ref.shape[0], :] = ref[...]
        first += ref.shape[0]


def join(*arrays):
    depth = sum(x.shape[0] for x in arrays)
    return pl.pallas_call(
        join_kernel,
        out_shape=jax.ShapeDtypeStruct((depth, arrays[0].shape[1]), arrays[0].dtype),
        in_specs=[VMEM] * len(arrays),
        out_specs=VMEM,
        compiler_params=PARAMS,
    )(*arrays)


def cut_kernel(x_ref, q_ref, kv_ref):
    peers, depth, _ = x_ref.shape
    tok = depth // 3
    for g in range(peers):
        q_ref[g * tok:(g + 1) * tok, :] = x_ref[g, :tok, :]
        for i in range(2):
            kv_ref[(i * peers + g) * tok:(i * peers + g + 1) * tok, :] = x_ref[
                g, (i + 1) * tok:(i + 2) * tok, :
            ]


def cut(x):
    peers, depth, width = x.shape
    count = peers * depth // 3
    return pl.pallas_call(
        cut_kernel,
        out_shape=[jax.ShapeDtypeStruct((size, width), x.dtype) for size in (count, 2 * count)],
        in_specs=[VMEM],
        out_specs=[VMEM, VMEM],
        compiler_params=PARAMS,
    )(x)


def after_kernel(*refs):
    pass


def after(passed, *first, cost=None):
    return pl.pallas_call(
        after_kernel,
        out_shape=jax.ShapeDtypeStruct(passed.shape, passed.dtype),
        in_specs=[ANY] * (1 + len(first)),
        out_specs=ANY,
        input_output_aliases={0: 0},
        compiler_params=PARAMS,
        cost_estimate=cost,
    )(passed, *first)


def clip_of(token, base, span, tok_dev, clip_ref):
    frame = base + token // span * FRB + token % tok_dev // TPF
    clip = jnp.zeros_like(token)
    for f in range(clip_ref.shape[0]):
        clip = jnp.where(frame == f, clip_ref[f], clip)
    return clip


def mask_kernel(span, tok, base_ref, clip_ref, *out_refs):
    count = out_refs[0].shape[0]
    row = lax.broadcasted_iota(jnp.int32, (count, 1), 0)
    col = lax.broadcasted_iota(jnp.int32, (1, count), 1)
    row_clip = clip_of(row, base_ref[0], span, tok, clip_ref)
    for i, out_ref in enumerate(out_refs):
        allowed = row_clip == clip_of(col, base_ref[i], span, tok, clip_ref)
        out_ref[...] = jnp.where(allowed, 0.0, -1e30)


def masks(bases, span, tok, count, frame_clip):
    return pl.pallas_call(
        functools.partial(mask_kernel, span, tok),
        out_shape=[jax.ShapeDtypeStruct((count, count), jnp.float32)] * len(bases),
        in_specs=[SMEM, SMEM],
        out_specs=[VMEM] * len(bases),
        compiler_params=PARAMS,
    )(index_array(*bases), frame_clip)


def attention_kernel(head_dim, n_mask, which, joint, q_ref, *refs):
    *refs, out_ref = refs
    mask_refs, refs = refs[:n_mask], refs[n_mask:]
    count, width = q_ref.shape
    k_refs, v_refs = [], []
    for both in joint:
        ref, *refs = refs
        if both:
            k_refs.append(ref.at[0:count])
            v_refs.append(ref.at[count:2 * count])
        else:
            value_ref, *refs = refs
            k_refs.append(ref)
            v_refs.append(value_ref)
    scale = math.log2(math.e) / math.sqrt(head_dim)
    per_step = max(1, 1024 // count)
    for h in range(width // head_dim):
        cols = slice(h * head_dim, (h + 1) * head_dim)
        queries = q_ref[:, cols]
        top = total = acc = None
        for first in range(0, len(k_refs), per_step):
            here = range(first, min(first + per_step, len(k_refs)))
            scores = []
            for i in here:
                s = lax.dot_general(
                    queries, k_refs[i][:, cols], (((1,), (1,)), ((), ())),
                    preferred_element_type=jnp.float32,
                )
                scores.append(s * scale + mask_refs[which[i]][...])
            new_top = functools.reduce(
                jnp.maximum, [jnp.max(s, axis=1, keepdims=True) for s in scores]
            )
            if top is not None:
                new_top = jnp.maximum(top, new_top)
                factor = jnp.exp2(top - new_top)
                total, acc = total * factor, acc * factor
            top = new_top
            for i, s in zip(here, scores):
                p = jnp.exp2(s - top)
                part = jnp.sum(p, axis=1, keepdims=True)
                dot = jnp.dot(
                    p.astype(jnp.bfloat16), v_refs[i][:, cols], preferred_element_type=jnp.float32
                )
                total = part if total is None else total + part
                acc = dot if acc is None else acc + dot
        out_ref[:, cols] = (acc / total).astype(out_ref.dtype)


def attention(q, kvs, mask_of, which, head_dim):
    joint = [not isinstance(kv, tuple) for kv in kvs]
    arrays = [x for kv, both in zip(kvs, joint) for x in ((kv,) if both else kv)]
    return pl.pallas_call(
        functools.partial(attention_kernel, head_dim, len(mask_of), which, joint),
        out_shape=jax.ShapeDtypeStruct(q.shape, q.dtype),
        in_specs=[VMEM] * (1 + len(mask_of) + len(arrays)),
        out_specs=VMEM,
        compiler_params=PARAMS,
    )(q, *mask_of, *arrays)


def project_kernel(n_attn, sizes, at_ref, place_ref, *refs):
    attn_refs, w_refs = refs[:n_attn], refs[n_attn:-3]
    out_ref, a_ref, w_all = refs[-3:]
    width = attn_refs[0].shape[1]
    blks, tok, cols = out_ref.shape
    blk, other = place_ref[0] // 2, 1 - place_ref[0] % 2
    for k, ref in enumerate(attn_refs):
        at = rows_at(blk ^ k, width)
        for b in range(blks):
            a_ref[b * tok:(b + 1) * tok, at] = ref[rows_at(2 * b + other, tok), :]
            a_ref[(blks + b) * tok:(blks + b + 1) * tok, at] = ref[rows_at(2 * b + 1 - other, tok), :]
    for i, (ref, rows) in enumerate(zip(w_refs, sizes)):
        at = rows_at(at_ref[i], rows)
        if ref.shape[1] >= cols:
            w_all[at, :] = ref[:, rows_at(blk, cols)] if ref.shape[1] > cols else ref[...]
        else:
            first = ref.shape[0] - cols // LANES * rows
            for j in range(cols // LANES):
                w_all[at, j * LANES:(j + 1) * LANES] = ref[first + j * rows:first + (j + 1) * rows]
    dot = jnp.dot(a_ref[:blks * tok, :], w_all[...], preferred_element_type=jnp.float32)
    out_ref[...] = dot.astype(out_ref.dtype).reshape(out_ref.shape)


def rest_kernel(a_ref, w_ref, out_ref):
    blks, tok, _ = out_ref.shape
    dot = jnp.dot(a_ref[blks * tok:, :], w_ref[...], preferred_element_type=jnp.float32)
    out_ref[...] = dot.astype(out_ref.dtype).reshape(out_ref.shape)


def project(attns, w_parts, sizes, at, place, tok, cols):
    count, width = attns[0].shape
    blks, dtype = len(attns), attns[0].dtype
    like = jax.ShapeDtypeStruct((blks, tok, cols), dtype)
    theirs, a_all, w_all = pl.pallas_call(
        functools.partial(project_kernel, blks, sizes),
        out_shape=(
            like,
            jax.ShapeDtypeStruct((count, blks * width), dtype),
            jax.ShapeDtypeStruct((blks * width, cols), dtype),
        ),
        in_specs=[SMEM, SMEM] + [VMEM] * (blks + len(w_parts)),
        out_specs=(VMEM, VMEM, VMEM),
        compiler_params=PARAMS,
    )(index_array(*at), place, *attns, *w_parts)
    got = xor(theirs, ("core",), 1)
    ours = pl.pallas_call(
        rest_kernel,
        out_shape=like,
        in_specs=[VMEM, VMEM],
        out_specs=VMEM,
        compiler_params=PARAMS,
    )(a_all, w_all)
    return add(ours, got, place)


def add_kernel(place_ref, x_ref, y_ref, *out_refs):
    for k, out_ref in enumerate(out_refs):
        at = place_ref[0] // 2 ^ k
        both = x_ref[at].astype(jnp.float32) + y_ref[at].astype(jnp.float32)
        out_ref[...] = both.astype(out_ref.dtype)


def add(x, y, place):
    blks = x.shape[0]
    return pl.pallas_call(
        add_kernel,
        out_shape=[jax.ShapeDtypeStruct(x.shape[1:], x.dtype)] * blks,
        in_specs=[SMEM, VMEM, VMEM],
        out_specs=[VMEM] * blks,
        compiler_params=PARAMS,
    )(place, x, y)


def unpack_kernel(place_ref, *refs):
    *in_refs, out_ref = refs
    width = in_refs[0].shape[1]
    for k, ref in enumerate(in_refs[::-1]):
        out_ref[:, rows_at(place_ref[0] // 2 ^ k, width)] = ref[...]


def unpack(parts, place):
    tok, width = parts[0].shape
    return pl.pallas_call(
        unpack_kernel,
        out_shape=jax.ShapeDtypeStruct((tok, len(parts) * width), parts[0].dtype),
        in_specs=[SMEM] + [VMEM] * len(parts),
        out_specs=VMEM,
        compiler_params=PARAMS,
    )(place, *parts[::-1])


def xor(x, axis, by):
    size = math.prod(lax.axis_size(name) for name in axis)
    return lax.ppermute(x, axis, [(i, i ^ by) for i in range(size)])


def swap_all(parts, axis):
    return [parts[0]] + [xor(parts[m], axis, m) for m in range(1, len(parts))]


def squares(qkv, frame_clip, w_out):
    quarter = ("x", "zl")
    y, x, zh, zl, core = (lax.axis_index(n) for n in ("y", "x", "zh", "zl", "core"))
    tok, head_dim, cols = qkv.shape[1], w_out.shape[0], w_out.shape[1] // 4
    place = index_array((x * 2 + zl) * 2 + core)
    theirs = x * 2 + 1 - zl
    row, half = zh * 2 + zl, head_dim // 2

    w_far = blocks(w_out, half, cols, "y", quarter)
    far = after(xor(w_far, ("zh",), 1), cost=AHEAD)
    w_corner, w_near = pieces(w_out, y, theirs, cols)
    kept, given = lanes(qkv, core, head_dim)
    shared = swap_all(deal(kept, xor(given, ("core",), 1), place), quarter)
    q, k, v = sort(shared, place)
    k_far, v_far = xor(k, ("zh",), 1), xor(v, ("zh",), 1)
    near = xor(join(k, v, far), ("y",), 1)
    corner = xor(after(w_corner, k), ("zh", "zl"), 3)
    w_next = xor(after(w_near, k), ("zl",), 1)
    kvs = [(k, v), (k_far, v_far), near, (xor(k_far, ("y",), 1), xor(v_far, ("y",), 1))]

    bases = [y * 2 * FRB, (1 - y) * 2 * FRB]
    mask_of = masks(bases, 4 * tok, tok, 8 * tok, frame_clip)
    attn = attention(q, kvs, mask_of, [0, 0, 1, 1], head_dim)
    corner = after(corner, attn)
    corner_rest = xor(corner, ("y",), 1)
    attns = swap_all([attn] * 4, quarter)
    w_parts = [w_out, w_next, far, near, corner, corner_rest]
    sizes = [head_dim, head_dim, half, half, half, half]
    at = [row, row ^ 1] + [2 * (row ^ by) + h for by in (2, 3) for h in (y, 1 - y)]
    parts = project(attns, w_parts, sizes, at, place, tok, cols)
    return unpack(swap_all(parts, quarter), place)


def layers(qkv, frame_clip, w_out):
    rows, blks = lax.axis_size("row"), lax.axis_size("blk")
    row, blk = lax.axis_index("row"), lax.axis_index("blk")
    tok, head_dim, cols = qkv.shape[1], w_out.shape[0], w_out.shape[1] // blks
    place = index_array(blk * 2 + lax.axis_index("core"))
    others = range(1, rows)

    (w_own,) = columns(w_out, [(head_dim, 0, blk)], cols)
    w_parts = [w_out] + [xor(w_own, ("row",), by) for by in others]
    packed = pack(qkv, 2 * blks, head_dim)
    own = lax.all_to_all(packed, ("blk", "core"), split_axis=0, concat_axis=0, tiled=True)
    q, kv = cut(own)
    kvs = [kv] + [xor(kv, ("row",), by) for by in others]
    mask_of = masks([0], 2 * tok, tok, 2 * blks * tok, frame_clip)
    attn = attention(q, kvs, mask_of, [0] * rows, head_dim)
    attns = swap_all([attn] * blks, ("blk",))
    at = [row ^ by for by in range(rows)]
    parts = project(attns, w_parts, [head_dim] * rows, at, place, tok, cols)
    return unpack(swap_all(parts, ("blk",)), place)


def solution(mesh):
    blk, tile = mesh.shape["blk"], mesh.shape["tile"]
    if (blk, tile) == (4, 8):
        plan, names, shape = squares, ("y", "x", "zh", "zl", "core"), (2, 2, 2, 2, 2)
    else:
        plan, names, shape = layers, ("blk", "row", "core"), (blk, tile // 2, 2)
    fine = Mesh(mesh.devices.reshape(shape), names)
    tiles = names[2:] if plan is squares else names[1:]
    in_specs = (P(None, names, None), P(), P(tiles, None))
    return jax.shard_map(
        plan, mesh=fine, in_specs=in_specs, out_specs=P(names, None), check_vma=False
    )
```

```python
import functools
import math

import jax
import jax.numpy as jnp
from jax import lax
from jax.experimental import pallas as pl
from jax.experimental.pallas import tpu as pltpu
from jax.sharding import Mesh
from jax.sharding import PartitionSpec as P

FRB = 2
TPF = 16
LANES = 128
UNIT = 16
VMEM = pl.BlockSpec(memory_space=pltpu.VMEM)
SMEM = pl.BlockSpec(memory_space=pltpu.SMEM)
ANY = pl.BlockSpec(memory_space=pl.ANY)
PARAMS = pltpu.CompilerParams(vmem_limit_bytes=48 * 1024 * 1024)
AHEAD = pl.CostEstimate(flops=20_000_000_000, bytes_accessed=1_000_000, transcendentals=0)
SOON = pl.CostEstimate(flops=6_000_000_000, bytes_accessed=1_000_000, transcendentals=0)


def rows_at(index, size):
    return pl.ds(pl.multiple_of(index * size, size), size)


def index_array(*numbers):
    return jnp.stack([jnp.asarray(i, jnp.int32) for i in numbers])


def pack_kernel(head_dim, x_ref, out_ref):
    peers, _, width = out_ref.shape
    kinds, tok, _ = x_ref.shape
    heads = width // head_dim
    for g in range(peers):
        for i in range(heads):
            head = (g // 2 * heads + i) * 2 + g % 2
            for k in range(kinds):
                out_ref[g, k * tok:(k + 1) * tok, i * head_dim:(i + 1) * head_dim] = x_ref[
                    k, :, head * head_dim:(head + 1) * head_dim
                ]


def pack(x, peers, head_dim):
    kinds, tok, cols = x.shape
    return pl.pallas_call(
        functools.partial(pack_kernel, head_dim),
        out_shape=jax.ShapeDtypeStruct((peers, kinds * tok, cols // peers), x.dtype),
        in_specs=[VMEM],
        out_specs=VMEM,
        compiler_params=PARAMS,
    )(x)


def columns_kernel(at_ref, x_ref, *refs):
    *out_refs, sems = refs
    copies = []
    for i, ref in enumerate(out_refs):
        depth, cols = ref.shape
        piece = x_ref.at[rows_at(at_ref[2 * i], depth), rows_at(at_ref[2 * i + 1], cols)]
        copies.append(pltpu.make_async_copy(piece, ref, sems.at[i]))
    for copy in copies:
        copy.start()
    for copy in copies:
        copy.wait()


def columns(x, pieces, cols):
    return pl.pallas_call(
        columns_kernel,
        out_shape=[jax.ShapeDtypeStruct((piece[0], cols), x.dtype) for piece in pieces],
        in_specs=[SMEM, pl.BlockSpec(memory_space=pltpu.HBM)],
        out_specs=[VMEM] * len(pieces),
        scratch_shapes=[pltpu.SemaphoreType.DMA((len(pieces),))],
        compiler_params=PARAMS,
    )(
        index_array(*[i for piece in pieces for i in piece[1:]]),
        pltpu.with_memory_space_constraint(x, pltpu.HBM),
    )


def blocks_kernel(row_axis, col_axes, x_ref, *refs):
    *out_refs, held, sem = refs
    depth, cols = held.shape
    col = 0
    for axis in col_axes:
        col = col * lax.axis_size(axis) + lax.axis_index(axis)
    piece = x_ref.at[rows_at(lax.axis_index(row_axis), depth), rows_at(col, cols)]
    copy = pltpu.make_async_copy(piece, held, sem)
    copy.start()
    copy.wait()
    first = 0
    for out_ref in out_refs:
        part = out_ref.shape[0] // (cols // LANES)
        for j in range(cols // LANES):
            out_ref[j * part:(j + 1) * part, :] = held[
                first:first + part, j * LANES:(j + 1) * LANES
            ]
        first += part


def blocks(x, cuts, cols, row_axis, col_axes):
    depth = sum(cuts)
    return pl.pallas_call(
        functools.partial(blocks_kernel, row_axis, col_axes),
        out_shape=[jax.ShapeDtypeStruct((cols // LANES * n, LANES), x.dtype) for n in cuts],
        in_specs=[pl.BlockSpec(memory_space=pltpu.HBM)],
        out_specs=[VMEM] * len(cuts),
        scratch_shapes=[pltpu.VMEM((depth, cols), x.dtype), pltpu.SemaphoreType.DMA],
        compiler_params=PARAMS,
    )(pltpu.with_memory_space_constraint(x, pltpu.HBM))


def pieces_kernel(at_ref, x_ref, corner_ref, near_ref):
    half, cols = corner_ref.shape
    corner_ref[...] = x_ref[rows_at(at_ref[0], half), rows_at(at_ref[1], cols)]
    near_ref[...] = x_ref[:, rows_at(at_ref[1], cols)]


def pieces(x, half, at, cols):
    depth = x.shape[0]
    return pl.pallas_call(
        pieces_kernel,
        out_shape=[jax.ShapeDtypeStruct((rows, cols), x.dtype) for rows in (depth // 2, depth)],
        in_specs=[SMEM, VMEM],
        out_specs=[VMEM, VMEM],
        compiler_params=PARAMS,
    )(index_array(half, at), x)


def lane_kernel(head_dim, core_ref, x_ref, mine_ref, theirs_ref):
    kinds, tok, _ = x_ref.shape
    for out_ref, core in ((mine_ref, core_ref[0]), (theirs_ref, 1 - core_ref[0])):
        for g in range(out_ref.shape[0]):
            cols = rows_at(2 * g + core, head_dim)
            for k in range(kinds):
                out_ref[g, k * tok:(k + 1) * tok, :] = x_ref[k, :, cols]


def lanes(x, core, head_dim):
    kinds, tok, cols = x.shape
    like = jax.ShapeDtypeStruct((cols // head_dim // 2, kinds * tok, head_dim), x.dtype)
    return pl.pallas_call(
        functools.partial(lane_kernel, head_dim),
        out_shape=(like, like),
        in_specs=[SMEM, VMEM],
        out_specs=(VMEM, VMEM),
        compiler_params=PARAMS,
    )(index_array(core), x)


def deal_kernel(place_ref, mine_ref, got_ref, *out_refs):
    quarter, core = place_ref[0] // 2, place_ref[0] % 2
    for k, out_ref in enumerate(out_refs):
        out_ref[core] = mine_ref[quarter ^ k]
        out_ref[1 - core] = got_ref[quarter ^ k]


def deal(mine, got, place):
    quarters, depth, width = mine.shape
    return pl.pallas_call(
        deal_kernel,
        out_shape=[jax.ShapeDtypeStruct((2, depth, width), mine.dtype)] * quarters,
        in_specs=[SMEM, VMEM, VMEM],
        out_specs=[VMEM] * quarters,
        compiler_params=PARAMS,
    )(place, mine, got)


def sort_kernel(place_ref, *refs):
    *in_refs, q_ref, k_ref, v_ref = refs
    tok = q_ref.shape[0] // (2 * len(in_refs))
    for i, ref in enumerate(in_refs[::-1]):
        for core in range(2):
            at = rows_at((place_ref[0] // 2 ^ i) * 2 + core, tok)
            for j, out_ref in enumerate((q_ref, k_ref, v_ref)):
                out_ref[at, :] = ref[core, j * tok:(j + 1) * tok, :]


def sort(parts, place):
    both, depth, width = parts[0].shape
    count = both * len(parts) * (depth // 3)
    return pl.pallas_call(
        sort_kernel,
        out_shape=[jax.ShapeDtypeStruct((count, width), parts[0].dtype)] * 3,
        in_specs=[SMEM] + [VMEM] * len(parts),
        out_specs=[VMEM] * 3,
        compiler_params=PARAMS,
    )(place, *parts[::-1])


def join_kernel(*refs):
    *in_refs, out_ref = refs
    first = 0
    for ref in in_refs:
        out_ref[first:first + ref.shape[0], :] = ref[...]
        first += ref.shape[0]


def join(*arrays):
    depth = sum(x.shape[0] for x in arrays)
    return pl.pallas_call(
        join_kernel,
        out_shape=jax.ShapeDtypeStruct((depth, arrays[0].shape[1]), arrays[0].dtype),
        in_specs=[VMEM] * len(arrays),
        out_specs=VMEM,
        compiler_params=PARAMS,
    )(*arrays)


def cut_kernel(x_ref, q_ref, kv_ref):
    peers, depth, _ = x_ref.shape
    tok = depth // 3
    for g in range(peers):
        q_ref[g * tok:(g + 1) * tok, :] = x_ref[g, :tok, :]
        for i in range(2):
            kv_ref[(i * peers + g) * tok:(i * peers + g + 1) * tok, :] = x_ref[
                g, (i + 1) * tok:(i + 2) * tok, :
            ]


def cut(x):
    peers, depth, width = x.shape
    count = peers * depth // 3
    return pl.pallas_call(
        cut_kernel,
        out_shape=[jax.ShapeDtypeStruct((size, width), x.dtype) for size in (count, 2 * count)],
        in_specs=[VMEM],
        out_specs=[VMEM, VMEM],
        compiler_params=PARAMS,
    )(x)


def after_kernel(*refs):
    pass


def after(passed, *first, cost=None):
    return pl.pallas_call(
        after_kernel,
        out_shape=jax.ShapeDtypeStruct(passed.shape, passed.dtype),
        in_specs=[ANY] * (1 + len(first)),
        out_specs=ANY,
        input_output_aliases={0: 0},
        compiler_params=PARAMS,
        cost_estimate=cost,
    )(passed, *first)


def clip_of(token, base, span, tok_dev, clip_ref):
    frame = base + token // span * FRB + token % tok_dev // TPF
    clip = jnp.zeros_like(token)
    for f in range(clip_ref.shape[0]):
        clip = jnp.where(frame == f, clip_ref[f], clip)
    return clip


def mask_kernel(span, tok, base_ref, clip_ref, *out_refs):
    count = out_refs[0].shape[0]
    row = lax.broadcasted_iota(jnp.int32, (count, 1), 0)
    col = lax.broadcasted_iota(jnp.int32, (1, count), 1)
    row_clip = clip_of(row, base_ref[0], span, tok, clip_ref)
    for i, out_ref in enumerate(out_refs):
        allowed = row_clip == clip_of(col, base_ref[i], span, tok, clip_ref)
        out_ref[...] = jnp.where(allowed, 0.0, -1e30)


def masks(bases, span, tok, count, frame_clip):
    return pl.pallas_call(
        functools.partial(mask_kernel, span, tok),
        out_shape=[jax.ShapeDtypeStruct((count, count), jnp.float32)] * len(bases),
        in_specs=[SMEM, SMEM],
        out_specs=[VMEM] * len(bases),
        compiler_params=PARAMS,
    )(index_array(*bases), frame_clip)


def attention_kernel(head_dim, n_mask, which, joint, q_ref, *refs):
    *refs, out_ref = refs
    mask_refs, refs = refs[:n_mask], refs[n_mask:]
    count, width = q_ref.shape
    k_refs, v_refs = [], []
    for both in joint:
        ref, *refs = refs
        if both:
            k_refs.append(ref.at[0:count])
            v_refs.append(ref.at[count:2 * count])
        else:
            value_ref, *refs = refs
            k_refs.append(ref)
            v_refs.append(value_ref)
    scale = math.log2(math.e) / math.sqrt(head_dim)
    per_step = max(1, 1024 // count)
    for h in range(width // head_dim):
        cols = slice(h * head_dim, (h + 1) * head_dim)
        queries = q_ref[:, cols]
        top = total = acc = None
        for first in range(0, len(k_refs), per_step):
            here = range(first, min(first + per_step, len(k_refs)))
            scores = []
            for i in here:
                s = lax.dot_general(
                    queries, k_refs[i][:, cols], (((1,), (1,)), ((), ())),
                    preferred_element_type=jnp.float32,
                )
                scores.append(s * scale + mask_refs[which[i]][...])
            new_top = functools.reduce(
                jnp.maximum, [jnp.max(s, axis=1, keepdims=True) for s in scores]
            )
            if top is not None:
                new_top = jnp.maximum(top, new_top)
                factor = jnp.exp2(top - new_top)
                total, acc = total * factor, acc * factor
            top = new_top
            for i, s in zip(here, scores):
                p = jnp.exp2(s - top)
                part = jnp.sum(p, axis=1, keepdims=True)
                dot = jnp.dot(
                    p.astype(jnp.bfloat16), v_refs[i][:, cols], preferred_element_type=jnp.float32
                )
                total = part if total is None else total + part
                acc = dot if acc is None else acc + dot
        out_ref[:, cols] = (acc / total).astype(out_ref.dtype)


def attention(q, kvs, mask_of, which, head_dim):
    joint = [not isinstance(kv, tuple) for kv in kvs]
    arrays = [x for kv, both in zip(kvs, joint) for x in ((kv,) if both else kv)]
    return pl.pallas_call(
        functools.partial(attention_kernel, head_dim, len(mask_of), which, joint),
        out_shape=jax.ShapeDtypeStruct(q.shape, q.dtype),
        in_specs=[VMEM] * (1 + len(mask_of) + len(arrays)),
        out_specs=VMEM,
        compiler_params=PARAMS,
    )(q, *mask_of, *arrays)


def project_kernel(n_attn, sizes, at_ref, place_ref, *refs):
    attn_refs, w_refs = refs[:n_attn], refs[n_attn:-3]
    out_ref, a_ref, w_all = refs[-3:]
    width = attn_refs[0].shape[1]
    blks, tok, cols = out_ref.shape
    blk, other = place_ref[0] // 2, 1 - place_ref[0] % 2
    for k, ref in enumerate(attn_refs):
        at = rows_at(blk ^ k, width)
        for b in range(blks):
            a_ref[b * tok:(b + 1) * tok, at] = ref[rows_at(2 * b + other, tok), :]
            a_ref[(blks + b) * tok:(blks + b + 1) * tok, at] = ref[rows_at(2 * b + 1 - other, tok), :]
    for i, (ref, (rows, first)) in enumerate(zip(w_refs, sizes)):
        at = pl.ds(pl.multiple_of(at_ref[i] * UNIT, UNIT), rows)
        if ref.shape[1] >= cols:
            w_all[at, :] = ref[:, rows_at(blk, cols)] if ref.shape[1] > cols else ref[...]
        else:
            for j in range(cols // LANES):
                w_all[at, j * LANES:(j + 1) * LANES] = ref[first + j * rows:first + (j + 1) * rows]
    dot = jnp.dot(a_ref[:blks * tok, :], w_all[...], preferred_element_type=jnp.float32)
    out_ref[...] = dot.astype(out_ref.dtype).reshape(out_ref.shape)


def rest_kernel(a_ref, w_ref, out_ref):
    blks, tok, _ = out_ref.shape
    dot = jnp.dot(a_ref[blks * tok:, :], w_ref[...], preferred_element_type=jnp.float32)
    out_ref[...] = dot.astype(out_ref.dtype).reshape(out_ref.shape)


def project(attns, w_parts, sizes, at, place, tok, cols):
    count, width = attns[0].shape
    blks, dtype = len(attns), attns[0].dtype
    like = jax.ShapeDtypeStruct((blks, tok, cols), dtype)
    theirs, a_all, w_all = pl.pallas_call(
        functools.partial(project_kernel, blks, sizes),
        out_shape=(
            like,
            jax.ShapeDtypeStruct((count, blks * width), dtype),
            jax.ShapeDtypeStruct((blks * width, cols), dtype),
        ),
        in_specs=[SMEM, SMEM] + [VMEM] * (blks + len(w_parts)),
        out_specs=(VMEM, VMEM, VMEM),
        compiler_params=PARAMS,
    )(index_array(*at), place, *attns, *w_parts)
    got = xor(theirs, ("core",), 1)
    ours = pl.pallas_call(
        rest_kernel,
        out_shape=like,
        in_specs=[VMEM, VMEM],
        out_specs=VMEM,
        compiler_params=PARAMS,
    )(a_all, w_all)
    return add(ours, got, place)


def add_kernel(place_ref, x_ref, y_ref, *out_refs):
    for k, out_ref in enumerate(out_refs):
        at = place_ref[0] // 2 ^ k
        both = x_ref[at].astype(jnp.float32) + y_ref[at].astype(jnp.float32)
        out_ref[...] = both.astype(out_ref.dtype)


def add(x, y, place):
    blks = x.shape[0]
    return pl.pallas_call(
        add_kernel,
        out_shape=[jax.ShapeDtypeStruct(x.shape[1:], x.dtype)] * blks,
        in_specs=[SMEM, VMEM, VMEM],
        out_specs=[VMEM] * blks,
        compiler_params=PARAMS,
    )(place, x, y)


def unpack_kernel(place_ref, *refs):
    *in_refs, out_ref = refs
    width = in_refs[0].shape[1]
    for k, ref in enumerate(in_refs[::-1]):
        out_ref[:, rows_at(place_ref[0] // 2 ^ k, width)] = ref[...]


def unpack(parts, place):
    tok, width = parts[0].shape
    return pl.pallas_call(
        unpack_kernel,
        out_shape=jax.ShapeDtypeStruct((tok, len(parts) * width), parts[0].dtype),
        in_specs=[SMEM] + [VMEM] * len(parts),
        out_specs=VMEM,
        compiler_params=PARAMS,
    )(place, *parts[::-1])


def xor(x, axis, by):
    size = math.prod(lax.axis_size(name) for name in axis)
    return lax.ppermute(x, axis, [(i, i ^ by) for i in range(size)])


def swap_all(parts, axis):
    return [parts[0]] + [xor(parts[m], axis, m) for m in range(1, len(parts))]


def squares(qkv, frame_clip, w_out):
    quarter = ("x", "zl")
    y, x, zh, zl, core = (lax.axis_index(n) for n in ("y", "x", "zh", "zl", "core"))
    tok, head_dim, cols = qkv.shape[1], w_out.shape[0], w_out.shape[1] // 4
    place = index_array((x * 2 + zl) * 2 + core)
    theirs = x * 2 + 1 - zl
    row, half = zh * 2 + zl, head_dim // 2

    cuts = (half - half // 4, half // 4)
    w_first, w_second = blocks(w_out, cuts, cols, "y", quarter)
    first = after(xor(w_first, ("zh",), 1), cost=AHEAD)
    w_corner, w_near = pieces(w_out, y, theirs, cols)
    kept, given = lanes(qkv, core, head_dim)
    got = xor(given, ("core",), 1)
    shared = swap_all(deal(kept, got, place), quarter)
    second = after(xor(after(w_second, got), ("zh",), 1), cost=None)
    q, k, v = sort(shared, place)
    k_far, v_far = xor(k, ("zh",), 1), xor(v, ("zh",), 1)
    near = xor(join(k, v, first, second), ("y",), 1)
    corner = xor(after(w_corner, k), ("zh", "zl"), 3)
    w_next = xor(after(w_near, k), ("zl",), 1)
    kvs = [(k, v), (k_far, v_far), near, (xor(k_far, ("y",), 1), xor(v_far, ("y",), 1))]

    bases = [y * 2 * FRB, (1 - y) * 2 * FRB]
    mask_of = masks(bases, 4 * tok, tok, 8 * tok, frame_clip)
    attn = attention(q, kvs, mask_of, [0, 0, 1, 1], head_dim)
    corner = after(corner, attn)
    corner_rest = xor(corner, ("y",), 1)
    attns = swap_all([attn] * 4, quarter)
    w_parts = [w_out, w_next, first, second, near, near, corner, corner_rest]
    tail = 2 * k.shape[0]
    sizes = [(head_dim, 0), (head_dim, 0), (cuts[0], 0), (cuts[1], 0)]
    sizes += [(cuts[0], tail), (cuts[1], tail + first.shape[0]), (half, 0), (half, 0)]
    unit = head_dim // UNIT
    at = [row * unit, (row ^ 1) * unit]
    at += [(2 * (row ^ 2) + h) * (unit // 2) + i for h in (y, 1 - y) for i in (0, cuts[0] // UNIT)]
    at += [(2 * (row ^ 3) + h) * (unit // 2) for h in (y, 1 - y)]
    parts = project(attns, w_parts, sizes, at, place, tok, cols)
    return unpack(swap_all(parts, quarter), place)


def layers(qkv, frame_clip, w_out):
    rows, blks = lax.axis_size("row"), lax.axis_size("blk")
    row, blk = lax.axis_index("row"), lax.axis_index("blk")
    tok, head_dim, cols = qkv.shape[1], w_out.shape[0], w_out.shape[1] // blks
    place = index_array(blk * 2 + lax.axis_index("core"))
    others = range(1, rows)

    (w_own,) = columns(w_out, [(head_dim, 0, blk)], cols)
    w_parts = [w_out] + [xor(w_own, ("row",), by) for by in others]
    packed = pack(qkv, 2 * blks, head_dim)
    own = lax.all_to_all(packed, ("blk", "core"), split_axis=0, concat_axis=0, tiled=True)
    q, kv = cut(own)
    kvs = [kv] + [xor(kv, ("row",), by) for by in others]
    mask_of = masks([0], 2 * tok, tok, 2 * blks * tok, frame_clip)
    attn = attention(q, kvs, mask_of, [0] * rows, head_dim)
    attns = swap_all([attn] * blks, ("blk",))
    at = [(row ^ by) * (head_dim // UNIT) for by in range(rows)]
    parts = project(attns, w_parts, [(head_dim, 0)] * rows, at, place, tok, cols)
    return unpack(swap_all(parts, ("blk",)), place)


def solution(mesh):
    blk, tile = mesh.shape["blk"], mesh.shape["tile"]
    if (blk, tile) == (4, 8):
        plan, names, shape = squares, ("y", "x", "zh", "zl", "core"), (2, 2, 2, 2, 2)
    else:
        plan, names, shape = layers, ("blk", "row", "core"), (blk, tile // 2, 2)
    fine = Mesh(mesh.devices.reshape(shape), names)
    tiles = names[2:] if plan is squares else names[1:]
    in_specs = (P(None, names, None), P(), P(tiles, None))
    return jax.shard_map(
        plan, mesh=fine, in_specs=in_specs, out_specs=P(names, None), check_vma=False
    )
```

```python
import functools
import math

import jax
import jax.numpy as jnp
from jax import lax
from jax.experimental import pallas as pl
from jax.experimental.pallas import tpu as pltpu
from jax.sharding import Mesh
from jax.sharding import PartitionSpec as P

FRB = 2
TPF = 16
LANES = 128
VMEM = pl.BlockSpec(memory_space=pltpu.VMEM)
SMEM = pl.BlockSpec(memory_space=pltpu.SMEM)
ANY = pl.BlockSpec(memory_space=pl.ANY)
PARAMS = pltpu.CompilerParams(vmem_limit_bytes=48 * 1024 * 1024)
AHEAD = pl.CostEstimate(flops=20_000_000_000, bytes_accessed=1_000_000, transcendentals=0)
SOON = pl.CostEstimate(flops=6_000_000_000, bytes_accessed=1_000_000, transcendentals=0)


def rows_at(index, size):
    return pl.ds(pl.multiple_of(index * size, size), size)


def index_array(*numbers):
    return jnp.stack([jnp.asarray(i, jnp.int32) for i in numbers])


def pack_kernel(head_dim, x_ref, out_ref):
    peers, _, width = out_ref.shape
    kinds, tok, _ = x_ref.shape
    heads = width // head_dim
    for g in range(peers):
        for i in range(heads):
            head = (g // 2 * heads + i) * 2 + g % 2
            for k in range(kinds):
                out_ref[g, k * tok:(k + 1) * tok, i * head_dim:(i + 1) * head_dim] = x_ref[
                    k, :, head * head_dim:(head + 1) * head_dim
                ]


def pack(x, peers, head_dim):
    kinds, tok, cols = x.shape
    return pl.pallas_call(
        functools.partial(pack_kernel, head_dim),
        out_shape=jax.ShapeDtypeStruct((peers, kinds * tok, cols // peers), x.dtype),
        in_specs=[VMEM],
        out_specs=VMEM,
        compiler_params=PARAMS,
    )(x)


def columns_kernel(at_ref, x_ref, *refs):
    *out_refs, sems = refs
    copies = []
    for i, ref in enumerate(out_refs):
        depth, cols = ref.shape
        piece = x_ref.at[rows_at(at_ref[2 * i], depth), rows_at(at_ref[2 * i + 1], cols)]
        copies.append(pltpu.make_async_copy(piece, ref, sems.at[i]))
    for copy in copies:
        copy.start()
    for copy in copies:
        copy.wait()


def columns(x, pieces, cols):
    return pl.pallas_call(
        columns_kernel,
        out_shape=[jax.ShapeDtypeStruct((piece[0], cols), x.dtype) for piece in pieces],
        in_specs=[SMEM, pl.BlockSpec(memory_space=pltpu.HBM)],
        out_specs=[VMEM] * len(pieces),
        scratch_shapes=[pltpu.SemaphoreType.DMA((len(pieces),))],
        compiler_params=PARAMS,
    )(
        index_array(*[i for piece in pieces for i in piece[1:]]),
        pltpu.with_memory_space_constraint(x, pltpu.HBM),
    )


def blocks_kernel(row_axis, col_axes, x_ref, out_ref, held, sem):
    depth, cols = held.shape
    col = 0
    for axis in col_axes:
        col = col * lax.axis_size(axis) + lax.axis_index(axis)
    piece = x_ref.at[rows_at(lax.axis_index(row_axis), depth), rows_at(col, cols)]
    copy = pltpu.make_async_copy(piece, held, sem)
    copy.start()
    copy.wait()
    for j in range(cols // LANES):
        out_ref[j * depth:(j + 1) * depth, :] = held[:, j * LANES:(j + 1) * LANES]


def blocks(x, depth, cols, row_axis, col_axes):
    return pl.pallas_call(
        functools.partial(blocks_kernel, row_axis, col_axes),
        out_shape=jax.ShapeDtypeStruct((cols // LANES * depth, LANES), x.dtype),
        in_specs=[pl.BlockSpec(memory_space=pltpu.HBM)],
        out_specs=VMEM,
        scratch_shapes=[pltpu.VMEM((depth, cols), x.dtype), pltpu.SemaphoreType.DMA],
        compiler_params=PARAMS,
    )(pltpu.with_memory_space_constraint(x, pltpu.HBM))


def pieces_kernel(at_ref, x_ref, corner_ref, near_ref):
    half, cols = corner_ref.shape
    corner_ref[...] = x_ref[rows_at(at_ref[0], half), rows_at(at_ref[1], cols)]
    near_ref[...] = x_ref[:, rows_at(at_ref[1], cols)]


def pieces(x, half, at, cols):
    depth = x.shape[0]
    return pl.pallas_call(
        pieces_kernel,
        out_shape=[jax.ShapeDtypeStruct((rows, cols), x.dtype) for rows in (depth // 2, depth)],
        in_specs=[SMEM, VMEM],
        out_specs=[VMEM, VMEM],
        compiler_params=PARAMS,
    )(index_array(half, at), x)


def lane_kernel(head_dim, core_ref, x_ref, mine_ref, theirs_ref):
    kinds, tok, _ = x_ref.shape
    for out_ref, core in ((mine_ref, core_ref[0]), (theirs_ref, 1 - core_ref[0])):
        for g in range(out_ref.shape[0]):
            cols = rows_at(2 * g + core, head_dim)
            for k in range(kinds):
                out_ref[g, k * tok:(k + 1) * tok, :] = x_ref[k, :, cols]


def lanes(x, core, head_dim):
    kinds, tok, cols = x.shape
    like = jax.ShapeDtypeStruct((cols // head_dim // 2, kinds * tok, head_dim), x.dtype)
    return pl.pallas_call(
        functools.partial(lane_kernel, head_dim),
        out_shape=(like, like),
        in_specs=[SMEM, VMEM],
        out_specs=(VMEM, VMEM),
        compiler_params=PARAMS,
    )(index_array(core), x)


def deal_kernel(place_ref, mine_ref, got_ref, *out_refs):
    quarter, core = place_ref[0] // 2, place_ref[0] % 2
    for k, out_ref in enumerate(out_refs):
        out_ref[core] = mine_ref[quarter ^ k]
        out_ref[1 - core] = got_ref[quarter ^ k]


def deal(mine, got, place):
    quarters, depth, width = mine.shape
    return pl.pallas_call(
        deal_kernel,
        out_shape=[jax.ShapeDtypeStruct((2, depth, width), mine.dtype)] * quarters,
        in_specs=[SMEM, VMEM, VMEM],
        out_specs=[VMEM] * quarters,
        compiler_params=PARAMS,
    )(place, mine, got)


def sort_kernel(place_ref, *refs):
    *in_refs, q_ref, kv_ref = refs
    peers = 2 * len(in_refs)
    tok = q_ref.shape[0] // peers
    for i, ref in enumerate(in_refs[::-1]):
        for core in range(2):
            at = (place_ref[0] // 2 ^ i) * 2 + core
            q_ref[rows_at(at, tok), :] = ref[core, 0:tok, :]
            for j in range(2):
                kv_ref[rows_at(at + j * peers, tok), :] = ref[
                    core, (j + 1) * tok:(j + 2) * tok, :
                ]


def sort(parts, place):
    both, depth, width = parts[0].shape
    count = both * len(parts) * (depth // 3)
    return pl.pallas_call(
        sort_kernel,
        out_shape=[
            jax.ShapeDtypeStruct((size, width), parts[0].dtype) for size in (count, 2 * count)
        ],
        in_specs=[SMEM] + [VMEM] * len(parts),
        out_specs=[VMEM] * 2,
        compiler_params=PARAMS,
    )(place, *parts[::-1])


def join_kernel(*refs):
    *in_refs, out_ref = refs
    first = 0
    for ref in in_refs:
        out_ref[first:first + ref.shape[0], :] = ref[...]
        first += ref.shape[0]


def join(*arrays):
    depth = sum(x.shape[0] for x in arrays)
    return pl.pallas_call(
        join_kernel,
        out_shape=jax.ShapeDtypeStruct((depth, arrays[0].shape[1]), arrays[0].dtype),
        in_specs=[VMEM] * len(arrays),
        out_specs=VMEM,
        compiler_params=PARAMS,
    )(*arrays)


def cut_kernel(x_ref, q_ref, kv_ref):
    peers, depth, _ = x_ref.shape
    tok = depth // 3
    for g in range(peers):
        q_ref[g * tok:(g + 1) * tok, :] = x_ref[g, :tok, :]
        for i in range(2):
            kv_ref[(i * peers + g) * tok:(i * peers + g + 1) * tok, :] = x_ref[
                g, (i + 1) * tok:(i + 2) * tok, :
            ]


def cut(x):
    peers, depth, width = x.shape
    count = peers * depth // 3
    return pl.pallas_call(
        cut_kernel,
        out_shape=[jax.ShapeDtypeStruct((size, width), x.dtype) for size in (count, 2 * count)],
        in_specs=[VMEM],
        out_specs=[VMEM, VMEM],
        compiler_params=PARAMS,
    )(x)


def after_kernel(*refs):
    pass


def after(passed, *first, cost=None):
    return pl.pallas_call(
        after_kernel,
        out_shape=jax.ShapeDtypeStruct(passed.shape, passed.dtype),
        in_specs=[ANY] * (1 + len(first)),
        out_specs=ANY,
        input_output_aliases={0: 0},
        compiler_params=PARAMS,
        cost_estimate=cost,
    )(passed, *first)


def clip_of(token, base, span, tok_dev, clip_ref):
    frame = base + token // span * FRB + token % tok_dev // TPF
    clip = jnp.zeros_like(token)
    for f in range(clip_ref.shape[0]):
        clip = jnp.where(frame == f, clip_ref[f], clip)
    return clip


def mask_kernel(span, tok, base_ref, clip_ref, *out_refs):
    count = out_refs[0].shape[0]
    row = lax.broadcasted_iota(jnp.int32, (count, 1), 0)
    col = lax.broadcasted_iota(jnp.int32, (1, count), 1)
    row_clip = clip_of(row, base_ref[0], span, tok, clip_ref)
    for i, out_ref in enumerate(out_refs):
        allowed = row_clip == clip_of(col, base_ref[i], span, tok, clip_ref)
        out_ref[...] = jnp.where(allowed, 0.0, -1e30)


def masks(bases, span, tok, count, frame_clip):
    return pl.pallas_call(
        functools.partial(mask_kernel, span, tok),
        out_shape=[jax.ShapeDtypeStruct((count, count), jnp.float32)] * len(bases),
        in_specs=[SMEM, SMEM],
        out_specs=[VMEM] * len(bases),
        compiler_params=PARAMS,
    )(index_array(*bases), frame_clip)


def attention_kernel(head_dim, n_mask, which, joint, q_ref, *refs):
    *refs, out_ref = refs
    mask_refs, refs = refs[:n_mask], refs[n_mask:]
    count, width = q_ref.shape
    k_refs, v_refs = [], []
    for both in joint:
        ref, *refs = refs
        if both:
            k_refs.append(ref.at[0:count])
            v_refs.append(ref.at[count:2 * count])
        else:
            value_ref, *refs = refs
            k_refs.append(ref)
            v_refs.append(value_ref)
    scale = math.log2(math.e) / math.sqrt(head_dim)
    per_step = max(1, 1024 // count)
    for h in range(width // head_dim):
        cols = slice(h * head_dim, (h + 1) * head_dim)
        queries = q_ref[:, cols]
        top = total = acc = None
        for first in range(0, len(k_refs), per_step):
            here = range(first, min(first + per_step, len(k_refs)))
            scores = []
            for i in here:
                s = lax.dot_general(
                    queries, k_refs[i][:, cols], (((1,), (1,)), ((), ())),
                    preferred_element_type=jnp.float32,
                )
                scores.append(s * scale + mask_refs[which[i]][...])
            new_top = functools.reduce(
                jnp.maximum, [jnp.max(s, axis=1, keepdims=True) for s in scores]
            )
            if top is not None:
                new_top = jnp.maximum(top, new_top)
                factor = jnp.exp2(top - new_top)
                total, acc = total * factor, acc * factor
            top = new_top
            for i, s in zip(here, scores):
                p = jnp.exp2(s - top)
                part = jnp.sum(p, axis=1, keepdims=True)
                dot = jnp.dot(
                    p.astype(jnp.bfloat16), v_refs[i][:, cols], preferred_element_type=jnp.float32
                )
                total = part if total is None else total + part
                acc = dot if acc is None else acc + dot
        out_ref[:, cols] = (acc / total).astype(out_ref.dtype)


def attention(q, kvs, mask_of, which, head_dim):
    joint = [not isinstance(kv, tuple) for kv in kvs]
    arrays = [x for kv, both in zip(kvs, joint) for x in ((kv,) if both else kv)]
    return pl.pallas_call(
        functools.partial(attention_kernel, head_dim, len(mask_of), which, joint),
        out_shape=jax.ShapeDtypeStruct(q.shape, q.dtype),
        in_specs=[VMEM] * (1 + len(mask_of) + len(arrays)),
        out_specs=VMEM,
        compiler_params=PARAMS,
    )(q, *mask_of, *arrays)


def project_kernel(n_attn, sizes, at_ref, place_ref, *refs):
    attn_refs, w_refs = refs[:n_attn], refs[n_attn:-3]
    out_ref, a_ref, w_all = refs[-3:]
    width = attn_refs[0].shape[1]
    blks, tok, cols = out_ref.shape
    blk, other = place_ref[0] // 2, 1 - place_ref[0] % 2
    for k, ref in enumerate(attn_refs):
        at = rows_at(blk ^ k, width)
        for b in range(blks):
            a_ref[b * tok:(b + 1) * tok, at] = ref[rows_at(2 * b + other, tok), :]
            a_ref[(blks + b) * tok:(blks + b + 1) * tok, at] = ref[rows_at(2 * b + 1 - other, tok), :]
    for i, (ref, rows) in enumerate(zip(w_refs, sizes)):
        at = rows_at(at_ref[i], rows)
        if ref.shape[1] >= cols:
            w_all[at, :] = ref[:, rows_at(blk, cols)] if ref.shape[1] > cols else ref[...]
        else:
            first = ref.shape[0] - cols // LANES * rows
            for j in range(cols // LANES):
                w_all[at, j * LANES:(j + 1) * LANES] = ref[first + j * rows:first + (j + 1) * rows]
    dot = jnp.dot(a_ref[:blks * tok, :], w_all[...], preferred_element_type=jnp.float32)
    out_ref[...] = dot.astype(out_ref.dtype).reshape(out_ref.shape)


def rest_kernel(a_ref, w_ref, out_ref):
    blks, tok, _ = out_ref.shape
    dot = jnp.dot(a_ref[blks * tok:, :], w_ref[...], preferred_element_type=jnp.float32)
    out_ref[...] = dot.astype(out_ref.dtype).reshape(out_ref.shape)


def project(attns, w_parts, sizes, at, place, tok, cols):
    count, width = attns[0].shape
    blks, dtype = len(attns), attns[0].dtype
    like = jax.ShapeDtypeStruct((blks, tok, cols), dtype)
    theirs, a_all, w_all = pl.pallas_call(
        functools.partial(project_kernel, blks, sizes),
        out_shape=(
            like,
            jax.ShapeDtypeStruct((count, blks * width), dtype),
            jax.ShapeDtypeStruct((blks * width, cols), dtype),
        ),
        in_specs=[SMEM, SMEM] + [VMEM] * (blks + len(w_parts)),
        out_specs=(VMEM, VMEM, VMEM),
        compiler_params=PARAMS,
    )(index_array(*at), place, *attns, *w_parts)
    got = xor(theirs, ("core",), 1)
    ours = pl.pallas_call(
        rest_kernel,
        out_shape=like,
        in_specs=[VMEM, VMEM],
        out_specs=VMEM,
        compiler_params=PARAMS,
    )(a_all, w_all)
    return add(ours, got, place)


def add_kernel(place_ref, x_ref, y_ref, *out_refs):
    for k, out_ref in enumerate(out_refs):
        at = place_ref[0] // 2 ^ k
        both = x_ref[at].astype(jnp.float32) + y_ref[at].astype(jnp.float32)
        out_ref[...] = both.astype(out_ref.dtype)


def add(x, y, place):
    blks = x.shape[0]
    return pl.pallas_call(
        add_kernel,
        out_shape=[jax.ShapeDtypeStruct(x.shape[1:], x.dtype)] * blks,
        in_specs=[SMEM, VMEM, VMEM],
        out_specs=[VMEM] * blks,
        compiler_params=PARAMS,
    )(place, x, y)


def unpack_kernel(place_ref, *refs):
    *in_refs, out_ref = refs
    width = in_refs[0].shape[1]
    for k, ref in enumerate(in_refs[::-1]):
        out_ref[:, rows_at(place_ref[0] // 2 ^ k, width)] = ref[...]


def unpack(parts, place):
    tok, width = parts[0].shape
    return pl.pallas_call(
        unpack_kernel,
        out_shape=jax.ShapeDtypeStruct((tok, len(parts) * width), parts[0].dtype),
        in_specs=[SMEM] + [VMEM] * len(parts),
        out_specs=VMEM,
        compiler_params=PARAMS,
    )(place, *parts[::-1])


def xor(x, axis, by):
    size = math.prod(lax.axis_size(name) for name in axis)
    return lax.ppermute(x, axis, [(i, i ^ by) for i in range(size)])


def swap_all(parts, axis):
    return [parts[0]] + [xor(parts[m], axis, m) for m in range(1, len(parts))]


def squares(qkv, frame_clip, w_out):
    quarter = ("x", "zl")
    y, x, zh, zl, core = (lax.axis_index(n) for n in ("y", "x", "zh", "zl", "core"))
    tok, head_dim, cols = qkv.shape[1], w_out.shape[0], w_out.shape[1] // 4
    place = index_array((x * 2 + zl) * 2 + core)
    theirs = x * 2 + 1 - zl
    row, half = zh * 2 + zl, head_dim // 2

    w_far = blocks(w_out, half, cols, "y", quarter)
    far = after(xor(w_far, ("zh",), 1), cost=AHEAD)
    w_corner, w_near = pieces(w_out, y, theirs, cols)
    kept, given = lanes(qkv, core, head_dim)
    shared = swap_all(deal(kept, xor(given, ("core",), 1), place), quarter)
    q, kv = sort(shared, place)
    kv_far = xor(kv, ("zh",), 1)
    near = xor(join(kv, far), ("y",), 1)
    corner = xor(after(w_corner, kv), ("zh", "zl"), 3)
    w_next = xor(after(w_near, kv), ("zl",), 1)
    kvs = [kv, kv_far, near, xor(kv_far, ("y",), 1)]

    bases = [y * 2 * FRB, (1 - y) * 2 * FRB]
    mask_of = masks(bases, 4 * tok, tok, 8 * tok, frame_clip)
    attn = attention(q, kvs, mask_of, [0, 0, 1, 1], head_dim)
    corner = after(corner, attn)
    corner_rest = xor(corner, ("y",), 1)
    attns = swap_all([attn] * 4, quarter)
    w_parts = [w_out, w_next, far, near, corner, corner_rest]
    sizes = [head_dim, head_dim, half, half, half, half]
    at = [row, row ^ 1] + [2 * (row ^ by) + h for by in (2, 3) for h in (y, 1 - y)]
    parts = project(attns, w_parts, sizes, at, place, tok, cols)
    return unpack(swap_all(parts, quarter), place)


def layers(qkv, frame_clip, w_out):
    rows, blks = lax.axis_size("row"), lax.axis_size("blk")
    row, blk = lax.axis_index("row"), lax.axis_index("blk")
    tok, head_dim, cols = qkv.shape[1], w_out.shape[0], w_out.shape[1] // blks
    place = index_array(blk * 2 + lax.axis_index("core"))
    others = range(1, rows)

    (w_own,) = columns(w_out, [(head_dim, 0, blk)], cols)
    w_parts = [w_out] + [xor(w_own, ("row",), by) for by in others]
    packed = pack(qkv, 2 * blks, head_dim)
    own = lax.all_to_all(packed, ("blk", "core"), split_axis=0, concat_axis=0, tiled=True)
    q, kv = cut(own)
    kvs = [kv] + [xor(kv, ("row",), by) for by in others]
    mask_of = masks([0], 2 * tok, tok, 2 * blks * tok, frame_clip)
    attn = attention(q, kvs, mask_of, [0] * rows, head_dim)
    attns = swap_all([attn] * blks, ("blk",))
    at = [row ^ by for by in range(rows)]
    parts = project(attns, w_parts, [head_dim] * rows, at, place, tok, cols)
    return unpack(swap_all(parts, ("blk",)), place)


def solution(mesh):
    blk, tile = mesh.shape["blk"], mesh.shape["tile"]
    if (blk, tile) == (4, 8):
        plan, names, shape = squares, ("y", "x", "zh", "zl", "core"), (2, 2, 2, 2, 2)
    else:
        plan, names, shape = layers, ("blk", "row", "core"), (blk, tile // 2, 2)
    fine = Mesh(mesh.devices.reshape(shape), names)
    tiles = names[2:] if plan is squares else names[1:]
    in_specs = (P(None, names, None), P(), P(tiles, None))
    return jax.shard_map(
        plan, mesh=fine, in_specs=in_specs, out_specs=P(names, None), check_vma=False
    )
```

```python
import functools
import math

import jax
import jax.numpy as jnp
from jax import lax
from jax.experimental import pallas as pl
from jax.experimental.pallas import tpu as pltpu
from jax.sharding import Mesh
from jax.sharding import PartitionSpec as P

FRB = 2
TPF = 16
LANES = 128
VMEM = pl.BlockSpec(memory_space=pltpu.VMEM)
SMEM = pl.BlockSpec(memory_space=pltpu.SMEM)
ANY = pl.BlockSpec(memory_space=pl.ANY)
PARAMS = pltpu.CompilerParams(vmem_limit_bytes=48 * 1024 * 1024)
AHEAD = pl.CostEstimate(flops=20_000_000_000, bytes_accessed=1_000_000, transcendentals=0)
SOON = pl.CostEstimate(flops=6_000_000_000, bytes_accessed=1_000_000, transcendentals=0)


def rows_at(index, size):
    return pl.ds(pl.multiple_of(index * size, size), size)


def index_array(*numbers):
    return jnp.stack([jnp.asarray(i, jnp.int32) for i in numbers])


def pack_kernel(head_dim, x_ref, out_ref):
    peers, _, width = out_ref.shape
    kinds, tok, _ = x_ref.shape
    heads = width // head_dim
    for g in range(peers):
        for i in range(heads):
            head = (g // 2 * heads + i) * 2 + g % 2
            for k in range(kinds):
                out_ref[g, k * tok:(k + 1) * tok, i * head_dim:(i + 1) * head_dim] = x_ref[
                    k, :, head * head_dim:(head + 1) * head_dim
                ]


def pack(x, peers, head_dim):
    kinds, tok, cols = x.shape
    return pl.pallas_call(
        functools.partial(pack_kernel, head_dim),
        out_shape=jax.ShapeDtypeStruct((peers, kinds * tok, cols // peers), x.dtype),
        in_specs=[VMEM],
        out_specs=VMEM,
        compiler_params=PARAMS,
    )(x)


def columns_kernel(at_ref, x_ref, *refs):
    *out_refs, sems = refs
    copies = []
    for i, ref in enumerate(out_refs):
        depth, cols = ref.shape
        piece = x_ref.at[rows_at(at_ref[2 * i], depth), rows_at(at_ref[2 * i + 1], cols)]
        copies.append(pltpu.make_async_copy(piece, ref, sems.at[i]))
    for copy in copies:
        copy.start()
    for copy in copies:
        copy.wait()


def columns(x, pieces, cols):
    return pl.pallas_call(
        columns_kernel,
        out_shape=[jax.ShapeDtypeStruct((piece[0], cols), x.dtype) for piece in pieces],
        in_specs=[SMEM, pl.BlockSpec(memory_space=pltpu.HBM)],
        out_specs=[VMEM] * len(pieces),
        scratch_shapes=[pltpu.SemaphoreType.DMA((len(pieces),))],
        compiler_params=PARAMS,
    )(
        index_array(*[i for piece in pieces for i in piece[1:]]),
        pltpu.with_memory_space_constraint(x, pltpu.HBM),
    )


def blocks_kernel(row_axis, col_axes, x_ref, out_ref, held, sem):
    depth, cols = held.shape
    col = 0
    for axis in col_axes:
        col = col * lax.axis_size(axis) + lax.axis_index(axis)
    piece = x_ref.at[rows_at(lax.axis_index(row_axis), depth), rows_at(col, cols)]
    copy = pltpu.make_async_copy(piece, held, sem)
    copy.start()
    copy.wait()
    for j in range(cols // LANES):
        out_ref[j * depth:(j + 1) * depth, :] = held[:, j * LANES:(j + 1) * LANES]


def blocks(x, depth, cols, row_axis, col_axes):
    return pl.pallas_call(
        functools.partial(blocks_kernel, row_axis, col_axes),
        out_shape=jax.ShapeDtypeStruct((cols // LANES * depth, LANES), x.dtype),
        in_specs=[pl.BlockSpec(memory_space=pltpu.HBM)],
        out_specs=VMEM,
        scratch_shapes=[pltpu.VMEM((depth, cols), x.dtype), pltpu.SemaphoreType.DMA],
        compiler_params=PARAMS,
    )(pltpu.with_memory_space_constraint(x, pltpu.HBM))


def pieces_kernel(at_ref, x_ref, corner_ref, near_ref, own_ref):
    half, cols = corner_ref.shape
    corner_ref[...] = x_ref[rows_at(at_ref[0], half), rows_at(at_ref[1], cols)]
    near_ref[...] = x_ref[:, rows_at(at_ref[1], cols)]
    own_ref[...] = x_ref[:, rows_at(at_ref[2], cols)]


def pieces(x, half, at, own_at, cols):
    depth = x.shape[0]
    sizes = (depth // 2, depth, depth)
    return pl.pallas_call(
        pieces_kernel,
        out_shape=[jax.ShapeDtypeStruct((rows, cols), x.dtype) for rows in sizes],
        in_specs=[SMEM, VMEM],
        out_specs=[VMEM] * 3,
        compiler_params=PARAMS,
    )(index_array(half, at, own_at), x)


def lane_kernel(head_dim, core_ref, x_ref, mine_ref, theirs_ref):
    kinds, tok, _ = x_ref.shape
    for out_ref, core in ((mine_ref, core_ref[0]), (theirs_ref, 1 - core_ref[0])):
        for g in range(out_ref.shape[0]):
            cols = rows_at(2 * g + core, head_dim)
            for k in range(kinds):
                out_ref[g, k * tok:(k + 1) * tok, :] = x_ref[k, :, cols]


def lanes(x, core, head_dim):
    kinds, tok, cols = x.shape
    like = jax.ShapeDtypeStruct((cols // head_dim // 2, kinds * tok, head_dim), x.dtype)
    return pl.pallas_call(
        functools.partial(lane_kernel, head_dim),
        out_shape=(like, like),
        in_specs=[SMEM, VMEM],
        out_specs=(VMEM, VMEM),
        compiler_params=PARAMS,
    )(index_array(core), x)


def deal_kernel(place_ref, mine_ref, got_ref, *out_refs):
    quarter, core = place_ref[0] // 2, place_ref[0] % 2
    for k, out_ref in enumerate(out_refs):
        out_ref[core] = mine_ref[quarter ^ k]
        out_ref[1 - core] = got_ref[quarter ^ k]


def deal(mine, got, place):
    quarters, depth, width = mine.shape
    return pl.pallas_call(
        deal_kernel,
        out_shape=[jax.ShapeDtypeStruct((2, depth, width), mine.dtype)] * quarters,
        in_specs=[SMEM, VMEM, VMEM],
        out_specs=[VMEM] * quarters,
        compiler_params=PARAMS,
    )(place, mine, got)


def sort_kernel(place_ref, *refs):
    *in_refs, q_ref, kv_ref = refs
    peers = 2 * len(in_refs)
    tok = q_ref.shape[0] // peers
    for i, ref in enumerate(in_refs[::-1]):
        for core in range(2):
            at = (place_ref[0] // 2 ^ i) * 2 + core
            q_ref[rows_at(at, tok), :] = ref[core, 0:tok, :]
            for j in range(2):
                kv_ref[rows_at(at + j * peers, tok), :] = ref[
                    core, (j + 1) * tok:(j + 2) * tok, :
                ]


def sort(parts, place):
    both, depth, width = parts[0].shape
    count = both * len(parts) * (depth // 3)
    return pl.pallas_call(
        sort_kernel,
        out_shape=[
            jax.ShapeDtypeStruct((size, width), parts[0].dtype) for size in (count, 2 * count)
        ],
        in_specs=[SMEM] + [VMEM] * len(parts),
        out_specs=[VMEM] * 2,
        compiler_params=PARAMS,
    )(place, *parts[::-1])


def join_kernel(*refs):
    *in_refs, out_ref = refs
    first = 0
    for ref in in_refs:
        out_ref[first:first + ref.shape[0], :] = ref[...]
        first += ref.shape[0]


def join(*arrays):
    depth = sum(x.shape[0] for x in arrays)
    return pl.pallas_call(
        join_kernel,
        out_shape=jax.ShapeDtypeStruct((depth, arrays[0].shape[1]), arrays[0].dtype),
        in_specs=[VMEM] * len(arrays),
        out_specs=VMEM,
        compiler_params=PARAMS,
    )(*arrays)


def cut_kernel(x_ref, q_ref, kv_ref):
    peers, depth, _ = x_ref.shape
    tok = depth // 3
    for g in range(peers):
        q_ref[g * tok:(g + 1) * tok, :] = x_ref[g, :tok, :]
        for i in range(2):
            kv_ref[(i * peers + g) * tok:(i * peers + g + 1) * tok, :] = x_ref[
                g, (i + 1) * tok:(i + 2) * tok, :
            ]


def cut(x):
    peers, depth, width = x.shape
    count = peers * depth // 3
    return pl.pallas_call(
        cut_kernel,
        out_shape=[jax.ShapeDtypeStruct((size, width), x.dtype) for size in (count, 2 * count)],
        in_specs=[VMEM],
        out_specs=[VMEM, VMEM],
        compiler_params=PARAMS,
    )(x)


def after_kernel(*refs):
    pass


def after(passed, *first, cost=None):
    return pl.pallas_call(
        after_kernel,
        out_shape=jax.ShapeDtypeStruct(passed.shape, passed.dtype),
        in_specs=[ANY] * (1 + len(first)),
        out_specs=ANY,
        input_output_aliases={0: 0},
        compiler_params=PARAMS,
        cost_estimate=cost,
    )(passed, *first)


def clip_of(token, base, span, tok_dev, clip_ref):
    frame = base + token // span * FRB + token % tok_dev // TPF
    clip = jnp.zeros_like(token)
    for f in range(clip_ref.shape[0]):
        clip = jnp.where(frame == f, clip_ref[f], clip)
    return clip


def mask_kernel(span, tok, base_ref, clip_ref, *out_refs):
    count = out_refs[0].shape[0]
    row = lax.broadcasted_iota(jnp.int32, (count, 1), 0)
    col = lax.broadcasted_iota(jnp.int32, (1, count), 1)
    row_clip = clip_of(row, base_ref[0], span, tok, clip_ref)
    for i, out_ref in enumerate(out_refs):
        allowed = row_clip == clip_of(col, base_ref[i], span, tok, clip_ref)
        out_ref[...] = jnp.where(allowed, 0.0, -1e30).astype(out_ref.dtype)


def masks(bases, span, tok, count, frame_clip):
    return pl.pallas_call(
        functools.partial(mask_kernel, span, tok),
        out_shape=[jax.ShapeDtypeStruct((count, count), jnp.bfloat16)] * len(bases),
        in_specs=[SMEM, SMEM],
        out_specs=[VMEM] * len(bases),
        compiler_params=PARAMS,
    )(index_array(*bases), frame_clip)


def attention_kernel(head_dim, n_mask, which, joint, q_ref, *refs):
    *refs, out_ref = refs
    mask_refs, refs = refs[:n_mask], refs[n_mask:]
    count, width = q_ref.shape
    k_refs, v_refs = [], []
    for both in joint:
        ref, *refs = refs
        if both:
            k_refs.append(ref.at[0:count])
            v_refs.append(ref.at[count:2 * count])
        else:
            value_ref, *refs = refs
            k_refs.append(ref)
            v_refs.append(value_ref)
    scale = math.log2(math.e) / math.sqrt(head_dim)
    per_step = max(1, 1024 // count)
    for h in range(width // head_dim):
        cols = slice(h * head_dim, (h + 1) * head_dim)
        queries = q_ref[:, cols]
        top = total = acc = None
        for first in range(0, len(k_refs), per_step):
            here = range(first, min(first + per_step, len(k_refs)))
            scores = []
            for i in here:
                s = lax.dot_general(
                    queries, k_refs[i][:, cols], (((1,), (1,)), ((), ())),
                    preferred_element_type=jnp.float32,
                )
                scores.append(s * scale + mask_refs[which[i]][...].astype(jnp.float32))
            new_top = functools.reduce(
                jnp.maximum, [jnp.max(s, axis=1, keepdims=True) for s in scores]
            )
            if top is not None:
                new_top = jnp.maximum(top, new_top)
                factor = jnp.exp2(top - new_top)
                total, acc = total * factor, acc * factor
            top = new_top
            for i, s in zip(here, scores):
                p = jnp.exp2(s - top)
                part = jnp.sum(p, axis=1, keepdims=True)
                dot = jnp.dot(
                    p.astype(jnp.bfloat16), v_refs[i][:, cols], preferred_element_type=jnp.float32
                )
                total = part if total is None else total + part
                acc = dot if acc is None else acc + dot
        out_ref[:, cols] = (acc / total).astype(out_ref.dtype)


def attention(q, kvs, mask_of, which, head_dim):
    joint = [not isinstance(kv, tuple) for kv in kvs]
    arrays = [x for kv, both in zip(kvs, joint) for x in ((kv,) if both else kv)]
    return pl.pallas_call(
        functools.partial(attention_kernel, head_dim, len(mask_of), which, joint),
        out_shape=jax.ShapeDtypeStruct(q.shape, q.dtype),
        in_specs=[VMEM] * (1 + len(mask_of) + len(arrays)),
        out_specs=VMEM,
        compiler_params=PARAMS,
    )(q, *mask_of, *arrays)


def project_kernel(n_attn, sizes, at_ref, place_ref, *refs):
    attn_refs, w_refs = refs[:n_attn], refs[n_attn:-3]
    out_ref, a_ref, w_all = refs[-3:]
    width = attn_refs[0].shape[1]
    blks, tok, cols = out_ref.shape
    blk, other = place_ref[0] // 2, 1 - place_ref[0] % 2
    for k, ref in enumerate(attn_refs):
        at = rows_at(blk ^ k, width)
        for b in range(blks):
            a_ref[b * tok:(b + 1) * tok, at] = ref[rows_at(2 * b + other, tok), :]
            a_ref[(blks + b) * tok:(blks + b + 1) * tok, at] = ref[rows_at(2 * b + 1 - other, tok), :]
    for i, (ref, rows) in enumerate(zip(w_refs, sizes)):
        at = rows_at(at_ref[i], rows)
        if ref.shape[1] >= cols:
            w_all[at, :] = ref[:, rows_at(blk, cols)] if ref.shape[1] > cols else ref[...]
        else:
            first = ref.shape[0] - cols // LANES * rows
            for j in range(cols // LANES):
                w_all[at, j * LANES:(j + 1) * LANES] = ref[first + j * rows:first + (j + 1) * rows]
    dot = jnp.dot(a_ref[:blks * tok, :], w_all[...], preferred_element_type=jnp.float32)
    out_ref[...] = dot.astype(out_ref.dtype).reshape(out_ref.shape)


def rest_kernel(a_ref, w_ref, out_ref):
    blks, tok, _ = out_ref.shape
    dot = jnp.dot(a_ref[blks * tok:, :], w_ref[...], preferred_element_type=jnp.float32)
    out_ref[...] = dot.astype(out_ref.dtype).reshape(out_ref.shape)


def project(attns, w_parts, sizes, at, place, tok, cols):
    count, width = attns[0].shape
    blks, dtype = len(attns), attns[0].dtype
    like = jax.ShapeDtypeStruct((blks, tok, cols), dtype)
    theirs, a_all, w_all = pl.pallas_call(
        functools.partial(project_kernel, blks, sizes),
        out_shape=(
            like,
            jax.ShapeDtypeStruct((count, blks * width), dtype),
            jax.ShapeDtypeStruct((blks * width, cols), dtype),
        ),
        in_specs=[SMEM, SMEM] + [VMEM] * (blks + len(w_parts)),
        out_specs=(VMEM, VMEM, VMEM),
        compiler_params=PARAMS,
    )(index_array(*at), place, *attns, *w_parts)
    got = xor(theirs, ("core",), 1)
    ours = pl.pallas_call(
        rest_kernel,
        out_shape=like,
        in_specs=[VMEM, VMEM],
        out_specs=VMEM,
        compiler_params=PARAMS,
    )(a_all, w_all)
    return add(ours, got, place)


def add_kernel(place_ref, x_ref, y_ref, *out_refs):
    for k, out_ref in enumerate(out_refs):
        at = place_ref[0] // 2 ^ k
        both = x_ref[at].astype(jnp.float32) + y_ref[at].astype(jnp.float32)
        out_ref[...] = both.astype(out_ref.dtype)


def add(x, y, place):
    blks = x.shape[0]
    return pl.pallas_call(
        add_kernel,
        out_shape=[jax.ShapeDtypeStruct(x.shape[1:], x.dtype)] * blks,
        in_specs=[SMEM, VMEM, VMEM],
        out_specs=[VMEM] * blks,
        compiler_params=PARAMS,
    )(place, x, y)


def unpack_kernel(place_ref, *refs):
    *in_refs, out_ref = refs
    width = in_refs[0].shape[1]
    for k, ref in enumerate(in_refs[::-1]):
        out_ref[:, rows_at(place_ref[0] // 2 ^ k, width)] = ref[...]


def unpack(parts, place):
    tok, width = parts[0].shape
    return pl.pallas_call(
        unpack_kernel,
        out_shape=jax.ShapeDtypeStruct((tok, len(parts) * width), parts[0].dtype),
        in_specs=[SMEM] + [VMEM] * len(parts),
        out_specs=VMEM,
        compiler_params=PARAMS,
    )(place, *parts[::-1])


def xor(x, axis, by):
    size = math.prod(lax.axis_size(name) for name in axis)
    return lax.ppermute(x, axis, [(i, i ^ by) for i in range(size)])


def swap_all(parts, axis):
    return [parts[0]] + [xor(parts[m], axis, m) for m in range(1, len(parts))]


def squares(qkv, frame_clip, w_out):
    quarter = ("x", "zl")
    y, x, zh, zl, core = (lax.axis_index(n) for n in ("y", "x", "zh", "zl", "core"))
    tok, head_dim, cols = qkv.shape[1], w_out.shape[0], w_out.shape[1] // 4
    place = index_array((x * 2 + zl) * 2 + core)
    mine, theirs = x * 2 + zl, x * 2 + 1 - zl
    row, half = zh * 2 + zl, head_dim // 2

    w_far = blocks(w_out, half, cols, "y", quarter)
    far = after(xor(w_far, ("zh",), 1), cost=AHEAD)
    w_corner, w_near, w_own = pieces(w_out, y, theirs, mine, cols)
    kept, given = lanes(qkv, core, head_dim)
    shared = swap_all(deal(kept, xor(given, ("core",), 1), place), quarter)
    q, kv = sort(shared, place)
    kv_far = xor(kv, ("zh",), 1)
    near = xor(join(kv, far), ("y",), 1)
    corner = xor(after(w_corner, kv), ("zh", "zl"), 3)
    w_next = xor(after(w_near, kv), ("zl",), 1)
    kvs = [kv, kv_far, near, xor(kv_far, ("y",), 1)]

    bases = [y * 2 * FRB, (1 - y) * 2 * FRB]
    mask_of = masks(bases, 4 * tok, tok, 8 * tok, frame_clip)
    attn = attention(q, kvs, mask_of, [0, 0, 1, 1], head_dim)
    corner = after(corner, attn)
    corner_rest = xor(corner, ("y",), 1)
    attns = swap_all([attn] * 4, quarter)
    w_parts = [w_own, w_next, far, near, corner, corner_rest]
    sizes = [head_dim, head_dim, half, half, half, half]
    at = [row, row ^ 1] + [2 * (row ^ by) + h for by in (2, 3) for h in (y, 1 - y)]
    parts = project(attns, w_parts, sizes, at, place, tok, cols)
    return unpack(swap_all(parts, quarter), place)


def layers(qkv, frame_clip, w_out):
    rows, blks = lax.axis_size("row"), lax.axis_size("blk")
    row, blk = lax.axis_index("row"), lax.axis_index("blk")
    tok, head_dim, cols = qkv.shape[1], w_out.shape[0], w_out.shape[1] // blks
    place = index_array(blk * 2 + lax.axis_index("core"))
    others = range(1, rows)

    (w_own,) = columns(w_out, [(head_dim, 0, blk)], cols)
    w_parts = [w_out] + [xor(w_own, ("row",), by) for by in others]
    packed = pack(qkv, 2 * blks, head_dim)
    own = lax.all_to_all(packed, ("blk", "core"), split_axis=0, concat_axis=0, tiled=True)
    q, kv = cut(own)
    kvs = [kv] + [xor(kv, ("row",), by) for by in others]
    mask_of = masks([0], 2 * tok, tok, 2 * blks * tok, frame_clip)
    attn = attention(q, kvs, mask_of, [0] * rows, head_dim)
    attns = swap_all([attn] * blks, ("blk",))
    at = [row ^ by for by in range(rows)]
    parts = project(attns, w_parts, [head_dim] * rows, at, place, tok, cols)
    return unpack(swap_all(parts, ("blk",)), place)


def solution(mesh):
    blk, tile = mesh.shape["blk"], mesh.shape["tile"]
    if (blk, tile) == (4, 8):
        plan, names, shape = squares, ("y", "x", "zh", "zl", "core"), (2, 2, 2, 2, 2)
    else:
        plan, names, shape = layers, ("blk", "row", "core"), (blk, tile // 2, 2)
    fine = Mesh(mesh.devices.reshape(shape), names)
    tiles = names[2:] if plan is squares else names[1:]
    in_specs = (P(None, names, None), P(), P(tiles, None))
    return jax.shard_map(
        plan, mesh=fine, in_specs=in_specs, out_specs=P(names, None), check_vma=False
    )
```

```python
import functools
import math

import jax
import jax.numpy as jnp
from jax import lax
from jax.experimental import pallas as pl
from jax.experimental.pallas import tpu as pltpu
from jax.sharding import Mesh
from jax.sharding import PartitionSpec as P

FRB = 2
TPF = 16
LANES = 128
VMEM = pl.BlockSpec(memory_space=pltpu.VMEM)
SMEM = pl.BlockSpec(memory_space=pltpu.SMEM)
ANY = pl.BlockSpec(memory_space=pl.ANY)
PARAMS = pltpu.CompilerParams(vmem_limit_bytes=48 * 1024 * 1024)
AHEAD = pl.CostEstimate(flops=20_000_000_000, bytes_accessed=1_000_000, transcendentals=0)
FIRST = pl.CostEstimate(flops=380_000_000, bytes_accessed=1_000, transcendentals=0)
SOON = pl.CostEstimate(flops=6_000_000_000, bytes_accessed=1_000_000, transcendentals=0)


def rows_at(index, size):
    return pl.ds(pl.multiple_of(index * size, size), size)


def index_array(*numbers):
    return jnp.stack([jnp.asarray(i, jnp.int32) for i in numbers])


def pack_kernel(head_dim, x_ref, out_ref):
    peers, _, width = out_ref.shape
    kinds, tok, _ = x_ref.shape
    heads = width // head_dim
    for g in range(peers):
        for i in range(heads):
            head = (g // 2 * heads + i) * 2 + g % 2
            for k in range(kinds):
                out_ref[g, k * tok:(k + 1) * tok, i * head_dim:(i + 1) * head_dim] = x_ref[
                    k, :, head * head_dim:(head + 1) * head_dim
                ]


def pack(x, peers, head_dim):
    kinds, tok, cols = x.shape
    return pl.pallas_call(
        functools.partial(pack_kernel, head_dim),
        out_shape=jax.ShapeDtypeStruct((peers, kinds * tok, cols // peers), x.dtype),
        in_specs=[VMEM],
        out_specs=VMEM,
        compiler_params=PARAMS,
    )(x)


def columns_kernel(at_ref, x_ref, *refs):
    *out_refs, sems = refs
    copies = []
    for i, ref in enumerate(out_refs):
        depth, cols = ref.shape
        piece = x_ref.at[rows_at(at_ref[2 * i], depth), rows_at(at_ref[2 * i + 1], cols)]
        copies.append(pltpu.make_async_copy(piece, ref, sems.at[i]))
    for copy in copies:
        copy.start()
    for copy in copies:
        copy.wait()


def columns(x, pieces, cols):
    return pl.pallas_call(
        columns_kernel,
        out_shape=[jax.ShapeDtypeStruct((piece[0], cols), x.dtype) for piece in pieces],
        in_specs=[SMEM, pl.BlockSpec(memory_space=pltpu.HBM)],
        out_specs=[VMEM] * len(pieces),
        scratch_shapes=[pltpu.SemaphoreType.DMA((len(pieces),))],
        compiler_params=PARAMS,
    )(
        index_array(*[i for piece in pieces for i in piece[1:]]),
        pltpu.with_memory_space_constraint(x, pltpu.HBM),
    )


def blocks_kernel(row_axis, col_axes, x_ref, out_ref, held, sem):
    depth, cols = held.shape
    col = 0
    for axis in col_axes:
        col = col * lax.axis_size(axis) + lax.axis_index(axis)
    piece = x_ref.at[rows_at(lax.axis_index(row_axis), depth), rows_at(col, cols)]
    copy = pltpu.make_async_copy(piece, held, sem)
    copy.start()
    copy.wait()
    for j in range(cols // LANES):
        out_ref[j * depth:(j + 1) * depth, :] = held[:, j * LANES:(j + 1) * LANES]


def blocks(x, depth, cols, row_axis, col_axes):
    return pl.pallas_call(
        functools.partial(blocks_kernel, row_axis, col_axes),
        out_shape=jax.ShapeDtypeStruct((cols // LANES * depth, LANES), x.dtype),
        in_specs=[pl.BlockSpec(memory_space=pltpu.HBM)],
        out_specs=VMEM,
        scratch_shapes=[pltpu.VMEM((depth, cols), x.dtype), pltpu.SemaphoreType.DMA],
        compiler_params=PARAMS,
    )(pltpu.with_memory_space_constraint(x, pltpu.HBM))


def pieces_kernel(at_ref, x_ref, corner_ref, near_ref, own_ref):
    half, cols = corner_ref.shape
    corner_ref[...] = x_ref[rows_at(at_ref[0], half), rows_at(at_ref[1], cols)]
    near_ref[...] = x_ref[:, rows_at(at_ref[1], cols)]
    own_ref[...] = x_ref[:, rows_at(at_ref[2], cols)]


def pieces(x, half, at, own_at, cols):
    depth = x.shape[0]
    sizes = (depth // 2, depth, depth)
    return pl.pallas_call(
        pieces_kernel,
        out_shape=[jax.ShapeDtypeStruct((rows, cols), x.dtype) for rows in sizes],
        in_specs=[SMEM, VMEM],
        out_specs=[VMEM] * 3,
        compiler_params=PARAMS,
    )(index_array(half, at, own_at), x)


def lane_kernel(head_dim, core_ref, x_ref, mine_ref, theirs_ref):
    kinds, tok, _ = x_ref.shape
    for out_ref, core in ((mine_ref, core_ref[0]), (theirs_ref, 1 - core_ref[0])):
        for g in range(out_ref.shape[0]):
            cols = rows_at(2 * g + core, head_dim)
            for k in range(kinds):
                out_ref[g, k * tok:(k + 1) * tok, :] = x_ref[k, :, cols]


def lanes(x, core, head_dim):
    kinds, tok, cols = x.shape
    like = jax.ShapeDtypeStruct((cols // head_dim // 2, kinds * tok, head_dim), x.dtype)
    return pl.pallas_call(
        functools.partial(lane_kernel, head_dim),
        out_shape=(like, like),
        in_specs=[SMEM, VMEM],
        out_specs=(VMEM, VMEM),
        compiler_params=PARAMS,
    )(index_array(core), x)


def deal_kernel(place_ref, mine_ref, got_ref, *out_refs):
    quarter, core = place_ref[0] // 2, place_ref[0] % 2
    for k, out_ref in enumerate(out_refs):
        out_ref[core] = mine_ref[quarter ^ k]
        out_ref[1 - core] = got_ref[quarter ^ k]


def deal(mine, got, place):
    quarters, depth, width = mine.shape
    return pl.pallas_call(
        deal_kernel,
        out_shape=[jax.ShapeDtypeStruct((2, depth, width), mine.dtype)] * quarters,
        in_specs=[SMEM, VMEM, VMEM],
        out_specs=[VMEM] * quarters,
        compiler_params=PARAMS,
    )(place, mine, got)


def sort_kernel(place_ref, *refs):
    *in_refs, q_ref, kv_ref = refs
    peers = 2 * len(in_refs)
    tok = q_ref.shape[0] // peers
    for i, ref in enumerate(in_refs[::-1]):
        for core in range(2):
            at = (place_ref[0] // 2 ^ i) * 2 + core
            q_ref[rows_at(at, tok), :] = ref[core, 0:tok, :]
            for j in range(2):
                kv_ref[rows_at(at + j * peers, tok), :] = ref[
                    core, (j + 1) * tok:(j + 2) * tok, :
                ]


def sort(parts, place):
    both, depth, width = parts[0].shape
    count = both * len(parts) * (depth // 3)
    return pl.pallas_call(
        sort_kernel,
        out_shape=[
            jax.ShapeDtypeStruct((size, width), parts[0].dtype) for size in (count, 2 * count)
        ],
        in_specs=[SMEM] + [VMEM] * len(parts),
        out_specs=[VMEM] * 2,
        compiler_params=PARAMS,
    )(place, *parts[::-1])


def join_kernel(*refs):
    *in_refs, out_ref = refs
    first = 0
    for ref in in_refs:
        out_ref[first:first + ref.shape[0], :] = ref[...]
        first += ref.shape[0]


def join(*arrays):
    depth = sum(x.shape[0] for x in arrays)
    return pl.pallas_call(
        join_kernel,
        out_shape=jax.ShapeDtypeStruct((depth, arrays[0].shape[1]), arrays[0].dtype),
        in_specs=[VMEM] * len(arrays),
        out_specs=VMEM,
        compiler_params=PARAMS,
    )(*arrays)


def cut_kernel(x_ref, q_ref, kv_ref):
    peers, depth, _ = x_ref.shape
    tok = depth // 3
    for g in range(peers):
        q_ref[g * tok:(g + 1) * tok, :] = x_ref[g, :tok, :]
        for i in range(2):
            kv_ref[(i * peers + g) * tok:(i * peers + g + 1) * tok, :] = x_ref[
                g, (i + 1) * tok:(i + 2) * tok, :
            ]


def cut(x):
    peers, depth, width = x.shape
    count = peers * depth // 3
    return pl.pallas_call(
        cut_kernel,
        out_shape=[jax.ShapeDtypeStruct((size, width), x.dtype) for size in (count, 2 * count)],
        in_specs=[VMEM],
        out_specs=[VMEM, VMEM],
        compiler_params=PARAMS,
    )(x)


def after_kernel(*refs):
    pass


def after(passed, *first, cost=None):
    return pl.pallas_call(
        after_kernel,
        out_shape=jax.ShapeDtypeStruct(passed.shape, passed.dtype),
        in_specs=[ANY] * (1 + len(first)),
        out_specs=ANY,
        input_output_aliases={0: 0},
        compiler_params=PARAMS,
        cost_estimate=cost,
    )(passed, *first)


def clip_of(token, base, span, tok_dev, clip_ref):
    frame = base + token // span * FRB + token % tok_dev // TPF
    clip = jnp.zeros_like(token)
    for f in range(clip_ref.shape[0]):
        clip = jnp.where(frame == f, clip_ref[f], clip)
    return clip


def mask_kernel(span, tok, base_ref, clip_ref, *out_refs):
    count = out_refs[0].shape[0]
    row = lax.broadcasted_iota(jnp.int32, (count, 1), 0)
    col = lax.broadcasted_iota(jnp.int32, (1, count), 1)
    row_clip = clip_of(row, base_ref[0], span, tok, clip_ref)
    for i, out_ref in enumerate(out_refs):
        allowed = row_clip == clip_of(col, base_ref[i], span, tok, clip_ref)
        out_ref[...] = jnp.where(allowed, 0.0, -1e30).astype(out_ref.dtype)


def masks(bases, span, tok, count, frame_clip):
    return pl.pallas_call(
        functools.partial(mask_kernel, span, tok),
        out_shape=[jax.ShapeDtypeStruct((count, count), jnp.bfloat16)] * len(bases),
        in_specs=[SMEM, SMEM],
        out_specs=[VMEM] * len(bases),
        compiler_params=PARAMS,
    )(index_array(*bases), frame_clip)


def attention_kernel(head_dim, n_mask, which, joint, q_ref, *refs):
    *refs, out_ref = refs
    mask_refs, refs = refs[:n_mask], refs[n_mask:]
    count, width = q_ref.shape
    k_refs, v_refs = [], []
    for both in joint:
        ref, *refs = refs
        if both:
            k_refs.append(ref.at[0:count])
            v_refs.append(ref.at[count:2 * count])
        else:
            value_ref, *refs = refs
            k_refs.append(ref)
            v_refs.append(value_ref)
    scale = math.log2(math.e) / math.sqrt(head_dim)
    per_step = max(1, 1024 // count)
    for h in range(width // head_dim):
        cols = slice(h * head_dim, (h + 1) * head_dim)
        queries = q_ref[:, cols]
        top = total = acc = None
        for first in range(0, len(k_refs), per_step):
            here = range(first, min(first + per_step, len(k_refs)))
            scores = []
            for i in here:
                s = lax.dot_general(
                    queries, k_refs[i][:, cols], (((1,), (1,)), ((), ())),
                    preferred_element_type=jnp.float32,
                )
                scores.append(s * scale + mask_refs[which[i]][...].astype(jnp.float32))
            new_top = functools.reduce(
                jnp.maximum, [jnp.max(s, axis=1, keepdims=True) for s in scores]
            )
            if top is not None:
                new_top = jnp.maximum(top, new_top)
                factor = jnp.exp2(top - new_top)
                total, acc = total * factor, acc * factor
            top = new_top
            for i, s in zip(here, scores):
                p = jnp.exp2(s - top)
                part = jnp.sum(p, axis=1, keepdims=True)
                dot = jnp.dot(
                    p.astype(jnp.bfloat16), v_refs[i][:, cols], preferred_element_type=jnp.float32
                )
                total = part if total is None else total + part
                acc = dot if acc is None else acc + dot
        out_ref[:, cols] = (acc / total).astype(out_ref.dtype)


def attention(q, kvs, mask_of, which, head_dim):
    joint = [not isinstance(kv, tuple) for kv in kvs]
    arrays = [x for kv, both in zip(kvs, joint) for x in ((kv,) if both else kv)]
    return pl.pallas_call(
        functools.partial(attention_kernel, head_dim, len(mask_of), which, joint),
        out_shape=jax.ShapeDtypeStruct(q.shape, q.dtype),
        in_specs=[VMEM] * (1 + len(mask_of) + len(arrays)),
        out_specs=VMEM,
        compiler_params=PARAMS,
    )(q, *mask_of, *arrays)


def project_kernel(n_attn, sizes, at_ref, place_ref, *refs):
    attn_refs, w_refs = refs[:n_attn], refs[n_attn:-3]
    out_ref, a_ref, w_all = refs[-3:]
    width = attn_refs[0].shape[1]
    blks, tok, cols = out_ref.shape
    blk, other = place_ref[0] // 2, 1 - place_ref[0] % 2
    for k, ref in enumerate(attn_refs):
        at = rows_at(blk ^ k, width)
        for b in range(blks):
            a_ref[b * tok:(b + 1) * tok, at] = ref[rows_at(2 * b + other, tok), :]
            a_ref[(blks + b) * tok:(blks + b + 1) * tok, at] = ref[rows_at(2 * b + 1 - other, tok), :]
    for i, (ref, rows) in enumerate(zip(w_refs, sizes)):
        at = rows_at(at_ref[i], rows)
        if ref.shape[1] >= cols:
            w_all[at, :] = ref[:, rows_at(blk, cols)] if ref.shape[1] > cols else ref[...]
        else:
            first = ref.shape[0] - cols // LANES * rows
            for j in range(cols // LANES):
                w_all[at, j * LANES:(j + 1) * LANES] = ref[first + j * rows:first + (j + 1) * rows]
    dot = jnp.dot(a_ref[:blks * tok, :], w_all[...], preferred_element_type=jnp.float32)
    out_ref[...] = dot.astype(out_ref.dtype).reshape(out_ref.shape)


def rest_kernel(a_ref, w_ref, out_ref):
    blks, tok, _ = out_ref.shape
    dot = jnp.dot(a_ref[blks * tok:, :], w_ref[...], preferred_element_type=jnp.float32)
    out_ref[...] = dot.astype(out_ref.dtype).reshape(out_ref.shape)


def project(attns, w_parts, sizes, at, place, tok, cols):
    count, width = attns[0].shape
    blks, dtype = len(attns), attns[0].dtype
    like = jax.ShapeDtypeStruct((blks, tok, cols), dtype)
    theirs, a_all, w_all = pl.pallas_call(
        functools.partial(project_kernel, blks, sizes),
        out_shape=(
            like,
            jax.ShapeDtypeStruct((count, blks * width), dtype),
            jax.ShapeDtypeStruct((blks * width, cols), dtype),
        ),
        in_specs=[SMEM, SMEM] + [VMEM] * (blks + len(w_parts)),
        out_specs=(VMEM, VMEM, VMEM),
        compiler_params=PARAMS,
    )(index_array(*at), place, *attns, *w_parts)
    got = xor(theirs, ("core",), 1)
    ours = pl.pallas_call(
        rest_kernel,
        out_shape=like,
        in_specs=[VMEM, VMEM],
        out_specs=VMEM,
        compiler_params=PARAMS,
    )(a_all, w_all)
    return add(ours, got, place)


def add_kernel(place_ref, x_ref, y_ref, *out_refs):
    for k, out_ref in enumerate(out_refs):
        at = place_ref[0] // 2 ^ k
        both = x_ref[at].astype(jnp.float32) + y_ref[at].astype(jnp.float32)
        out_ref[...] = both.astype(out_ref.dtype)


def add(x, y, place):
    blks = x.shape[0]
    return pl.pallas_call(
        add_kernel,
        out_shape=[jax.ShapeDtypeStruct(x.shape[1:], x.dtype)] * blks,
        in_specs=[SMEM, VMEM, VMEM],
        out_specs=[VMEM] * blks,
        compiler_params=PARAMS,
    )(place, x, y)


def unpack_kernel(place_ref, *refs):
    *in_refs, out_ref = refs
    width = in_refs[0].shape[1]
    for k, ref in enumerate(in_refs[::-1]):
        out_ref[:, rows_at(place_ref[0] // 2 ^ k, width)] = ref[...]


def unpack(parts, place):
    tok, width = parts[0].shape
    return pl.pallas_call(
        unpack_kernel,
        out_shape=jax.ShapeDtypeStruct((tok, len(parts) * width), parts[0].dtype),
        in_specs=[SMEM] + [VMEM] * len(parts),
        out_specs=VMEM,
        compiler_params=PARAMS,
    )(place, *parts[::-1])


def xor(x, axis, by):
    size = math.prod(lax.axis_size(name) for name in axis)
    return lax.ppermute(x, axis, [(i, i ^ by) for i in range(size)])


def swap_all(parts, axis):
    return [parts[0]] + [xor(parts[m], axis, m) for m in range(1, len(parts))]


def squares(qkv, frame_clip, w_out):
    quarter = ("x", "zl")
    y, x, zh, zl, core = (lax.axis_index(n) for n in ("y", "x", "zh", "zl", "core"))
    tok, head_dim, cols = qkv.shape[1], w_out.shape[0], w_out.shape[1] // 4
    place = index_array((x * 2 + zl) * 2 + core)
    mine, theirs = x * 2 + zl, x * 2 + 1 - zl
    row, half = zh * 2 + zl, head_dim // 2

    w_far = blocks(w_out, half, cols, "y", quarter)
    far = after(xor(w_far, ("zh",), 1), cost=AHEAD)
    w_corner, w_near, w_own = pieces(w_out, y, theirs, mine, cols)
    kept, given = lanes(qkv, core, head_dim)
    shared = swap_all(deal(kept, xor(given, ("core",), 1), place), quarter)
    q, kv = sort(shared, place)
    kv_far = after(xor(kv, ("zh",), 1), cost=FIRST)
    near = xor(join(kv, far), ("y",), 1)
    corner = xor(after(w_corner, kv), ("zh", "zl"), 3)
    w_next = xor(after(w_near, kv), ("zl",), 1)
    kvs = [kv, kv_far, near, xor(kv_far, ("y",), 1)]

    bases = [y * 2 * FRB, (1 - y) * 2 * FRB]
    mask_of = masks(bases, 4 * tok, tok, 8 * tok, frame_clip)
    attn = attention(q, kvs, mask_of, [0, 0, 1, 1], head_dim)
    corner = after(corner, attn)
    corner_rest = xor(corner, ("y",), 1)
    attns = swap_all([attn] * 4, quarter)
    w_parts = [w_own, w_next, far, near, corner, corner_rest]
    sizes = [head_dim, head_dim, half, half, half, half]
    at = [row, row ^ 1] + [2 * (row ^ by) + h for by in (2, 3) for h in (y, 1 - y)]
    parts = project(attns, w_parts, sizes, at, place, tok, cols)
    return unpack(swap_all(parts, quarter), place)


def layers(qkv, frame_clip, w_out):
    rows, blks = lax.axis_size("row"), lax.axis_size("blk")
    row, blk = lax.axis_index("row"), lax.axis_index("blk")
    tok, head_dim, cols = qkv.shape[1], w_out.shape[0], w_out.shape[1] // blks
    place = index_array(blk * 2 + lax.axis_index("core"))
    others = range(1, rows)

    (w_own,) = columns(w_out, [(head_dim, 0, blk)], cols)
    w_parts = [w_out] + [xor(w_own, ("row",), by) for by in others]
    packed = pack(qkv, 2 * blks, head_dim)
    own = lax.all_to_all(packed, ("blk", "core"), split_axis=0, concat_axis=0, tiled=True)
    q, kv = cut(own)
    kvs = [kv] + [xor(kv, ("row",), by) for by in others]
    mask_of = masks([0], 2 * tok, tok, 2 * blks * tok, frame_clip)
    attn = attention(q, kvs, mask_of, [0] * rows, head_dim)
    attns = swap_all([attn] * blks, ("blk",))
    at = [row ^ by for by in range(rows)]
    parts = project(attns, w_parts, [head_dim] * rows, at, place, tok, cols)
    return unpack(swap_all(parts, ("blk",)), place)


def solution(mesh):
    blk, tile = mesh.shape["blk"], mesh.shape["tile"]
    if (blk, tile) == (4, 8):
        plan, names, shape = squares, ("y", "x", "zh", "zl", "core"), (2, 2, 2, 2, 2)
    else:
        plan, names, shape = layers, ("blk", "row", "core"), (blk, tile // 2, 2)
    fine = Mesh(mesh.devices.reshape(shape), names)
    tiles = names[2:] if plan is squares else names[1:]
    in_specs = (P(None, names, None), P(), P(tiles, None))
    return jax.shard_map(
        plan, mesh=fine, in_specs=in_specs, out_specs=P(names, None), check_vma=False
    )
```

```python
import functools
import math

import jax
import jax.numpy as jnp
from jax import lax
from jax.experimental import pallas as pl
from jax.experimental.pallas import tpu as pltpu
from jax.sharding import Mesh
from jax.sharding import PartitionSpec as P

FRB = 2
TPF = 16
LANES = 128
VMEM = pl.BlockSpec(memory_space=pltpu.VMEM)
SMEM = pl.BlockSpec(memory_space=pltpu.SMEM)
ANY = pl.BlockSpec(memory_space=pl.ANY)
PARAMS = pltpu.CompilerParams(vmem_limit_bytes=48 * 1024 * 1024)
AHEAD = pl.CostEstimate(flops=20_000_000_000, bytes_accessed=1_000_000, transcendentals=0)
SOON = pl.CostEstimate(flops=6_000_000_000, bytes_accessed=1_000_000, transcendentals=0)


def rows_at(index, size):
    return pl.ds(pl.multiple_of(index * size, size), size)


def index_array(*numbers):
    return jnp.stack([jnp.asarray(i, jnp.int32) for i in numbers])


def pack_kernel(head_dim, x_ref, out_ref):
    peers, _, width = out_ref.shape
    kinds, tok, _ = x_ref.shape
    heads = width // head_dim
    for g in range(peers):
        for i in range(heads):
            head = (g // 2 * heads + i) * 2 + g % 2
            for k in range(kinds):
                out_ref[g, k * tok:(k + 1) * tok, i * head_dim:(i + 1) * head_dim] = x_ref[
                    k, :, head * head_dim:(head + 1) * head_dim
                ]


def pack(x, peers, head_dim):
    kinds, tok, cols = x.shape
    return pl.pallas_call(
        functools.partial(pack_kernel, head_dim),
        out_shape=jax.ShapeDtypeStruct((peers, kinds * tok, cols // peers), x.dtype),
        in_specs=[VMEM],
        out_specs=VMEM,
        compiler_params=PARAMS,
    )(x)


def columns_kernel(at_ref, x_ref, *refs):
    *out_refs, sems = refs
    copies = []
    for i, ref in enumerate(out_refs):
        depth, cols = ref.shape
        piece = x_ref.at[rows_at(at_ref[2 * i], depth), rows_at(at_ref[2 * i + 1], cols)]
        copies.append(pltpu.make_async_copy(piece, ref, sems.at[i]))
    for copy in copies:
        copy.start()
    for copy in copies:
        copy.wait()


def columns(x, pieces, cols):
    return pl.pallas_call(
        columns_kernel,
        out_shape=[jax.ShapeDtypeStruct((piece[0], cols), x.dtype) for piece in pieces],
        in_specs=[SMEM, pl.BlockSpec(memory_space=pltpu.HBM)],
        out_specs=[VMEM] * len(pieces),
        scratch_shapes=[pltpu.SemaphoreType.DMA((len(pieces),))],
        compiler_params=PARAMS,
    )(
        index_array(*[i for piece in pieces for i in piece[1:]]),
        pltpu.with_memory_space_constraint(x, pltpu.HBM),
    )


def blocks_kernel(row_axis, col_axes, x_ref, out_ref, held, sem):
    depth, cols = held.shape
    col = 0
    for axis in col_axes:
        col = col * lax.axis_size(axis) + lax.axis_index(axis)
    piece = x_ref.at[rows_at(lax.axis_index(row_axis), depth), rows_at(col, cols)]
    copy = pltpu.make_async_copy(piece, held, sem)
    copy.start()
    copy.wait()
    for j in range(cols // LANES):
        out_ref[j * depth:(j + 1) * depth, :] = held[:, j * LANES:(j + 1) * LANES]


def blocks(x, depth, cols, row_axis, col_axes):
    return pl.pallas_call(
        functools.partial(blocks_kernel, row_axis, col_axes),
        out_shape=jax.ShapeDtypeStruct((cols // LANES * depth, LANES), x.dtype),
        in_specs=[pl.BlockSpec(memory_space=pltpu.HBM)],
        out_specs=VMEM,
        scratch_shapes=[pltpu.VMEM((depth, cols), x.dtype), pltpu.SemaphoreType.DMA],
        compiler_params=PARAMS,
    )(pltpu.with_memory_space_constraint(x, pltpu.HBM))


def pieces_kernel(at_ref, x_ref, corner_ref, near_ref, own_ref):
    half, cols = corner_ref.shape
    corner_ref[...] = x_ref[rows_at(at_ref[0], half), rows_at(at_ref[1], cols)]
    near_ref[...] = x_ref[:, rows_at(at_ref[1], cols)]
    own_ref[...] = x_ref[:, rows_at(at_ref[2], cols)]


def pieces(x, half, at, own_at, cols):
    depth = x.shape[0]
    sizes = (depth // 2, depth, depth)
    return pl.pallas_call(
        pieces_kernel,
        out_shape=[jax.ShapeDtypeStruct((rows, cols), x.dtype) for rows in sizes],
        in_specs=[SMEM, VMEM],
        out_specs=[VMEM] * 3,
        compiler_params=PARAMS,
    )(index_array(half, at, own_at), x)


def lane_kernel(head_dim, core_ref, x_ref, mine_ref, theirs_ref):
    kinds, tok, _ = x_ref.shape
    for out_ref, core in ((mine_ref, core_ref[0]), (theirs_ref, 1 - core_ref[0])):
        for g in range(out_ref.shape[0]):
            cols = rows_at(2 * g + core, head_dim)
            for k in range(kinds):
                out_ref[g, k * tok:(k + 1) * tok, :] = x_ref[k, :, cols]


def lanes(x, core, head_dim):
    kinds, tok, cols = x.shape
    like = jax.ShapeDtypeStruct((cols // head_dim // 2, kinds * tok, head_dim), x.dtype)
    return pl.pallas_call(
        functools.partial(lane_kernel, head_dim),
        out_shape=(like, like),
        in_specs=[SMEM, VMEM],
        out_specs=(VMEM, VMEM),
        compiler_params=PARAMS,
    )(index_array(core), x)


def deal_kernel(place_ref, mine_ref, got_ref, *out_refs):
    quarter, core = place_ref[0] // 2, place_ref[0] % 2
    for k, out_ref in enumerate(out_refs):
        out_ref[core] = mine_ref[quarter ^ k]
        out_ref[1 - core] = got_ref[quarter ^ k]


def deal(mine, got, place):
    quarters, depth, width = mine.shape
    return pl.pallas_call(
        deal_kernel,
        out_shape=[jax.ShapeDtypeStruct((2, depth, width), mine.dtype)] * quarters,
        in_specs=[SMEM, VMEM, VMEM],
        out_specs=[VMEM] * quarters,
        compiler_params=PARAMS,
    )(place, mine, got)


def sort_kernel(place_ref, *refs):
    *in_refs, q_ref, kv_ref = refs
    peers = 2 * len(in_refs)
    tok = q_ref.shape[0] // peers
    for i, ref in enumerate(in_refs[::-1]):
        for core in range(2):
            at = (place_ref[0] // 2 ^ i) * 2 + core
            q_ref[rows_at(at, tok), :] = ref[core, 0:tok, :]
            for j in range(2):
                kv_ref[rows_at(at + j * peers, tok), :] = ref[
                    core, (j + 1) * tok:(j + 2) * tok, :
                ]


def sort(parts, place):
    both, depth, width = parts[0].shape
    count = both * len(parts) * (depth // 3)
    return pl.pallas_call(
        sort_kernel,
        out_shape=[
            jax.ShapeDtypeStruct((size, width), parts[0].dtype) for size in (count, 2 * count)
        ],
        in_specs=[SMEM] + [VMEM] * len(parts),
        out_specs=[VMEM] * 2,
        compiler_params=PARAMS,
    )(place, *parts[::-1])


def join_kernel(*refs):
    *in_refs, out_ref = refs
    first = 0
    for ref in in_refs:
        out_ref[first:first + ref.shape[0], :] = ref[...]
        first += ref.shape[0]


def join(*arrays):
    depth = sum(x.shape[0] for x in arrays)
    return pl.pallas_call(
        join_kernel,
        out_shape=jax.ShapeDtypeStruct((depth, arrays[0].shape[1]), arrays[0].dtype),
        in_specs=[VMEM] * len(arrays),
        out_specs=VMEM,
        compiler_params=PARAMS,
    )(*arrays)


def cut_kernel(x_ref, q_ref, kv_ref):
    peers, depth, _ = x_ref.shape
    tok = depth // 3
    for g in range(peers):
        q_ref[g * tok:(g + 1) * tok, :] = x_ref[g, :tok, :]
        for i in range(2):
            kv_ref[(i * peers + g) * tok:(i * peers + g + 1) * tok, :] = x_ref[
                g, (i + 1) * tok:(i + 2) * tok, :
            ]


def cut(x):
    peers, depth, width = x.shape
    count = peers * depth // 3
    return pl.pallas_call(
        cut_kernel,
        out_shape=[jax.ShapeDtypeStruct((size, width), x.dtype) for size in (count, 2 * count)],
        in_specs=[VMEM],
        out_specs=[VMEM, VMEM],
        compiler_params=PARAMS,
    )(x)


def after_kernel(*refs):
    pass


def after(passed, *first, cost=None):
    return pl.pallas_call(
        after_kernel,
        out_shape=jax.ShapeDtypeStruct(passed.shape, passed.dtype),
        in_specs=[ANY] * (1 + len(first)),
        out_specs=ANY,
        input_output_aliases={0: 0},
        compiler_params=PARAMS,
        cost_estimate=cost,
    )(passed, *first)


def clip_of(token, base, span, tok_dev, clip_ref):
    frame = base + token // span * FRB + token % tok_dev // TPF
    clip = jnp.zeros_like(token)
    for f in range(clip_ref.shape[0]):
        clip = jnp.where(frame == f, clip_ref[f], clip)
    return clip


def mask_kernel(span, tok, base_ref, clip_ref, *out_refs):
    count = out_refs[0].shape[0]
    row = lax.broadcasted_iota(jnp.int32, (count, 1), 0)
    col = lax.broadcasted_iota(jnp.int32, (1, count), 1)
    row_clip = clip_of(row, base_ref[0], span, tok, clip_ref)
    for i, out_ref in enumerate(out_refs):
        allowed = row_clip == clip_of(col, base_ref[i], span, tok, clip_ref)
        out_ref[...] = jnp.where(allowed, 0.0, -1e30).astype(out_ref.dtype)


def masks(bases, span, tok, count, frame_clip):
    return pl.pallas_call(
        functools.partial(mask_kernel, span, tok),
        out_shape=[jax.ShapeDtypeStruct((count, count), jnp.bfloat16)] * len(bases),
        in_specs=[SMEM, SMEM],
        out_specs=[VMEM] * len(bases),
        compiler_params=PARAMS,
    )(index_array(*bases), frame_clip)


def attention_kernel(head_dim, tok, n_mask, which, joint, place_ref, q_ref, *refs):
    *refs, out_ref = refs
    mask_refs, refs = refs[:n_mask], refs[n_mask:]
    count, width = q_ref.shape
    k_refs, v_refs = [], []
    for both in joint:
        ref, *refs = refs
        if both:
            k_refs.append(ref.at[0:count])
            v_refs.append(ref.at[count:2 * count])
        else:
            value_ref, *refs = refs
            k_refs.append(ref)
            v_refs.append(value_ref)
    scale = math.log2(math.e) / math.sqrt(head_dim)
    per_step = max(1, 1024 // count)
    for h in range(width // head_dim):
        cols = slice(h * head_dim, (h + 1) * head_dim)
        queries = q_ref[:, cols]
        top = total = acc = None
        for first in range(0, len(k_refs), per_step):
            here = range(first, min(first + per_step, len(k_refs)))
            scores = []
            for i in here:
                s = lax.dot_general(
                    queries, k_refs[i][:, cols], (((1,), (1,)), ((), ())),
                    preferred_element_type=jnp.float32,
                )
                scores.append(s * scale + mask_refs[which[i]][...].astype(jnp.float32))
            new_top = functools.reduce(
                jnp.maximum, [jnp.max(s, axis=1, keepdims=True) for s in scores]
            )
            if top is not None:
                new_top = jnp.maximum(top, new_top)
                factor = jnp.exp2(top - new_top)
                total, acc = total * factor, acc * factor
            top = new_top
            for i, s in zip(here, scores):
                p = jnp.exp2(s - top)
                part = jnp.sum(p, axis=1, keepdims=True)
                dot = jnp.dot(
                    p.astype(jnp.bfloat16), v_refs[i][:, cols], preferred_element_type=jnp.float32
                )
                total = part if total is None else total + part
                acc = dot if acc is None else acc + dot
        result = (acc / total).astype(out_ref.dtype)
        half = count // (2 * tok)
        for g in range(2 * half):
            at = (place_ref[0] % 2 ^ g % 2 ^ 1) * half + g // 2
            out_ref[rows_at(at, tok), cols] = result[g * tok:(g + 1) * tok, :]


def attention(q, kvs, mask_of, which, head_dim, place, tok):
    joint = [not isinstance(kv, tuple) for kv in kvs]
    arrays = [x for kv, both in zip(kvs, joint) for x in ((kv,) if both else kv)]
    return pl.pallas_call(
        functools.partial(attention_kernel, head_dim, tok, len(mask_of), which, joint),
        out_shape=jax.ShapeDtypeStruct(q.shape, q.dtype),
        in_specs=[SMEM] + [VMEM] * (1 + len(mask_of) + len(arrays)),
        out_specs=VMEM,
        compiler_params=PARAMS,
    )(place, q, *mask_of, *arrays)


def project_kernel(n_attn, sizes, at_ref, place_ref, *refs):
    attn_refs, w_refs = refs[:n_attn], refs[n_attn:-3]
    out_ref, a_ref, w_all = refs[-3:]
    width = attn_refs[0].shape[1]
    blks, tok, cols = out_ref.shape
    blk = place_ref[0] // 2
    for k, ref in enumerate(attn_refs):
        a_ref[:, rows_at(blk ^ k, width)] = ref[...]
    for i, (ref, rows) in enumerate(zip(w_refs, sizes)):
        at = rows_at(at_ref[i], rows)
        if ref.shape[1] >= cols:
            w_all[at, :] = ref[:, rows_at(blk, cols)] if ref.shape[1] > cols else ref[...]
        else:
            first = ref.shape[0] - cols // LANES * rows
            for j in range(cols // LANES):
                w_all[at, j * LANES:(j + 1) * LANES] = ref[first + j * rows:first + (j + 1) * rows]
    dot = jnp.dot(a_ref[:blks * tok, :], w_all[...], preferred_element_type=jnp.float32)
    out_ref[...] = dot.astype(out_ref.dtype).reshape(out_ref.shape)


def rest_kernel(a_ref, w_ref, out_ref):
    blks, tok, _ = out_ref.shape
    dot = jnp.dot(a_ref[blks * tok:, :], w_ref[...], preferred_element_type=jnp.float32)
    out_ref[...] = dot.astype(out_ref.dtype).reshape(out_ref.shape)


def project(attns, w_parts, sizes, at, place, tok, cols):
    count, width = attns[0].shape
    blks, dtype = len(attns), attns[0].dtype
    like = jax.ShapeDtypeStruct((blks, tok, cols), dtype)
    theirs, a_all, w_all = pl.pallas_call(
        functools.partial(project_kernel, blks, sizes),
        out_shape=(
            like,
            jax.ShapeDtypeStruct((count, blks * width), dtype),
            jax.ShapeDtypeStruct((blks * width, cols), dtype),
        ),
        in_specs=[SMEM, SMEM] + [VMEM] * (blks + len(w_parts)),
        out_specs=(VMEM, VMEM, VMEM),
        compiler_params=PARAMS,
    )(index_array(*at), place, *attns, *w_parts)
    got = xor(theirs, ("core",), 1)
    ours = pl.pallas_call(
        rest_kernel,
        out_shape=like,
        in_specs=[VMEM, VMEM],
        out_specs=VMEM,
        compiler_params=PARAMS,
    )(a_all, w_all)
    return add(ours, got, place)


def add_kernel(place_ref, x_ref, y_ref, *out_refs):
    for k, out_ref in enumerate(out_refs):
        at = place_ref[0] // 2 ^ k
        both = x_ref[at].astype(jnp.float32) + y_ref[at].astype(jnp.float32)
        out_ref[...] = both.astype(out_ref.dtype)


def add(x, y, place):
    blks = x.shape[0]
    return pl.pallas_call(
        add_kernel,
        out_shape=[jax.ShapeDtypeStruct(x.shape[1:], x.dtype)] * blks,
        in_specs=[SMEM, VMEM, VMEM],
        out_specs=[VMEM] * blks,
        compiler_params=PARAMS,
    )(place, x, y)


def unpack_kernel(place_ref, *refs):
    *in_refs, out_ref = refs
    width = in_refs[0].shape[1]
    for k, ref in enumerate(in_refs[::-1]):
        out_ref[:, rows_at(place_ref[0] // 2 ^ k, width)] = ref[...]


def unpack(parts, place):
    tok, width = parts[0].shape
    return pl.pallas_call(
        unpack_kernel,
        out_shape=jax.ShapeDtypeStruct((tok, len(parts) * width), parts[0].dtype),
        in_specs=[SMEM] + [VMEM] * len(parts),
        out_specs=VMEM,
        compiler_params=PARAMS,
    )(place, *parts[::-1])


def xor(x, axis, by):
    size = math.prod(lax.axis_size(name) for name in axis)
    return lax.ppermute(x, axis, [(i, i ^ by) for i in range(size)])


def swap_all(parts, axis):
    return [parts[0]] + [xor(parts[m], axis, m) for m in range(1, len(parts))]


def squares(qkv, frame_clip, w_out):
    quarter = ("x", "zl")
    y, x, zh, zl, core = (lax.axis_index(n) for n in ("y", "x", "zh", "zl", "core"))
    tok, head_dim, cols = qkv.shape[1], w_out.shape[0], w_out.shape[1] // 4
    place = index_array((x * 2 + zl) * 2 + core)
    mine, theirs = x * 2 + zl, x * 2 + 1 - zl
    row, half = zh * 2 + zl, head_dim // 2

    w_far = blocks(w_out, half, cols, "y", quarter)
    far = after(xor(w_far, ("zh",), 1), cost=AHEAD)
    w_corner, w_near, w_own = pieces(w_out, y, theirs, mine, cols)
    kept, given = lanes(qkv, core, head_dim)
    shared = swap_all(deal(kept, xor(given, ("core",), 1), place), quarter)
    q, kv = sort(shared, place)
    kv_far = xor(kv, ("zh",), 1)
    near = xor(join(kv, far), ("y",), 1)
    corner = xor(after(w_corner, kv), ("zh", "zl"), 3)
    w_next = xor(after(w_near, kv), ("zl",), 1)
    kvs = [kv, kv_far, near, xor(kv_far, ("y",), 1)]

    bases = [y * 2 * FRB, (1 - y) * 2 * FRB]
    mask_of = masks(bases, 4 * tok, tok, 8 * tok, frame_clip)
    attn = attention(q, kvs, mask_of, [0, 0, 1, 1], head_dim, place, tok)
    corner = after(corner, attn)
    corner_rest = xor(corner, ("y",), 1)
    attns = swap_all([attn] * 4, quarter)
    w_parts = [w_own, w_next, far, near, corner, corner_rest]
    sizes = [head_dim, head_dim, half, half, half, half]
    at = [row, row ^ 1] + [2 * (row ^ by) + h for by in (2, 3) for h in (y, 1 - y)]
    parts = project(attns, w_parts, sizes, at, place, tok, cols)
    return unpack(swap_all(parts, quarter), place)


def layers(qkv, frame_clip, w_out):
    rows, blks = lax.axis_size("row"), lax.axis_size("blk")
    row, blk = lax.axis_index("row"), lax.axis_index("blk")
    tok, head_dim, cols = qkv.shape[1], w_out.shape[0], w_out.shape[1] // blks
    place = index_array(blk * 2 + lax.axis_index("core"))
    others = range(1, rows)

    (w_own,) = columns(w_out, [(head_dim, 0, blk)], cols)
    w_parts = [w_out] + [xor(w_own, ("row",), by) for by in others]
    packed = pack(qkv, 2 * blks, head_dim)
    own = lax.all_to_all(packed, ("blk", "core"), split_axis=0, concat_axis=0, tiled=True)
    q, kv = cut(own)
    kvs = [kv] + [xor(kv, ("row",), by) for by in others]
    mask_of = masks([0], 2 * tok, tok, 2 * blks * tok, frame_clip)
    attn = attention(q, kvs, mask_of, [0] * rows, head_dim, place, tok)
    attns = swap_all([attn] * blks, ("blk",))
    at = [row ^ by for by in range(rows)]
    parts = project(attns, w_parts, [head_dim] * rows, at, place, tok, cols)
    return unpack(swap_all(parts, ("blk",)), place)


def solution(mesh):
    blk, tile = mesh.shape["blk"], mesh.shape["tile"]
    if (blk, tile) == (4, 8):
        plan, names, shape = squares, ("y", "x", "zh", "zl", "core"), (2, 2, 2, 2, 2)
    else:
        plan, names, shape = layers, ("blk", "row", "core"), (blk, tile // 2, 2)
    fine = Mesh(mesh.devices.reshape(shape), names)
    tiles = names[2:] if plan is squares else names[1:]
    in_specs = (P(None, names, None), P(), P(tiles, None))
    return jax.shard_map(
        plan, mesh=fine, in_specs=in_specs, out_specs=P(names, None), check_vma=False
    )
```
